32 devices in a mesh: seq: 8 (over y, x, core), chan: 4 (over z).
Axes of the slice: x: 2, y: 2, z: 4, core: 2. Of those that a mesh axis runs over, the one named last changes fastest.
Arguments:
- streams: bfloat16 [3, 1024, 4096], P(None, 'seq', 'chan'), may hold values from -6 to 6
- short_taps: float32 [3, 7, 4096], P(None, None, 'chan'), may hold values from -2.5 to 2.5
- spectrum: float32 [4096, 2, 2048], P(('chan', 'seq')), may hold values from -6 to 6
- residual: bfloat16 [1024, 4096], P('seq', 'chan'), may hold values from -6 to 6
Outputs:
- output: bfloat16 [1024, 4096], P('seq', 'chan')
The draws below stay inside these ranges and needn't reach their ends.
All inputs are finite; a program needn't handle non-finite values.
Results may differ from the reference program's by a relative error of at most 0.0056.
Values may be sent and summed in bfloat16 or wider, within the bound.
No kernel may reach another device: no remote copies, remote signals or barrier semaphores. Data moves between devices by JAX's collectives and lax.ppermute only.
A program may use at most 64 MiB of HBM per device.

```python
import jax
import jax.numpy as jnp
from jax import lax

D = 4096
TAPS = 7
SEQ_LEN = 1024
FFT_LEN = 2048


def level_of(stream_key, shape, pieces, smallest, high):
    def one(axis_at, blocks):
        draws = jax.random.uniform(jax.random.fold_in(jax.random.fold_in(stream_key, 6), axis_at), (blocks,), jnp.float32, smallest / len(pieces), high / len(pieces))
        return jnp.repeat(jnp.exp(draws), shape[axis_at] // blocks).reshape((-1,) + (1,) * (len(shape) - axis_at - 1))

    loudness = one(*pieces[0])
    for cut in pieces[1:]:
        loudness = loudness * one(*cut)
    return loudness


def noise(own_key, shape, scale, limit, cuts=(), held_as=jnp.bfloat16):
    drawn = scale * jax.random.normal(own_key, shape, jnp.float32)
    if cuts:
        drawn = drawn * level_of(own_key, shape, cuts, -0.22, 0.18)
    return jnp.clip(drawn, -limit, limit).astype(held_as)


def setup_inputs(seed: int = 0) -> dict:
    key_of = jax.random.split(jax.random.key(seed), 5)
    streams = noise(key_of[0], (3, SEQ_LEN, D), 1.0, 6.0, ((1, 8), (2, 4)))
    short_taps = noise(key_of[1], (3, TAPS, D), 0.4, 2.5, ((2, 4),), jnp.float32)
    spectrum = noise(key_of[2], (D, 2, FFT_LEN), 1.0, 6.0, ((0, 32),), jnp.float32)
    residual = noise(key_of[3], (SEQ_LEN, D), 1.0, 6.0, ((0, 8), (1, 4)))
    return {"streams": streams, "short_taps": short_taps, "spectrum": spectrum, "residual": residual}


def short_conv(stream, weights):
    span = weights.shape[0] - 1
    length_all = stream.shape[0]
    padded = jnp.pad(stream.astype(jnp.float32), ((span, 0), (0, 0)))
    total = jnp.zeros(stream.shape, jnp.float32)
    for offset in range(span + 1):
        total = total + weights[offset][None, :] * padded[span - offset:span - offset + length_all]
    return total.astype(jnp.bfloat16)


def reference(streams, short_taps, spectrum, residual):
    q_conv = short_conv(streams[0], short_taps[0])
    k_conv = short_conv(streams[1], short_taps[1])
    v_conv = short_conv(streams[2], short_taps[2])
    gated = (k_conv.astype(jnp.float32) * v_conv.astype(jnp.float32)).astype(jnp.bfloat16)
    length_all = gated.shape[0]
    width_all = gated.shape[1]
    block_width = min(width_all, 256)
    block_count = width_all // block_width

    def one_block(block_index):
        start = (block_index * block_width).astype(jnp.int32)
        column = lax.dynamic_slice_in_dim(gated, start, block_width, 1).astype(jnp.float32)
        padded = jnp.concatenate([column, jnp.zeros_like(column)], axis=0)
        freq = jnp.fft.fft(padded, axis=0)
        filt = lax.dynamic_slice_in_dim(spectrum, start, block_width, 0)
        product = freq * lax.complex(jnp.transpose(filt[:, 0, :]), jnp.transpose(filt[:, 1, :]))
        back = jnp.real(jnp.fft.ifft(product, axis=0))[:length_all]
        return back.astype(jnp.float32).astype(jnp.bfloat16)

    blocks = lax.map(one_block, jnp.arange(block_count, dtype=jnp.int32))
    filtered = jnp.transpose(blocks, (1, 0, 2)).reshape(length_all, width_all)
    resid = residual.astype(jnp.float32)
    mixed = resid + jax.nn.silu(resid) * q_conv.astype(jnp.float32) * filtered.astype(jnp.float32)
    return mixed.astype(jnp.bfloat16)
```

```python
import functools
import math

import jax
import jax.numpy as jnp
import numpy as np
from jax import lax
from jax.experimental import pallas as pl
from jax.experimental.pallas import tpu as pltpu
from jax.sharding import PartitionSpec as P

LANES = 128
TILE = 16
VMEM_LIMIT = 24 * 1024 * 1024


def passed_along(block, axis, distance):
    devices = range(lax.axis_size(axis))
    route = [(i - distance, i) for i in devices if i - distance in devices]
    return lax.ppermute(block, axis, route)


def section_sizes(length_all):
    power = length_all.bit_length() - 1
    first = (power + 2) // 3
    second = (power - first + 1) // 2
    third = power - first - second
    result = [2**first, 2**second]
    result.append(2**third)
    return result


def matmul_high(left, right):
    return jnp.dot(left, right, precision=lax.Precision.HIGHEST, preferred_element_type=jnp.float32)


def section_high(table, values):
    return jnp.einsum(
        "ka,cab->ckb",
        table,
        values,
        precision=lax.Precision.HIGHEST,
        preferred_element_type=jnp.float32,
    )


def dft_table(order, direction):
    index = jnp.arange(order, dtype=jnp.int32)
    product = index[:, None] * index[None, :] % order
    angle = direction * 2.0 * math.pi * product.astype(jnp.float32) / order
    return (jnp.cos(angle), jnp.sin(angle))


def transform(real_part, imag_part, factors, direction):
    columns, length_now = real_part.shape
    first = factors[0]
    table_cos, table_sin = dft_table(first, direction)
    if len(factors) == 1:
        real_out = matmul_high(real_part, table_cos) - matmul_high(imag_part, table_sin)
        imag_out = matmul_high(imag_part, table_cos) + matmul_high(real_part, table_sin)
        return (real_out, imag_out)
    rest = length_now // first
    real_wide = real_part.reshape(columns, first, rest)
    if imag_part is None:
        section_real = section_high(table_cos, real_wide)
        section_imag = section_high(table_sin, real_wide)
    else:
        imag_wide = imag_part.reshape(columns, first, rest)
        section_real = section_high(table_cos, real_wide) - section_high(table_sin, imag_wide)
        section_imag = section_high(table_cos, imag_wide) + section_high(table_sin, real_wide)
    outer = jnp.arange(first, dtype=jnp.int32)[:, None]
    inner = jnp.arange(rest, dtype=jnp.int32)[None, :]
    twist = (
        direction * 2.0 * math.pi * (outer * inner % length_now).astype(jnp.float32) / length_now
    )
    twist_cos = jnp.cos(twist)[None, :, :]
    twist_sin = jnp.sin(twist)[None, :, :]
    turned_real = (section_real * twist_cos - section_imag * twist_sin).reshape(
        columns * first, rest
    )
    turned_imag = (section_real * twist_sin + section_imag * twist_cos).reshape(
        columns * first, rest
    )
    real_out, imag_out = transform(turned_real, turned_imag, factors[1:], direction)
    real_out = jnp.transpose(real_out.reshape(columns, first, rest), (0, 2, 1)).reshape(
        columns, length_now
    )
    imag_out = jnp.transpose(imag_out.reshape(columns, first, rest), (0, 2, 1)).reshape(
        columns, length_now
    )
    return (real_out, imag_out)


def long_filter(gated_rows, spectrum):
    columns, length_all = gated_rows.shape
    padded = jnp.concatenate(
        [gated_rows.astype(jnp.float32), jnp.zeros((columns, length_all), jnp.float32)], axis=1
    )
    factors = section_sizes(2 * length_all)
    freq_real, freq_imag = transform(padded, None, factors, -1.0)
    spec_real = spectrum[:, 0, :]
    spec_imag = spectrum[:, 1, :]
    prod_real = freq_real * spec_real - freq_imag * spec_imag
    prod_imag = freq_real * spec_imag + freq_imag * spec_real
    back_real, back_imag = transform(prod_real, prod_imag, factors, 1.0)
    return (back_real[:, :length_all] / (2 * length_all)).astype(jnp.bfloat16)


def local_general(streams, short_taps, spectrum, residual):
    row_count = streams.shape[1]
    channels = streams.shape[2]
    span = short_taps.shape[1] - 1
    rim_rows = passed_along(streams[:, row_count - span :, :], "seq", 1)
    extended = jnp.concatenate([rim_rows, streams], axis=1)
    total = jnp.zeros((3, row_count, channels), jnp.float32)
    for offset in range(span + 1):
        total = total + short_taps[:, offset, None, :] * extended[
            :, span - offset : span - offset + row_count, :
        ].astype(jnp.float32)
    convolved = total.astype(jnp.bfloat16)
    q_conv = convolved[0]
    k_conv = convolved[1]
    v_conv = convolved[2]
    seq_devices = lax.axis_size("seq")
    owned_count = channels // seq_devices
    length_all = row_count * seq_devices
    gated = (k_conv.astype(jnp.float32) * v_conv.astype(jnp.float32)).astype(jnp.bfloat16)
    owned = lax.all_to_all(
        gated.reshape(row_count, seq_devices, owned_count),
        "seq",
        split_axis=1,
        concat_axis=0,
        tiled=True,
    )
    gated_whole = owned.reshape(length_all, owned_count)
    filtered = jnp.transpose(long_filter(jnp.transpose(gated_whole), spectrum))
    returned = lax.all_to_all(
        filtered.reshape(length_all, 1, owned_count), "seq", split_axis=0, concat_axis=1, tiled=True
    )
    filtered_local = returned.reshape(row_count, channels)
    resid = residual.astype(jnp.float32)
    mixed = resid + jax.nn.silu(resid) * q_conv.astype(jnp.float32) * filtered_local.astype(
        jnp.float32
    )
    return mixed.astype(jnp.bfloat16)


def rounded(values):
    return values.astype(jnp.bfloat16).astype(jnp.float32)


def short_conv_rolled(rows, taps):
    total = taps(0) * rows
    for offset in range(1, 7):
        total = total + taps(offset) * pltpu.roll(rows, offset, 0)
    return rounded(total)


def row_index(count):
    return lax.broadcasted_iota(jnp.int32, (count, LANES), 0)


def pack_kernel(streams_ref, taps_ref, out_ref):
    rows = streams_ref.shape[1]
    row = row_index(TILE)
    for c in range(out_ref.shape[0]):
        lanes = slice(c * LANES, (c + 1) * LANES)
        conv = []
        for s in (1, 2):
            x = streams_ref[s, :, lanes].astype(jnp.float32)
            conv.append(
                short_conv_rolled(x, lambda j, s=s: taps_ref[s, j : j + 1, lanes])
            )
            edge = jnp.where(row < 8, x[:TILE], x[rows - TILE :])
            out_ref[c, rows + (s - 1) * TILE : rows + s * TILE, :] = edge.astype(jnp.bfloat16)
        gated = conv[0] * conv[1]
        q_last = streams_ref[0, rows - TILE :, lanes].astype(jnp.float32)
        top = jnp.where(row < 6, pltpu.roll(q_last, 6, 0), gated[:TILE])
        out_ref[c, :TILE, :] = top.astype(jnp.bfloat16)
        out_ref[c, TILE:rows, :] = gated[TILE:].astype(jnp.bfloat16)


def spectrum_kernel(quarter, view_ref, out_ref):
    blocks = view_ref.shape[0] // (2 * LANES)
    length = blocks * LANES
    per = quarter // LANES
    lane = lax.broadcasted_iota(jnp.int32, (LANES, LANES), 1)
    back = (LANES - lane) % LANES

    def block(part, k):
        return view_ref[pl.ds(2 * (k % blocks) + part, LANES, stride=2 * blocks), :]

    def turned(part, k):
        flipped = jnp.take_along_axis(block(part, k), back, axis=1, mode="promise_in_bounds")
        return jnp.where(lane == 0, block(part, k + 1), flipped)

    tail = jnp.zeros((LANES, LANES), jnp.float32)
    for m in range(4):
        for part in range(2):
            sign = 1.0 if part == 0 else -1.0
            for i in range(per):
                k = 2 * per * m + i
                folded = block(part, k) + sign * turned(part, blocks - k - 1)
                weight = 1.0 / length
                if i == 0:
                    weight = jnp.where(lane == 0, 0.5 / length, 1.0 / length)
                out_ref[2 * m + part, i * LANES : (i + 1) * LANES, :] = jnp.transpose(
                    folded * weight
                )
            k = 2 * per * m + per
            folded = (block(part, k) + sign * block(part, blocks - k)) * (0.5 / length)
            tail = jnp.where(
                lane == 8 * (2 * m + part),
                jnp.broadcast_to(folded[:, 0:1], (LANES, LANES)),
                tail,
            )
    tail = jnp.transpose(tail)
    for j in range(8):
        out_ref[j, quarter : quarter + 8, :] = tail[8 * j : 8 * j + 8]


def filter_kernel(
    msg_ref, taps_ref, h_ref, high_ref, low_ref, twist_ref, out_ref, x_ref, z_ref, q_ref
):
    shards = msg_ref.shape[0]
    rows = msg_ref.shape[1] - 2 * TILE
    quarter = high_ref.shape[1]
    row = row_index(TILE)

    before = None
    for s in range(shards):
        top = msg_ref[s, :TILE, :].astype(jnp.float32)
        edges = [
            msg_ref[s, rows + i * TILE : rows + (i + 1) * TILE, :].astype(jnp.float32)
            for i in range(2)
        ]
        conv = []
        for i in range(2):
            above = jnp.zeros_like(edges[i]) if before is None else before[1][i]
            window = jnp.where(row < 8, edges[i], above)
            conv.append(
                short_conv_rolled(window, lambda j, i=i: taps_ref[1 + i, j : j + 1, :])
            )
        x_ref[s * rows : s * rows + TILE, :] = jnp.where(
            row < 6, rounded(conv[0] * conv[1]), top
        )
        x_ref[s * rows + TILE : (s + 1) * rows, :] = msg_ref[s, TILE:rows, :].astype(jnp.float32)
        if before is None:
            halo = jnp.zeros_like(top)
        else:
            halo = pltpu.roll(before[0], TILE - 6, 0)
        out_ref[s, rows : rows + TILE, :] = halo.astype(jnp.bfloat16)
        before = (top, edges)

    x = jnp.concatenate(
        [x_ref[pl.ds(a, quarter, stride=4), :].astype(jnp.bfloat16) for a in range(4)], axis=1
    )
    z_ref[...] = jnp.dot(high_ref[...], x, preferred_element_type=jnp.float32) + jnp.dot(
        low_ref[...], x, preferred_element_type=jnp.float32
    )

    def combine(real, imag, g, count):
        u = []
        for a in range(4):
            if a == 0:
                u.append((real[0], imag[0]))
                continue
            wr = jnp.broadcast_to(twist_ref[g : g + count, 2 * a : 2 * a + 1], (count, LANES))
            wi = jnp.broadcast_to(
                twist_ref[g : g + count, 2 * a + 1 : 2 * a + 2], (count, LANES)
            )
            u.append((real[a] * wr - imag[a] * wi, real[a] * wi + imag[a] * wr, wr, wi))

        def four(v, sign):
            er, ei = v[0][0] + v[2][0], v[0][1] + v[2][1]
            dr, di = v[0][0] - v[2][0], v[0][1] - v[2][1]
            pr, pi = v[1][0] + v[3][0], v[1][1] + v[3][1]
            qr, qi = v[1][0] - v[3][0], v[1][1] - v[3][1]
            if sign < 0:
                one, three = (dr + qi, di - qr), (dr - qi, di + qr)
            else:
                one, three = (dr - qi, di + qr), (dr + qi, di - qr)
            return [(er + pr, ei + pi), one, (er - pr, ei - pi), three]

        freq = four(u, -1)
        prod = []
        for m in range(4):
            hr = h_ref[2 * m, g : g + count, :]
            hi = h_ref[2 * m + 1, g : g + count, :]
            xr, xi = freq[m]
            prod.append((xr * hr - xi * hi, xr * hi + xi * hr))
        v = four(prod, 1)
        out = [v[0]]
        for a in range(1, 4):
            wr, wi = u[a][2], u[a][3]
            vr, vi = v[a]
            out.append((vr * wr + vi * wi, vi * wr - vr * wi))
        return out

    for g in range(0, quarter, TILE):
        real = [z_ref[g : g + TILE, a * LANES : (a + 1) * LANES] for a in range(4)]
        imag = [
            z_ref[quarter + g : quarter + g + TILE, a * LANES : (a + 1) * LANES] for a in range(4)
        ]
        out = combine(real, imag, g, TILE)
        for a in range(4):
            lanes = slice(a * LANES, (a + 1) * LANES)
            for part in range(2):
                high = out[a][part].astype(jnp.bfloat16)
                low = (out[a][part] - high.astype(jnp.float32)).astype(jnp.bfloat16)
                q_ref[2 * part, g : g + TILE, lanes] = high
                q_ref[2 * part + 1, g : g + TILE, lanes] = low
    real = [z_ref[2 * quarter : 2 * quarter + 8, a * LANES : (a + 1) * LANES] for a in range(4)]
    last = combine(real, [jnp.zeros_like(r) for r in real], quarter, 8)

    y = None
    for part in range(2):
        high = high_ref[part * quarter : (part + 1) * quarter, :]
        low = low_ref[part * quarter : (part + 1) * quarter, :]
        for left, right in ((high, 0), (high, 1), (low, 0)):
            term = jnp.dot(left, q_ref[2 * part + right], preferred_element_type=jnp.float32)
            y = term if y is None else y + term
    sign = 1.0 - 2.0 * (row_index(quarter) % 2).astype(jnp.float32)
    for a in range(4):
        x_ref[pl.ds(a, quarter, stride=4), :] = (
            y[:, a * LANES : (a + 1) * LANES] + sign * last[a][0][0:1, :]
        )
    for s in range(shards):
        out_ref[s, :rows, :] = x_ref[s * rows : (s + 1) * rows, :].astype(jnp.bfloat16)


def silu(values):
    return values / (1.0 + jnp.exp(-values))


def gain_kernel(q_ref, taps_ref, residual_ref, out_ref):
    for c in range(out_ref.shape[1] // LANES):
        lanes = slice(c * LANES, (c + 1) * LANES)
        conv = short_conv_rolled(
            q_ref[0, :, lanes].astype(jnp.float32), lambda j: taps_ref[0, j : j + 1, lanes]
        )
        out_ref[:, lanes] = silu(residual_ref[:, lanes].astype(jnp.float32)) * conv


def mix_kernel(msg_ref, gain_ref, residual_ref, q_ref, taps_ref, out_ref):
    rows = residual_ref.shape[0]
    row = row_index(TILE)
    for c in range(msg_ref.shape[0]):
        lanes = slice(c * LANES, (c + 1) * LANES)
        window = jnp.where(
            row < 8,
            q_ref[0, :, lanes].astype(jnp.float32),
            msg_ref[c, rows : rows + TILE, :].astype(jnp.float32),
        )
        conv = short_conv_rolled(window, lambda j: taps_ref[0, j : j + 1, lanes])
        resid = residual_ref[:TILE, lanes].astype(jnp.float32)
        gain = jnp.where(row < 6, silu(resid) * conv, gain_ref[:TILE, lanes])
        out_ref[:TILE, lanes] = (
            resid + gain * msg_ref[c, :TILE, :].astype(jnp.float32)
        ).astype(jnp.bfloat16)
        out_ref[TILE:, lanes] = (
            residual_ref[TILE:, lanes].astype(jnp.float32)
            + gain_ref[TILE:, lanes] * msg_ref[c, TILE:rows, :].astype(jnp.float32)
        ).astype(jnp.bfloat16)


def split_table(table):
    high = table.astype(jnp.bfloat16)
    low = (table - high.astype(np.float64)).astype(jnp.bfloat16)
    return high, low


def filter_tables(quarter):
    index = np.arange(quarter)
    angle = 2.0 * np.pi * (index[:, None] * index[None, :] % (2 * quarter)) / (2 * quarter)
    alternate = np.zeros((TILE, quarter))
    alternate[0] = 1.0 - 2.0 * (index % 2)
    high, low = split_table(np.concatenate([np.cos(angle), -np.sin(angle), alternate], axis=0))
    g = np.arange(quarter + 8)[:, None]
    a = np.arange(4)[None, :]
    turn = 2.0 * np.pi * (g * a) / (8 * quarter)
    twist = np.stack([np.cos(turn), -np.sin(turn)], axis=-1).reshape(quarter + 8, 8)
    return high, low, twist.astype(np.float32)


def estimate(flops, moved):
    return pl.CostEstimate(flops=flops, bytes_accessed=moved, transcendentals=0)


def local_kernels(streams, short_taps, spectrum, residual):
    rows, channels = residual.shape
    shards = lax.axis_size("seq")
    length = rows * shards
    quarter = length // 4
    params = pltpu.CompilerParams(vmem_limit_bytes=VMEM_LIMIT)
    packed = pl.pallas_call(
        pack_kernel,
        out_shape=jax.ShapeDtypeStruct((shards, rows + 2 * TILE, LANES), jnp.bfloat16),
        compiler_params=params,
        cost_estimate=estimate(1 << 23, 1 << 20),
        name="pack",
    )(streams, short_taps)
    gathered = lax.all_to_all(packed, "seq", split_axis=0, concat_axis=0, tiled=True)

    blocks = 2 * length // LANES
    view = jnp.transpose(spectrum.reshape(LANES, 2, blocks, LANES), (0, 2, 1, 3)).reshape(
        2 * blocks * LANES, LANES
    )
    folded = pl.pallas_call(
        functools.partial(spectrum_kernel, quarter),
        out_shape=jax.ShapeDtypeStruct((8, quarter + 8, LANES), jnp.float32),
        compiler_params=params,
        cost_estimate=estimate(1 << 24, 1 << 22),
        name="spectrum",
    )(view)
    own_taps = lax.dynamic_slice_in_dim(short_taps, lax.axis_index("seq") * LANES, LANES, 2)
    high, low, twist = filter_tables(quarter)
    filtered = pl.pallas_call(
        filter_kernel,
        out_shape=jax.ShapeDtypeStruct((shards, rows + TILE, LANES), jnp.bfloat16),
        scratch_shapes=[
            pltpu.VMEM((length, LANES), jnp.float32),
            pltpu.VMEM((2 * quarter + TILE, 4 * LANES), jnp.float32),
            pltpu.VMEM((4, quarter, 4 * LANES), jnp.bfloat16),
        ],
        compiler_params=params,
        cost_estimate=estimate(1 << 30, 1 << 22),
        name="filter",
    )(gathered, own_taps, folded, high, low, twist)
    returned = lax.all_to_all(filtered, "seq", split_axis=0, concat_axis=0, tiled=True)

    whole = lambda *shape: pl.BlockSpec(shape, lambda i: (0,) * len(shape))
    gain = pl.pallas_call(
        gain_kernel,
        grid=(1,),
        in_specs=[
            whole(1, rows, channels),
            whole(*short_taps.shape),
            whole(rows, channels),
        ],
        out_specs=whole(rows, channels),
        out_shape=jax.ShapeDtypeStruct((rows, channels), jnp.float32),
        compiler_params=params,
        cost_estimate=estimate(1 << 23, 1 << 20),
        name="gain",
    )(streams, short_taps, residual)
    return pl.pallas_call(
        mix_kernel,
        grid=(1,),
        in_specs=[
            whole(shards, rows + TILE, LANES),
            whole(rows, channels),
            whole(rows, channels),
            whole(1, TILE, channels),
            whole(*short_taps.shape),
        ],
        out_specs=whole(rows, channels),
        out_shape=jax.ShapeDtypeStruct((rows, channels), jnp.bfloat16),
        compiler_params=params,
        cost_estimate=estimate(1 << 20, 1 << 20),
        name="mix",
    )(returned, gain, residual, streams, short_taps)


def local(streams, short_taps, spectrum, residual):
    rows, channels = residual.shape
    shards = lax.axis_size("seq")
    length = rows * shards
    fits = (
        channels == shards * LANES
        and rows % TILE == 0
        and rows >= 2 * TILE
        and length % (4 * LANES) == 0
        and length <= 2048
        and short_taps.shape[1] == 7
    )
    if fits:
        return local_kernels(streams, short_taps, spectrum, residual)
    return local_general(streams, short_taps, spectrum, residual)


def solution(mesh):
    placed = (
        P(None, "seq", "chan"),
        P(None, None, "chan"),
        P(("chan", "seq"), None, None),
        P("seq", "chan"),
    )
    return jax.shard_map(
        local, mesh=mesh, in_specs=placed, out_specs=P("seq", "chan"), check_vma=False
    )
```

```python
import functools
import math

import jax
import jax.numpy as jnp
import numpy as np
from jax import lax
from jax.experimental import pallas as pl
from jax.experimental.pallas import tpu as pltpu
from jax.sharding import PartitionSpec as P

LANES = 128
TILE = 16
VMEM_LIMIT = 24 * 1024 * 1024


def passed_along(block, axis, distance):
    devices = range(lax.axis_size(axis))
    route = [(i - distance, i) for i in devices if i - distance in devices]
    return lax.ppermute(block, axis, route)


def section_sizes(length_all):
    power = length_all.bit_length() - 1
    first = (power + 2) // 3
    second = (power - first + 1) // 2
    third = power - first - second
    result = [2**first, 2**second]
    result.append(2**third)
    return result


def matmul_high(left, right):
    return jnp.dot(left, right, precision=lax.Precision.HIGHEST, preferred_element_type=jnp.float32)


def section_high(table, values):
    return jnp.einsum(
        "ka,cab->ckb",
        table,
        values,
        precision=lax.Precision.HIGHEST,
        preferred_element_type=jnp.float32,
    )


def dft_table(order, direction):
    index = jnp.arange(order, dtype=jnp.int32)
    product = index[:, None] * index[None, :] % order
    angle = direction * 2.0 * math.pi * product.astype(jnp.float32) / order
    return (jnp.cos(angle), jnp.sin(angle))


def transform(real_part, imag_part, factors, direction):
    columns, length_now = real_part.shape
    first = factors[0]
    table_cos, table_sin = dft_table(first, direction)
    if len(factors) == 1:
        real_out = matmul_high(real_part, table_cos) - matmul_high(imag_part, table_sin)
        imag_out = matmul_high(imag_part, table_cos) + matmul_high(real_part, table_sin)
        return (real_out, imag_out)
    rest = length_now // first
    real_wide = real_part.reshape(columns, first, rest)
    if imag_part is None:
        section_real = section_high(table_cos, real_wide)
        section_imag = section_high(table_sin, real_wide)
    else:
        imag_wide = imag_part.reshape(columns, first, rest)
        section_real = section_high(table_cos, real_wide) - section_high(table_sin, imag_wide)
        section_imag = section_high(table_cos, imag_wide) + section_high(table_sin, real_wide)
    outer = jnp.arange(first, dtype=jnp.int32)[:, None]
    inner = jnp.arange(rest, dtype=jnp.int32)[None, :]
    twist = (
        direction * 2.0 * math.pi * (outer * inner % length_now).astype(jnp.float32) / length_now
    )
    twist_cos = jnp.cos(twist)[None, :, :]
    twist_sin = jnp.sin(twist)[None, :, :]
    turned_real = (section_real * twist_cos - section_imag * twist_sin).reshape(
        columns * first, rest
    )
    turned_imag = (section_real * twist_sin + section_imag * twist_cos).reshape(
        columns * first, rest
    )
    real_out, imag_out = transform(turned_real, turned_imag, factors[1:], direction)
    real_out = jnp.transpose(real_out.reshape(columns, first, rest), (0, 2, 1)).reshape(
        columns, length_now
    )
    imag_out = jnp.transpose(imag_out.reshape(columns, first, rest), (0, 2, 1)).reshape(
        columns, length_now
    )
    return (real_out, imag_out)


def long_filter(gated_rows, spectrum):
    columns, length_all = gated_rows.shape
    padded = jnp.concatenate(
        [gated_rows.astype(jnp.float32), jnp.zeros((columns, length_all), jnp.float32)], axis=1
    )
    factors = section_sizes(2 * length_all)
    freq_real, freq_imag = transform(padded, None, factors, -1.0)
    spec_real = spectrum[:, 0, :]
    spec_imag = spectrum[:, 1, :]
    prod_real = freq_real * spec_real - freq_imag * spec_imag
    prod_imag = freq_real * spec_imag + freq_imag * spec_real
    back_real, back_imag = transform(prod_real, prod_imag, factors, 1.0)
    return (back_real[:, :length_all] / (2 * length_all)).astype(jnp.bfloat16)


def local_general(streams, short_taps, spectrum, residual):
    row_count = streams.shape[1]
    channels = streams.shape[2]
    span = short_taps.shape[1] - 1
    rim_rows = passed_along(streams[:, row_count - span :, :], "seq", 1)
    extended = jnp.concatenate([rim_rows, streams], axis=1)
    total = jnp.zeros((3, row_count, channels), jnp.float32)
    for offset in range(span + 1):
        total = total + short_taps[:, offset, None, :] * extended[
            :, span - offset : span - offset + row_count, :
        ].astype(jnp.float32)
    convolved = total.astype(jnp.bfloat16)
    q_conv = convolved[0]
    k_conv = convolved[1]
    v_conv = convolved[2]
    seq_devices = lax.axis_size("seq")
    owned_count = channels // seq_devices
    length_all = row_count * seq_devices
    gated = (k_conv.astype(jnp.float32) * v_conv.astype(jnp.float32)).astype(jnp.bfloat16)
    owned = lax.all_to_all(
        gated.reshape(row_count, seq_devices, owned_count),
        "seq",
        split_axis=1,
        concat_axis=0,
        tiled=True,
    )
    gated_whole = owned.reshape(length_all, owned_count)
    filtered = jnp.transpose(long_filter(jnp.transpose(gated_whole), spectrum))
    returned = lax.all_to_all(
        filtered.reshape(length_all, 1, owned_count), "seq", split_axis=0, concat_axis=1, tiled=True
    )
    filtered_local = returned.reshape(row_count, channels)
    resid = residual.astype(jnp.float32)
    mixed = resid + jax.nn.silu(resid) * q_conv.astype(jnp.float32) * filtered_local.astype(
        jnp.float32
    )
    return mixed.astype(jnp.bfloat16)


def rounded(values):
    return values.astype(jnp.bfloat16).astype(jnp.float32)


def short_conv_rolled(rows, taps):
    total = taps(0) * rows
    for offset in range(1, 7):
        total = total + taps(offset) * pltpu.roll(rows, offset, 0)
    return rounded(total)


def row_index(count):
    return lax.broadcasted_iota(jnp.int32, (count, LANES), 0)


def pack_kernel(streams_ref, taps_ref, place_ref, *out_refs):
    rows = streams_ref.shape[1]
    row = row_index(TILE)
    for k, out_ref in enumerate(out_refs):
        owner = place_ref[0] ^ k
        lanes = pl.ds(pl.multiple_of(owner * LANES, LANES), LANES)
        conv = []
        for s in (1, 2):
            x = streams_ref[s, :, lanes].astype(jnp.float32)
            conv.append(
                short_conv_rolled(x, lambda j, s=s: taps_ref[s, j : j + 1, lanes])
            )
            edge = jnp.where(row < 8, x[:TILE], x[rows - TILE :])
            out_ref[rows + (s - 1) * TILE : rows + s * TILE, :] = edge.astype(jnp.bfloat16)
        gated = conv[0] * conv[1]
        q_last = streams_ref[0, rows - TILE :, lanes].astype(jnp.float32)
        top = jnp.where(row < 6, pltpu.roll(q_last, 6, 0), gated[:TILE])
        out_ref[:TILE, :] = top.astype(jnp.bfloat16)
        out_ref[TILE:rows, :] = gated[TILE:].astype(jnp.bfloat16)


def spectrum_kernel(quarter, view_ref, out_ref):
    blocks = view_ref.shape[0] // (2 * LANES)
    length = blocks * LANES
    per = quarter // LANES
    lane = lax.broadcasted_iota(jnp.int32, (LANES, LANES), 1)
    back = (LANES - lane) % LANES

    def block(part, k):
        return view_ref[pl.ds(2 * (k % blocks) + part, LANES, stride=2 * blocks), :]

    def turned(part, k):
        flipped = jnp.take_along_axis(block(part, k), back, axis=1, mode="promise_in_bounds")
        return jnp.where(lane == 0, block(part, k + 1), flipped)

    tail = jnp.zeros((LANES, LANES), jnp.float32)
    for m in range(4):
        for part in range(2):
            sign = 1.0 if part == 0 else -1.0
            for i in range(per):
                k = 2 * per * m + i
                folded = block(part, k) + sign * turned(part, blocks - k - 1)
                weight = 1.0 / length
                if i == 0:
                    weight = jnp.where(lane == 0, 0.5 / length, 1.0 / length)
                out_ref[2 * m + part, i * LANES : (i + 1) * LANES, :] = jnp.transpose(
                    folded * weight
                )
            k = 2 * per * m + per
            folded = (block(part, k) + sign * block(part, blocks - k)) * (0.5 / length)
            tail = jnp.where(
                lane == 8 * (2 * m + part),
                jnp.broadcast_to(folded[:, 0:1], (LANES, LANES)),
                tail,
            )
    tail = jnp.transpose(tail)
    for j in range(8):
        out_ref[j, quarter : quarter + 8, :] = tail[8 * j : 8 * j + 8]


def filter_kernel(shards, place_ref, *refs):
    parts, refs = refs[:shards], refs[shards:]
    (taps_ref, h_ref, high_ref, low_ref, twist_ref), refs = refs[:5], refs[5:]
    outs, (msg_ref, x_ref, z_ref, q_ref) = refs[:shards], refs[shards:]
    rows = parts[0].shape[0] - 2 * TILE
    for k in range(shards):
        msg_ref[place_ref[0] ^ k] = parts[k][...]
    quarter = high_ref.shape[1]
    row = row_index(TILE)

    before = None
    for s in range(shards):
        top = msg_ref[s, :TILE, :].astype(jnp.float32)
        edges = [
            msg_ref[s, rows + i * TILE : rows + (i + 1) * TILE, :].astype(jnp.float32)
            for i in range(2)
        ]
        conv = []
        for i in range(2):
            above = jnp.zeros_like(edges[i]) if before is None else before[1][i]
            window = jnp.where(row < 8, edges[i], above)
            conv.append(
                short_conv_rolled(window, lambda j, i=i: taps_ref[1 + i, j : j + 1, :])
            )
        x_ref[s * rows : s * rows + TILE, :] = jnp.where(
            row < 6, rounded(conv[0] * conv[1]), top
        )
        x_ref[s * rows + TILE : (s + 1) * rows, :] = msg_ref[s, TILE:rows, :].astype(jnp.float32)
        if before is None:
            halo = jnp.zeros_like(top)
        else:
            halo = pltpu.roll(before[0], TILE - 6, 0)
        msg_ref[s, rows : rows + TILE, :] = halo.astype(jnp.bfloat16)
        before = (top, edges)

    x = jnp.concatenate(
        [x_ref[pl.ds(a, quarter, stride=4), :].astype(jnp.bfloat16) for a in range(4)], axis=1
    )
    z_ref[...] = jnp.dot(high_ref[...], x, preferred_element_type=jnp.float32) + jnp.dot(
        low_ref[...], x, preferred_element_type=jnp.float32
    )

    def combine(real, imag, g, count):
        u = []
        for a in range(4):
            if a == 0:
                u.append((real[0], imag[0]))
                continue
            wr = jnp.broadcast_to(twist_ref[g : g + count, 2 * a : 2 * a + 1], (count, LANES))
            wi = jnp.broadcast_to(
                twist_ref[g : g + count, 2 * a + 1 : 2 * a + 2], (count, LANES)
            )
            u.append((real[a] * wr - imag[a] * wi, real[a] * wi + imag[a] * wr, wr, wi))

        def four(v, sign):
            er, ei = v[0][0] + v[2][0], v[0][1] + v[2][1]
            dr, di = v[0][0] - v[2][0], v[0][1] - v[2][1]
            pr, pi = v[1][0] + v[3][0], v[1][1] + v[3][1]
            qr, qi = v[1][0] - v[3][0], v[1][1] - v[3][1]
            if sign < 0:
                one, three = (dr + qi, di - qr), (dr - qi, di + qr)
            else:
                one, three = (dr - qi, di + qr), (dr + qi, di - qr)
            return [(er + pr, ei + pi), one, (er - pr, ei - pi), three]

        freq = four(u, -1)
        prod = []
        for m in range(4):
            hr = h_ref[2 * m, g : g + count, :]
            hi = h_ref[2 * m + 1, g : g + count, :]
            xr, xi = freq[m]
            prod.append((xr * hr - xi * hi, xr * hi + xi * hr))
        v = four(prod, 1)
        out = [v[0]]
        for a in range(1, 4):
            wr, wi = u[a][2], u[a][3]
            vr, vi = v[a]
            out.append((vr * wr + vi * wi, vi * wr - vr * wi))
        return out

    for g in range(0, quarter, TILE):
        real = [z_ref[g : g + TILE, a * LANES : (a + 1) * LANES] for a in range(4)]
        imag = [
            z_ref[quarter + g : quarter + g + TILE, a * LANES : (a + 1) * LANES] for a in range(4)
        ]
        out = combine(real, imag, g, TILE)
        for a in range(4):
            lanes = slice(a * LANES, (a + 1) * LANES)
            for part in range(2):
                high = out[a][part].astype(jnp.bfloat16)
                low = (out[a][part] - high.astype(jnp.float32)).astype(jnp.bfloat16)
                q_ref[2 * part, g : g + TILE, lanes] = high
                q_ref[2 * part + 1, g : g + TILE, lanes] = low
    real = [z_ref[2 * quarter : 2 * quarter + 8, a * LANES : (a + 1) * LANES] for a in range(4)]
    last = combine(real, [jnp.zeros_like(r) for r in real], quarter, 8)

    y = None
    for part in range(2):
        high = high_ref[part * quarter : (part + 1) * quarter, :]
        low = low_ref[part * quarter : (part + 1) * quarter, :]
        for left, right in ((high, 0), (high, 1), (low, 0)):
            term = jnp.dot(left, q_ref[2 * part + right], preferred_element_type=jnp.float32)
            y = term if y is None else y + term
    sign = 1.0 - 2.0 * (row_index(quarter) % 2).astype(jnp.float32)
    for a in range(4):
        x_ref[pl.ds(a, quarter, stride=4), :] = (
            y[:, a * LANES : (a + 1) * LANES] + sign * last[a][0][0:1, :]
        )
    for k in range(shards):
        target = place_ref[0] ^ k
        start = pl.multiple_of(target * rows, rows)
        outs[k][:rows, :] = x_ref[pl.ds(start, rows), :].astype(jnp.bfloat16)
        outs[k][rows:, :] = msg_ref[target, rows : rows + TILE, :]


def silu(values):
    return values / (1.0 + jnp.exp(-values))


def gain_kernel(q_ref, taps_ref, residual_ref, out_ref):
    for c in range(out_ref.shape[1] // LANES):
        lanes = slice(c * LANES, (c + 1) * LANES)
        conv = short_conv_rolled(
            q_ref[0, :, lanes].astype(jnp.float32), lambda j: taps_ref[0, j : j + 1, lanes]
        )
        out_ref[:, lanes] = silu(residual_ref[:, lanes].astype(jnp.float32)) * conv


def mix_kernel(shards, place_ref, *refs):
    parts, (gain_ref, residual_ref, q_ref, taps_ref, out_ref) = refs[:shards], refs[shards:]
    rows = residual_ref.shape[0]
    row = row_index(TILE)
    for k, msg_ref in enumerate(parts):
        owner = place_ref[0] ^ k
        lanes = pl.ds(pl.multiple_of(owner * LANES, LANES), LANES)
        window = jnp.where(
            row < 8,
            q_ref[0, :, lanes].astype(jnp.float32),
            msg_ref[rows : rows + TILE, :].astype(jnp.float32),
        )
        conv = short_conv_rolled(window, lambda j: taps_ref[0, j : j + 1, lanes])
        resid = residual_ref[:TILE, lanes].astype(jnp.float32)
        gain = jnp.where(row < 6, silu(resid) * conv, gain_ref[:TILE, lanes])
        out_ref[:TILE, lanes] = (
            resid + gain * msg_ref[:TILE, :].astype(jnp.float32)
        ).astype(jnp.bfloat16)
        out_ref[TILE:, lanes] = (
            residual_ref[TILE:, lanes].astype(jnp.float32)
            + gain_ref[TILE:, lanes] * msg_ref[TILE:rows, :].astype(jnp.float32)
        ).astype(jnp.bfloat16)


def split_table(table):
    high = table.astype(jnp.bfloat16)
    low = (table - high.astype(np.float64)).astype(jnp.bfloat16)
    return high, low


def filter_tables(quarter):
    index = np.arange(quarter)
    angle = 2.0 * np.pi * (index[:, None] * index[None, :] % (2 * quarter)) / (2 * quarter)
    alternate = np.zeros((TILE, quarter))
    alternate[0] = 1.0 - 2.0 * (index % 2)
    high, low = split_table(np.concatenate([np.cos(angle), -np.sin(angle), alternate], axis=0))
    g = np.arange(quarter + 8)[:, None]
    a = np.arange(4)[None, :]
    turn = 2.0 * np.pi * (g * a) / (8 * quarter)
    twist = np.stack([np.cos(turn), -np.sin(turn)], axis=-1).reshape(quarter + 8, 8)
    return high, low, twist.astype(np.float32)


def estimate(flops, moved):
    return pl.CostEstimate(flops=flops, bytes_accessed=moved, transcendentals=0)


def exchanged(blocks):
    count = len(blocks)
    result = list(blocks)
    for k in sorted(range(1, count), key=lambda k: -bin(k >> 1).count("1")):
        result[k] = lax.ppermute(blocks[k], "seq", [(i, i ^ k) for i in range(count)])
    return result


def local_kernels(streams, short_taps, spectrum, residual):
    rows, channels = residual.shape
    shards = lax.axis_size("seq")
    length = rows * shards
    quarter = length // 4
    params = pltpu.CompilerParams(vmem_limit_bytes=VMEM_LIMIT)
    place = lax.axis_index("seq").astype(jnp.int32).reshape(1)
    scalar = pl.BlockSpec(memory_space=pltpu.SMEM)
    vector = pl.BlockSpec(memory_space=pltpu.VMEM)
    packed = pl.pallas_call(
        pack_kernel,
        in_specs=[vector, vector, scalar],
        out_shape=[jax.ShapeDtypeStruct((rows + 2 * TILE, LANES), jnp.bfloat16)] * shards,
        compiler_params=params,
        cost_estimate=estimate(1 << 23, 1 << 20),
        name="pack",
    )(streams, short_taps, place)
    gathered = exchanged(packed)

    blocks = 2 * length // LANES
    view = jnp.transpose(spectrum.reshape(LANES, 2, blocks, LANES), (0, 2, 1, 3)).reshape(
        2 * blocks * LANES, LANES
    )
    folded = pl.pallas_call(
        functools.partial(spectrum_kernel, quarter),
        out_shape=jax.ShapeDtypeStruct((8, quarter + 8, LANES), jnp.float32),
        compiler_params=params,
        cost_estimate=estimate(1 << 24, 1 << 22),
        name="spectrum",
    )(view)
    own_taps = lax.dynamic_slice_in_dim(short_taps, lax.axis_index("seq") * LANES, LANES, 2)
    high, low, twist = filter_tables(quarter)
    filtered = pl.pallas_call(
        functools.partial(filter_kernel, shards),
        in_specs=[scalar] + [vector] * (shards + 5),
        out_shape=[jax.ShapeDtypeStruct((rows + TILE, LANES), jnp.bfloat16)] * shards,
        scratch_shapes=[
            pltpu.VMEM((shards, rows + 2 * TILE, LANES), jnp.bfloat16),
            pltpu.VMEM((length, LANES), jnp.float32),
            pltpu.VMEM((2 * quarter + TILE, 4 * LANES), jnp.float32),
            pltpu.VMEM((4, quarter, 4 * LANES), jnp.bfloat16),
        ],
        compiler_params=params,
        cost_estimate=estimate(1 << 30, 1 << 22),
        name="filter",
    )(place, *gathered, own_taps, folded, high, low, twist)
    returned = exchanged(filtered)

    whole = lambda *shape: pl.BlockSpec(shape, lambda i: (0,) * len(shape))
    gain = pl.pallas_call(
        gain_kernel,
        grid=(1,),
        in_specs=[
            whole(1, rows, channels),
            whole(*short_taps.shape),
            whole(rows, channels),
        ],
        out_specs=whole(rows, channels),
        out_shape=jax.ShapeDtypeStruct((rows, channels), jnp.float32),
        compiler_params=params,
        cost_estimate=estimate(1 << 23, 1 << 20),
        name="gain",
    )(streams, short_taps, residual)
    return pl.pallas_call(
        functools.partial(mix_kernel, shards),
        grid=(1,),
        in_specs=[scalar]
        + [whole(rows + TILE, LANES)] * shards
        + [
            whole(rows, channels),
            whole(rows, channels),
            whole(1, TILE, channels),
            whole(*short_taps.shape),
        ],
        out_specs=whole(rows, channels),
        out_shape=jax.ShapeDtypeStruct((rows, channels), jnp.bfloat16),
        compiler_params=params,
        cost_estimate=estimate(1 << 20, 1 << 20),
        name="mix",
    )(place, *returned, gain, residual, streams, short_taps)


def local(streams, short_taps, spectrum, residual):
    rows, channels = residual.shape
    shards = lax.axis_size("seq")
    length = rows * shards
    fits = (
        channels == shards * LANES
        and rows % TILE == 0
        and rows >= 2 * TILE
        and length % (4 * LANES) == 0
        and length <= 2048
        and short_taps.shape[1] == 7
        and shards & (shards - 1) == 0
    )
    if fits:
        return local_kernels(streams, short_taps, spectrum, residual)
    return local_general(streams, short_taps, spectrum, residual)


def solution(mesh):
    placed = (
        P(None, "seq", "chan"),
        P(None, None, "chan"),
        P(("chan", "seq"), None, None),
        P("seq", "chan"),
    )
    return jax.shard_map(
        local, mesh=mesh, in_specs=placed, out_specs=P("seq", "chan"), check_vma=False
    )
```

```python
import functools
import math

import jax
import jax.numpy as jnp
import numpy as np
from jax import lax
from jax.experimental import pallas as pl
from jax.experimental.pallas import tpu as pltpu
from jax.sharding import PartitionSpec as P

LANES = 128
TILE = 16
VMEM_LIMIT = 24 * 1024 * 1024


def passed_along(block, axis, distance):
    devices = range(lax.axis_size(axis))
    route = [(i - distance, i) for i in devices if i - distance in devices]
    return lax.ppermute(block, axis, route)


def section_sizes(length_all):
    power = length_all.bit_length() - 1
    first = (power + 2) // 3
    second = (power - first + 1) // 2
    third = power - first - second
    result = [2**first, 2**second]
    result.append(2**third)
    return result


def matmul_high(left, right):
    return jnp.dot(left, right, precision=lax.Precision.HIGHEST, preferred_element_type=jnp.float32)


def section_high(table, values):
    return jnp.einsum(
        "ka,cab->ckb",
        table,
        values,
        precision=lax.Precision.HIGHEST,
        preferred_element_type=jnp.float32,
    )


def dft_table(order, direction):
    index = jnp.arange(order, dtype=jnp.int32)
    product = index[:, None] * index[None, :] % order
    angle = direction * 2.0 * math.pi * product.astype(jnp.float32) / order
    return (jnp.cos(angle), jnp.sin(angle))


def transform(real_part, imag_part, factors, direction):
    columns, length_now = real_part.shape
    first = factors[0]
    table_cos, table_sin = dft_table(first, direction)
    if len(factors) == 1:
        real_out = matmul_high(real_part, table_cos) - matmul_high(imag_part, table_sin)
        imag_out = matmul_high(imag_part, table_cos) + matmul_high(real_part, table_sin)
        return (real_out, imag_out)
    rest = length_now // first
    real_wide = real_part.reshape(columns, first, rest)
    if imag_part is None:
        section_real = section_high(table_cos, real_wide)
        section_imag = section_high(table_sin, real_wide)
    else:
        imag_wide = imag_part.reshape(columns, first, rest)
        section_real = section_high(table_cos, real_wide) - section_high(table_sin, imag_wide)
        section_imag = section_high(table_cos, imag_wide) + section_high(table_sin, real_wide)
    outer = jnp.arange(first, dtype=jnp.int32)[:, None]
    inner = jnp.arange(rest, dtype=jnp.int32)[None, :]
    twist = (
        direction * 2.0 * math.pi * (outer * inner % length_now).astype(jnp.float32) / length_now
    )
    twist_cos = jnp.cos(twist)[None, :, :]
    twist_sin = jnp.sin(twist)[None, :, :]
    turned_real = (section_real * twist_cos - section_imag * twist_sin).reshape(
        columns * first, rest
    )
    turned_imag = (section_real * twist_sin + section_imag * twist_cos).reshape(
        columns * first, rest
    )
    real_out, imag_out = transform(turned_real, turned_imag, factors[1:], direction)
    real_out = jnp.transpose(real_out.reshape(columns, first, rest), (0, 2, 1)).reshape(
        columns, length_now
    )
    imag_out = jnp.transpose(imag_out.reshape(columns, first, rest), (0, 2, 1)).reshape(
        columns, length_now
    )
    return (real_out, imag_out)


def long_filter(gated_rows, spectrum):
    columns, length_all = gated_rows.shape
    padded = jnp.concatenate(
        [gated_rows.astype(jnp.float32), jnp.zeros((columns, length_all), jnp.float32)], axis=1
    )
    factors = section_sizes(2 * length_all)
    freq_real, freq_imag = transform(padded, None, factors, -1.0)
    spec_real = spectrum[:, 0, :]
    spec_imag = spectrum[:, 1, :]
    prod_real = freq_real * spec_real - freq_imag * spec_imag
    prod_imag = freq_real * spec_imag + freq_imag * spec_real
    back_real, back_imag = transform(prod_real, prod_imag, factors, 1.0)
    return (back_real[:, :length_all] / (2 * length_all)).astype(jnp.bfloat16)


def local_general(streams, short_taps, spectrum, residual):
    row_count = streams.shape[1]
    channels = streams.shape[2]
    span = short_taps.shape[1] - 1
    rim_rows = passed_along(streams[:, row_count - span :, :], "seq", 1)
    extended = jnp.concatenate([rim_rows, streams], axis=1)
    total = jnp.zeros((3, row_count, channels), jnp.float32)
    for offset in range(span + 1):
        total = total + short_taps[:, offset, None, :] * extended[
            :, span - offset : span - offset + row_count, :
        ].astype(jnp.float32)
    convolved = total.astype(jnp.bfloat16)
    q_conv = convolved[0]
    k_conv = convolved[1]
    v_conv = convolved[2]
    seq_devices = lax.axis_size("seq")
    owned_count = channels // seq_devices
    length_all = row_count * seq_devices
    gated = (k_conv.astype(jnp.float32) * v_conv.astype(jnp.float32)).astype(jnp.bfloat16)
    owned = lax.all_to_all(
        gated.reshape(row_count, seq_devices, owned_count),
        "seq",
        split_axis=1,
        concat_axis=0,
        tiled=True,
    )
    gated_whole = owned.reshape(length_all, owned_count)
    filtered = jnp.transpose(long_filter(jnp.transpose(gated_whole), spectrum))
    returned = lax.all_to_all(
        filtered.reshape(length_all, 1, owned_count), "seq", split_axis=0, concat_axis=1, tiled=True
    )
    filtered_local = returned.reshape(row_count, channels)
    resid = residual.astype(jnp.float32)
    mixed = resid + jax.nn.silu(resid) * q_conv.astype(jnp.float32) * filtered_local.astype(
        jnp.float32
    )
    return mixed.astype(jnp.bfloat16)


def rounded(values):
    return values.astype(jnp.bfloat16).astype(jnp.float32)


def short_conv_rolled(rows, taps):
    total = taps(0) * rows
    for offset in range(1, 7):
        total = total + taps(offset) * pltpu.roll(rows, offset, 0)
    return rounded(total)


def row_index(count):
    return lax.broadcasted_iota(jnp.int32, (count, LANES), 0)


def pack_kernel(streams_ref, taps_ref, place_ref, *out_refs):
    rows = streams_ref.shape[1]
    row = row_index(TILE)
    for k in range(2 * len(out_refs)):
        out_ref = out_refs[k // 2].at[k % 2]
        owner = place_ref[0] ^ k
        lanes = pl.ds(pl.multiple_of(owner * LANES, LANES), LANES)
        conv = []
        for s in (1, 2):
            x = streams_ref[s, :, lanes].astype(jnp.float32)
            conv.append(
                short_conv_rolled(x, lambda j, s=s: taps_ref[s, j : j + 1, lanes])
            )
            edge = jnp.where(row < 8, x[:TILE], x[rows - TILE :])
            out_ref[rows + (s - 1) * TILE : rows + s * TILE, :] = edge.astype(jnp.bfloat16)
        gated = conv[0] * conv[1]
        q_last = streams_ref[0, rows - TILE :, lanes].astype(jnp.float32)
        top = jnp.where(row < 6, pltpu.roll(q_last, 6, 0), gated[:TILE])
        out_ref[:TILE, :] = top.astype(jnp.bfloat16)
        out_ref[TILE:rows, :] = gated[TILE:].astype(jnp.bfloat16)


def spectrum_kernel(quarter, view_ref, out_ref):
    blocks = view_ref.shape[0] // (2 * LANES)
    length = blocks * LANES
    per = quarter // LANES
    lane = lax.broadcasted_iota(jnp.int32, (LANES, LANES), 1)
    back = (LANES - lane) % LANES

    def block(part, k):
        return view_ref[pl.ds(2 * (k % blocks) + part, LANES, stride=2 * blocks), :]

    def turned(part, k):
        flipped = jnp.take_along_axis(block(part, k), back, axis=1, mode="promise_in_bounds")
        return jnp.where(lane == 0, block(part, k + 1), flipped)

    tail = jnp.zeros((LANES, LANES), jnp.float32)
    for m in range(4):
        for part in range(2):
            sign = 1.0 if part == 0 else -1.0
            for i in range(per):
                k = 2 * per * m + i
                folded = block(part, k) + sign * turned(part, blocks - k - 1)
                weight = 1.0 / length
                if i == 0:
                    weight = jnp.where(lane == 0, 0.5 / length, 1.0 / length)
                out_ref[2 * m + part, i * LANES : (i + 1) * LANES, :] = jnp.transpose(
                    folded * weight
                )
            k = 2 * per * m + per
            folded = (block(part, k) + sign * block(part, blocks - k)) * (0.5 / length)
            tail = jnp.where(
                lane == 8 * (2 * m + part),
                jnp.broadcast_to(folded[:, 0:1], (LANES, LANES)),
                tail,
            )
    tail = jnp.transpose(tail)
    for j in range(8):
        out_ref[j, quarter : quarter + 8, :] = tail[8 * j : 8 * j + 8]


def merge_kernel(*refs):
    for j, ref in enumerate(refs[:-2]):
        refs[-1][j] = ref[1]


def filter_kernel(shards, place_ref, *refs):
    chips = shards // 2
    parts, other, refs = refs[:chips], refs[chips], refs[chips + 1 :]
    (taps_ref, h_ref, high_ref, low_ref, twist_ref), refs = refs[:5], refs[5:]
    outs, (msg_ref, x_ref, z_ref, q_ref) = refs[:chips], refs[chips:]
    rows = other.shape[1] - 2 * TILE
    for j in range(chips):
        msg_ref[place_ref[0] ^ (2 * j)] = parts[j][0]
        msg_ref[place_ref[0] ^ (2 * j + 1)] = other[j]
    quarter = high_ref.shape[1]
    row = row_index(TILE)
    own = own_lanes(place_ref, 0)

    before = None
    for s in range(shards):
        top = msg_ref[s, :TILE, :].astype(jnp.float32)
        edges = [
            msg_ref[s, rows + i * TILE : rows + (i + 1) * TILE, :].astype(jnp.float32)
            for i in range(2)
        ]
        conv = []
        for i in range(2):
            above = jnp.zeros_like(edges[i]) if before is None else before[1][i]
            window = jnp.where(row < 8, edges[i], above)
            conv.append(
                short_conv_rolled(window, lambda j, i=i: taps_ref[1 + i, j : j + 1, own])
            )
        x_ref[s * rows : s * rows + TILE, :] = jnp.where(
            row < 6, rounded(conv[0] * conv[1]), top
        )
        x_ref[s * rows + TILE : (s + 1) * rows, :] = msg_ref[s, TILE:rows, :].astype(jnp.float32)
        if before is None:
            halo = jnp.zeros_like(top)
        else:
            halo = pltpu.roll(before[0], TILE - 6, 0)
        msg_ref[s, rows : rows + TILE, :] = halo.astype(jnp.bfloat16)
        before = (top, edges)

    x = jnp.concatenate(
        [x_ref[pl.ds(a, quarter, stride=4), :].astype(jnp.bfloat16) for a in range(4)], axis=1
    )
    z_ref[...] = jnp.dot(high_ref[...], x, preferred_element_type=jnp.float32) + jnp.dot(
        low_ref[...], x, preferred_element_type=jnp.float32
    )

    def combine(real, imag, g, count):
        u = []
        for a in range(4):
            if a == 0:
                u.append((real[0], imag[0]))
                continue
            wr = jnp.broadcast_to(twist_ref[g : g + count, 2 * a : 2 * a + 1], (count, LANES))
            wi = jnp.broadcast_to(
                twist_ref[g : g + count, 2 * a + 1 : 2 * a + 2], (count, LANES)
            )
            u.append((real[a] * wr - imag[a] * wi, real[a] * wi + imag[a] * wr, wr, wi))

        def four(v, sign):
            er, ei = v[0][0] + v[2][0], v[0][1] + v[2][1]
            dr, di = v[0][0] - v[2][0], v[0][1] - v[2][1]
            pr, pi = v[1][0] + v[3][0], v[1][1] + v[3][1]
            qr, qi = v[1][0] - v[3][0], v[1][1] - v[3][1]
            if sign < 0:
                one, three = (dr + qi, di - qr), (dr - qi, di + qr)
            else:
                one, three = (dr - qi, di + qr), (dr + qi, di - qr)
            return [(er + pr, ei + pi), one, (er - pr, ei - pi), three]

        freq = four(u, -1)
        prod = []
        for m in range(4):
            hr = h_ref[2 * m, g : g + count, :]
            hi = h_ref[2 * m + 1, g : g + count, :]
            xr, xi = freq[m]
            prod.append((xr * hr - xi * hi, xr * hi + xi * hr))
        v = four(prod, 1)
        out = [v[0]]
        for a in range(1, 4):
            wr, wi = u[a][2], u[a][3]
            vr, vi = v[a]
            out.append((vr * wr + vi * wi, vi * wr - vr * wi))
        return out

    for g in range(0, quarter, TILE):
        real = [z_ref[g : g + TILE, a * LANES : (a + 1) * LANES] for a in range(4)]
        imag = [
            z_ref[quarter + g : quarter + g + TILE, a * LANES : (a + 1) * LANES] for a in range(4)
        ]
        out = combine(real, imag, g, TILE)
        for a in range(4):
            lanes = slice(a * LANES, (a + 1) * LANES)
            for part in range(2):
                high = out[a][part].astype(jnp.bfloat16)
                low = (out[a][part] - high.astype(jnp.float32)).astype(jnp.bfloat16)
                q_ref[2 * part, g : g + TILE, lanes] = high
                q_ref[2 * part + 1, g : g + TILE, lanes] = low
    real = [z_ref[2 * quarter : 2 * quarter + 8, a * LANES : (a + 1) * LANES] for a in range(4)]
    last = combine(real, [jnp.zeros_like(r) for r in real], quarter, 8)

    y = None
    for part in range(2):
        high = high_ref[part * quarter : (part + 1) * quarter, :]
        low = low_ref[part * quarter : (part + 1) * quarter, :]
        for left, right in ((high, 0), (high, 1), (low, 0)):
            term = jnp.dot(left, q_ref[2 * part + right], preferred_element_type=jnp.float32)
            y = term if y is None else y + term
    sign = 1.0 - 2.0 * (row_index(quarter) % 2).astype(jnp.float32)
    for a in range(4):
        x_ref[pl.ds(a, quarter, stride=4), :] = (
            y[:, a * LANES : (a + 1) * LANES] + sign * last[a][0][0:1, :]
        )
    for k in range(shards):
        target = place_ref[0] ^ k
        start = pl.multiple_of(target * rows, rows)
        outs[k // 2][k % 2, :rows, :] = x_ref[pl.ds(start, rows), :].astype(jnp.bfloat16)
        outs[k // 2][k % 2, rows:, :] = msg_ref[target, rows : rows + TILE, :]


def silu(values):
    return values / (1.0 + jnp.exp(-values))


def gain_kernel(q_ref, taps_ref, residual_ref, out_ref):
    for c in range(out_ref.shape[1] // LANES):
        lanes = slice(c * LANES, (c + 1) * LANES)
        conv = short_conv_rolled(
            q_ref[0, :, lanes].astype(jnp.float32), lambda j: taps_ref[0, j : j + 1, lanes]
        )
        out_ref[:, lanes] = silu(residual_ref[:, lanes].astype(jnp.float32)) * conv


def mixed_block(msg, lanes, gain_ref, residual_ref, q_ref, taps_ref, store):
    rows = residual_ref.shape[0]
    row = row_index(TILE)
    window = jnp.where(
        row < 8,
        q_ref[0, :, lanes].astype(jnp.float32),
        msg[rows : rows + TILE, :].astype(jnp.float32),
    )
    conv = short_conv_rolled(window, lambda j: taps_ref[0, j : j + 1, lanes])
    resid = residual_ref[:TILE, lanes].astype(jnp.float32)
    gain = jnp.where(row < 6, silu(resid) * conv, gain_ref[:TILE, lanes])
    store(
        slice(0, TILE),
        (resid + gain * msg[:TILE, :].astype(jnp.float32)).astype(jnp.bfloat16),
    )
    store(
        slice(TILE, rows),
        (
            residual_ref[TILE:, lanes].astype(jnp.float32)
            + gain_ref[TILE:, lanes] * msg[TILE:rows, :].astype(jnp.float32)
        ).astype(jnp.bfloat16),
    )


def own_lanes(place_ref, k):
    return pl.ds(pl.multiple_of((place_ref[0] ^ k) * LANES, LANES), LANES)


def mix_near_kernel(chips, place_ref, *refs):
    parts, rest, out_ref = refs[:chips], refs[chips:-1], refs[-1]
    for j in range(chips):

        def store(rows, value, j=j):
            out_ref[j, rows, :] = value

        mixed_block(parts[j].at[0], own_lanes(place_ref, 2 * j), *rest, store)


def mix_far_kernel(place_ref, near_ref, msg_ref, *refs):
    rest, out_ref = refs[:-1], refs[-1]
    for j in range(near_ref.shape[0]):
        out_ref[:, own_lanes(place_ref, 2 * j)] = near_ref[j]
        lanes = own_lanes(place_ref, 2 * j + 1)

        def store(rows, value, lanes=lanes):
            out_ref[rows, lanes] = value

        mixed_block(msg_ref.at[j], lanes, *rest, store)


def split_table(table):
    high = table.astype(jnp.bfloat16)
    low = (table - high.astype(np.float64)).astype(jnp.bfloat16)
    return high, low


def filter_tables(quarter):
    index = np.arange(quarter)
    angle = 2.0 * np.pi * (index[:, None] * index[None, :] % (2 * quarter)) / (2 * quarter)
    alternate = np.zeros((TILE, quarter))
    alternate[0] = 1.0 - 2.0 * (index % 2)
    high, low = split_table(np.concatenate([np.cos(angle), -np.sin(angle), alternate], axis=0))
    g = np.arange(quarter + 8)[:, None]
    a = np.arange(4)[None, :]
    turn = 2.0 * np.pi * (g * a) / (8 * quarter)
    twist = np.stack([np.cos(turn), -np.sin(turn)], axis=-1).reshape(quarter + 8, 8)
    return high, low, twist.astype(np.float32)


def estimate(flops, moved):
    return pl.CostEstimate(flops=flops, bytes_accessed=moved, transcendentals=0)


def exchanged(parts, beside):
    chips = len(parts)
    count = 2 * chips
    near = list(parts)
    for j in sorted(range(1, chips), key=lambda j: -bin(j).count("1")):
        near[j] = lax.ppermute(parts[j], "seq", [(i, i ^ (2 * j)) for i in range(count)])
    merged = pl.pallas_call(
        merge_kernel,
        in_specs=[pl.BlockSpec(memory_space=pltpu.VMEM)] * chips
        + [pl.BlockSpec(memory_space=pl.ANY)],
        out_shape=jax.ShapeDtypeStruct((chips,) + parts[0].shape[1:], parts[0].dtype),
        cost_estimate=estimate(1 << 10, 1 << 17),
        name="merge",
    )(*near, beside)
    return near, lax.ppermute(merged, "seq", [(i, i ^ 1) for i in range(count)])


def local_kernels(streams, short_taps, spectrum, residual):
    rows, channels = residual.shape
    shards = lax.axis_size("seq")
    length = rows * shards
    quarter = length // 4
    params = pltpu.CompilerParams(vmem_limit_bytes=VMEM_LIMIT)
    chips = shards // 2
    place = lax.axis_index("seq").astype(jnp.int32).reshape(1)
    scalar = pl.BlockSpec(memory_space=pltpu.SMEM)
    vector = pl.BlockSpec(memory_space=pltpu.VMEM)
    packed = pl.pallas_call(
        pack_kernel,
        in_specs=[vector, vector, scalar],
        out_shape=[jax.ShapeDtypeStruct((2, rows + 2 * TILE, LANES), jnp.bfloat16)] * chips,
        compiler_params=params,
        cost_estimate=estimate(1 << 23, 1 << 20),
        name="pack",
    )(streams, short_taps, place)

    blocks = 2 * length // LANES
    view = jnp.transpose(spectrum.reshape(LANES, 2, blocks, LANES), (0, 2, 1, 3)).reshape(
        2 * blocks * LANES, LANES
    )
    folded = pl.pallas_call(
        functools.partial(spectrum_kernel, quarter),
        out_shape=jax.ShapeDtypeStruct((8, quarter + 8, LANES), jnp.float32),
        compiler_params=params,
        cost_estimate=estimate(1 << 24, 1 << 22),
        name="spectrum",
    )(view)
    near, far = exchanged(packed, folded)
    high, low, twist = filter_tables(quarter)
    filtered = pl.pallas_call(
        functools.partial(filter_kernel, shards),
        in_specs=[scalar] + [vector] * (chips + 6),
        out_shape=[jax.ShapeDtypeStruct((2, rows + TILE, LANES), jnp.bfloat16)] * chips,
        scratch_shapes=[
            pltpu.VMEM((shards, rows + 2 * TILE, LANES), jnp.bfloat16),
            pltpu.VMEM((length, LANES), jnp.float32),
            pltpu.VMEM((2 * quarter + TILE, 4 * LANES), jnp.float32),
            pltpu.VMEM((4, quarter, 4 * LANES), jnp.bfloat16),
        ],
        compiler_params=params,
        cost_estimate=estimate(1 << 30, 1 << 22),
        name="filter",
    )(place, *near, far, short_taps, folded, high, low, twist)
    whole = lambda *shape: pl.BlockSpec(shape, lambda i: (0,) * len(shape))
    gain = pl.pallas_call(
        gain_kernel,
        grid=(1,),
        in_specs=[
            whole(1, rows, channels),
            whole(*short_taps.shape),
            whole(rows, channels),
        ],
        out_specs=whole(rows, channels),
        out_shape=jax.ShapeDtypeStruct((rows, channels), jnp.float32),
        compiler_params=params,
        cost_estimate=estimate(1 << 23, 1 << 20),
        name="gain",
    )(streams, short_taps, residual)
    near, far = exchanged(filtered, gain)

    rest = [
        whole(rows, channels),
        whole(rows, channels),
        whole(1, TILE, channels),
        whole(*short_taps.shape),
    ]
    mixed = pl.pallas_call(
        functools.partial(mix_near_kernel, chips),
        grid=(1,),
        in_specs=[scalar] + [whole(2, rows + TILE, LANES)] * chips + rest,
        out_specs=whole(chips, rows, LANES),
        out_shape=jax.ShapeDtypeStruct((chips, rows, LANES), jnp.bfloat16),
        compiler_params=params,
        cost_estimate=estimate(1 << 20, 1 << 20),
        name="mix_near",
    )(place, *near, gain, residual, streams, short_taps)
    return pl.pallas_call(
        mix_far_kernel,
        grid=(1,),
        in_specs=[scalar, whole(chips, rows, LANES), whole(chips, rows + TILE, LANES)] + rest,
        out_specs=whole(rows, channels),
        out_shape=jax.ShapeDtypeStruct((rows, channels), jnp.bfloat16),
        compiler_params=params,
        cost_estimate=estimate(1 << 20, 1 << 20),
        name="mix_far",
    )(place, mixed, far, gain, residual, streams, short_taps)


def local(streams, short_taps, spectrum, residual):
    rows, channels = residual.shape
    shards = lax.axis_size("seq")
    length = rows * shards
    fits = (
        channels == shards * LANES
        and rows % TILE == 0
        and rows >= 2 * TILE
        and length % (4 * LANES) == 0
        and length <= 2048
        and short_taps.shape[1] == 7
        and shards & (shards - 1) == 0
        and shards >= 2
    )
    if fits:
        return local_kernels(streams, short_taps, spectrum, residual)
    return local_general(streams, short_taps, spectrum, residual)


def solution(mesh):
    placed = (
        P(None, "seq", "chan"),
        P(None, None, "chan"),
        P(("chan", "seq"), None, None),
        P("seq", "chan"),
    )
    return jax.shard_map(
        local, mesh=mesh, in_specs=placed, out_specs=P("seq", "chan"), check_vma=False
    )
```

```python
import functools
import math

import jax
import jax.numpy as jnp
import numpy as np
from jax import lax
from jax.experimental import pallas as pl
from jax.experimental.pallas import tpu as pltpu
from jax.sharding import PartitionSpec as P

LANES = 128
TILE = 16
VMEM_LIMIT = 16 * 1024 * 1024


def passed_along(block, axis, distance):
    devices = range(lax.axis_size(axis))
    route = [(i - distance, i) for i in devices if i - distance in devices]
    return lax.ppermute(block, axis, route)


def section_sizes(length_all):
    power = length_all.bit_length() - 1
    first = (power + 2) // 3
    second = (power - first + 1) // 2
    third = power - first - second
    result = [2**first, 2**second]
    result.append(2**third)
    return result


def matmul_high(left, right):
    return jnp.dot(left, right, precision=lax.Precision.HIGHEST, preferred_element_type=jnp.float32)


def section_high(table, values):
    return jnp.einsum(
        "ka,cab->ckb",
        table,
        values,
        precision=lax.Precision.HIGHEST,
        preferred_element_type=jnp.float32,
    )


def dft_table(order, direction):
    index = jnp.arange(order, dtype=jnp.int32)
    product = index[:, None] * index[None, :] % order
    angle = direction * 2.0 * math.pi * product.astype(jnp.float32) / order
    return (jnp.cos(angle), jnp.sin(angle))


def transform(real_part, imag_part, factors, direction):
    columns, length_now = real_part.shape
    first = factors[0]
    table_cos, table_sin = dft_table(first, direction)
    if len(factors) == 1:
        real_out = matmul_high(real_part, table_cos) - matmul_high(imag_part, table_sin)
        imag_out = matmul_high(imag_part, table_cos) + matmul_high(real_part, table_sin)
        return (real_out, imag_out)
    rest = length_now // first
    real_wide = real_part.reshape(columns, first, rest)
    if imag_part is None:
        section_real = section_high(table_cos, real_wide)
        section_imag = section_high(table_sin, real_wide)
    else:
        imag_wide = imag_part.reshape(columns, first, rest)
        section_real = section_high(table_cos, real_wide) - section_high(table_sin, imag_wide)
        section_imag = section_high(table_cos, imag_wide) + section_high(table_sin, real_wide)
    outer = jnp.arange(first, dtype=jnp.int32)[:, None]
    inner = jnp.arange(rest, dtype=jnp.int32)[None, :]
    twist = (
        direction * 2.0 * math.pi * (outer * inner % length_now).astype(jnp.float32) / length_now
    )
    twist_cos = jnp.cos(twist)[None, :, :]
    twist_sin = jnp.sin(twist)[None, :, :]
    turned_real = (section_real * twist_cos - section_imag * twist_sin).reshape(
        columns * first, rest
    )
    turned_imag = (section_real * twist_sin + section_imag * twist_cos).reshape(
        columns * first, rest
    )
    real_out, imag_out = transform(turned_real, turned_imag, factors[1:], direction)
    real_out = jnp.transpose(real_out.reshape(columns, first, rest), (0, 2, 1)).reshape(
        columns, length_now
    )
    imag_out = jnp.transpose(imag_out.reshape(columns, first, rest), (0, 2, 1)).reshape(
        columns, length_now
    )
    return (real_out, imag_out)


def long_filter(gated_rows, spectrum):
    columns, length_all = gated_rows.shape
    padded = jnp.concatenate(
        [gated_rows.astype(jnp.float32), jnp.zeros((columns, length_all), jnp.float32)], axis=1
    )
    factors = section_sizes(2 * length_all)
    freq_real, freq_imag = transform(padded, None, factors, -1.0)
    spec_real = spectrum[:, 0, :]
    spec_imag = spectrum[:, 1, :]
    prod_real = freq_real * spec_real - freq_imag * spec_imag
    prod_imag = freq_real * spec_imag + freq_imag * spec_real
    back_real, back_imag = transform(prod_real, prod_imag, factors, 1.0)
    return (back_real[:, :length_all] / (2 * length_all)).astype(jnp.bfloat16)


def local_general(streams, short_taps, spectrum, residual):
    row_count = streams.shape[1]
    channels = streams.shape[2]
    span = short_taps.shape[1] - 1
    rim_rows = passed_along(streams[:, row_count - span :, :], "seq", 1)
    extended = jnp.concatenate([rim_rows, streams], axis=1)
    total = jnp.zeros((3, row_count, channels), jnp.float32)
    for offset in range(span + 1):
        total = total + short_taps[:, offset, None, :] * extended[
            :, span - offset : span - offset + row_count, :
        ].astype(jnp.float32)
    convolved = total.astype(jnp.bfloat16)
    q_conv = convolved[0]
    k_conv = convolved[1]
    v_conv = convolved[2]
    seq_devices = lax.axis_size("seq")
    owned_count = channels // seq_devices
    length_all = row_count * seq_devices
    gated = (k_conv.astype(jnp.float32) * v_conv.astype(jnp.float32)).astype(jnp.bfloat16)
    owned = lax.all_to_all(
        gated.reshape(row_count, seq_devices, owned_count),
        "seq",
        split_axis=1,
        concat_axis=0,
        tiled=True,
    )
    gated_whole = owned.reshape(length_all, owned_count)
    filtered = jnp.transpose(long_filter(jnp.transpose(gated_whole), spectrum))
    returned = lax.all_to_all(
        filtered.reshape(length_all, 1, owned_count), "seq", split_axis=0, concat_axis=1, tiled=True
    )
    filtered_local = returned.reshape(row_count, channels)
    resid = residual.astype(jnp.float32)
    mixed = resid + jax.nn.silu(resid) * q_conv.astype(jnp.float32) * filtered_local.astype(
        jnp.float32
    )
    return mixed.astype(jnp.bfloat16)


def rounded(values):
    return values.astype(jnp.bfloat16).astype(jnp.float32)


def short_conv_rolled(rows, taps):
    total = taps(0) * rows
    for offset in range(1, 7):
        total = total + taps(offset) * pltpu.roll(rows, offset, 0)
    return rounded(total)


def row_index(count):
    return lax.broadcasted_iota(jnp.int32, (count, LANES), 0)


def pack_kernel(streams_ref, taps_ref, place_ref, *out_refs):
    rows = streams_ref.shape[1]
    row = row_index(TILE)
    for k in range(2 * len(out_refs)):
        out_ref = out_refs[k // 2].at[k % 2]
        owner = place_ref[0] ^ k
        lanes = pl.ds(pl.multiple_of(owner * LANES, LANES), LANES)
        conv = []
        for s in (1, 2):
            x = streams_ref[s, :, lanes].astype(jnp.float32)
            conv.append(
                short_conv_rolled(x, lambda j, s=s: taps_ref[s, j : j + 1, lanes])
            )
            edge = jnp.where(row < 8, x[:TILE], x[rows - TILE :])
            out_ref[rows + (s - 1) * TILE : rows + s * TILE, :] = edge.astype(jnp.bfloat16)
        gated = conv[0] * conv[1]
        q_last = streams_ref[0, rows - TILE :, lanes].astype(jnp.float32)
        top = jnp.where(row < 6, pltpu.roll(q_last, 6, 0), gated[:TILE])
        out_ref[:TILE, :] = top.astype(jnp.bfloat16)
        out_ref[TILE:rows, :] = gated[TILE:].astype(jnp.bfloat16)


def spectrum_kernel(quarter, view_ref, out_ref):
    blocks = view_ref.shape[0] // (2 * LANES)
    length = blocks * LANES
    per = quarter // LANES
    lane = lax.broadcasted_iota(jnp.int32, (LANES, LANES), 1)
    back = (LANES - lane) % LANES

    def block(part, k):
        return view_ref[pl.ds(2 * (k % blocks) + part, LANES, stride=2 * blocks), :]

    def turned(part, k):
        flipped = jnp.take_along_axis(block(part, k), back, axis=1, mode="promise_in_bounds")
        return jnp.where(lane == 0, block(part, k + 1), flipped)

    tail = jnp.zeros((LANES, LANES), jnp.float32)
    for m in range(4):
        for part in range(2):
            sign = 1.0 if part == 0 else -1.0
            for i in range(per):
                k = 2 * per * m + i
                folded = block(part, k) + sign * turned(part, blocks - k - 1)
                weight = 1.0 / length
                if i == 0:
                    weight = jnp.where(lane == 0, 0.5 / length, 1.0 / length)
                out_ref[2 * m + part, i * LANES : (i + 1) * LANES, :] = jnp.transpose(
                    folded * weight
                )
            k = 2 * per * m + per
            folded = (block(part, k) + sign * block(part, blocks - k)) * (0.5 / length)
            tail = jnp.where(
                lane == 8 * (2 * m + part),
                jnp.broadcast_to(folded[:, 0:1], (LANES, LANES)),
                tail,
            )
    tail = jnp.transpose(tail)
    for j in range(8):
        out_ref[j, quarter : quarter + 8, :] = tail[8 * j : 8 * j + 8]


def merge_kernel(*refs):
    for j, ref in enumerate(refs[:-2]):
        refs[-1][j] = ref[1]


def filter_kernel(shards, place_ref, *refs):
    chips = shards // 2
    parts, other, refs = refs[:chips], refs[chips], refs[chips + 1 :]
    (taps_ref, h_ref, high_ref, low_ref, twist_ref), refs = refs[:5], refs[5:]
    outs, (msg_ref, x_ref, z_ref, q_ref) = refs[:chips], refs[chips:]
    rows = other.shape[1] - 2 * TILE
    for j in range(chips):
        msg_ref[place_ref[0] ^ (2 * j)] = parts[j][0]
        msg_ref[place_ref[0] ^ (2 * j + 1)] = other[j]
    quarter = high_ref.shape[1]
    row = row_index(TILE)
    own = own_lanes(place_ref, 0)

    before = None
    for s in range(shards):
        top = msg_ref[s, :TILE, :].astype(jnp.float32)
        edges = [
            msg_ref[s, rows + i * TILE : rows + (i + 1) * TILE, :].astype(jnp.float32)
            for i in range(2)
        ]
        conv = []
        for i in range(2):
            above = jnp.zeros_like(edges[i]) if before is None else before[1][i]
            window = jnp.where(row < 8, edges[i], above)
            conv.append(
                short_conv_rolled(window, lambda j, i=i: taps_ref[1 + i, j : j + 1, own])
            )
        x_ref[s * rows : s * rows + TILE, :] = jnp.where(
            row < 6, rounded(conv[0] * conv[1]), top
        )
        x_ref[s * rows + TILE : (s + 1) * rows, :] = msg_ref[s, TILE:rows, :].astype(jnp.float32)
        if before is None:
            halo = jnp.zeros_like(top)
        else:
            halo = pltpu.roll(before[0], TILE - 6, 0)
        msg_ref[s, rows : rows + TILE, :] = halo.astype(jnp.bfloat16)
        before = (top, edges)

    x = jnp.concatenate(
        [x_ref[pl.ds(a, quarter, stride=4), :].astype(jnp.bfloat16) for a in range(4)], axis=1
    )
    z_ref[...] = jnp.dot(high_ref[...], x, preferred_element_type=jnp.float32) + jnp.dot(
        low_ref[...], x, preferred_element_type=jnp.float32
    )

    def combine(real, imag, g, count):
        u = []
        for a in range(4):
            if a == 0:
                u.append((real[0], imag[0]))
                continue
            wr = jnp.broadcast_to(twist_ref[g : g + count, 2 * a : 2 * a + 1], (count, LANES))
            wi = jnp.broadcast_to(
                twist_ref[g : g + count, 2 * a + 1 : 2 * a + 2], (count, LANES)
            )
            u.append((real[a] * wr - imag[a] * wi, real[a] * wi + imag[a] * wr, wr, wi))

        def four(v, sign):
            er, ei = v[0][0] + v[2][0], v[0][1] + v[2][1]
            dr, di = v[0][0] - v[2][0], v[0][1] - v[2][1]
            pr, pi = v[1][0] + v[3][0], v[1][1] + v[3][1]
            qr, qi = v[1][0] - v[3][0], v[1][1] - v[3][1]
            if sign < 0:
                one, three = (dr + qi, di - qr), (dr - qi, di + qr)
            else:
                one, three = (dr - qi, di + qr), (dr + qi, di - qr)
            return [(er + pr, ei + pi), one, (er - pr, ei - pi), three]

        freq = four(u, -1)
        prod = []
        for m in range(4):
            hr = h_ref[2 * m, g : g + count, :]
            hi = h_ref[2 * m + 1, g : g + count, :]
            xr, xi = freq[m]
            prod.append((xr * hr - xi * hi, xr * hi + xi * hr))
        v = four(prod, 1)
        out = [v[0]]
        for a in range(1, 4):
            wr, wi = u[a][2], u[a][3]
            vr, vi = v[a]
            out.append((vr * wr + vi * wi, vi * wr - vr * wi))
        return out

    for g in range(0, quarter, TILE):
        real = [z_ref[g : g + TILE, a * LANES : (a + 1) * LANES] for a in range(4)]
        imag = [
            z_ref[quarter + g : quarter + g + TILE, a * LANES : (a + 1) * LANES] for a in range(4)
        ]
        out = combine(real, imag, g, TILE)
        for a in range(4):
            lanes = slice(a * LANES, (a + 1) * LANES)
            for part in range(2):
                high = out[a][part].astype(jnp.bfloat16)
                low = (out[a][part] - high.astype(jnp.float32)).astype(jnp.bfloat16)
                q_ref[2 * part, g : g + TILE, lanes] = high
                q_ref[2 * part + 1, g : g + TILE, lanes] = low
    real = [z_ref[2 * quarter : 2 * quarter + 8, a * LANES : (a + 1) * LANES] for a in range(4)]
    last = combine(real, [jnp.zeros_like(r) for r in real], quarter, 8)

    y = None
    for part in range(2):
        high = high_ref[part * quarter : (part + 1) * quarter, :]
        low = low_ref[part * quarter : (part + 1) * quarter, :]
        for left, right in ((high, 0), (high, 1), (low, 0)):
            term = jnp.dot(left, q_ref[2 * part + right], preferred_element_type=jnp.float32)
            y = term if y is None else y + term
    sign = 1.0 - 2.0 * (row_index(quarter) % 2).astype(jnp.float32)
    for a in range(4):
        x_ref[pl.ds(a, quarter, stride=4), :] = (
            y[:, a * LANES : (a + 1) * LANES] + sign * last[a][0][0:1, :]
        )
    for k in range(shards):
        target = place_ref[0] ^ k
        start = pl.multiple_of(target * rows, rows)
        outs[k // 2][k % 2, :rows, :] = x_ref[pl.ds(start, rows), :].astype(jnp.bfloat16)
        outs[k // 2][k % 2, rows:, :] = msg_ref[target, rows : rows + TILE, :]


def silu(values):
    return values / (1.0 + jnp.exp(-values))


def gain_kernel(q_ref, taps_ref, residual_ref, out_ref):
    for c in range(out_ref.shape[1] // LANES):
        lanes = slice(c * LANES, (c + 1) * LANES)
        conv = short_conv_rolled(
            q_ref[0, :, lanes].astype(jnp.float32), lambda j: taps_ref[0, j : j + 1, lanes]
        )
        out_ref[:, lanes] = silu(residual_ref[:, lanes].astype(jnp.float32)) * conv


def mixed_block(msg, lanes, gain_ref, residual_ref, q_ref, taps_ref, store):
    rows = residual_ref.shape[0]
    row = row_index(TILE)
    window = jnp.where(
        row < 8,
        q_ref[0, :, lanes].astype(jnp.float32),
        msg[rows : rows + TILE, :].astype(jnp.float32),
    )
    conv = short_conv_rolled(window, lambda j: taps_ref[0, j : j + 1, lanes])
    resid = residual_ref[:TILE, lanes].astype(jnp.float32)
    gain = jnp.where(row < 6, silu(resid) * conv, gain_ref[:TILE, lanes])
    store(
        slice(0, TILE),
        (resid + gain * msg[:TILE, :].astype(jnp.float32)).astype(jnp.bfloat16),
    )
    store(
        slice(TILE, rows),
        (
            residual_ref[TILE:, lanes].astype(jnp.float32)
            + gain_ref[TILE:, lanes] * msg[TILE:rows, :].astype(jnp.float32)
        ).astype(jnp.bfloat16),
    )


def own_lanes(place_ref, k):
    return pl.ds(pl.multiple_of((place_ref[0] ^ k) * LANES, LANES), LANES)


def mix_near_kernel(chips, place_ref, *refs):
    parts, rest, out_ref = refs[:chips], refs[chips:-1], refs[-1]
    for j in range(chips):

        def store(rows, value, j=j):
            out_ref[j, rows, :] = value

        mixed_block(parts[j].at[0], own_lanes(place_ref, 2 * j), *rest, store)


def mix_far_kernel(place_ref, near_ref, msg_ref, *refs):
    rest, out_ref = refs[:-1], refs[-1]
    for j in range(near_ref.shape[0]):
        out_ref[:, own_lanes(place_ref, 2 * j)] = near_ref[j]
        lanes = own_lanes(place_ref, 2 * j + 1)

        def store(rows, value, lanes=lanes):
            out_ref[rows, lanes] = value

        mixed_block(msg_ref.at[j], lanes, *rest, store)


def split_table(table):
    high = table.astype(jnp.bfloat16)
    low = (table - high.astype(np.float64)).astype(jnp.bfloat16)
    return high, low


def filter_tables(quarter):
    index = np.arange(quarter)
    angle = 2.0 * np.pi * (index[:, None] * index[None, :] % (2 * quarter)) / (2 * quarter)
    alternate = np.zeros((TILE, quarter))
    alternate[0] = 1.0 - 2.0 * (index % 2)
    high, low = split_table(np.concatenate([np.cos(angle), -np.sin(angle), alternate], axis=0))
    g = np.arange(quarter + 8)[:, None]
    a = np.arange(4)[None, :]
    turn = 2.0 * np.pi * (g * a) / (8 * quarter)
    twist = np.stack([np.cos(turn), -np.sin(turn)], axis=-1).reshape(quarter + 8, 8)
    return high, low, twist.astype(np.float32)


def estimate(flops, moved):
    return pl.CostEstimate(flops=flops, bytes_accessed=moved, transcendentals=0)


def exchanged(parts, beside):
    chips = len(parts)
    count = 2 * chips
    near = list(parts)
    for j in sorted(range(1, chips), key=lambda j: -bin(j).count("1")):
        near[j] = lax.ppermute(parts[j], "seq", [(i, i ^ (2 * j)) for i in range(count)])
    merged = pl.pallas_call(
        merge_kernel,
        in_specs=[pl.BlockSpec(memory_space=pltpu.VMEM)] * chips
        + [pl.BlockSpec(memory_space=pl.ANY)],
        out_shape=jax.ShapeDtypeStruct((chips,) + parts[0].shape[1:], parts[0].dtype),
        compiler_params=pltpu.CompilerParams(vmem_limit_bytes=VMEM_LIMIT),
        cost_estimate=estimate(1 << 10, 1 << 17),
        name="merge",
    )(*near, beside)
    return near, lax.ppermute(merged, "seq", [(i, i ^ 1) for i in range(count)])


def local_kernels(streams, short_taps, spectrum, residual):
    rows, channels = residual.shape
    shards = lax.axis_size("seq")
    length = rows * shards
    quarter = length // 4
    params = pltpu.CompilerParams(vmem_limit_bytes=VMEM_LIMIT)
    chips = shards // 2
    place = lax.axis_index("seq").astype(jnp.int32).reshape(1)
    scalar = pl.BlockSpec(memory_space=pltpu.SMEM)
    vector = pl.BlockSpec(memory_space=pltpu.VMEM)
    packed = pl.pallas_call(
        pack_kernel,
        in_specs=[vector, vector, scalar],
        out_shape=[jax.ShapeDtypeStruct((2, rows + 2 * TILE, LANES), jnp.bfloat16)] * chips,
        compiler_params=params,
        cost_estimate=estimate(1 << 23, 1 << 20),
        name="pack",
    )(streams, short_taps, place)

    blocks = 2 * length // LANES
    view = jnp.transpose(spectrum.reshape(LANES, 2, blocks, LANES), (0, 2, 1, 3)).reshape(
        2 * blocks * LANES, LANES
    )
    folded = pl.pallas_call(
        functools.partial(spectrum_kernel, quarter),
        out_shape=jax.ShapeDtypeStruct((8, quarter + 8, LANES), jnp.float32),
        compiler_params=params,
        cost_estimate=estimate(1 << 24, 1 << 22),
        name="spectrum",
    )(view)
    near, far = exchanged(packed, folded)
    high, low, twist = filter_tables(quarter)
    filtered = pl.pallas_call(
        functools.partial(filter_kernel, shards),
        in_specs=[scalar] + [vector] * (chips + 6),
        out_shape=[jax.ShapeDtypeStruct((2, rows + TILE, LANES), jnp.bfloat16)] * chips,
        scratch_shapes=[
            pltpu.VMEM((shards, rows + 2 * TILE, LANES), jnp.bfloat16),
            pltpu.VMEM((length, LANES), jnp.float32),
            pltpu.VMEM((2 * quarter + TILE, 4 * LANES), jnp.float32),
            pltpu.VMEM((4, quarter, 4 * LANES), jnp.bfloat16),
        ],
        compiler_params=params,
        cost_estimate=estimate(1 << 30, 1 << 22),
        name="filter",
    )(place, *near, far, short_taps, folded, high, low, twist)
    whole = lambda *shape: pl.BlockSpec(shape, lambda i: (0,) * len(shape))
    gain = pl.pallas_call(
        gain_kernel,
        grid=(1,),
        in_specs=[
            whole(1, rows, channels),
            whole(*short_taps.shape),
            whole(rows, channels),
        ],
        out_specs=whole(rows, channels),
        out_shape=jax.ShapeDtypeStruct((rows, channels), jnp.float32),
        compiler_params=params,
        cost_estimate=estimate(1 << 23, 1 << 20),
        name="gain",
    )(streams, short_taps, residual)
    near, far = exchanged(filtered, gain)

    rest = [
        whole(rows, channels),
        whole(rows, channels),
        whole(1, TILE, channels),
        whole(*short_taps.shape),
    ]
    mixed = pl.pallas_call(
        functools.partial(mix_near_kernel, chips),
        grid=(1,),
        in_specs=[scalar] + [whole(2, rows + TILE, LANES)] * chips + rest,
        out_specs=whole(chips, rows, LANES),
        out_shape=jax.ShapeDtypeStruct((chips, rows, LANES), jnp.bfloat16),
        compiler_params=params,
        cost_estimate=estimate(1 << 20, 1 << 20),
        name="mix_near",
    )(place, *near, gain, residual, streams, short_taps)
    return pl.pallas_call(
        mix_far_kernel,
        grid=(1,),
        in_specs=[scalar, whole(chips, rows, LANES), whole(chips, rows + TILE, LANES)] + rest,
        out_specs=whole(rows, channels),
        out_shape=jax.ShapeDtypeStruct((rows, channels), jnp.bfloat16),
        compiler_params=params,
        cost_estimate=estimate(1 << 20, 1 << 20),
        name="mix_far",
    )(place, mixed, far, gain, residual, streams, short_taps)


def local(streams, short_taps, spectrum, residual):
    rows, channels = residual.shape
    shards = lax.axis_size("seq")
    length = rows * shards
    fits = (
        channels == shards * LANES
        and rows % TILE == 0
        and rows >= 2 * TILE
        and length % (4 * LANES) == 0
        and length <= 2048
        and short_taps.shape[1] == 7
        and shards & (shards - 1) == 0
        and shards >= 2
    )
    if fits:
        return local_kernels(streams, short_taps, spectrum, residual)
    return local_general(streams, short_taps, spectrum, residual)


def solution(mesh):
    placed = (
        P(None, "seq", "chan"),
        P(None, None, "chan"),
        P(("chan", "seq"), None, None),
        P("seq", "chan"),
    )
    return jax.shard_map(
        local, mesh=mesh, in_specs=placed, out_specs=P("seq", "chan"), check_vma=False
    )
```

```python
import functools
import math

import jax
import jax.numpy as jnp
import numpy as np
from jax import lax
from jax.experimental import pallas as pl
from jax.experimental.pallas import tpu as pltpu
from jax.sharding import PartitionSpec as P

LANES = 128
TILE = 16
VMEM_LIMIT = 16 * 1024 * 1024


def passed_along(block, axis, distance):
    devices = range(lax.axis_size(axis))
    route = [(i - distance, i) for i in devices if i - distance in devices]
    return lax.ppermute(block, axis, route)


def section_sizes(length_all):
    power = length_all.bit_length() - 1
    first = (power + 2) // 3
    second = (power - first + 1) // 2
    third = power - first - second
    result = [2**first, 2**second]
    result.append(2**third)
    return result


def matmul_high(left, right):
    return jnp.dot(left, right, precision=lax.Precision.HIGHEST, preferred_element_type=jnp.float32)


def section_high(table, values):
    return jnp.einsum(
        "ka,cab->ckb",
        table,
        values,
        precision=lax.Precision.HIGHEST,
        preferred_element_type=jnp.float32,
    )


def dft_table(order, direction):
    index = jnp.arange(order, dtype=jnp.int32)
    product = index[:, None] * index[None, :] % order
    angle = direction * 2.0 * math.pi * product.astype(jnp.float32) / order
    return (jnp.cos(angle), jnp.sin(angle))


def transform(real_part, imag_part, factors, direction):
    columns, length_now = real_part.shape
    first = factors[0]
    table_cos, table_sin = dft_table(first, direction)
    if len(factors) == 1:
        real_out = matmul_high(real_part, table_cos) - matmul_high(imag_part, table_sin)
        imag_out = matmul_high(imag_part, table_cos) + matmul_high(real_part, table_sin)
        return (real_out, imag_out)
    rest = length_now // first
    real_wide = real_part.reshape(columns, first, rest)
    if imag_part is None:
        section_real = section_high(table_cos, real_wide)
        section_imag = section_high(table_sin, real_wide)
    else:
        imag_wide = imag_part.reshape(columns, first, rest)
        section_real = section_high(table_cos, real_wide) - section_high(table_sin, imag_wide)
        section_imag = section_high(table_cos, imag_wide) + section_high(table_sin, real_wide)
    outer = jnp.arange(first, dtype=jnp.int32)[:, None]
    inner = jnp.arange(rest, dtype=jnp.int32)[None, :]
    twist = (
        direction * 2.0 * math.pi * (outer * inner % length_now).astype(jnp.float32) / length_now
    )
    twist_cos = jnp.cos(twist)[None, :, :]
    twist_sin = jnp.sin(twist)[None, :, :]
    turned_real = (section_real * twist_cos - section_imag * twist_sin).reshape(
        columns * first, rest
    )
    turned_imag = (section_real * twist_sin + section_imag * twist_cos).reshape(
        columns * first, rest
    )
    real_out, imag_out = transform(turned_real, turned_imag, factors[1:], direction)
    real_out = jnp.transpose(real_out.reshape(columns, first, rest), (0, 2, 1)).reshape(
        columns, length_now
    )
    imag_out = jnp.transpose(imag_out.reshape(columns, first, rest), (0, 2, 1)).reshape(
        columns, length_now
    )
    return (real_out, imag_out)


def long_filter(gated_rows, spectrum):
    columns, length_all = gated_rows.shape
    padded = jnp.concatenate(
        [gated_rows.astype(jnp.float32), jnp.zeros((columns, length_all), jnp.float32)], axis=1
    )
    factors = section_sizes(2 * length_all)
    freq_real, freq_imag = transform(padded, None, factors, -1.0)
    spec_real = spectrum[:, 0, :]
    spec_imag = spectrum[:, 1, :]
    prod_real = freq_real * spec_real - freq_imag * spec_imag
    prod_imag = freq_real * spec_imag + freq_imag * spec_real
    back_real, back_imag = transform(prod_real, prod_imag, factors, 1.0)
    return (back_real[:, :length_all] / (2 * length_all)).astype(jnp.bfloat16)


def local_general(streams, short_taps, spectrum, residual):
    row_count = streams.shape[1]
    channels = streams.shape[2]
    span = short_taps.shape[1] - 1
    rim_rows = passed_along(streams[:, row_count - span :, :], "seq", 1)
    extended = jnp.concatenate([rim_rows, streams], axis=1)
    total = jnp.zeros((3, row_count, channels), jnp.float32)
    for offset in range(span + 1):
        total = total + short_taps[:, offset, None, :] * extended[
            :, span - offset : span - offset + row_count, :
        ].astype(jnp.float32)
    convolved = total.astype(jnp.bfloat16)
    q_conv = convolved[0]
    k_conv = convolved[1]
    v_conv = convolved[2]
    seq_devices = lax.axis_size("seq")
    owned_count = channels // seq_devices
    length_all = row_count * seq_devices
    gated = (k_conv.astype(jnp.float32) * v_conv.astype(jnp.float32)).astype(jnp.bfloat16)
    owned = lax.all_to_all(
        gated.reshape(row_count, seq_devices, owned_count),
        "seq",
        split_axis=1,
        concat_axis=0,
        tiled=True,
    )
    gated_whole = owned.reshape(length_all, owned_count)
    filtered = jnp.transpose(long_filter(jnp.transpose(gated_whole), spectrum))
    returned = lax.all_to_all(
        filtered.reshape(length_all, 1, owned_count), "seq", split_axis=0, concat_axis=1, tiled=True
    )
    filtered_local = returned.reshape(row_count, channels)
    resid = residual.astype(jnp.float32)
    mixed = resid + jax.nn.silu(resid) * q_conv.astype(jnp.float32) * filtered_local.astype(
        jnp.float32
    )
    return mixed.astype(jnp.bfloat16)


def rounded(values):
    return values.astype(jnp.bfloat16).astype(jnp.float32)


def short_conv_rolled(rows, taps):
    total = taps(0) * rows
    for offset in range(1, 7):
        total = total + taps(offset) * pltpu.roll(rows, offset, 0)
    return rounded(total)


def row_index(count):
    return lax.broadcasted_iota(jnp.int32, (count, LANES), 0)


def own_lanes(place_ref, k):
    return pl.ds(pl.multiple_of((place_ref[0] ^ k) * LANES, LANES), LANES)


def first_link(place_ref):
    return 2 + 2 * (place_ref[0] & 1)


def pack_block(k, v, q_last, taps, out_ref):
    rows = k.shape[0]
    row = row_index(TILE)
    gated = short_conv_rolled(k, lambda j: taps(1, j)) * short_conv_rolled(
        v, lambda j: taps(2, j)
    )
    out_ref[:TILE, :] = jnp.where(row < 6, k[:TILE], gated[:TILE]).astype(jnp.bfloat16)
    out_ref[TILE:rows, :] = gated[TILE:].astype(jnp.bfloat16)
    edge = jnp.where(row < 6, v[:TILE], v[rows - TILE :])
    edge = jnp.where((row >= 6) & (row < 10), pltpu.roll(q_last, 12, 0), edge)
    out_ref[rows : rows + TILE, :] = edge.astype(jnp.bfloat16)
    half = jnp.where(row_index(8) < 2, pltpu.roll(q_last[8:], 2, 0), k[rows - 8 :])
    out_ref[rows + TILE :, :] = half.astype(jnp.bfloat16)


def pack_chip(place_ref, kv_ref, q_ref, taps_ref, k, out_refs):
    for p in range(2):
        lanes = pl.ds(pl.multiple_of(((place_ref[0] & 1) ^ p) * LANES, LANES), LANES)
        owner = own_lanes(place_ref, k ^ p)
        pack_block(
            kv_ref[0, :, lanes].astype(jnp.float32),
            kv_ref[1, :, lanes].astype(jnp.float32),
            q_ref[:, lanes].astype(jnp.float32),
            lambda s, j: taps_ref[s, j : j + 1, owner],
            out_refs[p],
        )


def pack_first_kernel(
    place_ref, streams_ref, taps_hbm_ref, a_ref, b_ref, kv_out, q_out, taps_ref, kv, q, sems
):
    rows = streams_ref.shape[1]
    first = first_link(place_ref)
    order = (first, 6 - first, 0, 6)
    taps_copy = pltpu.make_async_copy(taps_hbm_ref, taps_ref, sems.at[8])
    copies = []
    for i, k in enumerate(order):
        chip = (place_ref[0] ^ k) >> 1
        lanes = pl.ds(pl.multiple_of(chip * (2 * LANES), 2 * LANES), 2 * LANES)
        to_kv, to_q = (kv, q) if i < 2 else (kv_out, q_out)
        pair = (
            pltpu.make_async_copy(
                streams_ref.at[pl.ds(1, 2), :, lanes], to_kv.at[i % 2], sems.at[2 * i]
            ),
            pltpu.make_async_copy(
                streams_ref.at[0, pl.ds(rows - TILE, TILE), lanes],
                to_q.at[i % 2],
                sems.at[2 * i + 1],
            ),
        )
        for copy in pair:
            copy.start()
        if i == 0:
            taps_copy.start()
        copies.append(pair)
    taps_copy.wait()
    for i, out_ref in enumerate((a_ref, b_ref)):
        for copy in copies[i]:
            copy.wait()
        pack_chip(
            place_ref, kv.at[i], q.at[i], taps_ref, order[i], [out_ref.at[0], out_ref.at[1]]
        )
    for pair in copies[2:]:
        for copy in pair:
            copy.wait()


def pack_second_kernel(place_ref, kv_ref, q_ref, taps_ref, own_ref, far_ref):
    for i, k, out_ref in ((1, 6, far_ref), (0, 0, own_ref)):
        pack_chip(
            place_ref, kv_ref.at[i], q_ref.at[i], taps_ref, k, [out_ref.at[0], out_ref.at[1]]
        )


def spectrum_kernel(quarter, view_ref, out_ref):
    blocks = view_ref.shape[0] // (2 * LANES)
    length = blocks * LANES
    per = quarter // LANES
    lane = lax.broadcasted_iota(jnp.int32, (LANES, LANES), 1)
    back = (LANES - lane) % LANES

    def block(part, k):
        return view_ref[pl.ds(2 * (k % blocks) + part, LANES, stride=2 * blocks), :]

    def turned(part, k):
        flipped = jnp.take_along_axis(block(part, k), back, axis=1, mode="promise_in_bounds")
        return jnp.where(lane == 0, block(part, k + 1), flipped)

    tail = jnp.zeros((LANES, LANES), jnp.float32)
    for m in range(4):
        for part in range(2):
            sign = 1.0 if part == 0 else -1.0
            for i in range(per):
                k = 2 * per * m + i
                folded = block(part, k) + sign * turned(part, blocks - k - 1)
                weight = 1.0 / length
                if i == 0:
                    weight = jnp.where(lane == 0, 0.5 / length, 1.0 / length)
                out_ref[2 * m + part, i * LANES : (i + 1) * LANES, :] = jnp.transpose(
                    folded * weight
                )
            k = 2 * per * m + per
            folded = (block(part, k) + sign * block(part, blocks - k)) * (0.5 / length)
            tail = jnp.where(
                lane == 8 * (2 * m + part),
                jnp.broadcast_to(folded[:, 0:1], (LANES, LANES)),
                tail,
            )
    tail = jnp.transpose(tail)
    for j in range(8):
        out_ref[j, quarter : quarter + 8, :] = tail[8 * j : 8 * j + 8]


def merge_kernel(*refs):
    for j, ref in enumerate(refs[:-2]):
        refs[-1][j] = ref[1]


def forward_kernel(far_ref, out_ref):
    out_ref[...] = far_ref[1]


def received(place_ref, own, first, second, core, far, cross):
    link = first_link(place_ref)
    return [
        (0, own.at[0]),
        (link, first.at[0]),
        (6 - link, second.at[0]),
        (1, core.at[0]),
        (1 ^ (6 - link), core.at[1]),
        (1 ^ link, core.at[2]),
        (6, far.at[0]),
        (7, cross),
    ]


def filter_kernel(
    place_ref,
    own_ref,
    first_ref,
    second_ref,
    core_ref,
    far_ref,
    cross_ref,
    taps_ref,
    h_ref,
    high_ref,
    low_ref,
    twist_ref,
    own_out,
    first_out,
    second_out,
    far_out,
    msg_ref,
    x_ref,
    z_ref,
    q_ref,
):
    shards = msg_ref.shape[0]
    rows = cross_ref.shape[0] - 24
    quarter = high_ref.shape[1]
    blocks = received(
        place_ref, own_ref, first_ref, second_ref, core_ref, far_ref, cross_ref
    )
    for k, block in blocks:
        msg_ref[place_ref[0] ^ k] = block[...]
    row = row_index(TILE)
    own = own_lanes(place_ref, 0)

    before = None
    for s in range(shards):
        top = msg_ref[s, :TILE, :].astype(jnp.float32)
        edge = msg_ref[s, rows : rows + TILE, :].astype(jnp.float32)
        half = msg_ref[s, rows + TILE :, :].astype(jnp.float32)
        if before is None:
            above_k = above_v = jnp.zeros_like(edge)
            halo = jnp.zeros_like(half)
        else:
            above_v, half_before = before
            above_k = jnp.concatenate([half_before, half_before], axis=0)
            halo = jnp.where(
                row_index(8) < 6,
                pltpu.roll(above_v, 12, 0)[:8],
                pltpu.roll(half_before, 6, 0),
            )
        k_conv = short_conv_rolled(
            jnp.where(row < 8, top, above_k), lambda j: taps_ref[1, j : j + 1, own]
        )
        v_conv = short_conv_rolled(
            jnp.where(row < 8, edge, above_v), lambda j: taps_ref[2, j : j + 1, own]
        )
        x_ref[s * rows : s * rows + TILE, :] = jnp.where(row < 6, rounded(k_conv * v_conv), top)
        x_ref[s * rows + TILE : (s + 1) * rows, :] = msg_ref[s, TILE:rows, :].astype(jnp.float32)
        msg_ref[s, rows : rows + 8, :] = halo.astype(jnp.bfloat16)
        before = (edge, half)

    x = jnp.concatenate(
        [x_ref[pl.ds(a, quarter, stride=4), :].astype(jnp.bfloat16) for a in range(4)], axis=1
    )
    z_ref[...] = jnp.dot(high_ref[...], x, preferred_element_type=jnp.float32) + jnp.dot(
        low_ref[...], x, preferred_element_type=jnp.float32
    )

    def combine(real, imag, g, count):
        u = []
        for a in range(4):
            if a == 0:
                u.append((real[0], imag[0]))
                continue
            wr = jnp.broadcast_to(twist_ref[g : g + count, 2 * a : 2 * a + 1], (count, LANES))
            wi = jnp.broadcast_to(
                twist_ref[g : g + count, 2 * a + 1 : 2 * a + 2], (count, LANES)
            )
            u.append((real[a] * wr - imag[a] * wi, real[a] * wi + imag[a] * wr, wr, wi))

        def four(v, sign):
            er, ei = v[0][0] + v[2][0], v[0][1] + v[2][1]
            dr, di = v[0][0] - v[2][0], v[0][1] - v[2][1]
            pr, pi = v[1][0] + v[3][0], v[1][1] + v[3][1]
            qr, qi = v[1][0] - v[3][0], v[1][1] - v[3][1]
            if sign < 0:
                one, three = (dr + qi, di - qr), (dr - qi, di + qr)
            else:
                one, three = (dr - qi, di + qr), (dr + qi, di - qr)
            return [(er + pr, ei + pi), one, (er - pr, ei - pi), three]

        freq = four(u, -1)
        prod = []
        for m in range(4):
            hr = h_ref[2 * m, g : g + count, :]
            hi = h_ref[2 * m + 1, g : g + count, :]
            xr, xi = freq[m]
            prod.append((xr * hr - xi * hi, xr * hi + xi * hr))
        v = four(prod, 1)
        out = [v[0]]
        for a in range(1, 4):
            wr, wi = u[a][2], u[a][3]
            vr, vi = v[a]
            out.append((vr * wr + vi * wi, vi * wr - vr * wi))
        return out

    for g in range(0, quarter, TILE):
        real = [z_ref[g : g + TILE, a * LANES : (a + 1) * LANES] for a in range(4)]
        imag = [
            z_ref[quarter + g : quarter + g + TILE, a * LANES : (a + 1) * LANES] for a in range(4)
        ]
        out = combine(real, imag, g, TILE)
        for a in range(4):
            lanes = slice(a * LANES, (a + 1) * LANES)
            for part in range(2):
                high = out[a][part].astype(jnp.bfloat16)
                low = (out[a][part] - high.astype(jnp.float32)).astype(jnp.bfloat16)
                q_ref[2 * part, g : g + TILE, lanes] = high
                q_ref[2 * part + 1, g : g + TILE, lanes] = low
    real = [z_ref[2 * quarter : 2 * quarter + 8, a * LANES : (a + 1) * LANES] for a in range(4)]
    last = combine(real, [jnp.zeros_like(r) for r in real], quarter, 8)

    y = None
    for part in range(2):
        high = high_ref[part * quarter : (part + 1) * quarter, :]
        low = low_ref[part * quarter : (part + 1) * quarter, :]
        for left, right in ((high, 0), (high, 1), (low, 0)):
            term = jnp.dot(left, q_ref[2 * part + right], preferred_element_type=jnp.float32)
            y = term if y is None else y + term
    sign = 1.0 - 2.0 * (row_index(quarter) % 2).astype(jnp.float32)
    for a in range(4):
        x_ref[pl.ds(a, quarter, stride=4), :] = (
            y[:, a * LANES : (a + 1) * LANES] + sign * last[a][0][0:1, :]
        )
    link = first_link(place_ref)
    for k, out_ref in (
        (link, first_out.at[0]),
        (link ^ 1, first_out.at[1]),
        (6 - link, second_out.at[0]),
        ((6 - link) ^ 1, second_out.at[1]),
        (6, far_out.at[0]),
        (7, far_out.at[1]),
        (0, own_out.at[0]),
        (1, own_out.at[1]),
    ):
        target = place_ref[0] ^ k
        start = pl.multiple_of(target * rows, rows)
        out_ref[:rows, :] = x_ref[pl.ds(start, rows), :].astype(jnp.bfloat16)
        out_ref[rows:, :] = msg_ref[target, rows : rows + 8, :]


def silu(values):
    return values / (1.0 + jnp.exp(-values))


def gain_kernel(q_ref, taps_ref, residual_ref, out_ref):
    for c in range(out_ref.shape[1] // LANES):
        lanes = slice(c * LANES, (c + 1) * LANES)
        conv = short_conv_rolled(
            q_ref[0, :, lanes].astype(jnp.float32), lambda j: taps_ref[0, j : j + 1, lanes]
        )
        out_ref[:, lanes] = silu(residual_ref[:, lanes].astype(jnp.float32)) * conv


def mixed_block(msg, lanes, gain_ref, residual_ref, q_ref, taps_ref, out_ref):
    rows = residual_ref.shape[0]
    row = row_index(TILE)
    halo = msg[rows:, :].astype(jnp.float32)
    window = jnp.where(
        row < 8, q_ref[0, :, lanes].astype(jnp.float32), jnp.concatenate([halo, halo], axis=0)
    )
    conv = short_conv_rolled(window, lambda j: taps_ref[0, j : j + 1, lanes])
    resid = residual_ref[:TILE, lanes].astype(jnp.float32)
    gain = jnp.where(row < 6, silu(resid) * conv, gain_ref[:TILE, lanes])
    out_ref[:TILE, :] = (resid + gain * msg[:TILE, :].astype(jnp.float32)).astype(jnp.bfloat16)
    out_ref[TILE:, :] = (
        residual_ref[TILE:, lanes].astype(jnp.float32)
        + gain_ref[TILE:, lanes] * msg[TILE:rows, :].astype(jnp.float32)
    ).astype(jnp.bfloat16)


def mix_and_store(place_ref, blocks, rest, out_ref, held, sems):
    copies = []
    for i, (k, block) in enumerate(blocks):
        lanes = own_lanes(place_ref, k)
        mixed_block(block, lanes, *rest, held.at[i])
        copy = pltpu.make_async_copy(held.at[i], out_ref.at[:, lanes], sems.at[i])
        copy.start()
        copies.append(copy)
    for copy in copies:
        copy.wait()


def mix_early_kernel(place_ref, own, first, second, core, far, *refs):
    rest, (out_ref, held, sems) = refs[:4], refs[4:]
    blocks = received(place_ref, own, first, second, core, far, None)[:7]
    mix_and_store(place_ref, blocks, rest, out_ref, held, sems)


def mix_late_kernel(place_ref, early_ref, cross, *refs):
    rest, (out_ref, held, sems) = refs[:4], refs[4:]
    mix_and_store(place_ref, [(7, cross)], rest, out_ref, held, sems)


def split_table(table):
    high = table.astype(jnp.bfloat16)
    low = (table - high.astype(np.float64)).astype(jnp.bfloat16)
    return high, low


def filter_tables(quarter):
    index = np.arange(quarter)
    angle = 2.0 * np.pi * (index[:, None] * index[None, :] % (2 * quarter)) / (2 * quarter)
    alternate = np.zeros((TILE, quarter))
    alternate[0] = 1.0 - 2.0 * (index % 2)
    high, low = split_table(np.concatenate([np.cos(angle), -np.sin(angle), alternate], axis=0))
    g = np.arange(quarter + 8)[:, None]
    a = np.arange(4)[None, :]
    turn = 2.0 * np.pi * (g * a) / (8 * quarter)
    twist = np.stack([np.cos(turn), -np.sin(turn)], axis=-1).reshape(quarter + 8, 8)
    return high, low, twist.astype(np.float32)


def estimate(flops, moved):
    return pl.CostEstimate(flops=flops, bytes_accessed=moved, transcendentals=0)


def exchanged(beside, own, first, second, far):
    def swap(block, partner):
        return lax.ppermute(block, "seq", [(i, partner(i)) for i in range(8)])

    first = swap(first, lambda i: i ^ (2 + 2 * (i & 1)))
    second = swap(second, lambda i: i ^ (4 - 2 * (i & 1)))
    far = swap(far, lambda i: i ^ 6)
    merged = pl.pallas_call(
        merge_kernel,
        in_specs=[pl.BlockSpec(memory_space=pltpu.VMEM)] * 3
        + [pl.BlockSpec(memory_space=pl.ANY)],
        out_shape=jax.ShapeDtypeStruct((3,) + own.shape[1:], own.dtype),
        compiler_params=pltpu.CompilerParams(vmem_limit_bytes=VMEM_LIMIT),
        cost_estimate=estimate(1 << 10, 1 << 17),
        name="merge",
    )(own, first, second, beside)
    cross = pl.pallas_call(
        forward_kernel,
        out_shape=jax.ShapeDtypeStruct(far.shape[1:], far.dtype),
        compiler_params=pltpu.CompilerParams(vmem_limit_bytes=VMEM_LIMIT),
        cost_estimate=estimate(1 << 31, 1 << 16),
        name="forward",
    )(far)
    core = swap(merged, lambda i: i ^ 1)
    return own, first, second, core, far, swap(cross, lambda i: i ^ 1)


def local_kernels(streams, short_taps, spectrum, residual):
    rows, channels = residual.shape
    shards = lax.axis_size("seq")
    length = rows * shards
    quarter = length // 4
    params = pltpu.CompilerParams(vmem_limit_bytes=VMEM_LIMIT)
    place = lax.axis_index("seq").astype(jnp.int32).reshape(1)
    scalar = pl.BlockSpec(memory_space=pltpu.SMEM)
    vector = pl.BlockSpec(memory_space=pltpu.VMEM)
    hbm = pl.BlockSpec(memory_space=pltpu.HBM)
    half = lambda *shape: jax.ShapeDtypeStruct(shape, jnp.bfloat16)
    full = lambda *shape: jax.ShapeDtypeStruct(shape, jnp.float32)
    sent = rows + 24
    first, second, kv, q_last, taps = pl.pallas_call(
        pack_first_kernel,
        in_specs=[scalar, hbm, hbm],
        out_shape=[
            half(2, sent, LANES),
            half(2, sent, LANES),
            half(2, 2, rows, 2 * LANES),
            half(2, TILE, 2 * LANES),
            full(*short_taps.shape),
        ],
        scratch_shapes=[
            pltpu.VMEM((2, 2, rows, 2 * LANES), jnp.bfloat16),
            pltpu.VMEM((2, TILE, 2 * LANES), jnp.bfloat16),
            pltpu.SemaphoreType.DMA((9,)),
        ],
        compiler_params=params,
        cost_estimate=estimate(1 << 22, 1 << 20),
        name="pack_first",
    )(
        place,
        pltpu.with_memory_space_constraint(streams, pltpu.HBM),
        pltpu.with_memory_space_constraint(short_taps, pltpu.HBM),
    )
    own, far = pl.pallas_call(
        pack_second_kernel,
        in_specs=[scalar] + [vector] * 3,
        out_shape=[half(2, sent, LANES)] * 2,
        compiler_params=params,
        cost_estimate=estimate(1 << 22, 1 << 20),
        name="pack_second",
    )(place, kv, q_last, taps)
    blocks = 2 * length // LANES
    view = jnp.transpose(spectrum.reshape(LANES, 2, blocks, LANES), (0, 2, 1, 3)).reshape(
        2 * blocks * LANES, LANES
    )
    folded = pl.pallas_call(
        functools.partial(spectrum_kernel, quarter),
        out_shape=full(8, quarter + 8, LANES),
        compiler_params=params,
        cost_estimate=estimate(1 << 32, 1 << 22),
        name="spectrum",
    )(view)
    arrived = exchanged(folded, own, first, second, far)
    high, low, twist = filter_tables(quarter)
    back = rows + 8
    filtered = pl.pallas_call(
        filter_kernel,
        in_specs=[scalar] + [vector] * 11,
        out_shape=[half(2, back, LANES)] * 4,
        scratch_shapes=[
            pltpu.VMEM((shards, sent, LANES), jnp.bfloat16),
            pltpu.VMEM((length, LANES), jnp.float32),
            pltpu.VMEM((2 * quarter + TILE, 4 * LANES), jnp.float32),
            pltpu.VMEM((4, quarter, 4 * LANES), jnp.bfloat16),
        ],
        compiler_params=params,
        cost_estimate=estimate(1 << 30, 1 << 22),
        name="filter",
    )(place, *arrived, taps, folded, high, low, twist)
    whole = lambda *shape: pl.BlockSpec(shape, lambda i: (0,) * len(shape))
    gain = pl.pallas_call(
        gain_kernel,
        grid=(1,),
        in_specs=[
            whole(1, rows, channels),
            whole(*short_taps.shape),
            whole(rows, channels),
        ],
        out_specs=whole(rows, channels),
        out_shape=full(rows, channels),
        compiler_params=params,
        cost_estimate=estimate(1 << 32, 1 << 20),
        name="gain",
    )(streams, taps, residual)
    own, first, second, core, far, cross = exchanged(gain, *filtered)
    rest = [
        whole(rows, channels),
        whole(rows, channels),
        whole(1, TILE, channels),
        whole(*short_taps.shape),
    ]
    mixed = pl.pallas_call(
        mix_early_kernel,
        grid=(1,),
        in_specs=[scalar]
        + [whole(2, back, LANES)] * 3
        + [whole(3, back, LANES), whole(2, back, LANES)]
        + rest,
        out_specs=hbm,
        out_shape=half(rows, channels),
        scratch_shapes=[
            pltpu.VMEM((7, rows, LANES), jnp.bfloat16),
            pltpu.SemaphoreType.DMA((7,)),
        ],
        compiler_params=params,
        cost_estimate=estimate(1 << 20, 1 << 20),
        name="mix_early",
    )(place, own, first, second, core, far, gain, residual, streams, taps)
    return pl.pallas_call(
        mix_late_kernel,
        grid=(1,),
        in_specs=[scalar, hbm, whole(back, LANES)] + rest,
        out_specs=hbm,
        out_shape=half(rows, channels),
        scratch_shapes=[
            pltpu.VMEM((1, rows, LANES), jnp.bfloat16),
            pltpu.SemaphoreType.DMA((1,)),
        ],
        input_output_aliases={1: 0},
        compiler_params=params,
        cost_estimate=estimate(1 << 20, 1 << 20),
        name="mix_late",
    )(place, mixed, cross, gain, residual, streams, taps)


def local(streams, short_taps, spectrum, residual):
    rows, channels = residual.shape
    shards = lax.axis_size("seq")
    length = rows * shards
    fits = (
        channels == shards * LANES
        and rows % TILE == 0
        and rows >= 2 * TILE
        and length % (4 * LANES) == 0
        and length <= 2048
        and short_taps.shape[1] == 7
        and shards == 8
    )
    if fits:
        return local_kernels(streams, short_taps, spectrum, residual)
    return local_general(streams, short_taps, spectrum, residual)


def solution(mesh):
    placed = (
        P(None, "seq", "chan"),
        P(None, None, "chan"),
        P(("chan", "seq"), None, None),
        P("seq", "chan"),
    )
    return jax.shard_map(
        local, mesh=mesh, in_specs=placed, out_specs=P("seq", "chan"), check_vma=False
    )
```

```python
import functools
import math

import jax
import jax.numpy as jnp
import numpy as np
from jax import lax
from jax.experimental import pallas as pl
from jax.experimental.pallas import tpu as pltpu
from jax.sharding import PartitionSpec as P

LANES = 128
TILE = 16
VMEM_LIMIT = 16 * 1024 * 1024


def passed_along(block, axis, distance):
    devices = range(lax.axis_size(axis))
    route = [(i - distance, i) for i in devices if i - distance in devices]
    return lax.ppermute(block, axis, route)


def section_sizes(length_all):
    power = length_all.bit_length() - 1
    first = (power + 2) // 3
    second = (power - first + 1) // 2
    third = power - first - second
    result = [2**first, 2**second]
    result.append(2**third)
    return result


def matmul_high(left, right):
    return jnp.dot(left, right, precision=lax.Precision.HIGHEST, preferred_element_type=jnp.float32)


def section_high(table, values):
    return jnp.einsum(
        "ka,cab->ckb",
        table,
        values,
        precision=lax.Precision.HIGHEST,
        preferred_element_type=jnp.float32,
    )


def dft_table(order, direction):
    index = jnp.arange(order, dtype=jnp.int32)
    product = index[:, None] * index[None, :] % order
    angle = direction * 2.0 * math.pi * product.astype(jnp.float32) / order
    return (jnp.cos(angle), jnp.sin(angle))


def transform(real_part, imag_part, factors, direction):
    columns, length_now = real_part.shape
    first = factors[0]
    table_cos, table_sin = dft_table(first, direction)
    if len(factors) == 1:
        real_out = matmul_high(real_part, table_cos) - matmul_high(imag_part, table_sin)
        imag_out = matmul_high(imag_part, table_cos) + matmul_high(real_part, table_sin)
        return (real_out, imag_out)
    rest = length_now // first
    real_wide = real_part.reshape(columns, first, rest)
    if imag_part is None:
        section_real = section_high(table_cos, real_wide)
        section_imag = section_high(table_sin, real_wide)
    else:
        imag_wide = imag_part.reshape(columns, first, rest)
        section_real = section_high(table_cos, real_wide) - section_high(table_sin, imag_wide)
        section_imag = section_high(table_cos, imag_wide) + section_high(table_sin, real_wide)
    outer = jnp.arange(first, dtype=jnp.int32)[:, None]
    inner = jnp.arange(rest, dtype=jnp.int32)[None, :]
    twist = (
        direction * 2.0 * math.pi * (outer * inner % length_now).astype(jnp.float32) / length_now
    )
    twist_cos = jnp.cos(twist)[None, :, :]
    twist_sin = jnp.sin(twist)[None, :, :]
    turned_real = (section_real * twist_cos - section_imag * twist_sin).reshape(
        columns * first, rest
    )
    turned_imag = (section_real * twist_sin + section_imag * twist_cos).reshape(
        columns * first, rest
    )
    real_out, imag_out = transform(turned_real, turned_imag, factors[1:], direction)
    real_out = jnp.transpose(real_out.reshape(columns, first, rest), (0, 2, 1)).reshape(
        columns, length_now
    )
    imag_out = jnp.transpose(imag_out.reshape(columns, first, rest), (0, 2, 1)).reshape(
        columns, length_now
    )
    return (real_out, imag_out)


def long_filter(gated_rows, spectrum):
    columns, length_all = gated_rows.shape
    padded = jnp.concatenate(
        [gated_rows.astype(jnp.float32), jnp.zeros((columns, length_all), jnp.float32)], axis=1
    )
    factors = section_sizes(2 * length_all)
    freq_real, freq_imag = transform(padded, None, factors, -1.0)
    spec_real = spectrum[:, 0, :]
    spec_imag = spectrum[:, 1, :]
    prod_real = freq_real * spec_real - freq_imag * spec_imag
    prod_imag = freq_real * spec_imag + freq_imag * spec_real
    back_real, back_imag = transform(prod_real, prod_imag, factors, 1.0)
    return (back_real[:, :length_all] / (2 * length_all)).astype(jnp.bfloat16)


def local_general(streams, short_taps, spectrum, residual):
    row_count = streams.shape[1]
    channels = streams.shape[2]
    span = short_taps.shape[1] - 1
    rim_rows = passed_along(streams[:, row_count - span :, :], "seq", 1)
    extended = jnp.concatenate([rim_rows, streams], axis=1)
    total = jnp.zeros((3, row_count, channels), jnp.float32)
    for offset in range(span + 1):
        total = total + short_taps[:, offset, None, :] * extended[
            :, span - offset : span - offset + row_count, :
        ].astype(jnp.float32)
    convolved = total.astype(jnp.bfloat16)
    q_conv = convolved[0]
    k_conv = convolved[1]
    v_conv = convolved[2]
    seq_devices = lax.axis_size("seq")
    owned_count = channels // seq_devices
    length_all = row_count * seq_devices
    gated = (k_conv.astype(jnp.float32) * v_conv.astype(jnp.float32)).astype(jnp.bfloat16)
    owned = lax.all_to_all(
        gated.reshape(row_count, seq_devices, owned_count),
        "seq",
        split_axis=1,
        concat_axis=0,
        tiled=True,
    )
    gated_whole = owned.reshape(length_all, owned_count)
    filtered = jnp.transpose(long_filter(jnp.transpose(gated_whole), spectrum))
    returned = lax.all_to_all(
        filtered.reshape(length_all, 1, owned_count), "seq", split_axis=0, concat_axis=1, tiled=True
    )
    filtered_local = returned.reshape(row_count, channels)
    resid = residual.astype(jnp.float32)
    mixed = resid + jax.nn.silu(resid) * q_conv.astype(jnp.float32) * filtered_local.astype(
        jnp.float32
    )
    return mixed.astype(jnp.bfloat16)


def rounded(values):
    return values.astype(jnp.bfloat16).astype(jnp.float32)


def short_conv_rolled(rows, taps):
    total = taps(0) * rows
    for offset in range(1, 7):
        total = total + taps(offset) * pltpu.roll(rows, offset, 0)
    return rounded(total)


def row_index(count):
    return lax.broadcasted_iota(jnp.int32, (count, LANES), 0)


def own_lanes(place_ref, k):
    return pl.ds(pl.multiple_of((place_ref[0] ^ k) * LANES, LANES), LANES)


def first_link(place_ref):
    return 2 + 2 * (place_ref[0] & 1)


def pack_block(k, v, q_last, taps, out_ref):
    rows = k.shape[0]
    row = row_index(TILE)
    gated = short_conv_rolled(k, lambda j: taps(1, j)) * short_conv_rolled(
        v, lambda j: taps(2, j)
    )
    out_ref[:TILE, :] = jnp.where(row < 6, k[:TILE], gated[:TILE]).astype(jnp.bfloat16)
    out_ref[TILE:rows, :] = gated[TILE:].astype(jnp.bfloat16)
    edge = jnp.where(row < 6, v[:TILE], v[rows - TILE :])
    edge = jnp.where((row >= 6) & (row < 10), pltpu.roll(q_last, 12, 0), edge)
    out_ref[rows : rows + TILE, :] = edge.astype(jnp.bfloat16)
    half = jnp.where(row_index(8) < 2, pltpu.roll(q_last[8:], 2, 0), k[rows - 8 :])
    out_ref[rows + TILE :, :] = half.astype(jnp.bfloat16)


def chip_order(place_ref):
    first = first_link(place_ref)
    return (0, first, 6 - first, 6)


def pack_one(place_ref, kv_ref, q_ref, taps_ref, chip, p, out_ref):
    lanes = pl.ds(pl.multiple_of(((place_ref[0] & 1) ^ p) * LANES, LANES), LANES)
    owner = own_lanes(place_ref, chip_order(place_ref)[chip] ^ p)
    pack_block(
        kv_ref[chip, 0, :, lanes].astype(jnp.float32),
        kv_ref[chip, 1, :, lanes].astype(jnp.float32),
        q_ref[chip, :, lanes].astype(jnp.float32),
        lambda s, j: taps_ref[s, j : j + 1, owner],
        out_ref,
    )


def pack_first_kernel(
    place_ref, streams_ref, taps_hbm_ref, core_ref, kv_ref, q_ref, taps_ref, sems
):
    rows = streams_ref.shape[1]
    order = chip_order(place_ref)
    copies = [pltpu.make_async_copy(taps_hbm_ref, taps_ref, sems.at[8])]
    copies[0].start()
    for i, k in enumerate(order):
        chip = (place_ref[0] ^ k) >> 1
        lanes = pl.ds(pl.multiple_of(chip * (2 * LANES), 2 * LANES), 2 * LANES)
        pair = (
            pltpu.make_async_copy(
                streams_ref.at[pl.ds(1, 2), :, lanes], kv_ref.at[i], sems.at[2 * i]
            ),
            pltpu.make_async_copy(
                streams_ref.at[0, pl.ds(rows - TILE, TILE), lanes],
                q_ref.at[i],
                sems.at[2 * i + 1],
            ),
        )
        for copy in pair:
            copy.start()
        copies.append(pair)
    copies[0].wait()
    for i in range(3):
        for copy in copies[1 + i]:
            copy.wait()
        slot = (0, 2, 1)[i]
        pack_one(place_ref, kv_ref, q_ref, taps_ref, i, 1, core_ref.at[slot])
    for copy in copies[4]:
        copy.wait()


def pack_far_kernel(place_ref, kv_ref, q_ref, taps_ref, same_ref, cross_ref):
    for p, out_ref in enumerate((same_ref, cross_ref)):
        pack_one(place_ref, kv_ref, q_ref, taps_ref, 3, p, out_ref)


def pack_near_kernel(place_ref, kv_ref, q_ref, taps_ref, *out_refs):
    for chip, out_ref in enumerate(out_refs):
        pack_one(place_ref, kv_ref, q_ref, taps_ref, chip, 0, out_ref)


def spectrum_kernel(quarter, view_ref, out_ref):
    blocks = view_ref.shape[0] // (2 * LANES)
    length = blocks * LANES
    per = quarter // LANES
    lane = lax.broadcasted_iota(jnp.int32, (LANES, LANES), 1)
    back = (LANES - lane) % LANES

    def block(part, k):
        return view_ref[pl.ds(2 * (k % blocks) + part, LANES, stride=2 * blocks), :]

    def turned(part, k):
        flipped = jnp.take_along_axis(block(part, k), back, axis=1, mode="promise_in_bounds")
        return jnp.where(lane == 0, block(part, k + 1), flipped)

    tail = jnp.zeros((LANES, LANES), jnp.float32)
    for m in range(4):
        for part in range(2):
            sign = 1.0 if part == 0 else -1.0
            for i in range(per):
                k = 2 * per * m + i
                folded = block(part, k) + sign * turned(part, blocks - k - 1)
                weight = 1.0 / length
                if i == 0:
                    weight = jnp.where(lane == 0, 0.5 / length, 1.0 / length)
                out_ref[2 * m + part, i * LANES : (i + 1) * LANES, :] = jnp.transpose(
                    folded * weight
                )
            k = 2 * per * m + per
            folded = (block(part, k) + sign * block(part, blocks - k)) * (0.5 / length)
            tail = jnp.where(
                lane == 8 * (2 * m + part),
                jnp.broadcast_to(folded[:, 0:1], (LANES, LANES)),
                tail,
            )
    tail = jnp.transpose(tail)
    for j in range(8):
        out_ref[j, quarter : quarter + 8, :] = tail[8 * j : 8 * j + 8]


def merge_kernel(first, second, core, first_out, second_out):
    for i, (near, out) in enumerate(((first, first_out), (second, second_out))):
        out[0] = near[...]
        out[1] = core[1 + i]


def received(place_ref, own, core, same, cross, first, second):
    link = first_link(place_ref)
    return [
        (0, own),
        (1, core.at[0]),
        (6, same),
        (7, cross),
        (link, first.at[0]),
        (link ^ 1, first.at[1]),
        (6 - link, second.at[0]),
        ((6 - link) ^ 1, second.at[1]),
    ]


def filter_kernel(
    place_ref,
    own_ref,
    core_ref,
    same_ref,
    cross_ref,
    first_ref,
    second_ref,
    taps_ref,
    h_ref,
    high_ref,
    low_ref,
    twist_ref,
    core_out,
    same_out,
    cross_out,
    own_out,
    first_out,
    second_out,
    msg_ref,
    x_ref,
    z_ref,
    q_ref,
):
    shards = msg_ref.shape[0]
    rows = own_ref.shape[0] - 24
    quarter = high_ref.shape[1]
    blocks = received(
        place_ref, own_ref, core_ref, same_ref, cross_ref, first_ref, second_ref
    )
    for k, block in blocks:
        msg_ref[place_ref[0] ^ k] = block[...]
    row = row_index(TILE)
    own = own_lanes(place_ref, 0)

    before = None
    for s in range(shards):
        top = msg_ref[s, :TILE, :].astype(jnp.float32)
        edge = msg_ref[s, rows : rows + TILE, :].astype(jnp.float32)
        half = msg_ref[s, rows + TILE :, :].astype(jnp.float32)
        if before is None:
            above_k = above_v = jnp.zeros_like(edge)
            halo = jnp.zeros_like(half)
        else:
            above_v, half_before = before
            above_k = jnp.concatenate([half_before, half_before], axis=0)
            halo = jnp.where(
                row_index(8) < 6,
                pltpu.roll(above_v, 12, 0)[:8],
                pltpu.roll(half_before, 6, 0),
            )
        k_conv = short_conv_rolled(
            jnp.where(row < 8, top, above_k), lambda j: taps_ref[1, j : j + 1, own]
        )
        v_conv = short_conv_rolled(
            jnp.where(row < 8, edge, above_v), lambda j: taps_ref[2, j : j + 1, own]
        )
        x_ref[s * rows : s * rows + TILE, :] = jnp.where(row < 6, rounded(k_conv * v_conv), top)
        x_ref[s * rows + TILE : (s + 1) * rows, :] = msg_ref[s, TILE:rows, :].astype(jnp.float32)
        msg_ref[s, rows : rows + 8, :] = halo.astype(jnp.bfloat16)
        before = (edge, half)

    x = jnp.concatenate(
        [x_ref[pl.ds(a, quarter, stride=4), :].astype(jnp.bfloat16) for a in range(4)], axis=1
    )
    z_ref[...] = jnp.dot(high_ref[...], x, preferred_element_type=jnp.float32) + jnp.dot(
        low_ref[...], x, preferred_element_type=jnp.float32
    )

    def combine(real, imag, g, count):
        u = []
        for a in range(4):
            if a == 0:
                u.append((real[0], imag[0]))
                continue
            wr = jnp.broadcast_to(twist_ref[g : g + count, 2 * a : 2 * a + 1], (count, LANES))
            wi = jnp.broadcast_to(
                twist_ref[g : g + count, 2 * a + 1 : 2 * a + 2], (count, LANES)
            )
            u.append((real[a] * wr - imag[a] * wi, real[a] * wi + imag[a] * wr, wr, wi))

        def four(v, sign):
            er, ei = v[0][0] + v[2][0], v[0][1] + v[2][1]
            dr, di = v[0][0] - v[2][0], v[0][1] - v[2][1]
            pr, pi = v[1][0] + v[3][0], v[1][1] + v[3][1]
            qr, qi = v[1][0] - v[3][0], v[1][1] - v[3][1]
            if sign < 0:
                one, three = (dr + qi, di - qr), (dr - qi, di + qr)
            else:
                one, three = (dr - qi, di + qr), (dr + qi, di - qr)
            return [(er + pr, ei + pi), one, (er - pr, ei - pi), three]

        freq = four(u, -1)
        prod = []
        for m in range(4):
            hr = h_ref[2 * m, g : g + count, :]
            hi = h_ref[2 * m + 1, g : g + count, :]
            xr, xi = freq[m]
            prod.append((xr * hr - xi * hi, xr * hi + xi * hr))
        v = four(prod, 1)
        out = [v[0]]
        for a in range(1, 4):
            wr, wi = u[a][2], u[a][3]
            vr, vi = v[a]
            out.append((vr * wr + vi * wi, vi * wr - vr * wi))
        return out

    for g in range(0, quarter, TILE):
        real = [z_ref[g : g + TILE, a * LANES : (a + 1) * LANES] for a in range(4)]
        imag = [
            z_ref[quarter + g : quarter + g + TILE, a * LANES : (a + 1) * LANES] for a in range(4)
        ]
        out = combine(real, imag, g, TILE)
        for a in range(4):
            lanes = slice(a * LANES, (a + 1) * LANES)
            for part in range(2):
                high = out[a][part].astype(jnp.bfloat16)
                low = (out[a][part] - high.astype(jnp.float32)).astype(jnp.bfloat16)
                q_ref[2 * part, g : g + TILE, lanes] = high
                q_ref[2 * part + 1, g : g + TILE, lanes] = low
    real = [z_ref[2 * quarter : 2 * quarter + 8, a * LANES : (a + 1) * LANES] for a in range(4)]
    last = combine(real, [jnp.zeros_like(r) for r in real], quarter, 8)

    y = None
    for part in range(2):
        high = high_ref[part * quarter : (part + 1) * quarter, :]
        low = low_ref[part * quarter : (part + 1) * quarter, :]
        for left, right in ((high, 0), (high, 1), (low, 0)):
            term = jnp.dot(left, q_ref[2 * part + right], preferred_element_type=jnp.float32)
            y = term if y is None else y + term
    sign = 1.0 - 2.0 * (row_index(quarter) % 2).astype(jnp.float32)
    for a in range(4):
        x_ref[pl.ds(a, quarter, stride=4), :] = (
            y[:, a * LANES : (a + 1) * LANES] + sign * last[a][0][0:1, :]
        )
    link = first_link(place_ref)
    for k, out_ref in (
        (1, core_out.at[0]),
        ((6 - link) ^ 1, core_out.at[1]),
        (link ^ 1, core_out.at[2]),
        (6, same_out),
        (7, cross_out),
        (0, own_out),
        (link, first_out),
        (6 - link, second_out),
    ):
        target = place_ref[0] ^ k
        start = pl.multiple_of(target * rows, rows)
        out_ref[:rows, :] = x_ref[pl.ds(start, rows), :].astype(jnp.bfloat16)
        out_ref[rows:, :] = msg_ref[target, rows : rows + 8, :]


def silu(values):
    return values / (1.0 + jnp.exp(-values))


def gain_kernel(q_ref, taps_ref, residual_ref, out_ref):
    for c in range(out_ref.shape[1] // LANES):
        lanes = slice(c * LANES, (c + 1) * LANES)
        conv = short_conv_rolled(
            q_ref[0, :, lanes].astype(jnp.float32), lambda j: taps_ref[0, j : j + 1, lanes]
        )
        out_ref[:, lanes] = silu(residual_ref[:, lanes].astype(jnp.float32)) * conv


def mixed_block(msg, lanes, gain_ref, residual_ref, q_ref, taps_ref, out_ref):
    rows = residual_ref.shape[0]
    row = row_index(TILE)
    halo = msg[rows:, :].astype(jnp.float32)
    window = jnp.where(
        row < 8, q_ref[0, :TILE, lanes].astype(jnp.float32), jnp.concatenate([halo, halo], axis=0)
    )
    conv = short_conv_rolled(window, lambda j: taps_ref[0, j : j + 1, lanes])
    resid = residual_ref[:TILE, lanes].astype(jnp.float32)
    gain = jnp.where(row < 6, silu(resid) * conv, gain_ref[:TILE, lanes])
    out_ref[:TILE, :] = (resid + gain * msg[:TILE, :].astype(jnp.float32)).astype(jnp.bfloat16)
    out_ref[TILE:, :] = (
        residual_ref[TILE:, lanes].astype(jnp.float32)
        + gain_ref[TILE:, lanes] * msg[TILE:rows, :].astype(jnp.float32)
    ).astype(jnp.bfloat16)


def mix_kernel(place_ref, *refs):
    arrived, rest, (out_ref, held, sems) = refs[:6], refs[6:10], refs[10:]
    copies = []
    for i, (k, block) in enumerate(received(place_ref, *arrived)):
        lanes = own_lanes(place_ref, k)
        mixed_block(block, lanes, *rest, held.at[i])
        copy = pltpu.make_async_copy(held.at[i], out_ref.at[:, lanes], sems.at[i])
        copy.start()
        copies.append(copy)
    for copy in copies:
        copy.wait()


def split_table(table):
    high = table.astype(jnp.bfloat16)
    low = (table - high.astype(np.float64)).astype(jnp.bfloat16)
    return high, low


def filter_tables(quarter):
    index = np.arange(quarter)
    angle = 2.0 * np.pi * (index[:, None] * index[None, :] % (2 * quarter)) / (2 * quarter)
    alternate = np.zeros((TILE, quarter))
    alternate[0] = 1.0 - 2.0 * (index % 2)
    high, low = split_table(np.concatenate([np.cos(angle), -np.sin(angle), alternate], axis=0))
    g = np.arange(quarter + 8)[:, None]
    a = np.arange(4)[None, :]
    turn = 2.0 * np.pi * (g * a) / (8 * quarter)
    twist = np.stack([np.cos(turn), -np.sin(turn)], axis=-1).reshape(quarter + 8, 8)
    return high, low, twist.astype(np.float32)


def estimate(flops, moved):
    return pl.CostEstimate(flops=flops, bytes_accessed=moved, transcendentals=0)


def exchanged(core, same, cross, own, first, second):
    def swap(block, partner):
        return lax.ppermute(block, "seq", [(i, partner(i)) for i in range(8)])

    core = swap(core, lambda i: i ^ 1)
    same = swap(same, lambda i: i ^ 6)
    cross = swap(cross, lambda i: i ^ 7)
    first, second = pl.pallas_call(
        merge_kernel,
        out_shape=[jax.ShapeDtypeStruct((2,) + own.shape, own.dtype)] * 2,
        compiler_params=pltpu.CompilerParams(vmem_limit_bytes=VMEM_LIMIT),
        cost_estimate=estimate(1 << 10, 1 << 17),
        name="merge",
    )(first, second, core)
    first = swap(first, lambda i: i ^ (2 + 2 * (i & 1)))
    second = swap(second, lambda i: i ^ (4 - 2 * (i & 1)))
    return own, core, same, cross, first, second


def local_kernels(streams, short_taps, spectrum, residual):
    rows, channels = residual.shape
    shards = lax.axis_size("seq")
    length = rows * shards
    quarter = length // 4
    params = pltpu.CompilerParams(vmem_limit_bytes=VMEM_LIMIT)
    place = lax.axis_index("seq").astype(jnp.int32).reshape(1)
    scalar = pl.BlockSpec(memory_space=pltpu.SMEM)
    vector = pl.BlockSpec(memory_space=pltpu.VMEM)
    hbm = pl.BlockSpec(memory_space=pltpu.HBM)
    half = lambda *shape: jax.ShapeDtypeStruct(shape, jnp.bfloat16)
    full = lambda *shape: jax.ShapeDtypeStruct(shape, jnp.float32)
    sent = rows + 24
    core, kv, q_last, taps = pl.pallas_call(
        pack_first_kernel,
        in_specs=[scalar, hbm, hbm],
        out_shape=[
            half(3, sent, LANES),
            half(4, 2, rows, 2 * LANES),
            half(4, TILE, 2 * LANES),
            full(*short_taps.shape),
        ],
        scratch_shapes=[pltpu.SemaphoreType.DMA((9,))],
        compiler_params=params,
        cost_estimate=estimate(1 << 22, 1 << 20),
        name="pack_first",
    )(
        place,
        pltpu.with_memory_space_constraint(streams, pltpu.HBM),
        pltpu.with_memory_space_constraint(short_taps, pltpu.HBM),
    )
    same, cross = pl.pallas_call(
        pack_far_kernel,
        in_specs=[scalar] + [vector] * 3,
        out_shape=[half(sent, LANES)] * 2,
        compiler_params=params,
        cost_estimate=estimate(1 << 22, 1 << 20),
        name="pack_far",
    )(place, kv, q_last, taps)
    own, first, second = pl.pallas_call(
        pack_near_kernel,
        in_specs=[scalar] + [vector] * 3,
        out_shape=[half(sent, LANES)] * 3,
        compiler_params=params,
        cost_estimate=estimate(1 << 22, 1 << 20),
        name="pack_near",
    )(place, kv, q_last, taps)
    arrived = exchanged(core, same, cross, own, first, second)

    blocks = 2 * length // LANES
    view = jnp.transpose(spectrum.reshape(LANES, 2, blocks, LANES), (0, 2, 1, 3)).reshape(
        2 * blocks * LANES, LANES
    )
    folded = pl.pallas_call(
        functools.partial(spectrum_kernel, quarter),
        out_shape=full(8, quarter + 8, LANES),
        compiler_params=params,
        cost_estimate=estimate(1 << 32, 1 << 22),
        name="spectrum",
    )(view)
    high, low, twist = filter_tables(quarter)
    back = rows + 8
    filtered = pl.pallas_call(
        filter_kernel,
        in_specs=[scalar] + [vector] * 11,
        out_shape=[half(3, back, LANES)] + [half(back, LANES)] * 5,
        scratch_shapes=[
            pltpu.VMEM((shards, sent, LANES), jnp.bfloat16),
            pltpu.VMEM((length, LANES), jnp.float32),
            pltpu.VMEM((2 * quarter + TILE, 4 * LANES), jnp.float32),
            pltpu.VMEM((4, quarter, 4 * LANES), jnp.bfloat16),
        ],
        compiler_params=params,
        cost_estimate=estimate(1 << 30, 1 << 22),
        name="filter",
    )(place, *arrived, taps, folded, high, low, twist)
    whole = lambda *shape: pl.BlockSpec(shape, lambda i: (0,) * len(shape))
    gain = pl.pallas_call(
        gain_kernel,
        grid=(1,),
        in_specs=[
            whole(1, rows, channels),
            whole(*short_taps.shape),
            whole(rows, channels),
        ],
        out_specs=whole(rows, channels),
        out_shape=full(rows, channels),
        compiler_params=params,
        cost_estimate=estimate(1 << 32, 1 << 20),
        name="gain",
    )(streams, taps, residual)
    arrived = exchanged(*filtered)
    return pl.pallas_call(
        mix_kernel,
        in_specs=[scalar] + [vector] * 10,
        out_specs=hbm,
        out_shape=half(rows, channels),
        scratch_shapes=[
            pltpu.VMEM((shards, rows, LANES), jnp.bfloat16),
            pltpu.SemaphoreType.DMA((shards,)),
        ],
        compiler_params=params,
        cost_estimate=estimate(1 << 20, 1 << 20),
        name="mix",
    )(place, *arrived, gain, residual, streams, taps)


def local(streams, short_taps, spectrum, residual):
    rows, channels = residual.shape
    shards = lax.axis_size("seq")
    length = rows * shards
    fits = (
        channels == shards * LANES
        and rows % TILE == 0
        and rows >= 2 * TILE
        and length % (4 * LANES) == 0
        and length <= 2048
        and short_taps.shape[1] == 7
        and shards == 8
    )
    if fits:
        return local_kernels(streams, short_taps, spectrum, residual)
    return local_general(streams, short_taps, spectrum, residual)


def solution(mesh):
    placed = (
        P(None, "seq", "chan"),
        P(None, None, "chan"),
        P(("chan", "seq"), None, None),
        P("seq", "chan"),
    )
    return jax.shard_map(
        local, mesh=mesh, in_specs=placed, out_specs=P("seq", "chan"), check_vma=False
    )
```

```python
import functools
import math

import jax
import jax.numpy as jnp
import numpy as np
from jax import lax
from jax.experimental import pallas as pl
from jax.experimental.pallas import tpu as pltpu
from jax.sharding import PartitionSpec as P

LANES = 128
TILE = 16
VMEM_LIMIT = 16 * 1024 * 1024


def passed_along(block, axis, distance):
    devices = range(lax.axis_size(axis))
    route = [(i - distance, i) for i in devices if i - distance in devices]
    return lax.ppermute(block, axis, route)


def section_sizes(length_all):
    power = length_all.bit_length() - 1
    first = (power + 2) // 3
    second = (power - first + 1) // 2
    third = power - first - second
    result = [2**first, 2**second]
    result.append(2**third)
    return result


def matmul_high(left, right):
    return jnp.dot(left, right, precision=lax.Precision.HIGHEST, preferred_element_type=jnp.float32)


def section_high(table, values):
    return jnp.einsum(
        "ka,cab->ckb",
        table,
        values,
        precision=lax.Precision.HIGHEST,
        preferred_element_type=jnp.float32,
    )


def dft_table(order, direction):
    index = jnp.arange(order, dtype=jnp.int32)
    product = index[:, None] * index[None, :] % order
    angle = direction * 2.0 * math.pi * product.astype(jnp.float32) / order
    return (jnp.cos(angle), jnp.sin(angle))


def transform(real_part, imag_part, factors, direction):
    columns, length_now = real_part.shape
    first = factors[0]
    table_cos, table_sin = dft_table(first, direction)
    if len(factors) == 1:
        real_out = matmul_high(real_part, table_cos) - matmul_high(imag_part, table_sin)
        imag_out = matmul_high(imag_part, table_cos) + matmul_high(real_part, table_sin)
        return (real_out, imag_out)
    rest = length_now // first
    real_wide = real_part.reshape(columns, first, rest)
    if imag_part is None:
        section_real = section_high(table_cos, real_wide)
        section_imag = section_high(table_sin, real_wide)
    else:
        imag_wide = imag_part.reshape(columns, first, rest)
        section_real = section_high(table_cos, real_wide) - section_high(table_sin, imag_wide)
        section_imag = section_high(table_cos, imag_wide) + section_high(table_sin, real_wide)
    outer = jnp.arange(first, dtype=jnp.int32)[:, None]
    inner = jnp.arange(rest, dtype=jnp.int32)[None, :]
    twist = (
        direction * 2.0 * math.pi * (outer * inner % length_now).astype(jnp.float32) / length_now
    )
    twist_cos = jnp.cos(twist)[None, :, :]
    twist_sin = jnp.sin(twist)[None, :, :]
    turned_real = (section_real * twist_cos - section_imag * twist_sin).reshape(
        columns * first, rest
    )
    turned_imag = (section_real * twist_sin + section_imag * twist_cos).reshape(
        columns * first, rest
    )
    real_out, imag_out = transform(turned_real, turned_imag, factors[1:], direction)
    real_out = jnp.transpose(real_out.reshape(columns, first, rest), (0, 2, 1)).reshape(
        columns, length_now
    )
    imag_out = jnp.transpose(imag_out.reshape(columns, first, rest), (0, 2, 1)).reshape(
        columns, length_now
    )
    return (real_out, imag_out)


def long_filter(gated_rows, spectrum):
    columns, length_all = gated_rows.shape
    padded = jnp.concatenate(
        [gated_rows.astype(jnp.float32), jnp.zeros((columns, length_all), jnp.float32)], axis=1
    )
    factors = section_sizes(2 * length_all)
    freq_real, freq_imag = transform(padded, None, factors, -1.0)
    spec_real = spectrum[:, 0, :]
    spec_imag = spectrum[:, 1, :]
    prod_real = freq_real * spec_real - freq_imag * spec_imag
    prod_imag = freq_real * spec_imag + freq_imag * spec_real
    back_real, back_imag = transform(prod_real, prod_imag, factors, 1.0)
    return (back_real[:, :length_all] / (2 * length_all)).astype(jnp.bfloat16)


def local_general(streams, short_taps, spectrum, residual):
    row_count = streams.shape[1]
    channels = streams.shape[2]
    span = short_taps.shape[1] - 1
    rim_rows = passed_along(streams[:, row_count - span :, :], "seq", 1)
    extended = jnp.concatenate([rim_rows, streams], axis=1)
    total = jnp.zeros((3, row_count, channels), jnp.float32)
    for offset in range(span + 1):
        total = total + short_taps[:, offset, None, :] * extended[
            :, span - offset : span - offset + row_count, :
        ].astype(jnp.float32)
    convolved = total.astype(jnp.bfloat16)
    q_conv = convolved[0]
    k_conv = convolved[1]
    v_conv = convolved[2]
    seq_devices = lax.axis_size("seq")
    owned_count = channels // seq_devices
    length_all = row_count * seq_devices
    gated = (k_conv.astype(jnp.float32) * v_conv.astype(jnp.float32)).astype(jnp.bfloat16)
    owned = lax.all_to_all(
        gated.reshape(row_count, seq_devices, owned_count),
        "seq",
        split_axis=1,
        concat_axis=0,
        tiled=True,
    )
    gated_whole = owned.reshape(length_all, owned_count)
    filtered = jnp.transpose(long_filter(jnp.transpose(gated_whole), spectrum))
    returned = lax.all_to_all(
        filtered.reshape(length_all, 1, owned_count), "seq", split_axis=0, concat_axis=1, tiled=True
    )
    filtered_local = returned.reshape(row_count, channels)
    resid = residual.astype(jnp.float32)
    mixed = resid + jax.nn.silu(resid) * q_conv.astype(jnp.float32) * filtered_local.astype(
        jnp.float32
    )
    return mixed.astype(jnp.bfloat16)


def rounded(values):
    return values.astype(jnp.bfloat16).astype(jnp.float32)


def short_conv_rolled(rows, taps):
    total = taps(0) * rows
    for offset in range(1, 7):
        total = total + taps(offset) * pltpu.roll(rows, offset, 0)
    return rounded(total)


def row_index(count):
    return lax.broadcasted_iota(jnp.int32, (count, LANES), 0)


def own_lanes(place_ref, k):
    return pl.ds(pl.multiple_of((place_ref[0] ^ k) * LANES, LANES), LANES)


def first_link(place_ref):
    return 2 + 2 * (place_ref[0] & 1)


def pack_block(k, v, q_last, taps, out_ref):
    rows = k.shape[0]
    row = row_index(TILE)
    gated = short_conv_rolled(k, lambda j: taps(1, j)) * short_conv_rolled(
        v, lambda j: taps(2, j)
    )
    out_ref[:TILE, :] = jnp.where(row < 6, k[:TILE], gated[:TILE]).astype(jnp.bfloat16)
    out_ref[TILE:rows, :] = gated[TILE:].astype(jnp.bfloat16)
    edge = jnp.where(row < 6, v[:TILE], v[rows - TILE :])
    edge = jnp.where((row >= 6) & (row < 10), pltpu.roll(q_last, 12, 0), edge)
    out_ref[rows : rows + TILE, :] = edge.astype(jnp.bfloat16)
    half = jnp.where(row_index(8) < 2, pltpu.roll(q_last[8:], 2, 0), k[rows - 8 :])
    out_ref[rows + TILE :, :] = half.astype(jnp.bfloat16)


def chip_order(place_ref):
    first = first_link(place_ref)
    return (0, first, 6 - first, 6)


def pack_one(place_ref, kv_ref, q_ref, taps_ref, chip, p, out_ref):
    lanes = pl.ds(pl.multiple_of(((place_ref[0] & 1) ^ p) * LANES, LANES), LANES)
    owner = own_lanes(place_ref, chip_order(place_ref)[chip] ^ p)
    pack_block(
        kv_ref[chip, 0, :, lanes].astype(jnp.float32),
        kv_ref[chip, 1, :, lanes].astype(jnp.float32),
        q_ref[chip, :, lanes].astype(jnp.float32),
        lambda s, j: taps_ref[s, j : j + 1, owner],
        out_ref,
    )


def pack_first_kernel(
    place_ref, streams_ref, taps_hbm_ref, first_ref, second_ref, kv_ref, q_ref, taps_ref, sems
):
    rows = streams_ref.shape[1]
    order = chip_order(place_ref)
    taps_copy = pltpu.make_async_copy(taps_hbm_ref, taps_ref, sems.at[8])
    taps_copy.start()
    copies = {}
    for i in (1, 2, 3, 0):
        chip = (place_ref[0] ^ order[i]) >> 1
        lanes = pl.ds(pl.multiple_of(chip * (2 * LANES), 2 * LANES), 2 * LANES)
        copies[i] = (
            pltpu.make_async_copy(
                streams_ref.at[pl.ds(1, 2), :, lanes], kv_ref.at[i], sems.at[2 * i]
            ),
            pltpu.make_async_copy(
                streams_ref.at[0, pl.ds(rows - TILE, TILE), lanes],
                q_ref.at[i],
                sems.at[2 * i + 1],
            ),
        )
        for copy in copies[i]:
            copy.start()
    taps_copy.wait()
    for i, out_ref in ((1, first_ref), (2, second_ref)):
        for copy in copies[i]:
            copy.wait()
        for p in range(2):
            pack_one(place_ref, kv_ref, q_ref, taps_ref, i, p, out_ref.at[p])
    for i in (3, 0):
        for copy in copies[i]:
            copy.wait()


def pack_pair_kernel(chip, place_ref, kv_ref, q_ref, taps_ref, *out_refs):
    for p, out_ref in enumerate(out_refs):
        pack_one(place_ref, kv_ref, q_ref, taps_ref, chip, p, out_ref)


def spectrum_kernel(quarter, view_ref, out_ref):
    blocks = view_ref.shape[0] // (2 * LANES)
    length = blocks * LANES
    per = quarter // LANES
    lane = lax.broadcasted_iota(jnp.int32, (LANES, LANES), 1)
    back = (LANES - lane) % LANES

    def block(part, k):
        return view_ref[pl.ds(2 * (k % blocks) + part, LANES, stride=2 * blocks), :]

    def turned(part, k):
        flipped = jnp.take_along_axis(block(part, k), back, axis=1, mode="promise_in_bounds")
        return jnp.where(lane == 0, block(part, k + 1), flipped)

    tail = jnp.zeros((LANES, LANES), jnp.float32)
    for m in range(4):
        for part in range(2):
            sign = 1.0 if part == 0 else -1.0
            for i in range(per):
                k = 2 * per * m + i
                folded = block(part, k) + sign * turned(part, blocks - k - 1)
                weight = 1.0 / length
                if i == 0:
                    weight = jnp.where(lane == 0, 0.5 / length, 1.0 / length)
                out_ref[2 * m + part, i * LANES : (i + 1) * LANES, :] = jnp.transpose(
                    folded * weight
                )
            k = 2 * per * m + per
            folded = (block(part, k) + sign * block(part, blocks - k)) * (0.5 / length)
            tail = jnp.where(
                lane == 8 * (2 * m + part),
                jnp.broadcast_to(folded[:, 0:1], (LANES, LANES)),
                tail,
            )
    tail = jnp.transpose(tail)
    for j in range(8):
        out_ref[j, quarter : quarter + 8, :] = tail[8 * j : 8 * j + 8]


def forward_kernel(pair_ref, out_ref):
    out_ref[...] = pair_ref[1]


def received(place_ref, own, sibling, first, second, first_on, second_on, same, cross):
    link = first_link(place_ref)
    return [
        (0, own),
        (1, sibling),
        (link, first.at[0]),
        (6 - link, second.at[0]),
        ((6 - link) ^ 1, first_on),
        (link ^ 1, second_on),
        (6, same),
        (7, cross),
    ]


def filter_kernel(
    place_ref,
    own_ref,
    sibling_ref,
    first_ref,
    second_ref,
    first_on_ref,
    second_on_ref,
    same_ref,
    cross_ref,
    taps_ref,
    h_ref,
    high_ref,
    low_ref,
    twist_ref,
    own_out,
    sibling_out,
    first_out,
    second_out,
    same_out,
    cross_out,
    msg_ref,
    x_ref,
    z_ref,
    q_ref,
):
    shards = msg_ref.shape[0]
    rows = own_ref.shape[0] - 24
    quarter = high_ref.shape[1]
    blocks = received(
        place_ref,
        own_ref,
        sibling_ref,
        first_ref,
        second_ref,
        first_on_ref,
        second_on_ref,
        same_ref,
        cross_ref,
    )
    for k, block in blocks:
        msg_ref[place_ref[0] ^ k] = block[...]
    row = row_index(TILE)
    own = own_lanes(place_ref, 0)

    before = None
    for s in range(shards):
        top = msg_ref[s, :TILE, :].astype(jnp.float32)
        edge = msg_ref[s, rows : rows + TILE, :].astype(jnp.float32)
        half = msg_ref[s, rows + TILE :, :].astype(jnp.float32)
        if before is None:
            above_k = above_v = jnp.zeros_like(edge)
            halo = jnp.zeros_like(half)
        else:
            above_v, half_before = before
            above_k = jnp.concatenate([half_before, half_before], axis=0)
            halo = jnp.where(
                row_index(8) < 6,
                pltpu.roll(above_v, 12, 0)[:8],
                pltpu.roll(half_before, 6, 0),
            )
        k_conv = short_conv_rolled(
            jnp.where(row < 8, top, above_k), lambda j: taps_ref[1, j : j + 1, own]
        )
        v_conv = short_conv_rolled(
            jnp.where(row < 8, edge, above_v), lambda j: taps_ref[2, j : j + 1, own]
        )
        x_ref[s * rows : s * rows + TILE, :] = jnp.where(row < 6, rounded(k_conv * v_conv), top)
        x_ref[s * rows + TILE : (s + 1) * rows, :] = msg_ref[s, TILE:rows, :].astype(jnp.float32)
        msg_ref[s, rows : rows + 8, :] = halo.astype(jnp.bfloat16)
        before = (edge, half)

    x = jnp.concatenate(
        [x_ref[pl.ds(a, quarter, stride=4), :].astype(jnp.bfloat16) for a in range(4)], axis=1
    )
    z_ref[...] = jnp.dot(high_ref[...], x, preferred_element_type=jnp.float32) + jnp.dot(
        low_ref[...], x, preferred_element_type=jnp.float32
    )

    def combine(real, imag, g, count):
        u = []
        for a in range(4):
            if a == 0:
                u.append((real[0], imag[0]))
                continue
            wr = jnp.broadcast_to(twist_ref[g : g + count, 2 * a : 2 * a + 1], (count, LANES))
            wi = jnp.broadcast_to(
                twist_ref[g : g + count, 2 * a + 1 : 2 * a + 2], (count, LANES)
            )
            u.append((real[a] * wr - imag[a] * wi, real[a] * wi + imag[a] * wr, wr, wi))

        def four(v, sign):
            er, ei = v[0][0] + v[2][0], v[0][1] + v[2][1]
            dr, di = v[0][0] - v[2][0], v[0][1] - v[2][1]
            pr, pi = v[1][0] + v[3][0], v[1][1] + v[3][1]
            qr, qi = v[1][0] - v[3][0], v[1][1] - v[3][1]
            if sign < 0:
                one, three = (dr + qi, di - qr), (dr - qi, di + qr)
            else:
                one, three = (dr - qi, di + qr), (dr + qi, di - qr)
            return [(er + pr, ei + pi), one, (er - pr, ei - pi), three]

        freq = four(u, -1)
        prod = []
        for m in range(4):
            hr = h_ref[2 * m, g : g + count, :]
            hi = h_ref[2 * m + 1, g : g + count, :]
            xr, xi = freq[m]
            prod.append((xr * hr - xi * hi, xr * hi + xi * hr))
        v = four(prod, 1)
        out = [v[0]]
        for a in range(1, 4):
            wr, wi = u[a][2], u[a][3]
            vr, vi = v[a]
            out.append((vr * wr + vi * wi, vi * wr - vr * wi))
        return out

    for g in range(0, quarter, TILE):
        real = [z_ref[g : g + TILE, a * LANES : (a + 1) * LANES] for a in range(4)]
        imag = [
            z_ref[quarter + g : quarter + g + TILE, a * LANES : (a + 1) * LANES] for a in range(4)
        ]
        out = combine(real, imag, g, TILE)
        for a in range(4):
            lanes = slice(a * LANES, (a + 1) * LANES)
            for part in range(2):
                high = out[a][part].astype(jnp.bfloat16)
                low = (out[a][part] - high.astype(jnp.float32)).astype(jnp.bfloat16)
                q_ref[2 * part, g : g + TILE, lanes] = high
                q_ref[2 * part + 1, g : g + TILE, lanes] = low
    real = [z_ref[2 * quarter : 2 * quarter + 8, a * LANES : (a + 1) * LANES] for a in range(4)]
    last = combine(real, [jnp.zeros_like(r) for r in real], quarter, 8)

    y = None
    for part in range(2):
        high = high_ref[part * quarter : (part + 1) * quarter, :]
        low = low_ref[part * quarter : (part + 1) * quarter, :]
        for left, right in ((high, 0), (high, 1), (low, 0)):
            term = jnp.dot(left, q_ref[2 * part + right], preferred_element_type=jnp.float32)
            y = term if y is None else y + term
    sign = 1.0 - 2.0 * (row_index(quarter) % 2).astype(jnp.float32)
    for a in range(4):
        x_ref[pl.ds(a, quarter, stride=4), :] = (
            y[:, a * LANES : (a + 1) * LANES] + sign * last[a][0][0:1, :]
        )
    link = first_link(place_ref)
    for k, out_ref in (
        (link, first_out.at[0]),
        (link ^ 1, first_out.at[1]),
        (6 - link, second_out.at[0]),
        ((6 - link) ^ 1, second_out.at[1]),
        (6, same_out),
        (7, cross_out),
        (0, own_out),
        (1, sibling_out),
    ):
        target = place_ref[0] ^ k
        start = pl.multiple_of(target * rows, rows)
        out_ref[:rows, :] = x_ref[pl.ds(start, rows), :].astype(jnp.bfloat16)
        out_ref[rows:, :] = msg_ref[target, rows : rows + 8, :]


def silu(values):
    return values / (1.0 + jnp.exp(-values))


def gain_kernel(q_ref, taps_ref, residual_ref, out_ref):
    for c in range(out_ref.shape[1] // LANES):
        lanes = slice(c * LANES, (c + 1) * LANES)
        conv = short_conv_rolled(
            q_ref[0, :, lanes].astype(jnp.float32), lambda j: taps_ref[0, j : j + 1, lanes]
        )
        out_ref[:, lanes] = silu(residual_ref[:, lanes].astype(jnp.float32)) * conv


def mixed_block(msg, lanes, gain_ref, residual_ref, q_ref, taps_ref, out_ref):
    rows = residual_ref.shape[0]
    row = row_index(TILE)
    halo = msg[rows:, :].astype(jnp.float32)
    window = jnp.where(
        row < 8, q_ref[0, :TILE, lanes].astype(jnp.float32), jnp.concatenate([halo, halo], axis=0)
    )
    conv = short_conv_rolled(window, lambda j: taps_ref[0, j : j + 1, lanes])
    resid = residual_ref[:TILE, lanes].astype(jnp.float32)
    gain = jnp.where(row < 6, silu(resid) * conv, gain_ref[:TILE, lanes])
    out_ref[:TILE, :] = (resid + gain * msg[:TILE, :].astype(jnp.float32)).astype(jnp.bfloat16)
    out_ref[TILE:, :] = (
        residual_ref[TILE:, lanes].astype(jnp.float32)
        + gain_ref[TILE:, lanes] * msg[TILE:rows, :].astype(jnp.float32)
    ).astype(jnp.bfloat16)


def mix_kernel(place_ref, *refs):
    arrived, rest, (out_ref, held, sems) = refs[:8], refs[8:12], refs[12:]
    copies = []
    for i, (k, block) in enumerate(received(place_ref, *arrived)):
        lanes = own_lanes(place_ref, k)
        mixed_block(block, lanes, *rest, held.at[i])
        copy = pltpu.make_async_copy(held.at[i], out_ref.at[:, lanes], sems.at[i])
        copy.start()
        copies.append(copy)
    for copy in copies:
        copy.wait()


def split_table(table):
    high = table.astype(jnp.bfloat16)
    low = (table - high.astype(np.float64)).astype(jnp.bfloat16)
    return high, low


def filter_tables(quarter):
    index = np.arange(quarter)
    angle = 2.0 * np.pi * (index[:, None] * index[None, :] % (2 * quarter)) / (2 * quarter)
    alternate = np.zeros((TILE, quarter))
    alternate[0] = 1.0 - 2.0 * (index % 2)
    high, low = split_table(np.concatenate([np.cos(angle), -np.sin(angle), alternate], axis=0))
    g = np.arange(quarter + 8)[:, None]
    a = np.arange(4)[None, :]
    turn = 2.0 * np.pi * (g * a) / (8 * quarter)
    twist = np.stack([np.cos(turn), -np.sin(turn)], axis=-1).reshape(quarter + 8, 8)
    return high, low, twist.astype(np.float32)


def estimate(flops, moved):
    return pl.CostEstimate(flops=flops, bytes_accessed=moved, transcendentals=0)


def exchanged(own, sibling, first, second, same, cross):
    def swap(block, partner):
        return lax.ppermute(block, "seq", [(i, partner(i)) for i in range(8)])

    def sent_on(pair):
        block = pl.pallas_call(
            forward_kernel,
            out_shape=jax.ShapeDtypeStruct(own.shape, own.dtype),
            compiler_params=pltpu.CompilerParams(vmem_limit_bytes=VMEM_LIMIT),
            cost_estimate=estimate(1 << 10, 1 << 16),
            name="forward",
        )(pair)
        return swap(block, lambda i: i ^ 1)

    first = swap(first, lambda i: i ^ (2 + 2 * (i & 1)))
    second = swap(second, lambda i: i ^ (4 - 2 * (i & 1)))
    same = swap(same, lambda i: i ^ 6)
    cross = swap(cross, lambda i: i ^ 7)
    sibling = swap(sibling, lambda i: i ^ 1)
    return own, sibling, first, second, sent_on(first), sent_on(second), same, cross


def local_kernels(streams, short_taps, spectrum, residual):
    rows, channels = residual.shape
    shards = lax.axis_size("seq")
    length = rows * shards
    quarter = length // 4
    params = pltpu.CompilerParams(vmem_limit_bytes=VMEM_LIMIT)
    place = lax.axis_index("seq").astype(jnp.int32).reshape(1)
    scalar = pl.BlockSpec(memory_space=pltpu.SMEM)
    vector = pl.BlockSpec(memory_space=pltpu.VMEM)
    hbm = pl.BlockSpec(memory_space=pltpu.HBM)
    half = lambda *shape: jax.ShapeDtypeStruct(shape, jnp.bfloat16)
    full = lambda *shape: jax.ShapeDtypeStruct(shape, jnp.float32)
    sent = rows + 24
    first, second, kv, q_last, taps = pl.pallas_call(
        pack_first_kernel,
        in_specs=[scalar, hbm, hbm],
        out_shape=[
            half(2, sent, LANES),
            half(2, sent, LANES),
            half(4, 2, rows, 2 * LANES),
            half(4, TILE, 2 * LANES),
            full(*short_taps.shape),
        ],
        scratch_shapes=[pltpu.SemaphoreType.DMA((9,))],
        compiler_params=params,
        cost_estimate=estimate(1 << 22, 1 << 20),
        name="pack_first",
    )(
        place,
        pltpu.with_memory_space_constraint(streams, pltpu.HBM),
        pltpu.with_memory_space_constraint(short_taps, pltpu.HBM),
    )

    def pack_pair(chip, name):
        return pl.pallas_call(
            functools.partial(pack_pair_kernel, chip),
            in_specs=[scalar] + [vector] * 3,
            out_shape=[half(sent, LANES)] * 2,
            compiler_params=params,
            cost_estimate=estimate(1 << 22, 1 << 20),
            name=name,
        )(place, kv, q_last, taps)

    same, cross = pack_pair(3, "pack_far")
    own, sibling = pack_pair(0, "pack_own")
    arrived = exchanged(own, sibling, first, second, same, cross)

    blocks = 2 * length // LANES
    view = jnp.transpose(spectrum.reshape(LANES, 2, blocks, LANES), (0, 2, 1, 3)).reshape(
        2 * blocks * LANES, LANES
    )
    folded = pl.pallas_call(
        functools.partial(spectrum_kernel, quarter),
        out_shape=full(8, quarter + 8, LANES),
        compiler_params=params,
        cost_estimate=estimate(1 << 32, 1 << 22),
        name="spectrum",
    )(view)
    high, low, twist = filter_tables(quarter)
    back = rows + 8
    filtered = pl.pallas_call(
        filter_kernel,
        in_specs=[scalar] + [vector] * 13,
        out_shape=[half(back, LANES)] * 2
        + [half(2, back, LANES)] * 2
        + [half(back, LANES)] * 2,
        scratch_shapes=[
            pltpu.VMEM((shards, sent, LANES), jnp.bfloat16),
            pltpu.VMEM((length, LANES), jnp.float32),
            pltpu.VMEM((2 * quarter + TILE, 4 * LANES), jnp.float32),
            pltpu.VMEM((4, quarter, 4 * LANES), jnp.bfloat16),
        ],
        compiler_params=params,
        cost_estimate=estimate(1 << 30, 1 << 22),
        name="filter",
    )(place, *arrived, taps, folded, high, low, twist)
    whole = lambda *shape: pl.BlockSpec(shape, lambda i: (0,) * len(shape))
    gain = pl.pallas_call(
        gain_kernel,
        grid=(1,),
        in_specs=[
            whole(1, rows, channels),
            whole(*short_taps.shape),
            whole(rows, channels),
        ],
        out_specs=whole(rows, channels),
        out_shape=full(rows, channels),
        compiler_params=params,
        cost_estimate=estimate(1 << 32, 1 << 20),
        name="gain",
    )(streams, taps, residual)
    arrived = exchanged(*filtered)
    return pl.pallas_call(
        mix_kernel,
        in_specs=[scalar] + [vector] * 12,
        out_specs=hbm,
        out_shape=half(rows, channels),
        scratch_shapes=[
            pltpu.VMEM((shards, rows, LANES), jnp.bfloat16),
            pltpu.SemaphoreType.DMA((shards,)),
        ],
        compiler_params=params,
        cost_estimate=estimate(1 << 20, 1 << 20),
        name="mix",
    )(place, *arrived, gain, residual, streams, taps)


def local(streams, short_taps, spectrum, residual):
    rows, channels = residual.shape
    shards = lax.axis_size("seq")
    length = rows * shards
    fits = (
        channels == shards * LANES
        and rows % TILE == 0
        and rows >= 2 * TILE
        and length % (4 * LANES) == 0
        and length <= 2048
        and short_taps.shape[1] == 7
        and shards == 8
    )
    if fits:
        return local_kernels(streams, short_taps, spectrum, residual)
    return local_general(streams, short_taps, spectrum, residual)


def solution(mesh):
    placed = (
        P(None, "seq", "chan"),
        P(None, None, "chan"),
        P(("chan", "seq"), None, None),
        P("seq", "chan"),
    )
    return jax.shard_map(
        local, mesh=mesh, in_specs=placed, out_specs=P("seq", "chan"), check_vma=False
    )
```

```python
import functools
import math

import jax
import jax.numpy as jnp
import numpy as np
from jax import lax
from jax.experimental import pallas as pl
from jax.experimental.pallas import tpu as pltpu
from jax.sharding import PartitionSpec as P

LANES = 128
TILE = 16
VMEM_LIMIT = 16 * 1024 * 1024


def passed_along(block, axis, distance):
    devices = range(lax.axis_size(axis))
    route = [(i - distance, i) for i in devices if i - distance in devices]
    return lax.ppermute(block, axis, route)


def section_sizes(length_all):
    power = length_all.bit_length() - 1
    first = (power + 2) // 3
    second = (power - first + 1) // 2
    third = power - first - second
    result = [2**first, 2**second]
    result.append(2**third)
    return result


def matmul_high(left, right):
    return jnp.dot(left, right, precision=lax.Precision.HIGHEST, preferred_element_type=jnp.float32)


def section_high(table, values):
    return jnp.einsum(
        "ka,cab->ckb",
        table,
        values,
        precision=lax.Precision.HIGHEST,
        preferred_element_type=jnp.float32,
    )


def dft_table(order, direction):
    index = jnp.arange(order, dtype=jnp.int32)
    product = index[:, None] * index[None, :] % order
    angle = direction * 2.0 * math.pi * product.astype(jnp.float32) / order
    return (jnp.cos(angle), jnp.sin(angle))


def transform(real_part, imag_part, factors, direction):
    columns, length_now = real_part.shape
    first = factors[0]
    table_cos, table_sin = dft_table(first, direction)
    if len(factors) == 1:
        real_out = matmul_high(real_part, table_cos) - matmul_high(imag_part, table_sin)
        imag_out = matmul_high(imag_part, table_cos) + matmul_high(real_part, table_sin)
        return (real_out, imag_out)
    rest = length_now // first
    real_wide = real_part.reshape(columns, first, rest)
    if imag_part is None:
        section_real = section_high(table_cos, real_wide)
        section_imag = section_high(table_sin, real_wide)
    else:
        imag_wide = imag_part.reshape(columns, first, rest)
        section_real = section_high(table_cos, real_wide) - section_high(table_sin, imag_wide)
        section_imag = section_high(table_cos, imag_wide) + section_high(table_sin, real_wide)
    outer = jnp.arange(first, dtype=jnp.int32)[:, None]
    inner = jnp.arange(rest, dtype=jnp.int32)[None, :]
    twist = (
        direction * 2.0 * math.pi * (outer * inner % length_now).astype(jnp.float32) / length_now
    )
    twist_cos = jnp.cos(twist)[None, :, :]
    twist_sin = jnp.sin(twist)[None, :, :]
    turned_real = (section_real * twist_cos - section_imag * twist_sin).reshape(
        columns * first, rest
    )
    turned_imag = (section_real * twist_sin + section_imag * twist_cos).reshape(
        columns * first, rest
    )
    real_out, imag_out = transform(turned_real, turned_imag, factors[1:], direction)
    real_out = jnp.transpose(real_out.reshape(columns, first, rest), (0, 2, 1)).reshape(
        columns, length_now
    )
    imag_out = jnp.transpose(imag_out.reshape(columns, first, rest), (0, 2, 1)).reshape(
        columns, length_now
    )
    return (real_out, imag_out)


def long_filter(gated_rows, spectrum):
    columns, length_all = gated_rows.shape
    padded = jnp.concatenate(
        [gated_rows.astype(jnp.float32), jnp.zeros((columns, length_all), jnp.float32)], axis=1
    )
    factors = section_sizes(2 * length_all)
    freq_real, freq_imag = transform(padded, None, factors, -1.0)
    spec_real = spectrum[:, 0, :]
    spec_imag = spectrum[:, 1, :]
    prod_real = freq_real * spec_real - freq_imag * spec_imag
    prod_imag = freq_real * spec_imag + freq_imag * spec_real
    back_real, back_imag = transform(prod_real, prod_imag, factors, 1.0)
    return (back_real[:, :length_all] / (2 * length_all)).astype(jnp.bfloat16)


def local_general(streams, short_taps, spectrum, residual):
    row_count = streams.shape[1]
    channels = streams.shape[2]
    span = short_taps.shape[1] - 1
    rim_rows = passed_along(streams[:, row_count - span :, :], "seq", 1)
    extended = jnp.concatenate([rim_rows, streams], axis=1)
    total = jnp.zeros((3, row_count, channels), jnp.float32)
    for offset in range(span + 1):
        total = total + short_taps[:, offset, None, :] * extended[
            :, span - offset : span - offset + row_count, :
        ].astype(jnp.float32)
    convolved = total.astype(jnp.bfloat16)
    q_conv = convolved[0]
    k_conv = convolved[1]
    v_conv = convolved[2]
    seq_devices = lax.axis_size("seq")
    owned_count = channels // seq_devices
    length_all = row_count * seq_devices
    gated = (k_conv.astype(jnp.float32) * v_conv.astype(jnp.float32)).astype(jnp.bfloat16)
    owned = lax.all_to_all(
        gated.reshape(row_count, seq_devices, owned_count),
        "seq",
        split_axis=1,
        concat_axis=0,
        tiled=True,
    )
    gated_whole = owned.reshape(length_all, owned_count)
    filtered = jnp.transpose(long_filter(jnp.transpose(gated_whole), spectrum))
    returned = lax.all_to_all(
        filtered.reshape(length_all, 1, owned_count), "seq", split_axis=0, concat_axis=1, tiled=True
    )
    filtered_local = returned.reshape(row_count, channels)
    resid = residual.astype(jnp.float32)
    mixed = resid + jax.nn.silu(resid) * q_conv.astype(jnp.float32) * filtered_local.astype(
        jnp.float32
    )
    return mixed.astype(jnp.bfloat16)


def rounded(values):
    return values.astype(jnp.bfloat16).astype(jnp.float32)


def short_conv_rolled(rows, taps):
    total = taps(0) * rows
    for offset in range(1, 7):
        total = total + taps(offset) * pltpu.roll(rows, offset, 0)
    return rounded(total)


def row_index(count):
    return lax.broadcasted_iota(jnp.int32, (count, LANES), 0)


def own_lanes(place_ref, k):
    return pl.ds(pl.multiple_of((place_ref[0] ^ k) * LANES, LANES), LANES)


def first_link(place_ref):
    return 2 + 2 * (place_ref[0] & 1)


def pack_block(k, v, q_last, taps, out_ref):
    rows = k.shape[0]
    row = row_index(TILE)
    gated = short_conv_rolled(k, lambda j: taps(1, j)) * short_conv_rolled(
        v, lambda j: taps(2, j)
    )
    out_ref[:TILE, :] = jnp.where(row < 6, k[:TILE], gated[:TILE]).astype(jnp.bfloat16)
    out_ref[TILE:rows, :] = gated[TILE:].astype(jnp.bfloat16)
    edge = jnp.where(row < 6, v[:TILE], v[rows - TILE :])
    edge = jnp.where((row >= 6) & (row < 10), pltpu.roll(q_last, 12, 0), edge)
    out_ref[rows : rows + TILE, :] = edge.astype(jnp.bfloat16)
    half = jnp.where(row_index(8) < 2, pltpu.roll(q_last[8:], 2, 0), k[rows - 8 :])
    out_ref[rows + TILE :, :] = half.astype(jnp.bfloat16)


def chip_order(place_ref):
    first = first_link(place_ref)
    return (0, first, 6 - first, 6)


def pack_one(place_ref, kv_ref, q_ref, taps_ref, chip, p, out_ref):
    lanes = pl.ds(pl.multiple_of(((place_ref[0] & 1) ^ p) * LANES, LANES), LANES)
    owner = own_lanes(place_ref, chip_order(place_ref)[chip] ^ p)
    pack_block(
        kv_ref[chip, 0, :, lanes].astype(jnp.float32),
        kv_ref[chip, 1, :, lanes].astype(jnp.float32),
        q_ref[chip, :, lanes].astype(jnp.float32),
        lambda s, j: taps_ref[s, j : j + 1, owner],
        out_ref,
    )


def pack_first_kernel(
    place_ref, streams_ref, taps_hbm_ref, first_ref, second_ref, kv_ref, q_ref, taps_ref, sems
):
    rows = streams_ref.shape[1]
    order = chip_order(place_ref)
    taps_copy = pltpu.make_async_copy(taps_hbm_ref, taps_ref, sems.at[8])
    taps_copy.start()
    copies = {}
    for i in (1, 2, 3, 0):
        chip = (place_ref[0] ^ order[i]) >> 1
        lanes = pl.ds(pl.multiple_of(chip * (2 * LANES), 2 * LANES), 2 * LANES)
        copies[i] = (
            pltpu.make_async_copy(
                streams_ref.at[pl.ds(1, 2), :, lanes], kv_ref.at[i], sems.at[2 * i]
            ),
            pltpu.make_async_copy(
                streams_ref.at[0, pl.ds(rows - TILE, TILE), lanes],
                q_ref.at[i],
                sems.at[2 * i + 1],
            ),
        )
        for copy in copies[i]:
            copy.start()
    taps_copy.wait()
    for i, out_ref in ((1, first_ref), (2, second_ref)):
        for copy in copies[i]:
            copy.wait()
        for p in range(2):
            pack_one(place_ref, kv_ref, q_ref, taps_ref, i, p, out_ref.at[p])
    for i in (3, 0):
        for copy in copies[i]:
            copy.wait()


def pack_pair_kernel(chip, place_ref, kv_ref, q_ref, taps_ref, *out_refs):
    for p, out_ref in enumerate(out_refs):
        pack_one(place_ref, kv_ref, q_ref, taps_ref, chip, p, out_ref)


def spectrum_kernel(quarter, view_ref, out_ref):
    blocks = view_ref.shape[0] // (2 * LANES)
    per = quarter // LANES
    scale = 1.0 / (blocks * LANES)
    row = lax.broadcasted_iota(jnp.int32, (quarter + TILE, 2 * quarter), 0)
    col = lax.broadcasted_iota(jnp.int32, (quarter + TILE, 2 * quarter), 1)
    ahead = (col < quarter) & (row == col)
    back = (col >= quarter) & (row + col == 2 * quarter)
    turn = jnp.where(ahead | back, 1.0, 0.0).astype(jnp.bfloat16)

    def columns(part, start):
        return [
            view_ref[pl.ds(2 * (start + i) + part, LANES, stride=2 * blocks), :]
            for i in range(per)
        ]

    for part in range(2):
        sign = 1.0 if part == 0 else -1.0
        heads, tails = [], []
        for m in range(4):
            start = 2 * per * m
            values = columns(part, start) + [
                sign * v for v in columns(part, blocks - start - per)
            ]
            values = jnp.concatenate(values, axis=1)
            high = values.astype(jnp.bfloat16)
            low = (values - high.astype(jnp.float32)).astype(jnp.bfloat16)
            both = lax.dot_general(
                turn,
                jnp.concatenate([high, low], axis=0),
                (((1,), (1,)), ((), ())),
                preferred_element_type=jnp.float32,
            )
            folded = (both[: quarter + 8, :LANES] + both[: quarter + 8, LANES:]) * scale
            out_ref[2 * m + part, :, :] = folded
            heads.append(folded[0:1])
            tails.append(folded[quarter : quarter + 1])
        for m in range(4):
            out_ref[2 * m + part, 0:1, :] = 0.5 * (heads[m] + sign * heads[(4 - m) % 4])
            out_ref[2 * m + part, quarter : quarter + 1, :] = 0.5 * (
                tails[m] + sign * tails[3 - m]
            )


def forward_kernel(pair_ref, out_ref):
    out_ref[...] = pair_ref[1]


def received(place_ref, own, sibling, first, second, first_on, second_on, same, cross):
    link = first_link(place_ref)
    return [
        (0, own),
        (1, sibling),
        (link, first.at[0]),
        (6 - link, second.at[0]),
        ((6 - link) ^ 1, first_on),
        (link ^ 1, second_on),
        (6, same),
        (7, cross),
    ]


def filter_kernel(
    place_ref,
    own_ref,
    sibling_ref,
    first_ref,
    second_ref,
    first_on_ref,
    second_on_ref,
    same_ref,
    cross_ref,
    taps_ref,
    h_ref,
    high_ref,
    low_ref,
    twist_ref,
    own_out,
    sibling_out,
    first_out,
    second_out,
    same_out,
    cross_out,
    msg_ref,
    x_ref,
    z_ref,
    q_ref,
):
    shards = msg_ref.shape[0]
    rows = own_ref.shape[0] - 24
    quarter = high_ref.shape[1]
    blocks = received(
        place_ref,
        own_ref,
        sibling_ref,
        first_ref,
        second_ref,
        first_on_ref,
        second_on_ref,
        same_ref,
        cross_ref,
    )
    for k, block in blocks:
        msg_ref[place_ref[0] ^ k] = block[...]
    row = row_index(TILE)
    own = own_lanes(place_ref, 0)

    before = None
    for s in range(shards):
        top = msg_ref[s, :TILE, :].astype(jnp.float32)
        edge = msg_ref[s, rows : rows + TILE, :].astype(jnp.float32)
        half = msg_ref[s, rows + TILE :, :].astype(jnp.float32)
        if before is None:
            above_k = above_v = jnp.zeros_like(edge)
            halo = jnp.zeros_like(half)
        else:
            above_v, half_before = before
            above_k = jnp.concatenate([half_before, half_before], axis=0)
            halo = jnp.where(
                row_index(8) < 6,
                pltpu.roll(above_v, 12, 0)[:8],
                pltpu.roll(half_before, 6, 0),
            )
        k_conv = short_conv_rolled(
            jnp.where(row < 8, top, above_k), lambda j: taps_ref[1, j : j + 1, own]
        )
        v_conv = short_conv_rolled(
            jnp.where(row < 8, edge, above_v), lambda j: taps_ref[2, j : j + 1, own]
        )
        x_ref[s * rows : s * rows + TILE, :] = jnp.where(row < 6, rounded(k_conv * v_conv), top)
        x_ref[s * rows + TILE : (s + 1) * rows, :] = msg_ref[s, TILE:rows, :].astype(jnp.float32)
        msg_ref[s, rows : rows + 8, :] = halo.astype(jnp.bfloat16)
        before = (edge, half)

    x = jnp.concatenate(
        [x_ref[pl.ds(a, quarter, stride=4), :].astype(jnp.bfloat16) for a in range(4)], axis=1
    )
    z_ref[...] = jnp.dot(high_ref[...], x, preferred_element_type=jnp.float32) + jnp.dot(
        low_ref[...], x, preferred_element_type=jnp.float32
    )

    def combine(real, imag, g, count):
        u = []
        for a in range(4):
            if a == 0:
                u.append((real[0], imag[0]))
                continue
            wr = jnp.broadcast_to(twist_ref[g : g + count, 2 * a : 2 * a + 1], (count, LANES))
            wi = jnp.broadcast_to(
                twist_ref[g : g + count, 2 * a + 1 : 2 * a + 2], (count, LANES)
            )
            u.append((real[a] * wr - imag[a] * wi, real[a] * wi + imag[a] * wr, wr, wi))

        def four(v, sign):
            er, ei = v[0][0] + v[2][0], v[0][1] + v[2][1]
            dr, di = v[0][0] - v[2][0], v[0][1] - v[2][1]
            pr, pi = v[1][0] + v[3][0], v[1][1] + v[3][1]
            qr, qi = v[1][0] - v[3][0], v[1][1] - v[3][1]
            if sign < 0:
                one, three = (dr + qi, di - qr), (dr - qi, di + qr)
            else:
                one, three = (dr - qi, di + qr), (dr + qi, di - qr)
            return [(er + pr, ei + pi), one, (er - pr, ei - pi), three]

        freq = four(u, -1)
        prod = []
        for m in range(4):
            hr = h_ref[2 * m, g : g + count, :]
            hi = h_ref[2 * m + 1, g : g + count, :]
            xr, xi = freq[m]
            prod.append((xr * hr - xi * hi, xr * hi + xi * hr))
        v = four(prod, 1)
        out = [v[0]]
        for a in range(1, 4):
            wr, wi = u[a][2], u[a][3]
            vr, vi = v[a]
            out.append((vr * wr + vi * wi, vi * wr - vr * wi))
        return out

    for g in range(0, quarter, TILE):
        real = [z_ref[g : g + TILE, a * LANES : (a + 1) * LANES] for a in range(4)]
        imag = [
            z_ref[quarter + g : quarter + g + TILE, a * LANES : (a + 1) * LANES] for a in range(4)
        ]
        out = combine(real, imag, g, TILE)
        for a in range(4):
            lanes = slice(a * LANES, (a + 1) * LANES)
            for part in range(2):
                high = out[a][part].astype(jnp.bfloat16)
                low = (out[a][part] - high.astype(jnp.float32)).astype(jnp.bfloat16)
                q_ref[2 * part, g : g + TILE, lanes] = high
                q_ref[2 * part + 1, g : g + TILE, lanes] = low
    real = [z_ref[2 * quarter : 2 * quarter + 8, a * LANES : (a + 1) * LANES] for a in range(4)]
    last = combine(real, [jnp.zeros_like(r) for r in real], quarter, 8)

    y = None
    for part in range(2):
        high = high_ref[part * quarter : (part + 1) * quarter, :]
        low = low_ref[part * quarter : (part + 1) * quarter, :]
        for left, right in ((high, 0), (high, 1), (low, 0)):
            term = jnp.dot(left, q_ref[2 * part + right], preferred_element_type=jnp.float32)
            y = term if y is None else y + term
    sign = 1.0 - 2.0 * (row_index(quarter) % 2).astype(jnp.float32)
    for a in range(4):
        x_ref[pl.ds(a, quarter, stride=4), :] = (
            y[:, a * LANES : (a + 1) * LANES] + sign * last[a][0][0:1, :]
        )
    link = first_link(place_ref)
    for k, out_ref in (
        (link, first_out.at[0]),
        (link ^ 1, first_out.at[1]),
        (6 - link, second_out.at[0]),
        ((6 - link) ^ 1, second_out.at[1]),
        (6, same_out),
        (7, cross_out),
        (0, own_out),
        (1, sibling_out),
    ):
        target = place_ref[0] ^ k
        start = pl.multiple_of(target * rows, rows)
        out_ref[:rows, :] = x_ref[pl.ds(start, rows), :].astype(jnp.bfloat16)
        out_ref[rows:, :] = msg_ref[target, rows : rows + 8, :]


def silu(values):
    return values / (1.0 + jnp.exp(-values))


def gain_kernel(q_ref, taps_ref, residual_ref, out_ref):
    for c in range(out_ref.shape[1] // LANES):
        lanes = slice(c * LANES, (c + 1) * LANES)
        conv = short_conv_rolled(
            q_ref[0, :, lanes].astype(jnp.float32), lambda j: taps_ref[0, j : j + 1, lanes]
        )
        out_ref[:, lanes] = silu(residual_ref[:, lanes].astype(jnp.float32)) * conv


def mixed_block(msg, lanes, gain_ref, residual_ref, q_ref, taps_ref, out_ref):
    rows = residual_ref.shape[0]
    row = row_index(TILE)
    halo = msg[rows:, :].astype(jnp.float32)
    window = jnp.where(
        row < 8, q_ref[0, :TILE, lanes].astype(jnp.float32), jnp.concatenate([halo, halo], axis=0)
    )
    conv = short_conv_rolled(window, lambda j: taps_ref[0, j : j + 1, lanes])
    resid = residual_ref[:TILE, lanes].astype(jnp.float32)
    gain = jnp.where(row < 6, silu(resid) * conv, gain_ref[:TILE, lanes])
    out_ref[:TILE, :] = (resid + gain * msg[:TILE, :].astype(jnp.float32)).astype(jnp.bfloat16)
    out_ref[TILE:, :] = (
        residual_ref[TILE:, lanes].astype(jnp.float32)
        + gain_ref[TILE:, lanes] * msg[TILE:rows, :].astype(jnp.float32)
    ).astype(jnp.bfloat16)


def mix_kernel(place_ref, *refs):
    arrived, rest, (out_ref, held, sems) = refs[:8], refs[8:12], refs[12:]
    copies = []
    for i, (k, block) in enumerate(received(place_ref, *arrived)):
        lanes = own_lanes(place_ref, k)
        mixed_block(block, lanes, *rest, held.at[i])
        copy = pltpu.make_async_copy(held.at[i], out_ref.at[:, lanes], sems.at[i])
        copy.start()
        copies.append(copy)
    for copy in copies:
        copy.wait()


def split_table(table):
    high = table.astype(jnp.bfloat16)
    low = (table - high.astype(np.float64)).astype(jnp.bfloat16)
    return high, low


def filter_tables(quarter):
    index = np.arange(quarter)
    angle = 2.0 * np.pi * (index[:, None] * index[None, :] % (2 * quarter)) / (2 * quarter)
    alternate = np.zeros((TILE, quarter))
    alternate[0] = 1.0 - 2.0 * (index % 2)
    high, low = split_table(np.concatenate([np.cos(angle), -np.sin(angle), alternate], axis=0))
    g = np.arange(quarter + 8)[:, None]
    a = np.arange(4)[None, :]
    turn = 2.0 * np.pi * (g * a) / (8 * quarter)
    twist = np.stack([np.cos(turn), -np.sin(turn)], axis=-1).reshape(quarter + 8, 8)
    return high, low, twist.astype(np.float32)


def estimate(flops, moved):
    return pl.CostEstimate(flops=flops, bytes_accessed=moved, transcendentals=0)


def exchanged(own, sibling, first, second, same, cross):
    def swap(block, partner):
        return lax.ppermute(block, "seq", [(i, partner(i)) for i in range(8)])

    def sent_on(pair):
        block = pl.pallas_call(
            forward_kernel,
            out_shape=jax.ShapeDtypeStruct(own.shape, own.dtype),
            compiler_params=pltpu.CompilerParams(vmem_limit_bytes=VMEM_LIMIT),
            cost_estimate=estimate(1 << 10, 1 << 16),
            name="forward",
        )(pair)
        return swap(block, lambda i: i ^ 1)

    first = swap(first, lambda i: i ^ (2 + 2 * (i & 1)))
    second = swap(second, lambda i: i ^ (4 - 2 * (i & 1)))
    same = swap(same, lambda i: i ^ 6)
    cross = swap(cross, lambda i: i ^ 7)
    sibling = swap(sibling, lambda i: i ^ 1)
    return own, sibling, first, second, sent_on(first), sent_on(second), same, cross


def local_kernels(streams, short_taps, spectrum, residual):
    rows, channels = residual.shape
    shards = lax.axis_size("seq")
    length = rows * shards
    quarter = length // 4
    params = pltpu.CompilerParams(vmem_limit_bytes=VMEM_LIMIT)
    place = lax.axis_index("seq").astype(jnp.int32).reshape(1)
    scalar = pl.BlockSpec(memory_space=pltpu.SMEM)
    vector = pl.BlockSpec(memory_space=pltpu.VMEM)
    hbm = pl.BlockSpec(memory_space=pltpu.HBM)
    half = lambda *shape: jax.ShapeDtypeStruct(shape, jnp.bfloat16)
    full = lambda *shape: jax.ShapeDtypeStruct(shape, jnp.float32)
    sent = rows + 24
    first, second, kv, q_last, taps = pl.pallas_call(
        pack_first_kernel,
        in_specs=[scalar, hbm, hbm],
        out_shape=[
            half(2, sent, LANES),
            half(2, sent, LANES),
            half(4, 2, rows, 2 * LANES),
            half(4, TILE, 2 * LANES),
            full(*short_taps.shape),
        ],
        scratch_shapes=[pltpu.SemaphoreType.DMA((9,))],
        compiler_params=params,
        cost_estimate=estimate(1 << 22, 1 << 20),
        name="pack_first",
    )(
        place,
        pltpu.with_memory_space_constraint(streams, pltpu.HBM),
        pltpu.with_memory_space_constraint(short_taps, pltpu.HBM),
    )

    def pack_pair(chip, name):
        return pl.pallas_call(
            functools.partial(pack_pair_kernel, chip),
            in_specs=[scalar] + [vector] * 3,
            out_shape=[half(sent, LANES)] * 2,
            compiler_params=params,
            cost_estimate=estimate(1 << 22, 1 << 20),
            name=name,
        )(place, kv, q_last, taps)

    same, cross = pack_pair(3, "pack_far")
    own, sibling = pack_pair(0, "pack_own")
    arrived = exchanged(own, sibling, first, second, same, cross)

    blocks = 2 * length // LANES
    view = jnp.transpose(spectrum.reshape(LANES, 2, blocks, LANES), (0, 2, 1, 3)).reshape(
        2 * blocks * LANES, LANES
    )
    folded = pl.pallas_call(
        functools.partial(spectrum_kernel, quarter),
        out_shape=full(8, quarter + 8, LANES),
        compiler_params=params,
        cost_estimate=estimate(1 << 32, 1 << 22),
        name="spectrum",
    )(view)
    high, low, twist = filter_tables(quarter)
    back = rows + 8
    filtered = pl.pallas_call(
        filter_kernel,
        in_specs=[scalar] + [vector] * 13,
        out_shape=[half(back, LANES)] * 2
        + [half(2, back, LANES)] * 2
        + [half(back, LANES)] * 2,
        scratch_shapes=[
            pltpu.VMEM((shards, sent, LANES), jnp.bfloat16),
            pltpu.VMEM((length, LANES), jnp.float32),
            pltpu.VMEM((2 * quarter + TILE, 4 * LANES), jnp.float32),
            pltpu.VMEM((4, quarter, 4 * LANES), jnp.bfloat16),
        ],
        compiler_params=params,
        cost_estimate=estimate(1 << 30, 1 << 22),
        name="filter",
    )(place, *arrived, taps, folded, high, low, twist)
    whole = lambda *shape: pl.BlockSpec(shape, lambda i: (0,) * len(shape))
    gain = pl.pallas_call(
        gain_kernel,
        grid=(1,),
        in_specs=[
            whole(1, rows, channels),
            whole(*short_taps.shape),
            whole(rows, channels),
        ],
        out_specs=whole(rows, channels),
        out_shape=full(rows, channels),
        compiler_params=params,
        cost_estimate=estimate(1 << 32, 1 << 20),
        name="gain",
    )(streams, taps, residual)
    arrived = exchanged(*filtered)
    return pl.pallas_call(
        mix_kernel,
        in_specs=[scalar] + [vector] * 12,
        out_specs=hbm,
        out_shape=half(rows, channels),
        scratch_shapes=[
            pltpu.VMEM((shards, rows, LANES), jnp.bfloat16),
            pltpu.SemaphoreType.DMA((shards,)),
        ],
        compiler_params=params,
        cost_estimate=estimate(1 << 20, 1 << 20),
        name="mix",
    )(place, *arrived, gain, residual, streams, taps)


def local(streams, short_taps, spectrum, residual):
    rows, channels = residual.shape
    shards = lax.axis_size("seq")
    length = rows * shards
    fits = (
        channels == shards * LANES
        and rows % TILE == 0
        and rows >= 2 * TILE
        and length % (4 * LANES) == 0
        and length <= 2048
        and short_taps.shape[1] == 7
        and shards == 8
    )
    if fits:
        return local_kernels(streams, short_taps, spectrum, residual)
    return local_general(streams, short_taps, spectrum, residual)


def solution(mesh):
    placed = (
        P(None, "seq", "chan"),
        P(None, None, "chan"),
        P(("chan", "seq"), None, None),
        P("seq", "chan"),
    )
    return jax.shard_map(
        local, mesh=mesh, in_specs=placed, out_specs=P("seq", "chan"), check_vma=False
    )
```

```python
import functools
import math

import jax
import jax.numpy as jnp
import numpy as np
from jax import lax
from jax.experimental import pallas as pl
from jax.experimental.pallas import tpu as pltpu
from jax.sharding import PartitionSpec as P

LANES = 128
TILE = 16
VMEM_LIMIT = 16 * 1024 * 1024


def passed_along(block, axis, distance):
    devices = range(lax.axis_size(axis))
    route = [(i - distance, i) for i in devices if i - distance in devices]
    return lax.ppermute(block, axis, route)


def section_sizes(length_all):
    power = length_all.bit_length() - 1
    first = (power + 2) // 3
    second = (power - first + 1) // 2
    third = power - first - second
    result = [2**first, 2**second]
    result.append(2**third)
    return result


def matmul_high(left, right):
    return jnp.dot(left, right, precision=lax.Precision.HIGHEST, preferred_element_type=jnp.float32)


def section_high(table, values):
    return jnp.einsum(
        "ka,cab->ckb",
        table,
        values,
        precision=lax.Precision.HIGHEST,
        preferred_element_type=jnp.float32,
    )


def dft_table(order, direction):
    index = jnp.arange(order, dtype=jnp.int32)
    product = index[:, None] * index[None, :] % order
    angle = direction * 2.0 * math.pi * product.astype(jnp.float32) / order
    return (jnp.cos(angle), jnp.sin(angle))


def transform(real_part, imag_part, factors, direction):
    columns, length_now = real_part.shape
    first = factors[0]
    table_cos, table_sin = dft_table(first, direction)
    if len(factors) == 1:
        real_out = matmul_high(real_part, table_cos) - matmul_high(imag_part, table_sin)
        imag_out = matmul_high(imag_part, table_cos) + matmul_high(real_part, table_sin)
        return (real_out, imag_out)
    rest = length_now // first
    real_wide = real_part.reshape(columns, first, rest)
    if imag_part is None:
        section_real = section_high(table_cos, real_wide)
        section_imag = section_high(table_sin, real_wide)
    else:
        imag_wide = imag_part.reshape(columns, first, rest)
        section_real = section_high(table_cos, real_wide) - section_high(table_sin, imag_wide)
        section_imag = section_high(table_cos, imag_wide) + section_high(table_sin, real_wide)
    outer = jnp.arange(first, dtype=jnp.int32)[:, None]
    inner = jnp.arange(rest, dtype=jnp.int32)[None, :]
    twist = (
        direction * 2.0 * math.pi * (outer * inner % length_now).astype(jnp.float32) / length_now
    )
    twist_cos = jnp.cos(twist)[None, :, :]
    twist_sin = jnp.sin(twist)[None, :, :]
    turned_real = (section_real * twist_cos - section_imag * twist_sin).reshape(
        columns * first, rest
    )
    turned_imag = (section_real * twist_sin + section_imag * twist_cos).reshape(
        columns * first, rest
    )
    real_out, imag_out = transform(turned_real, turned_imag, factors[1:], direction)
    real_out = jnp.transpose(real_out.reshape(columns, first, rest), (0, 2, 1)).reshape(
        columns, length_now
    )
    imag_out = jnp.transpose(imag_out.reshape(columns, first, rest), (0, 2, 1)).reshape(
        columns, length_now
    )
    return (real_out, imag_out)


def long_filter(gated_rows, spectrum):
    columns, length_all = gated_rows.shape
    padded = jnp.concatenate(
        [gated_rows.astype(jnp.float32), jnp.zeros((columns, length_all), jnp.float32)], axis=1
    )
    factors = section_sizes(2 * length_all)
    freq_real, freq_imag = transform(padded, None, factors, -1.0)
    spec_real = spectrum[:, 0, :]
    spec_imag = spectrum[:, 1, :]
    prod_real = freq_real * spec_real - freq_imag * spec_imag
    prod_imag = freq_real * spec_imag + freq_imag * spec_real
    back_real, back_imag = transform(prod_real, prod_imag, factors, 1.0)
    return (back_real[:, :length_all] / (2 * length_all)).astype(jnp.bfloat16)


def local_general(streams, short_taps, spectrum, residual):
    row_count = streams.shape[1]
    channels = streams.shape[2]
    span = short_taps.shape[1] - 1
    rim_rows = passed_along(streams[:, row_count - span :, :], "seq", 1)
    extended = jnp.concatenate([rim_rows, streams], axis=1)
    total = jnp.zeros((3, row_count, channels), jnp.float32)
    for offset in range(span + 1):
        total = total + short_taps[:, offset, None, :] * extended[
            :, span - offset : span - offset + row_count, :
        ].astype(jnp.float32)
    convolved = total.astype(jnp.bfloat16)
    q_conv = convolved[0]
    k_conv = convolved[1]
    v_conv = convolved[2]
    seq_devices = lax.axis_size("seq")
    owned_count = channels // seq_devices
    length_all = row_count * seq_devices
    gated = (k_conv.astype(jnp.float32) * v_conv.astype(jnp.float32)).astype(jnp.bfloat16)
    owned = lax.all_to_all(
        gated.reshape(row_count, seq_devices, owned_count),
        "seq",
        split_axis=1,
        concat_axis=0,
        tiled=True,
    )
    gated_whole = owned.reshape(length_all, owned_count)
    filtered = jnp.transpose(long_filter(jnp.transpose(gated_whole), spectrum))
    returned = lax.all_to_all(
        filtered.reshape(length_all, 1, owned_count), "seq", split_axis=0, concat_axis=1, tiled=True
    )
    filtered_local = returned.reshape(row_count, channels)
    resid = residual.astype(jnp.float32)
    mixed = resid + jax.nn.silu(resid) * q_conv.astype(jnp.float32) * filtered_local.astype(
        jnp.float32
    )
    return mixed.astype(jnp.bfloat16)


def rounded(values):
    return values.astype(jnp.bfloat16).astype(jnp.float32)


def short_conv_rolled(rows, taps):
    total = taps(0) * rows
    for offset in range(1, 7):
        total = total + taps(offset) * pltpu.roll(rows, offset, 0)
    return rounded(total)


def row_index(count):
    return lax.broadcasted_iota(jnp.int32, (count, LANES), 0)


def own_lanes(place_ref, k):
    return pl.ds(pl.multiple_of((place_ref[0] ^ k) * LANES, LANES), LANES)


def first_link(place_ref):
    return 2 + 2 * (place_ref[0] & 1)


def pack_block(k, v, q_last, taps, out_ref):
    rows = k.shape[0]
    row = row_index(TILE)
    gated = short_conv_rolled(k, lambda j: taps(1, j)) * short_conv_rolled(
        v, lambda j: taps(2, j)
    )
    out_ref[:TILE, :] = jnp.where(row < 6, k[:TILE], gated[:TILE]).astype(jnp.bfloat16)
    out_ref[TILE:rows, :] = gated[TILE:].astype(jnp.bfloat16)
    edge = jnp.where(row < 6, v[:TILE], v[rows - TILE :])
    edge = jnp.where((row >= 6) & (row < 10), pltpu.roll(q_last, 12, 0), edge)
    out_ref[rows : rows + TILE, :] = edge.astype(jnp.bfloat16)
    half = jnp.where(row_index(8) < 2, pltpu.roll(q_last[8:], 2, 0), k[rows - 8 :])
    out_ref[rows + TILE :, :] = half.astype(jnp.bfloat16)


def chip_order(place_ref):
    first = first_link(place_ref)
    return (0, first, 6 - first, 6)


def pack_one(place_ref, kv_ref, q_ref, taps_ref, chip, p, out_ref):
    lanes = pl.ds(pl.multiple_of(((place_ref[0] & 1) ^ p) * LANES, LANES), LANES)
    owner = own_lanes(place_ref, chip_order(place_ref)[chip] ^ p)
    pack_block(
        kv_ref[chip, 0, :, lanes].astype(jnp.float32),
        kv_ref[chip, 1, :, lanes].astype(jnp.float32),
        q_ref[:, owner].astype(jnp.float32),
        lambda s, j: taps_ref[s, j : j + 1, owner],
        out_ref,
    )


def pack_first_kernel(
    place_ref, streams_ref, taps_hbm_ref, core_ref, first_ref, kv_ref, q_ref, taps_ref, sems
):
    rows = streams_ref.shape[1]
    order = chip_order(place_ref)
    shared = [
        pltpu.make_async_copy(taps_hbm_ref, taps_ref, sems.at[4]),
        pltpu.make_async_copy(
            streams_ref.at[0, pl.ds(rows - TILE, TILE), :], q_ref, sems.at[5]
        ),
    ]
    copies = {}
    for i in (1, 0, 3, 2):
        chip = (place_ref[0] ^ order[i]) >> 1
        lanes = pl.ds(pl.multiple_of(chip * (2 * LANES), 2 * LANES), 2 * LANES)
        copies[i] = pltpu.make_async_copy(
            streams_ref.at[pl.ds(1, 2), :, lanes], kv_ref.at[i], sems.at[i]
        )
        copies[i].start()
        if i == 1:
            for copy in shared:
                copy.start()
    for copy in shared:
        copy.wait()
    for i, p, out_ref in (
        (1, 0, first_ref.at[0]),
        (1, 1, first_ref.at[1]),
        (0, 1, core_ref.at[0]),
        (3, 1, core_ref.at[1]),
    ):
        if p == 0 or i != 1:
            copies[i].wait()
        pack_one(place_ref, kv_ref, q_ref, taps_ref, i, p, out_ref)
    copies[2].wait()


def pack_second_kernel(place_ref, kv_ref, q_ref, taps_ref, second_ref, far_ref, own_ref):
    for i, p, out_ref in (
        (2, 0, second_ref.at[0]),
        (2, 1, second_ref.at[1]),
        (3, 0, far_ref),
        (0, 0, own_ref),
    ):
        pack_one(place_ref, kv_ref, q_ref, taps_ref, i, p, out_ref)


def spectrum_kernel(quarter, view_ref, out_ref):
    blocks = view_ref.shape[0] // (2 * LANES)
    per = quarter // LANES
    scale = 1.0 / (blocks * LANES)
    row = lax.broadcasted_iota(jnp.int32, (quarter + TILE, 2 * quarter), 0)
    col = lax.broadcasted_iota(jnp.int32, (quarter + TILE, 2 * quarter), 1)
    ahead = (col < quarter) & (row == col)
    back = (col >= quarter) & (row + col == 2 * quarter)
    turn = jnp.where(ahead | back, 1.0, 0.0).astype(jnp.bfloat16)

    def columns(part, start):
        return [
            view_ref[pl.ds(2 * (start + i) + part, LANES, stride=2 * blocks), :]
            for i in range(per)
        ]

    for part in range(2):
        sign = 1.0 if part == 0 else -1.0
        heads, tails = [], []
        for m in range(4):
            start = 2 * per * m
            values = columns(part, start) + [
                sign * v for v in columns(part, blocks - start - per)
            ]
            values = jnp.concatenate(values, axis=1)
            high = values.astype(jnp.bfloat16)
            low = (values - high.astype(jnp.float32)).astype(jnp.bfloat16)
            both = lax.dot_general(
                turn,
                jnp.concatenate([high, low], axis=0),
                (((1,), (1,)), ((), ())),
                preferred_element_type=jnp.float32,
            )
            folded = (both[: quarter + 8, :LANES] + both[: quarter + 8, LANES:]) * scale
            out_ref[2 * m + part, :, :] = folded
            heads.append(folded[0:1])
            tails.append(folded[quarter : quarter + 1])
        for m in range(4):
            out_ref[2 * m + part, 0:1, :] = 0.5 * (heads[m] + sign * heads[(4 - m) % 4])
            out_ref[2 * m + part, quarter : quarter + 1, :] = 0.5 * (
                tails[m] + sign * tails[3 - m]
            )


def forward_kernel(pair_ref, out_ref):
    out_ref[...] = pair_ref[1]


def merge_kernel(far_ref, core_ref, out_ref):
    out_ref[0] = far_ref[...]
    out_ref[1] = core_ref[1]


def received(place_ref, own, core, first, second, first_on, second_on, far):
    link = first_link(place_ref)
    return [
        (0, own),
        (1, core.at[0]),
        (link, first.at[0]),
        (6 - link, second.at[0]),
        ((6 - link) ^ 1, first_on),
        (link ^ 1, second_on),
        (6, far.at[0]),
        (7, far.at[1]),
    ]


def filter_kernel(
    place_ref,
    own_ref,
    core_ref,
    first_ref,
    second_ref,
    first_on_ref,
    second_on_ref,
    far_ref,
    taps_ref,
    h_ref,
    high_ref,
    low_ref,
    twist_ref,
    own_out,
    core_out,
    first_out,
    second_out,
    far_out,
    msg_ref,
    x_ref,
    z_ref,
    q_ref,
):
    shards = msg_ref.shape[0]
    rows = own_ref.shape[0] - 24
    quarter = high_ref.shape[1]
    blocks = received(
        place_ref,
        own_ref,
        core_ref,
        first_ref,
        second_ref,
        first_on_ref,
        second_on_ref,
        far_ref,
    )
    for k, block in blocks:
        msg_ref[place_ref[0] ^ k] = block[...]
    row = row_index(TILE)
    own = own_lanes(place_ref, 0)

    before = None
    for s in range(shards):
        top = msg_ref[s, :TILE, :].astype(jnp.float32)
        edge = msg_ref[s, rows : rows + TILE, :].astype(jnp.float32)
        half = msg_ref[s, rows + TILE :, :].astype(jnp.float32)
        if before is None:
            above_k = above_v = jnp.zeros_like(edge)
            halo = jnp.zeros_like(half)
        else:
            above_v, half_before = before
            above_k = jnp.concatenate([half_before, half_before], axis=0)
            halo = jnp.where(
                row_index(8) < 6,
                pltpu.roll(above_v, 12, 0)[:8],
                pltpu.roll(half_before, 6, 0),
            )
        k_conv = short_conv_rolled(
            jnp.where(row < 8, top, above_k), lambda j: taps_ref[1, j : j + 1, own]
        )
        v_conv = short_conv_rolled(
            jnp.where(row < 8, edge, above_v), lambda j: taps_ref[2, j : j + 1, own]
        )
        x_ref[s * rows : s * rows + TILE, :] = jnp.where(row < 6, rounded(k_conv * v_conv), top)
        x_ref[s * rows + TILE : (s + 1) * rows, :] = msg_ref[s, TILE:rows, :].astype(jnp.float32)
        msg_ref[s, rows : rows + 8, :] = halo.astype(jnp.bfloat16)
        before = (edge, half)

    x = jnp.concatenate(
        [x_ref[pl.ds(a, quarter, stride=4), :].astype(jnp.bfloat16) for a in range(4)], axis=1
    )
    z_ref[...] = jnp.dot(high_ref[...], x, preferred_element_type=jnp.float32) + jnp.dot(
        low_ref[...], x, preferred_element_type=jnp.float32
    )

    def combine(real, imag, g, count):
        u = []
        for a in range(4):
            if a == 0:
                u.append((real[0], imag[0]))
                continue
            wr = jnp.broadcast_to(twist_ref[g : g + count, 2 * a : 2 * a + 1], (count, LANES))
            wi = jnp.broadcast_to(
                twist_ref[g : g + count, 2 * a + 1 : 2 * a + 2], (count, LANES)
            )
            u.append((real[a] * wr - imag[a] * wi, real[a] * wi + imag[a] * wr, wr, wi))

        def four(v, sign):
            er, ei = v[0][0] + v[2][0], v[0][1] + v[2][1]
            dr, di = v[0][0] - v[2][0], v[0][1] - v[2][1]
            pr, pi = v[1][0] + v[3][0], v[1][1] + v[3][1]
            qr, qi = v[1][0] - v[3][0], v[1][1] - v[3][1]
            if sign < 0:
                one, three = (dr + qi, di - qr), (dr - qi, di + qr)
            else:
                one, three = (dr - qi, di + qr), (dr + qi, di - qr)
            return [(er + pr, ei + pi), one, (er - pr, ei - pi), three]

        freq = four(u, -1)
        prod = []
        for m in range(4):
            hr = h_ref[2 * m, g : g + count, :]
            hi = h_ref[2 * m + 1, g : g + count, :]
            xr, xi = freq[m]
            prod.append((xr * hr - xi * hi, xr * hi + xi * hr))
        v = four(prod, 1)
        out = [v[0]]
        for a in range(1, 4):
            wr, wi = u[a][2], u[a][3]
            vr, vi = v[a]
            out.append((vr * wr + vi * wi, vi * wr - vr * wi))
        return out

    for g in range(0, quarter, TILE):
        real = [z_ref[g : g + TILE, a * LANES : (a + 1) * LANES] for a in range(4)]
        imag = [
            z_ref[quarter + g : quarter + g + TILE, a * LANES : (a + 1) * LANES] for a in range(4)
        ]
        out = combine(real, imag, g, TILE)
        for a in range(4):
            lanes = slice(a * LANES, (a + 1) * LANES)
            for part in range(2):
                high = out[a][part].astype(jnp.bfloat16)
                low = (out[a][part] - high.astype(jnp.float32)).astype(jnp.bfloat16)
                q_ref[2 * part, g : g + TILE, lanes] = high
                q_ref[2 * part + 1, g : g + TILE, lanes] = low
    real = [z_ref[2 * quarter : 2 * quarter + 8, a * LANES : (a + 1) * LANES] for a in range(4)]
    last = combine(real, [jnp.zeros_like(r) for r in real], quarter, 8)

    y = None
    for part in range(2):
        high = high_ref[part * quarter : (part + 1) * quarter, :]
        low = low_ref[part * quarter : (part + 1) * quarter, :]
        for left, right in ((high, 0), (high, 1), (low, 0)):
            term = jnp.dot(left, q_ref[2 * part + right], preferred_element_type=jnp.float32)
            y = term if y is None else y + term
    sign = 1.0 - 2.0 * (row_index(quarter) % 2).astype(jnp.float32)
    for a in range(4):
        x_ref[pl.ds(a, quarter, stride=4), :] = (
            y[:, a * LANES : (a + 1) * LANES] + sign * last[a][0][0:1, :]
        )
    link = first_link(place_ref)
    for k, out_ref in (
        (link, first_out.at[0]),
        (link ^ 1, first_out.at[1]),
        (6 - link, second_out.at[0]),
        ((6 - link) ^ 1, second_out.at[1]),
        (6, far_out),
        (7, core_out.at[1]),
        (0, own_out),
        (1, core_out.at[0]),
    ):
        target = place_ref[0] ^ k
        start = pl.multiple_of(target * rows, rows)
        out_ref[:rows, :] = x_ref[pl.ds(start, rows), :].astype(jnp.bfloat16)
        out_ref[rows:, :] = msg_ref[target, rows : rows + 8, :]


def silu(values):
    return values / (1.0 + jnp.exp(-values))


def gain_kernel(q_ref, taps_ref, residual_ref, out_ref):
    for c in range(out_ref.shape[1] // LANES):
        lanes = slice(c * LANES, (c + 1) * LANES)
        conv = short_conv_rolled(
            q_ref[0, :, lanes].astype(jnp.float32), lambda j: taps_ref[0, j : j + 1, lanes]
        )
        out_ref[:, lanes] = silu(residual_ref[:, lanes].astype(jnp.float32)) * conv


def mixed_block(msg, lanes, gain_ref, residual_ref, q_ref, taps_ref, out_ref):
    rows = residual_ref.shape[0]
    row = row_index(TILE)
    halo = msg[rows:, :].astype(jnp.float32)
    window = jnp.where(
        row < 8, q_ref[0, :TILE, lanes].astype(jnp.float32), jnp.concatenate([halo, halo], axis=0)
    )
    conv = short_conv_rolled(window, lambda j: taps_ref[0, j : j + 1, lanes])
    resid = residual_ref[:TILE, lanes].astype(jnp.float32)
    gain = jnp.where(row < 6, silu(resid) * conv, gain_ref[:TILE, lanes])
    out_ref[:TILE, :] = (resid + gain * msg[:TILE, :].astype(jnp.float32)).astype(jnp.bfloat16)
    out_ref[TILE:, :] = (
        residual_ref[TILE:, lanes].astype(jnp.float32)
        + gain_ref[TILE:, lanes] * msg[TILE:rows, :].astype(jnp.float32)
    ).astype(jnp.bfloat16)


def mix_kernel(place_ref, *refs):
    arrived, rest, (out_ref, held, sems) = refs[:7], refs[7:11], refs[11:]
    copies = []
    for i, (k, block) in enumerate(received(place_ref, *arrived)):
        lanes = own_lanes(place_ref, k)
        mixed_block(block, lanes, *rest, held.at[i])
        copy = pltpu.make_async_copy(held.at[i], out_ref.at[:, lanes], sems.at[i])
        copy.start()
        copies.append(copy)
    for copy in copies:
        copy.wait()


def split_table(table):
    high = table.astype(jnp.bfloat16)
    low = (table - high.astype(np.float64)).astype(jnp.bfloat16)
    return high, low


def filter_tables(quarter):
    index = np.arange(quarter)
    angle = 2.0 * np.pi * (index[:, None] * index[None, :] % (2 * quarter)) / (2 * quarter)
    alternate = np.zeros((TILE, quarter))
    alternate[0] = 1.0 - 2.0 * (index % 2)
    high, low = split_table(np.concatenate([np.cos(angle), -np.sin(angle), alternate], axis=0))
    g = np.arange(quarter + 8)[:, None]
    a = np.arange(4)[None, :]
    turn = 2.0 * np.pi * (g * a) / (8 * quarter)
    twist = np.stack([np.cos(turn), -np.sin(turn)], axis=-1).reshape(quarter + 8, 8)
    return high, low, twist.astype(np.float32)


def estimate(flops, moved):
    return pl.CostEstimate(flops=flops, bytes_accessed=moved, transcendentals=0)


def exchanged(own, core, first, second, far):
    def swap(block, partner):
        return lax.ppermute(block, "seq", [(i, partner(i)) for i in range(8)])

    def arranged(kernel, name, shape, *blocks):
        return pl.pallas_call(
            kernel,
            out_shape=jax.ShapeDtypeStruct(shape, own.dtype),
            compiler_params=pltpu.CompilerParams(vmem_limit_bytes=VMEM_LIMIT),
            cost_estimate=estimate(1 << 10, 1 << 16),
            name=name,
        )(*blocks)

    def sent_on(pair):
        return swap(arranged(forward_kernel, "forward", own.shape, pair), lambda i: i ^ 1)

    core = swap(core, lambda i: i ^ 1)
    first = swap(first, lambda i: i ^ (2 + 2 * (i & 1)))
    second = swap(second, lambda i: i ^ (4 - 2 * (i & 1)))
    far = swap(arranged(merge_kernel, "merge", core.shape, far, core), lambda i: i ^ 6)
    return own, core, first, second, sent_on(first), sent_on(second), far


def local_kernels(streams, short_taps, spectrum, residual):
    rows, channels = residual.shape
    shards = lax.axis_size("seq")
    length = rows * shards
    quarter = length // 4
    params = pltpu.CompilerParams(vmem_limit_bytes=VMEM_LIMIT)
    place = lax.axis_index("seq").astype(jnp.int32).reshape(1)
    scalar = pl.BlockSpec(memory_space=pltpu.SMEM)
    vector = pl.BlockSpec(memory_space=pltpu.VMEM)
    hbm = pl.BlockSpec(memory_space=pltpu.HBM)
    half = lambda *shape: jax.ShapeDtypeStruct(shape, jnp.bfloat16)
    full = lambda *shape: jax.ShapeDtypeStruct(shape, jnp.float32)
    sent = rows + 24
    core, first, kv, q_last, taps = pl.pallas_call(
        pack_first_kernel,
        in_specs=[scalar, hbm, hbm],
        out_shape=[
            half(2, sent, LANES),
            half(2, sent, LANES),
            half(4, 2, rows, 2 * LANES),
            half(TILE, channels),
            full(*short_taps.shape),
        ],
        scratch_shapes=[pltpu.SemaphoreType.DMA((6,))],
        compiler_params=params,
        cost_estimate=estimate(1 << 22, 1 << 20),
        name="pack_first",
    )(
        place,
        pltpu.with_memory_space_constraint(streams, pltpu.HBM),
        pltpu.with_memory_space_constraint(short_taps, pltpu.HBM),
    )
    second, far, own = pl.pallas_call(
        pack_second_kernel,
        in_specs=[scalar] + [vector] * 3,
        out_shape=[half(2, sent, LANES), half(sent, LANES), half(sent, LANES)],
        compiler_params=params,
        cost_estimate=estimate(1 << 22, 1 << 20),
        name="pack_second",
    )(place, kv, q_last, taps)
    arrived = exchanged(own, core, first, second, far)

    blocks = 2 * length // LANES
    view = jnp.transpose(spectrum.reshape(LANES, 2, blocks, LANES), (0, 2, 1, 3)).reshape(
        2 * blocks * LANES, LANES
    )
    folded = pl.pallas_call(
        functools.partial(spectrum_kernel, quarter),
        out_shape=full(8, quarter + 8, LANES),
        compiler_params=params,
        cost_estimate=estimate(1 << 32, 1 << 22),
        name="spectrum",
    )(view)
    high, low, twist = filter_tables(quarter)
    back = rows + 8
    filtered = pl.pallas_call(
        filter_kernel,
        in_specs=[scalar] + [vector] * 12,
        out_shape=[half(back, LANES)] + [half(2, back, LANES)] * 3 + [half(back, LANES)],
        scratch_shapes=[
            pltpu.VMEM((shards, sent, LANES), jnp.bfloat16),
            pltpu.VMEM((length, LANES), jnp.float32),
            pltpu.VMEM((2 * quarter + TILE, 4 * LANES), jnp.float32),
            pltpu.VMEM((4, quarter, 4 * LANES), jnp.bfloat16),
        ],
        compiler_params=params,
        cost_estimate=estimate(1 << 30, 1 << 22),
        name="filter",
    )(place, *arrived, taps, folded, high, low, twist)
    whole = lambda *shape: pl.BlockSpec(shape, lambda i: (0,) * len(shape))
    gain = pl.pallas_call(
        gain_kernel,
        grid=(1,),
        in_specs=[
            whole(1, rows, channels),
            whole(*short_taps.shape),
            whole(rows, channels),
        ],
        out_specs=whole(rows, channels),
        out_shape=full(rows, channels),
        compiler_params=params,
        cost_estimate=estimate(1 << 32, 1 << 20),
        name="gain",
    )(streams, taps, residual)
    arrived = exchanged(*filtered)
    return pl.pallas_call(
        mix_kernel,
        in_specs=[scalar] + [vector] * 11,
        out_specs=hbm,
        out_shape=half(rows, channels),
        scratch_shapes=[
            pltpu.VMEM((shards, rows, LANES), jnp.bfloat16),
            pltpu.SemaphoreType.DMA((shards,)),
        ],
        compiler_params=params,
        cost_estimate=estimate(1 << 20, 1 << 20),
        name="mix",
    )(place, *arrived, gain, residual, streams, taps)


def local(streams, short_taps, spectrum, residual):
    rows, channels = residual.shape
    shards = lax.axis_size("seq")
    length = rows * shards
    fits = (
        channels == shards * LANES
        and rows % TILE == 0
        and rows >= 2 * TILE
        and length % (4 * LANES) == 0
        and length <= 2048
        and short_taps.shape[1] == 7
        and shards == 8
    )
    if fits:
        return local_kernels(streams, short_taps, spectrum, residual)
    return local_general(streams, short_taps, spectrum, residual)


def solution(mesh):
    placed = (
        P(None, "seq", "chan"),
        P(None, None, "chan"),
        P(("chan", "seq"), None, None),
        P("seq", "chan"),
    )
    return jax.shard_map(
        local, mesh=mesh, in_specs=placed, out_specs=P("seq", "chan"), check_vma=False
    )
```

```python
import functools
import math

import jax
import jax.numpy as jnp
import numpy as np
from jax import lax
from jax.experimental import pallas as pl
from jax.experimental.pallas import tpu as pltpu
from jax.sharding import PartitionSpec as P

LANES = 128
TILE = 16
VMEM_LIMIT = 16 * 1024 * 1024


def passed_along(block, axis, distance):
    devices = range(lax.axis_size(axis))
    route = [(i - distance, i) for i in devices if i - distance in devices]
    return lax.ppermute(block, axis, route)


def section_sizes(length_all):
    power = length_all.bit_length() - 1
    first = (power + 2) // 3
    second = (power - first + 1) // 2
    third = power - first - second
    result = [2**first, 2**second]
    result.append(2**third)
    return result


def matmul_high(left, right):
    return jnp.dot(left, right, precision=lax.Precision.HIGHEST, preferred_element_type=jnp.float32)


def section_high(table, values):
    return jnp.einsum(
        "ka,cab->ckb",
        table,
        values,
        precision=lax.Precision.HIGHEST,
        preferred_element_type=jnp.float32,
    )


def dft_table(order, direction):
    index = jnp.arange(order, dtype=jnp.int32)
    product = index[:, None] * index[None, :] % order
    angle = direction * 2.0 * math.pi * product.astype(jnp.float32) / order
    return (jnp.cos(angle), jnp.sin(angle))


def transform(real_part, imag_part, factors, direction):
    columns, length_now = real_part.shape
    first = factors[0]
    table_cos, table_sin = dft_table(first, direction)
    if len(factors) == 1:
        real_out = matmul_high(real_part, table_cos) - matmul_high(imag_part, table_sin)
        imag_out = matmul_high(imag_part, table_cos) + matmul_high(real_part, table_sin)
        return (real_out, imag_out)
    rest = length_now // first
    real_wide = real_part.reshape(columns, first, rest)
    if imag_part is None:
        section_real = section_high(table_cos, real_wide)
        section_imag = section_high(table_sin, real_wide)
    else:
        imag_wide = imag_part.reshape(columns, first, rest)
        section_real = section_high(table_cos, real_wide) - section_high(table_sin, imag_wide)
        section_imag = section_high(table_cos, imag_wide) + section_high(table_sin, real_wide)
    outer = jnp.arange(first, dtype=jnp.int32)[:, None]
    inner = jnp.arange(rest, dtype=jnp.int32)[None, :]
    twist = (
        direction * 2.0 * math.pi * (outer * inner % length_now).astype(jnp.float32) / length_now
    )
    twist_cos = jnp.cos(twist)[None, :, :]
    twist_sin = jnp.sin(twist)[None, :, :]
    turned_real = (section_real * twist_cos - section_imag * twist_sin).reshape(
        columns * first, rest
    )
    turned_imag = (section_real * twist_sin + section_imag * twist_cos).reshape(
        columns * first, rest
    )
    real_out, imag_out = transform(turned_real, turned_imag, factors[1:], direction)
    real_out = jnp.transpose(real_out.reshape(columns, first, rest), (0, 2, 1)).reshape(
        columns, length_now
    )
    imag_out = jnp.transpose(imag_out.reshape(columns, first, rest), (0, 2, 1)).reshape(
        columns, length_now
    )
    return (real_out, imag_out)


def long_filter(gated_rows, spectrum):
    columns, length_all = gated_rows.shape
    padded = jnp.concatenate(
        [gated_rows.astype(jnp.float32), jnp.zeros((columns, length_all), jnp.float32)], axis=1
    )
    factors = section_sizes(2 * length_all)
    freq_real, freq_imag = transform(padded, None, factors, -1.0)
    spec_real = spectrum[:, 0, :]
    spec_imag = spectrum[:, 1, :]
    prod_real = freq_real * spec_real - freq_imag * spec_imag
    prod_imag = freq_real * spec_imag + freq_imag * spec_real
    back_real, back_imag = transform(prod_real, prod_imag, factors, 1.0)
    return (back_real[:, :length_all] / (2 * length_all)).astype(jnp.bfloat16)


def local_general(streams, short_taps, spectrum, residual):
    row_count = streams.shape[1]
    channels = streams.shape[2]
    span = short_taps.shape[1] - 1
    rim_rows = passed_along(streams[:, row_count - span :, :], "seq", 1)
    extended = jnp.concatenate([rim_rows, streams], axis=1)
    total = jnp.zeros((3, row_count, channels), jnp.float32)
    for offset in range(span + 1):
        total = total + short_taps[:, offset, None, :] * extended[
            :, span - offset : span - offset + row_count, :
        ].astype(jnp.float32)
    convolved = total.astype(jnp.bfloat16)
    q_conv = convolved[0]
    k_conv = convolved[1]
    v_conv = convolved[2]
    seq_devices = lax.axis_size("seq")
    owned_count = channels // seq_devices
    length_all = row_count * seq_devices
    gated = (k_conv.astype(jnp.float32) * v_conv.astype(jnp.float32)).astype(jnp.bfloat16)
    owned = lax.all_to_all(
        gated.reshape(row_count, seq_devices, owned_count),
        "seq",
        split_axis=1,
        concat_axis=0,
        tiled=True,
    )
    gated_whole = owned.reshape(length_all, owned_count)
    filtered = jnp.transpose(long_filter(jnp.transpose(gated_whole), spectrum))
    returned = lax.all_to_all(
        filtered.reshape(length_all, 1, owned_count), "seq", split_axis=0, concat_axis=1, tiled=True
    )
    filtered_local = returned.reshape(row_count, channels)
    resid = residual.astype(jnp.float32)
    mixed = resid + jax.nn.silu(resid) * q_conv.astype(jnp.float32) * filtered_local.astype(
        jnp.float32
    )
    return mixed.astype(jnp.bfloat16)


def rounded(values):
    return values.astype(jnp.bfloat16).astype(jnp.float32)


def short_conv_rolled(rows, taps):
    total = taps(0) * rows
    for offset in range(1, 7):
        total = total + taps(offset) * pltpu.roll(rows, offset, 0)
    return rounded(total)


def row_index(count):
    return lax.broadcasted_iota(jnp.int32, (count, LANES), 0)


def own_lanes(place_ref, k):
    return pl.ds(pl.multiple_of((place_ref[0] ^ k) * LANES, LANES), LANES)


def first_link(place_ref):
    return 2 + 2 * (place_ref[0] & 1)


def pack_block(k, v, q_last, taps, out_ref):
    rows = k.shape[0]
    row = row_index(TILE)
    gated = short_conv_rolled(k, lambda j: taps(1, j)) * short_conv_rolled(
        v, lambda j: taps(2, j)
    )
    out_ref[:TILE, :] = jnp.where(row < 6, k[:TILE], gated[:TILE]).astype(jnp.bfloat16)
    out_ref[TILE:rows, :] = gated[TILE:].astype(jnp.bfloat16)
    edge = jnp.where(row < 6, v[:TILE], v[rows - TILE :])
    edge = jnp.where((row >= 6) & (row < 10), pltpu.roll(q_last, 12, 0), edge)
    out_ref[rows : rows + TILE, :] = edge.astype(jnp.bfloat16)
    half = jnp.where(row_index(8) < 2, pltpu.roll(q_last[8:], 2, 0), k[rows - 8 :])
    out_ref[rows + TILE :, :] = half.astype(jnp.bfloat16)


def chip_order(place_ref):
    first = first_link(place_ref)
    return (0, first, 6 - first, 6)


def pack_one(place_ref, kv_ref, q_ref, taps_ref, chip, p, out_ref):
    lanes = pl.ds(pl.multiple_of(((place_ref[0] & 1) ^ p) * LANES, LANES), LANES)
    owner = own_lanes(place_ref, chip_order(place_ref)[chip] ^ p)
    pack_block(
        kv_ref[chip, 0, :, lanes].astype(jnp.float32),
        kv_ref[chip, 1, :, lanes].astype(jnp.float32),
        q_ref[:, owner].astype(jnp.float32),
        lambda s, j: taps_ref[s, j : j + 1, owner],
        out_ref,
    )


def pack_first_kernel(
    place_ref, streams_ref, taps_hbm_ref, core_ref, first_ref, kv_ref, q_ref, taps_ref, sems
):
    rows = streams_ref.shape[1]
    order = chip_order(place_ref)
    shared = [
        pltpu.make_async_copy(taps_hbm_ref, taps_ref, sems.at[4]),
        pltpu.make_async_copy(
            streams_ref.at[0, pl.ds(rows - TILE, TILE), :], q_ref, sems.at[5]
        ),
    ]
    copies = {}
    for i in (1, 0, 3, 2):
        chip = (place_ref[0] ^ order[i]) >> 1
        lanes = pl.ds(pl.multiple_of(chip * (2 * LANES), 2 * LANES), 2 * LANES)
        copies[i] = pltpu.make_async_copy(
            streams_ref.at[pl.ds(1, 2), :, lanes], kv_ref.at[i], sems.at[i]
        )
        copies[i].start()
        if i == 1:
            for copy in shared:
                copy.start()
    for copy in shared:
        copy.wait()
    for i, p, out_ref in (
        (1, 0, first_ref.at[0]),
        (1, 1, first_ref.at[1]),
        (0, 1, core_ref.at[0]),
        (3, 1, core_ref.at[1]),
    ):
        if p == 0 or i != 1:
            copies[i].wait()
        pack_one(place_ref, kv_ref, q_ref, taps_ref, i, p, out_ref)
    copies[2].wait()


def pack_second_kernel(place_ref, kv_ref, q_ref, taps_ref, second_ref, far_ref, own_ref):
    for i, p, out_ref in (
        (2, 0, second_ref.at[0]),
        (2, 1, second_ref.at[1]),
        (3, 0, far_ref),
        (0, 0, own_ref),
    ):
        pack_one(place_ref, kv_ref, q_ref, taps_ref, i, p, out_ref)


def spectrum_kernel(quarter, view_ref, out_ref):
    blocks = view_ref.shape[0] // (2 * LANES)
    per = quarter // LANES
    scale = 1.0 / (blocks * LANES)
    row = lax.broadcasted_iota(jnp.int32, (quarter + TILE, 2 * quarter), 0)
    col = lax.broadcasted_iota(jnp.int32, (quarter + TILE, 2 * quarter), 1)
    ahead = (col < quarter) & (row == col)
    back = (col >= quarter) & (row + col == 2 * quarter)
    turn = jnp.where(ahead | back, 1.0, 0.0).astype(jnp.bfloat16)

    def columns(part, start):
        return [
            view_ref[pl.ds(2 * (start + i) + part, LANES, stride=2 * blocks), :]
            for i in range(per)
        ]

    for part in range(2):
        sign = 1.0 if part == 0 else -1.0
        heads, tails = [], []
        for m in range(4):
            start = 2 * per * m
            values = columns(part, start) + [
                sign * v for v in columns(part, blocks - start - per)
            ]
            values = jnp.concatenate(values, axis=1)
            high = values.astype(jnp.bfloat16)
            low = (values - high.astype(jnp.float32)).astype(jnp.bfloat16)
            both = lax.dot_general(
                turn,
                jnp.concatenate([high, low], axis=0),
                (((1,), (1,)), ((), ())),
                preferred_element_type=jnp.float32,
            )
            folded = (both[: quarter + 8, :LANES] + both[: quarter + 8, LANES:]) * scale
            out_ref[2 * m + part, :, :] = folded
            heads.append(folded[0:1])
            tails.append(folded[quarter : quarter + 1])
        for m in range(4):
            out_ref[2 * m + part, 0:1, :] = 0.5 * (heads[m] + sign * heads[(4 - m) % 4])
            out_ref[2 * m + part, quarter : quarter + 1, :] = 0.5 * (
                tails[m] + sign * tails[3 - m]
            )


def forward_kernel(pair_ref, beside_ref, out_ref):
    out_ref[...] = pair_ref[1]


def merge_kernel(far_ref, core_ref, out_ref):
    out_ref[0] = far_ref[...]
    out_ref[1] = core_ref[1]


def received(place_ref, own, core, first, second, first_on, second_on, far):
    link = first_link(place_ref)
    return [
        (0, own),
        (1, core.at[0]),
        (link, first.at[0]),
        (6 - link, second.at[0]),
        ((6 - link) ^ 1, first_on),
        (link ^ 1, second_on),
        (6, far.at[0]),
        (7, far.at[1]),
    ]


def filter_kernel(
    place_ref,
    own_ref,
    core_ref,
    first_ref,
    second_ref,
    first_on_ref,
    second_on_ref,
    far_ref,
    taps_ref,
    h_ref,
    high_ref,
    low_ref,
    twist_ref,
    own_out,
    core_out,
    first_out,
    second_out,
    far_out,
    msg_ref,
    x_ref,
    z_ref,
    q_ref,
):
    shards = msg_ref.shape[0]
    rows = own_ref.shape[0] - 24
    quarter = high_ref.shape[1]
    blocks = received(
        place_ref,
        own_ref,
        core_ref,
        first_ref,
        second_ref,
        first_on_ref,
        second_on_ref,
        far_ref,
    )
    for k, block in blocks:
        msg_ref[place_ref[0] ^ k] = block[...]
    row = row_index(TILE)
    own = own_lanes(place_ref, 0)

    before = None
    for s in range(shards):
        top = msg_ref[s, :TILE, :].astype(jnp.float32)
        edge = msg_ref[s, rows : rows + TILE, :].astype(jnp.float32)
        half = msg_ref[s, rows + TILE :, :].astype(jnp.float32)
        if before is None:
            above_k = above_v = jnp.zeros_like(edge)
            halo = jnp.zeros_like(half)
        else:
            above_v, half_before = before
            above_k = jnp.concatenate([half_before, half_before], axis=0)
            halo = jnp.where(
                row_index(8) < 6,
                pltpu.roll(above_v, 12, 0)[:8],
                pltpu.roll(half_before, 6, 0),
            )
        k_conv = short_conv_rolled(
            jnp.where(row < 8, top, above_k), lambda j: taps_ref[1, j : j + 1, own]
        )
        v_conv = short_conv_rolled(
            jnp.where(row < 8, edge, above_v), lambda j: taps_ref[2, j : j + 1, own]
        )
        x_ref[s * rows : s * rows + TILE, :] = jnp.where(row < 6, rounded(k_conv * v_conv), top)
        x_ref[s * rows + TILE : (s + 1) * rows, :] = msg_ref[s, TILE:rows, :].astype(jnp.float32)
        msg_ref[s, rows : rows + 8, :] = halo.astype(jnp.bfloat16)
        before = (edge, half)

    x = jnp.concatenate(
        [x_ref[pl.ds(a, quarter, stride=4), :].astype(jnp.bfloat16) for a in range(4)], axis=1
    )
    z_ref[...] = jnp.dot(high_ref[...], x, preferred_element_type=jnp.float32) + jnp.dot(
        low_ref[...], x, preferred_element_type=jnp.float32
    )

    def combine(real, imag, g, count):
        u = []
        for a in range(4):
            if a == 0:
                u.append((real[0], imag[0]))
                continue
            wr = jnp.broadcast_to(twist_ref[g : g + count, 2 * a : 2 * a + 1], (count, LANES))
            wi = jnp.broadcast_to(
                twist_ref[g : g + count, 2 * a + 1 : 2 * a + 2], (count, LANES)
            )
            u.append((real[a] * wr - imag[a] * wi, real[a] * wi + imag[a] * wr, wr, wi))

        def four(v, sign):
            er, ei = v[0][0] + v[2][0], v[0][1] + v[2][1]
            dr, di = v[0][0] - v[2][0], v[0][1] - v[2][1]
            pr, pi = v[1][0] + v[3][0], v[1][1] + v[3][1]
            qr, qi = v[1][0] - v[3][0], v[1][1] - v[3][1]
            if sign < 0:
                one, three = (dr + qi, di - qr), (dr - qi, di + qr)
            else:
                one, three = (dr - qi, di + qr), (dr + qi, di - qr)
            return [(er + pr, ei + pi), one, (er - pr, ei - pi), three]

        freq = four(u, -1)
        prod = []
        for m in range(4):
            hr = h_ref[2 * m, g : g + count, :]
            hi = h_ref[2 * m + 1, g : g + count, :]
            xr, xi = freq[m]
            prod.append((xr * hr - xi * hi, xr * hi + xi * hr))
        v = four(prod, 1)
        out = [v[0]]
        for a in range(1, 4):
            wr, wi = u[a][2], u[a][3]
            vr, vi = v[a]
            out.append((vr * wr + vi * wi, vi * wr - vr * wi))
        return out

    for g in range(0, quarter, TILE):
        real = [z_ref[g : g + TILE, a * LANES : (a + 1) * LANES] for a in range(4)]
        imag = [
            z_ref[quarter + g : quarter + g + TILE, a * LANES : (a + 1) * LANES] for a in range(4)
        ]
        out = combine(real, imag, g, TILE)
        for a in range(4):
            lanes = slice(a * LANES, (a + 1) * LANES)
            for part in range(2):
                high = out[a][part].astype(jnp.bfloat16)
                low = (out[a][part] - high.astype(jnp.float32)).astype(jnp.bfloat16)
                q_ref[2 * part, g : g + TILE, lanes] = high
                q_ref[2 * part + 1, g : g + TILE, lanes] = low
    real = [z_ref[2 * quarter : 2 * quarter + 8, a * LANES : (a + 1) * LANES] for a in range(4)]
    last = combine(real, [jnp.zeros_like(r) for r in real], quarter, 8)

    y = None
    for part in range(2):
        high = high_ref[part * quarter : (part + 1) * quarter, :]
        low = low_ref[part * quarter : (part + 1) * quarter, :]
        for left, right in ((high, 0), (high, 1), (low, 0)):
            term = jnp.dot(left, q_ref[2 * part + right], preferred_element_type=jnp.float32)
            y = term if y is None else y + term
    sign = 1.0 - 2.0 * (row_index(quarter) % 2).astype(jnp.float32)
    for a in range(4):
        x_ref[pl.ds(a, quarter, stride=4), :] = (
            y[:, a * LANES : (a + 1) * LANES] + sign * last[a][0][0:1, :]
        )
    link = first_link(place_ref)
    for k, out_ref in (
        (link, first_out.at[0]),
        (link ^ 1, first_out.at[1]),
        (6 - link, second_out.at[0]),
        ((6 - link) ^ 1, second_out.at[1]),
        (6, far_out),
        (7, core_out.at[1]),
        (0, own_out),
        (1, core_out.at[0]),
    ):
        target = place_ref[0] ^ k
        start = pl.multiple_of(target * rows, rows)
        out_ref[:rows, :] = x_ref[pl.ds(start, rows), :].astype(jnp.bfloat16)
        out_ref[rows:, :] = msg_ref[target, rows : rows + 8, :]


def silu(values):
    return values / (1.0 + jnp.exp(-values))


def gain_kernel(q_ref, taps_ref, residual_ref, out_ref):
    for c in range(out_ref.shape[1] // LANES):
        lanes = slice(c * LANES, (c + 1) * LANES)
        conv = short_conv_rolled(
            q_ref[0, :, lanes].astype(jnp.float32), lambda j: taps_ref[0, j : j + 1, lanes]
        )
        out_ref[:, lanes] = silu(residual_ref[:, lanes].astype(jnp.float32)) * conv


def mixed_block(msg, lanes, gain_ref, residual_ref, q_ref, taps_ref, out_ref):
    rows = residual_ref.shape[0]
    row = row_index(TILE)
    halo = msg[rows:, :].astype(jnp.float32)
    window = jnp.where(
        row < 8, q_ref[0, :TILE, lanes].astype(jnp.float32), jnp.concatenate([halo, halo], axis=0)
    )
    conv = short_conv_rolled(window, lambda j: taps_ref[0, j : j + 1, lanes])
    resid = residual_ref[:TILE, lanes].astype(jnp.float32)
    gain = jnp.where(row < 6, silu(resid) * conv, gain_ref[:TILE, lanes])
    out_ref[:TILE, :] = (resid + gain * msg[:TILE, :].astype(jnp.float32)).astype(jnp.bfloat16)
    out_ref[TILE:, :] = (
        residual_ref[TILE:, lanes].astype(jnp.float32)
        + gain_ref[TILE:, lanes] * msg[TILE:rows, :].astype(jnp.float32)
    ).astype(jnp.bfloat16)


def mix_kernel(place_ref, *refs):
    arrived, rest, (out_ref, held, sems) = refs[:7], refs[7:11], refs[11:]
    copies = []
    for i, (k, block) in enumerate(received(place_ref, *arrived)):
        lanes = own_lanes(place_ref, k)
        mixed_block(block, lanes, *rest, held.at[i])
        copy = pltpu.make_async_copy(held.at[i], out_ref.at[:, lanes], sems.at[i])
        copy.start()
        copies.append(copy)
    for copy in copies:
        copy.wait()


def split_table(table):
    high = table.astype(jnp.bfloat16)
    low = (table - high.astype(np.float64)).astype(jnp.bfloat16)
    return high, low


def filter_tables(quarter):
    index = np.arange(quarter)
    angle = 2.0 * np.pi * (index[:, None] * index[None, :] % (2 * quarter)) / (2 * quarter)
    alternate = np.zeros((TILE, quarter))
    alternate[0] = 1.0 - 2.0 * (index % 2)
    high, low = split_table(np.concatenate([np.cos(angle), -np.sin(angle), alternate], axis=0))
    g = np.arange(quarter + 8)[:, None]
    a = np.arange(4)[None, :]
    turn = 2.0 * np.pi * (g * a) / (8 * quarter)
    twist = np.stack([np.cos(turn), -np.sin(turn)], axis=-1).reshape(quarter + 8, 8)
    return high, low, twist.astype(np.float32)


def estimate(flops, moved):
    return pl.CostEstimate(flops=flops, bytes_accessed=moved, transcendentals=0)


def exchanged(beside, own, core, first, second, far):
    def swap(block, partner):
        return lax.ppermute(block, "seq", [(i, partner(i)) for i in range(8)])

    def arranged(kernel, name, shape, *blocks, spaces=(pltpu.VMEM, pltpu.VMEM)):
        return pl.pallas_call(
            kernel,
            in_specs=[pl.BlockSpec(memory_space=space) for space in spaces],
            out_shape=jax.ShapeDtypeStruct(shape, own.dtype),
            compiler_params=pltpu.CompilerParams(vmem_limit_bytes=VMEM_LIMIT),
            cost_estimate=estimate(1 << 10, 1 << 16),
            name=name,
        )(*blocks)

    def sent_on(pair):
        block = arranged(
            forward_kernel, "forward", own.shape, pair, beside, spaces=(pltpu.VMEM, pl.ANY)
        )
        return swap(block, lambda i: i ^ 1)

    core = swap(core, lambda i: i ^ 1)
    first = swap(first, lambda i: i ^ (2 + 2 * (i & 1)))
    second = swap(second, lambda i: i ^ (4 - 2 * (i & 1)))
    far = swap(arranged(merge_kernel, "merge", core.shape, far, core), lambda i: i ^ 6)
    return own, core, first, second, sent_on(first), sent_on(second), far


def local_kernels(streams, short_taps, spectrum, residual):
    rows, channels = residual.shape
    shards = lax.axis_size("seq")
    length = rows * shards
    quarter = length // 4
    params = pltpu.CompilerParams(vmem_limit_bytes=VMEM_LIMIT)
    place = lax.axis_index("seq").astype(jnp.int32).reshape(1)
    scalar = pl.BlockSpec(memory_space=pltpu.SMEM)
    vector = pl.BlockSpec(memory_space=pltpu.VMEM)
    hbm = pl.BlockSpec(memory_space=pltpu.HBM)
    half = lambda *shape: jax.ShapeDtypeStruct(shape, jnp.bfloat16)
    full = lambda *shape: jax.ShapeDtypeStruct(shape, jnp.float32)
    sent = rows + 24
    core, first, kv, q_last, taps = pl.pallas_call(
        pack_first_kernel,
        in_specs=[scalar, hbm, hbm],
        out_shape=[
            half(2, sent, LANES),
            half(2, sent, LANES),
            half(4, 2, rows, 2 * LANES),
            half(TILE, channels),
            full(*short_taps.shape),
        ],
        scratch_shapes=[pltpu.SemaphoreType.DMA((6,))],
        compiler_params=params,
        cost_estimate=estimate(1 << 30, 1 << 20),
        name="pack_first",
    )(
        place,
        pltpu.with_memory_space_constraint(streams, pltpu.HBM),
        pltpu.with_memory_space_constraint(short_taps, pltpu.HBM),
    )
    second, far, own = pl.pallas_call(
        pack_second_kernel,
        in_specs=[scalar] + [vector] * 3,
        out_shape=[half(2, sent, LANES), half(sent, LANES), half(sent, LANES)],
        compiler_params=params,
        cost_estimate=estimate(1 << 30, 1 << 20),
        name="pack_second",
    )(place, kv, q_last, taps)
    blocks = 2 * length // LANES
    view = jnp.transpose(spectrum.reshape(LANES, 2, blocks, LANES), (0, 2, 1, 3)).reshape(
        2 * blocks * LANES, LANES
    )
    folded = pl.pallas_call(
        functools.partial(spectrum_kernel, quarter),
        out_shape=full(8, quarter + 8, LANES),
        compiler_params=params,
        cost_estimate=estimate(1 << 32, 1 << 22),
        name="spectrum",
    )(view)
    arrived = exchanged(folded, own, core, first, second, far)
    high, low, twist = filter_tables(quarter)
    back = rows + 8
    filtered = pl.pallas_call(
        filter_kernel,
        in_specs=[scalar] + [vector] * 12,
        out_shape=[half(back, LANES)] + [half(2, back, LANES)] * 3 + [half(back, LANES)],
        scratch_shapes=[
            pltpu.VMEM((shards, sent, LANES), jnp.bfloat16),
            pltpu.VMEM((length, LANES), jnp.float32),
            pltpu.VMEM((2 * quarter + TILE, 4 * LANES), jnp.float32),
            pltpu.VMEM((4, quarter, 4 * LANES), jnp.bfloat16),
        ],
        compiler_params=params,
        cost_estimate=estimate(1 << 30, 1 << 22),
        name="filter",
    )(place, *arrived, taps, folded, high, low, twist)
    whole = lambda *shape: pl.BlockSpec(shape, lambda i: (0,) * len(shape))
    gain = pl.pallas_call(
        gain_kernel,
        grid=(1,),
        in_specs=[
            whole(1, rows, channels),
            whole(*short_taps.shape),
            whole(rows, channels),
        ],
        out_specs=whole(rows, channels),
        out_shape=full(rows, channels),
        compiler_params=params,
        cost_estimate=estimate(1 << 32, 1 << 20),
        name="gain",
    )(streams, taps, residual)
    arrived = exchanged(gain, *filtered)
    return pl.pallas_call(
        mix_kernel,
        in_specs=[scalar] + [vector] * 11,
        out_specs=hbm,
        out_shape=half(rows, channels),
        scratch_shapes=[
            pltpu.VMEM((shards, rows, LANES), jnp.bfloat16),
            pltpu.SemaphoreType.DMA((shards,)),
        ],
        compiler_params=params,
        cost_estimate=estimate(1 << 20, 1 << 20),
        name="mix",
    )(place, *arrived, gain, residual, streams, taps)


def local(streams, short_taps, spectrum, residual):
    rows, channels = residual.shape
    shards = lax.axis_size("seq")
    length = rows * shards
    fits = (
        channels == shards * LANES
        and rows % TILE == 0
        and rows >= 2 * TILE
        and length % (4 * LANES) == 0
        and length <= 2048
        and short_taps.shape[1] == 7
        and shards == 8
    )
    if fits:
        return local_kernels(streams, short_taps, spectrum, residual)
    return local_general(streams, short_taps, spectrum, residual)


def solution(mesh):
    placed = (
        P(None, "seq", "chan"),
        P(None, None, "chan"),
        P(("chan", "seq"), None, None),
        P("seq", "chan"),
    )
    return jax.shard_map(
        local, mesh=mesh, in_specs=placed, out_specs=P("seq", "chan"), check_vma=False
    )
```

```python
import functools
import math

import jax
import jax.numpy as jnp
import numpy as np
from jax import lax
from jax.experimental import pallas as pl
from jax.experimental.pallas import tpu as pltpu
from jax.sharding import PartitionSpec as P

LANES = 128
TILE = 16
VMEM_LIMIT = 16 * 1024 * 1024


def passed_along(block, axis, distance):
    devices = range(lax.axis_size(axis))
    route = [(i - distance, i) for i in devices if i - distance in devices]
    return lax.ppermute(block, axis, route)


def section_sizes(length_all):
    power = length_all.bit_length() - 1
    first = (power + 2) // 3
    second = (power - first + 1) // 2
    third = power - first - second
    result = [2**first, 2**second]
    result.append(2**third)
    return result


def matmul_high(left, right):
    return jnp.dot(left, right, precision=lax.Precision.HIGHEST, preferred_element_type=jnp.float32)


def section_high(table, values):
    return jnp.einsum(
        "ka,cab->ckb",
        table,
        values,
        precision=lax.Precision.HIGHEST,
        preferred_element_type=jnp.float32,
    )


def dft_table(order, direction):
    index = jnp.arange(order, dtype=jnp.int32)
    product = index[:, None] * index[None, :] % order
    angle = direction * 2.0 * math.pi * product.astype(jnp.float32) / order
    return (jnp.cos(angle), jnp.sin(angle))


def transform(real_part, imag_part, factors, direction):
    columns, length_now = real_part.shape
    first = factors[0]
    table_cos, table_sin = dft_table(first, direction)
    if len(factors) == 1:
        real_out = matmul_high(real_part, table_cos) - matmul_high(imag_part, table_sin)
        imag_out = matmul_high(imag_part, table_cos) + matmul_high(real_part, table_sin)
        return (real_out, imag_out)
    rest = length_now // first
    real_wide = real_part.reshape(columns, first, rest)
    if imag_part is None:
        section_real = section_high(table_cos, real_wide)
        section_imag = section_high(table_sin, real_wide)
    else:
        imag_wide = imag_part.reshape(columns, first, rest)
        section_real = section_high(table_cos, real_wide) - section_high(table_sin, imag_wide)
        section_imag = section_high(table_cos, imag_wide) + section_high(table_sin, real_wide)
    outer = jnp.arange(first, dtype=jnp.int32)[:, None]
    inner = jnp.arange(rest, dtype=jnp.int32)[None, :]
    twist = (
        direction * 2.0 * math.pi * (outer * inner % length_now).astype(jnp.float32) / length_now
    )
    twist_cos = jnp.cos(twist)[None, :, :]
    twist_sin = jnp.sin(twist)[None, :, :]
    turned_real = (section_real * twist_cos - section_imag * twist_sin).reshape(
        columns * first, rest
    )
    turned_imag = (section_real * twist_sin + section_imag * twist_cos).reshape(
        columns * first, rest
    )
    real_out, imag_out = transform(turned_real, turned_imag, factors[1:], direction)
    real_out = jnp.transpose(real_out.reshape(columns, first, rest), (0, 2, 1)).reshape(
        columns, length_now
    )
    imag_out = jnp.transpose(imag_out.reshape(columns, first, rest), (0, 2, 1)).reshape(
        columns, length_now
    )
    return (real_out, imag_out)


def long_filter(gated_rows, spectrum):
    columns, length_all = gated_rows.shape
    padded = jnp.concatenate(
        [gated_rows.astype(jnp.float32), jnp.zeros((columns, length_all), jnp.float32)], axis=1
    )
    factors = section_sizes(2 * length_all)
    freq_real, freq_imag = transform(padded, None, factors, -1.0)
    spec_real = spectrum[:, 0, :]
    spec_imag = spectrum[:, 1, :]
    prod_real = freq_real * spec_real - freq_imag * spec_imag
    prod_imag = freq_real * spec_imag + freq_imag * spec_real
    back_real, back_imag = transform(prod_real, prod_imag, factors, 1.0)
    return (back_real[:, :length_all] / (2 * length_all)).astype(jnp.bfloat16)


def local_general(streams, short_taps, spectrum, residual):
    row_count = streams.shape[1]
    channels = streams.shape[2]
    span = short_taps.shape[1] - 1
    rim_rows = passed_along(streams[:, row_count - span :, :], "seq", 1)
    extended = jnp.concatenate([rim_rows, streams], axis=1)
    total = jnp.zeros((3, row_count, channels), jnp.float32)
    for offset in range(span + 1):
        total = total + short_taps[:, offset, None, :] * extended[
            :, span - offset : span - offset + row_count, :
        ].astype(jnp.float32)
    convolved = total.astype(jnp.bfloat16)
    q_conv = convolved[0]
    k_conv = convolved[1]
    v_conv = convolved[2]
    seq_devices = lax.axis_size("seq")
    owned_count = channels // seq_devices
    length_all = row_count * seq_devices
    gated = (k_conv.astype(jnp.float32) * v_conv.astype(jnp.float32)).astype(jnp.bfloat16)
    owned = lax.all_to_all(
        gated.reshape(row_count, seq_devices, owned_count),
        "seq",
        split_axis=1,
        concat_axis=0,
        tiled=True,
    )
    gated_whole = owned.reshape(length_all, owned_count)
    filtered = jnp.transpose(long_filter(jnp.transpose(gated_whole), spectrum))
    returned = lax.all_to_all(
        filtered.reshape(length_all, 1, owned_count), "seq", split_axis=0, concat_axis=1, tiled=True
    )
    filtered_local = returned.reshape(row_count, channels)
    resid = residual.astype(jnp.float32)
    mixed = resid + jax.nn.silu(resid) * q_conv.astype(jnp.float32) * filtered_local.astype(
        jnp.float32
    )
    return mixed.astype(jnp.bfloat16)


def rounded(values):
    return values.astype(jnp.bfloat16).astype(jnp.float32)


def short_conv_rolled(rows, taps):
    total = taps(0) * rows
    for offset in range(1, 7):
        total = total + taps(offset) * pltpu.roll(rows, offset, 0)
    return rounded(total)


def row_index(count):
    return lax.broadcasted_iota(jnp.int32, (count, LANES), 0)


def own_lanes(place_ref, k):
    return pl.ds(pl.multiple_of((place_ref[0] ^ k) * LANES, LANES), LANES)


def first_link(place_ref):
    return 2 + 2 * (place_ref[0] & 1)


def pack_block(k, v, q_last, taps, out_ref):
    rows = k.shape[0]
    row = row_index(TILE)
    gated = short_conv_rolled(k, lambda j: taps(1, j)) * short_conv_rolled(
        v, lambda j: taps(2, j)
    )
    out_ref[:TILE, :] = jnp.where(row < 6, k[:TILE], gated[:TILE]).astype(jnp.bfloat16)
    out_ref[TILE:rows, :] = gated[TILE:].astype(jnp.bfloat16)
    edge = jnp.where(row < 6, v[:TILE], v[rows - TILE :])
    edge = jnp.where((row >= 6) & (row < 10), pltpu.roll(q_last, 12, 0), edge)
    out_ref[rows : rows + TILE, :] = edge.astype(jnp.bfloat16)
    half = jnp.where(row_index(8) < 2, pltpu.roll(q_last[8:], 2, 0), k[rows - 8 :])
    out_ref[rows + TILE :, :] = half.astype(jnp.bfloat16)


def chip_order(place_ref):
    first = first_link(place_ref)
    return (0, first, 6 - first, 6)


def pack_one(place_ref, kv_ref, q_ref, taps_ref, chip, p, out_ref):
    lanes = pl.ds(pl.multiple_of(((place_ref[0] & 1) ^ p) * LANES, LANES), LANES)
    owner = own_lanes(place_ref, chip_order(place_ref)[chip] ^ p)
    pack_block(
        kv_ref[chip, 0, :, lanes].astype(jnp.float32),
        kv_ref[chip, 1, :, lanes].astype(jnp.float32),
        q_ref[:, owner].astype(jnp.float32),
        lambda s, j: taps_ref[s, j : j + 1, owner],
        out_ref,
    )


def pack_first_kernel(
    place_ref, streams_ref, taps_hbm_ref, core_ref, first_ref, kv_ref, q_ref, taps_ref, sems
):
    rows = streams_ref.shape[1]
    order = chip_order(place_ref)
    shared = [
        pltpu.make_async_copy(taps_hbm_ref, taps_ref, sems.at[4]),
        pltpu.make_async_copy(
            streams_ref.at[0, pl.ds(rows - TILE, TILE), :], q_ref, sems.at[5]
        ),
    ]
    copies = {}
    for i in (1, 0, 3, 2):
        chip = (place_ref[0] ^ order[i]) >> 1
        lanes = pl.ds(pl.multiple_of(chip * (2 * LANES), 2 * LANES), 2 * LANES)
        copies[i] = pltpu.make_async_copy(
            streams_ref.at[pl.ds(1, 2), :, lanes], kv_ref.at[i], sems.at[i]
        )
        copies[i].start()
        if i == 1:
            for copy in shared:
                copy.start()
    for copy in shared:
        copy.wait()
    for i, p, out_ref in (
        (1, 0, first_ref.at[0]),
        (1, 1, first_ref.at[1]),
        (0, 1, core_ref.at[0]),
        (3, 1, core_ref.at[1]),
    ):
        if p == 0 or i != 1:
            copies[i].wait()
        pack_one(place_ref, kv_ref, q_ref, taps_ref, i, p, out_ref)
    copies[2].wait()


def pack_second_kernel(place_ref, kv_ref, q_ref, taps_ref, second_ref, far_ref, own_ref):
    for i, p, out_ref in (
        (2, 0, second_ref.at[0]),
        (2, 1, second_ref.at[1]),
        (3, 0, far_ref),
        (0, 0, own_ref),
    ):
        pack_one(place_ref, kv_ref, q_ref, taps_ref, i, p, out_ref)


def spectrum_kernel(quarter, view_ref, out_ref):
    blocks = view_ref.shape[0] // (2 * LANES)
    per = quarter // LANES
    scale = 1.0 / (blocks * LANES)
    row = lax.broadcasted_iota(jnp.int32, (quarter + TILE, 2 * quarter), 0)
    col = lax.broadcasted_iota(jnp.int32, (quarter + TILE, 2 * quarter), 1)
    ahead = (col < quarter) & (row == col)
    back = (col >= quarter) & (row + col == 2 * quarter)
    turn = jnp.where(ahead | back, 1.0, 0.0).astype(jnp.bfloat16)

    def columns(part, start):
        return [
            view_ref[pl.ds(2 * (start + i) + part, LANES, stride=2 * blocks), :]
            for i in range(per)
        ]

    for part in range(2):
        sign = 1.0 if part == 0 else -1.0
        heads, tails = [], []
        for m in range(4):
            start = 2 * per * m
            values = columns(part, start) + [
                sign * v for v in columns(part, blocks - start - per)
            ]
            values = jnp.concatenate(values, axis=1)
            high = values.astype(jnp.bfloat16)
            low = (values - high.astype(jnp.float32)).astype(jnp.bfloat16)
            both = lax.dot_general(
                turn,
                jnp.concatenate([high, low], axis=0),
                (((1,), (1,)), ((), ())),
                preferred_element_type=jnp.float32,
            )
            folded = (both[: quarter + 8, :LANES] + both[: quarter + 8, LANES:]) * scale
            out_ref[2 * m + part, :, :] = folded
            heads.append(folded[0:1])
            tails.append(folded[quarter : quarter + 1])
        for m in range(4):
            out_ref[2 * m + part, 0:1, :] = 0.5 * (heads[m] + sign * heads[(4 - m) % 4])
            out_ref[2 * m + part, quarter : quarter + 1, :] = 0.5 * (
                tails[m] + sign * tails[3 - m]
            )


def forward_kernel(pair_ref, beside_ref, out_ref):
    out_ref[...] = pair_ref[1]


def merge_kernel(far_ref, core_ref, out_ref):
    out_ref[0] = far_ref[...]
    out_ref[1] = core_ref[1]


def received(place_ref, own, core, first, second, first_on, second_on, far):
    link = first_link(place_ref)
    return [
        (0, own),
        (1, core.at[0]),
        (link, first.at[0]),
        (6 - link, second.at[0]),
        ((6 - link) ^ 1, first_on),
        (link ^ 1, second_on),
        (6, far.at[0]),
        (7, far.at[1]),
    ]


def filter_kernel(
    place_ref,
    own_ref,
    core_ref,
    first_ref,
    second_ref,
    first_on_ref,
    second_on_ref,
    far_ref,
    taps_ref,
    h_ref,
    ahead_ref,
    back_ref,
    twist_ref,
    own_out,
    core_out,
    first_out,
    second_out,
    far_out,
    msg_ref,
    x_ref,
    z_ref,
    q_ref,
):
    shards = msg_ref.shape[0]
    rows = own_ref.shape[0] - 24
    quarter = back_ref.shape[0]
    blocks = received(
        place_ref,
        own_ref,
        core_ref,
        first_ref,
        second_ref,
        first_on_ref,
        second_on_ref,
        far_ref,
    )
    for k, block in blocks:
        msg_ref[place_ref[0] ^ k] = block[...]
    row = row_index(TILE)
    own = own_lanes(place_ref, 0)

    before = None
    for s in range(shards):
        top = msg_ref[s, :TILE, :].astype(jnp.float32)
        edge = msg_ref[s, rows : rows + TILE, :].astype(jnp.float32)
        half = msg_ref[s, rows + TILE :, :].astype(jnp.float32)
        if before is None:
            above_k = above_v = jnp.zeros_like(edge)
            halo = jnp.zeros_like(half)
        else:
            above_v, half_before = before
            above_k = jnp.concatenate([half_before, half_before], axis=0)
            halo = jnp.where(
                row_index(8) < 6,
                pltpu.roll(above_v, 12, 0)[:8],
                pltpu.roll(half_before, 6, 0),
            )
        k_conv = short_conv_rolled(
            jnp.where(row < 8, top, above_k), lambda j: taps_ref[1, j : j + 1, own]
        )
        v_conv = short_conv_rolled(
            jnp.where(row < 8, edge, above_v), lambda j: taps_ref[2, j : j + 1, own]
        )
        x_ref[s * rows : s * rows + TILE, :] = jnp.where(row < 6, rounded(k_conv * v_conv), top)
        x_ref[s * rows + TILE : (s + 1) * rows, :] = msg_ref[s, TILE:rows, :].astype(jnp.float32)
        msg_ref[s, rows : rows + 8, :] = halo.astype(jnp.bfloat16)
        before = (edge, half)

    x = jnp.concatenate(
        [x_ref[pl.ds(a, quarter, stride=4), :].astype(jnp.bfloat16) for a in range(4)], axis=1
    )
    z_ref[...] = jnp.dot(
        ahead_ref[...],
        jnp.concatenate([x, x], axis=0),
        preferred_element_type=jnp.float32,
    )

    def combine(real, imag, g, count):
        u = []
        for a in range(4):
            if a == 0:
                u.append((real[0], imag[0]))
                continue
            wr = jnp.broadcast_to(twist_ref[g : g + count, 2 * a : 2 * a + 1], (count, LANES))
            wi = jnp.broadcast_to(
                twist_ref[g : g + count, 2 * a + 1 : 2 * a + 2], (count, LANES)
            )
            u.append((real[a] * wr - imag[a] * wi, real[a] * wi + imag[a] * wr, wr, wi))

        def four(v, sign):
            er, ei = v[0][0] + v[2][0], v[0][1] + v[2][1]
            dr, di = v[0][0] - v[2][0], v[0][1] - v[2][1]
            pr, pi = v[1][0] + v[3][0], v[1][1] + v[3][1]
            qr, qi = v[1][0] - v[3][0], v[1][1] - v[3][1]
            if sign < 0:
                one, three = (dr + qi, di - qr), (dr - qi, di + qr)
            else:
                one, three = (dr - qi, di + qr), (dr + qi, di - qr)
            return [(er + pr, ei + pi), one, (er - pr, ei - pi), three]

        freq = four(u, -1)
        prod = []
        for m in range(4):
            hr = h_ref[2 * m, g : g + count, :]
            hi = h_ref[2 * m + 1, g : g + count, :]
            xr, xi = freq[m]
            prod.append((xr * hr - xi * hi, xr * hi + xi * hr))
        v = four(prod, 1)
        out = [v[0]]
        for a in range(1, 4):
            wr, wi = u[a][2], u[a][3]
            vr, vi = v[a]
            out.append((vr * wr + vi * wi, vi * wr - vr * wi))
        return out

    for g in range(0, quarter, TILE):
        real = [z_ref[g : g + TILE, a * LANES : (a + 1) * LANES] for a in range(4)]
        imag = [
            z_ref[quarter + g : quarter + g + TILE, a * LANES : (a + 1) * LANES] for a in range(4)
        ]
        out = combine(real, imag, g, TILE)
        for a in range(4):
            lanes = slice(a * LANES, (a + 1) * LANES)
            for part in range(2):
                start = part * quarter + g
                q_ref[start : start + TILE, lanes] = out[a][part].astype(jnp.bfloat16)
    real = [z_ref[2 * quarter : 2 * quarter + 8, a * LANES : (a + 1) * LANES] for a in range(4)]
    last = combine(real, [jnp.zeros_like(r) for r in real], quarter, 8)

    y = jnp.dot(back_ref[...], q_ref[...], preferred_element_type=jnp.float32)
    sign = 1.0 - 2.0 * (row_index(quarter) % 2).astype(jnp.float32)
    for a in range(4):
        x_ref[pl.ds(a, quarter, stride=4), :] = (
            y[:, a * LANES : (a + 1) * LANES] + sign * last[a][0][0:1, :]
        )
    link = first_link(place_ref)
    for k, out_ref in (
        (link, first_out.at[0]),
        (link ^ 1, first_out.at[1]),
        (6 - link, second_out.at[0]),
        ((6 - link) ^ 1, second_out.at[1]),
        (6, far_out),
        (7, core_out.at[1]),
        (0, own_out),
        (1, core_out.at[0]),
    ):
        target = place_ref[0] ^ k
        start = pl.multiple_of(target * rows, rows)
        out_ref[:rows, :] = x_ref[pl.ds(start, rows), :].astype(jnp.bfloat16)
        out_ref[rows:, :] = msg_ref[target, rows : rows + 8, :]


def silu(values):
    return values / (1.0 + jnp.exp(-values))


def gain_kernel(q_ref, taps_ref, residual_ref, out_ref):
    for c in range(out_ref.shape[1] // LANES):
        lanes = slice(c * LANES, (c + 1) * LANES)
        conv = short_conv_rolled(
            q_ref[0, :, lanes].astype(jnp.float32), lambda j: taps_ref[0, j : j + 1, lanes]
        )
        out_ref[:, lanes] = silu(residual_ref[:, lanes].astype(jnp.float32)) * conv


def mixed_block(msg, lanes, gain_ref, residual_ref, q_ref, taps_ref, out_ref):
    rows = residual_ref.shape[0]
    row = row_index(TILE)
    halo = msg[rows:, :].astype(jnp.float32)
    window = jnp.where(
        row < 8, q_ref[0, :TILE, lanes].astype(jnp.float32), jnp.concatenate([halo, halo], axis=0)
    )
    conv = short_conv_rolled(window, lambda j: taps_ref[0, j : j + 1, lanes])
    resid = residual_ref[:TILE, lanes].astype(jnp.float32)
    gain = jnp.where(row < 6, silu(resid) * conv, gain_ref[:TILE, lanes])
    out_ref[:TILE, :] = (resid + gain * msg[:TILE, :].astype(jnp.float32)).astype(jnp.bfloat16)
    out_ref[TILE:, :] = (
        residual_ref[TILE:, lanes].astype(jnp.float32)
        + gain_ref[TILE:, lanes] * msg[TILE:rows, :].astype(jnp.float32)
    ).astype(jnp.bfloat16)


def mix_kernel(place_ref, *refs):
    arrived, rest, (out_ref, held, sems) = refs[:7], refs[7:11], refs[11:]
    copies = []
    for i, (k, block) in enumerate(received(place_ref, *arrived)):
        lanes = own_lanes(place_ref, k)
        mixed_block(block, lanes, *rest, held.at[i])
        copy = pltpu.make_async_copy(held.at[i], out_ref.at[:, lanes], sems.at[i])
        copy.start()
        copies.append(copy)
    for copy in copies:
        copy.wait()


def filter_tables(quarter):
    index = np.arange(quarter)
    angle = 2.0 * np.pi * (index[:, None] * index[None, :] % (2 * quarter)) / (2 * quarter)
    alternate = np.zeros((TILE, quarter))
    alternate[0] = 1.0 - 2.0 * (index % 2)
    table = np.concatenate([np.cos(angle), -np.sin(angle), alternate], axis=0)
    high = table.astype(jnp.bfloat16)
    low = (table - high.astype(np.float64)).astype(jnp.bfloat16)
    ahead = np.concatenate([high, low], axis=1)
    back = np.concatenate([high[:quarter], high[quarter : 2 * quarter]], axis=1)
    g = np.arange(quarter + 8)[:, None]
    a = np.arange(4)[None, :]
    turn = 2.0 * np.pi * (g * a) / (8 * quarter)
    twist = np.stack([np.cos(turn), -np.sin(turn)], axis=-1).reshape(quarter + 8, 8)
    return ahead, back, twist.astype(np.float32)


def estimate(flops, moved):
    return pl.CostEstimate(flops=flops, bytes_accessed=moved, transcendentals=0)


def exchanged(beside, own, core, first, second, far):
    def swap(block, partner):
        return lax.ppermute(block, "seq", [(i, partner(i)) for i in range(8)])

    def arranged(kernel, name, shape, *blocks, spaces=(pltpu.VMEM, pltpu.VMEM)):
        return pl.pallas_call(
            kernel,
            in_specs=[pl.BlockSpec(memory_space=space) for space in spaces],
            out_shape=jax.ShapeDtypeStruct(shape, own.dtype),
            compiler_params=pltpu.CompilerParams(vmem_limit_bytes=VMEM_LIMIT),
            cost_estimate=estimate(1 << 10, 1 << 16),
            name=name,
        )(*blocks)

    def sent_on(pair):
        block = arranged(
            forward_kernel, "forward", own.shape, pair, beside, spaces=(pltpu.VMEM, pl.ANY)
        )
        return swap(block, lambda i: i ^ 1)

    core = swap(core, lambda i: i ^ 1)
    first = swap(first, lambda i: i ^ (2 + 2 * (i & 1)))
    second = swap(second, lambda i: i ^ (4 - 2 * (i & 1)))
    far = swap(arranged(merge_kernel, "merge", core.shape, far, core), lambda i: i ^ 6)
    return own, core, first, second, sent_on(first), sent_on(second), far


def local_kernels(streams, short_taps, spectrum, residual):
    rows, channels = residual.shape
    shards = lax.axis_size("seq")
    length = rows * shards
    quarter = length // 4
    params = pltpu.CompilerParams(vmem_limit_bytes=VMEM_LIMIT)
    place = lax.axis_index("seq").astype(jnp.int32).reshape(1)
    scalar = pl.BlockSpec(memory_space=pltpu.SMEM)
    vector = pl.BlockSpec(memory_space=pltpu.VMEM)
    hbm = pl.BlockSpec(memory_space=pltpu.HBM)
    half = lambda *shape: jax.ShapeDtypeStruct(shape, jnp.bfloat16)
    full = lambda *shape: jax.ShapeDtypeStruct(shape, jnp.float32)
    sent = rows + 24
    core, first, kv, q_last, taps = pl.pallas_call(
        pack_first_kernel,
        in_specs=[scalar, hbm, hbm],
        out_shape=[
            half(2, sent, LANES),
            half(2, sent, LANES),
            half(4, 2, rows, 2 * LANES),
            half(TILE, channels),
            full(*short_taps.shape),
        ],
        scratch_shapes=[pltpu.SemaphoreType.DMA((6,))],
        compiler_params=params,
        cost_estimate=estimate(1 << 30, 1 << 20),
        name="pack_first",
    )(
        place,
        pltpu.with_memory_space_constraint(streams, pltpu.HBM),
        pltpu.with_memory_space_constraint(short_taps, pltpu.HBM),
    )
    second, far, own = pl.pallas_call(
        pack_second_kernel,
        in_specs=[scalar] + [vector] * 3,
        out_shape=[half(2, sent, LANES), half(sent, LANES), half(sent, LANES)],
        compiler_params=params,
        cost_estimate=estimate(1 << 30, 1 << 20),
        name="pack_second",
    )(place, kv, q_last, taps)
    blocks = 2 * length // LANES
    view = jnp.transpose(spectrum.reshape(LANES, 2, blocks, LANES), (0, 2, 1, 3)).reshape(
        2 * blocks * LANES, LANES
    )
    folded = pl.pallas_call(
        functools.partial(spectrum_kernel, quarter),
        out_shape=full(8, quarter + 8, LANES),
        compiler_params=params,
        cost_estimate=estimate(1 << 32, 1 << 22),
        name="spectrum",
    )(view)
    arrived = exchanged(folded, own, core, first, second, far)
    ahead, back_table, twist = filter_tables(quarter)
    back = rows + 8
    filtered = pl.pallas_call(
        filter_kernel,
        in_specs=[scalar] + [vector] * 12,
        out_shape=[half(back, LANES)] + [half(2, back, LANES)] * 3 + [half(back, LANES)],
        scratch_shapes=[
            pltpu.VMEM((shards, sent, LANES), jnp.bfloat16),
            pltpu.VMEM((length, LANES), jnp.float32),
            pltpu.VMEM((2 * quarter + TILE, 4 * LANES), jnp.float32),
            pltpu.VMEM((2 * quarter, 4 * LANES), jnp.bfloat16),
        ],
        compiler_params=params,
        cost_estimate=estimate(1 << 30, 1 << 22),
        name="filter",
    )(place, *arrived, taps, folded, ahead, back_table, twist)
    whole = lambda *shape: pl.BlockSpec(shape, lambda i: (0,) * len(shape))
    gain = pl.pallas_call(
        gain_kernel,
        grid=(1,),
        in_specs=[
            whole(1, rows, channels),
            whole(*short_taps.shape),
            whole(rows, channels),
        ],
        out_specs=whole(rows, channels),
        out_shape=full(rows, channels),
        compiler_params=params,
        cost_estimate=estimate(1 << 32, 1 << 20),
        name="gain",
    )(streams, taps, residual)
    arrived = exchanged(gain, *filtered)
    return pl.pallas_call(
        mix_kernel,
        in_specs=[scalar] + [vector] * 11,
        out_specs=hbm,
        out_shape=half(rows, channels),
        scratch_shapes=[
            pltpu.VMEM((shards, rows, LANES), jnp.bfloat16),
            pltpu.SemaphoreType.DMA((shards,)),
        ],
        compiler_params=params,
        cost_estimate=estimate(1 << 20, 1 << 20),
        name="mix",
    )(place, *arrived, gain, residual, streams, taps)


def local(streams, short_taps, spectrum, residual):
    rows, channels = residual.shape
    shards = lax.axis_size("seq")
    length = rows * shards
    fits = (
        channels == shards * LANES
        and rows % TILE == 0
        and rows >= 2 * TILE
        and length % (4 * LANES) == 0
        and length <= 2048
        and short_taps.shape[1] == 7
        and shards == 8
    )
    if fits:
        return local_kernels(streams, short_taps, spectrum, residual)
    return local_general(streams, short_taps, spectrum, residual)


def solution(mesh):
    placed = (
        P(None, "seq", "chan"),
        P(None, None, "chan"),
        P(("chan", "seq"), None, None),
        P("seq", "chan"),
    )
    return jax.shard_map(
        local, mesh=mesh, in_specs=placed, out_specs=P("seq", "chan"), check_vma=False
    )
```

```python
import functools
import math

import jax
import jax.numpy as jnp
import numpy as np
from jax import lax
from jax.experimental import pallas as pl
from jax.experimental.pallas import tpu as pltpu
from jax.sharding import PartitionSpec as P

LANES = 128
TILE = 16
VMEM_LIMIT = 16 * 1024 * 1024


def passed_along(block, axis, distance):
    devices = range(lax.axis_size(axis))
    route = [(i - distance, i) for i in devices if i - distance in devices]
    return lax.ppermute(block, axis, route)


def section_sizes(length_all):
    power = length_all.bit_length() - 1
    first = (power + 2) // 3
    second = (power - first + 1) // 2
    third = power - first - second
    result = [2**first, 2**second]
    result.append(2**third)
    return result


def matmul_high(left, right):
    return jnp.dot(left, right, precision=lax.Precision.HIGHEST, preferred_element_type=jnp.float32)


def section_high(table, values):
    return jnp.einsum(
        "ka,cab->ckb",
        table,
        values,
        precision=lax.Precision.HIGHEST,
        preferred_element_type=jnp.float32,
    )


def dft_table(order, direction):
    index = jnp.arange(order, dtype=jnp.int32)
    product = index[:, None] * index[None, :] % order
    angle = direction * 2.0 * math.pi * product.astype(jnp.float32) / order
    return (jnp.cos(angle), jnp.sin(angle))


def transform(real_part, imag_part, factors, direction):
    columns, length_now = real_part.shape
    first = factors[0]
    table_cos, table_sin = dft_table(first, direction)
    if len(factors) == 1:
        real_out = matmul_high(real_part, table_cos) - matmul_high(imag_part, table_sin)
        imag_out = matmul_high(imag_part, table_cos) + matmul_high(real_part, table_sin)
        return (real_out, imag_out)
    rest = length_now // first
    real_wide = real_part.reshape(columns, first, rest)
    if imag_part is None:
        section_real = section_high(table_cos, real_wide)
        section_imag = section_high(table_sin, real_wide)
    else:
        imag_wide = imag_part.reshape(columns, first, rest)
        section_real = section_high(table_cos, real_wide) - section_high(table_sin, imag_wide)
        section_imag = section_high(table_cos, imag_wide) + section_high(table_sin, real_wide)
    outer = jnp.arange(first, dtype=jnp.int32)[:, None]
    inner = jnp.arange(rest, dtype=jnp.int32)[None, :]
    twist = (
        direction * 2.0 * math.pi * (outer * inner % length_now).astype(jnp.float32) / length_now
    )
    twist_cos = jnp.cos(twist)[None, :, :]
    twist_sin = jnp.sin(twist)[None, :, :]
    turned_real = (section_real * twist_cos - section_imag * twist_sin).reshape(
        columns * first, rest
    )
    turned_imag = (section_real * twist_sin + section_imag * twist_cos).reshape(
        columns * first, rest
    )
    real_out, imag_out = transform(turned_real, turned_imag, factors[1:], direction)
    real_out = jnp.transpose(real_out.reshape(columns, first, rest), (0, 2, 1)).reshape(
        columns, length_now
    )
    imag_out = jnp.transpose(imag_out.reshape(columns, first, rest), (0, 2, 1)).reshape(
        columns, length_now
    )
    return (real_out, imag_out)


def long_filter(gated_rows, spectrum):
    columns, length_all = gated_rows.shape
    padded = jnp.concatenate(
        [gated_rows.astype(jnp.float32), jnp.zeros((columns, length_all), jnp.float32)], axis=1
    )
    factors = section_sizes(2 * length_all)
    freq_real, freq_imag = transform(padded, None, factors, -1.0)
    spec_real = spectrum[:, 0, :]
    spec_imag = spectrum[:, 1, :]
    prod_real = freq_real * spec_real - freq_imag * spec_imag
    prod_imag = freq_real * spec_imag + freq_imag * spec_real
    back_real, back_imag = transform(prod_real, prod_imag, factors, 1.0)
    return (back_real[:, :length_all] / (2 * length_all)).astype(jnp.bfloat16)


def local_general(streams, short_taps, spectrum, residual):
    row_count = streams.shape[1]
    channels = streams.shape[2]
    span = short_taps.shape[1] - 1
    rim_rows = passed_along(streams[:, row_count - span :, :], "seq", 1)
    extended = jnp.concatenate([rim_rows, streams], axis=1)
    total = jnp.zeros((3, row_count, channels), jnp.float32)
    for offset in range(span + 1):
        total = total + short_taps[:, offset, None, :] * extended[
            :, span - offset : span - offset + row_count, :
        ].astype(jnp.float32)
    convolved = total.astype(jnp.bfloat16)
    q_conv = convolved[0]
    k_conv = convolved[1]
    v_conv = convolved[2]
    seq_devices = lax.axis_size("seq")
    owned_count = channels // seq_devices
    length_all = row_count * seq_devices
    gated = (k_conv.astype(jnp.float32) * v_conv.astype(jnp.float32)).astype(jnp.bfloat16)
    owned = lax.all_to_all(
        gated.reshape(row_count, seq_devices, owned_count),
        "seq",
        split_axis=1,
        concat_axis=0,
        tiled=True,
    )
    gated_whole = owned.reshape(length_all, owned_count)
    filtered = jnp.transpose(long_filter(jnp.transpose(gated_whole), spectrum))
    returned = lax.all_to_all(
        filtered.reshape(length_all, 1, owned_count), "seq", split_axis=0, concat_axis=1, tiled=True
    )
    filtered_local = returned.reshape(row_count, channels)
    resid = residual.astype(jnp.float32)
    mixed = resid + jax.nn.silu(resid) * q_conv.astype(jnp.float32) * filtered_local.astype(
        jnp.float32
    )
    return mixed.astype(jnp.bfloat16)


def rounded(values):
    return values.astype(jnp.bfloat16).astype(jnp.float32)


def short_conv_rolled(rows, taps):
    later = pltpu.roll(rows, 1, 0)
    pairs = [taps(2 * i) * rows + taps(2 * i + 1) * later for i in range(3)]
    pairs.append(taps(6) * rows)
    low = pairs[0] + pltpu.roll(pairs[1], 2, 0)
    high = pairs[2] + pltpu.roll(pairs[3], 2, 0)
    return rounded(low + pltpu.roll(high, 4, 0))


def row_index(count):
    return lax.broadcasted_iota(jnp.int32, (count, LANES), 0)


def own_lanes(place_ref, k):
    return pl.ds(pl.multiple_of((place_ref[0] ^ k) * LANES, LANES), LANES)


def first_link(place_ref):
    return 2 + 2 * (place_ref[0] & 1)


def pack_block(k, v, q_last, taps, out_ref):
    rows = k.shape[0]
    row = row_index(TILE)
    gated = short_conv_rolled(k, lambda j: taps(1, j)) * short_conv_rolled(
        v, lambda j: taps(2, j)
    )
    out_ref[:TILE, :] = jnp.where(row < 6, k[:TILE], gated[:TILE]).astype(jnp.bfloat16)
    out_ref[TILE:rows, :] = gated[TILE:].astype(jnp.bfloat16)
    edge = jnp.where(row < 6, v[:TILE], v[rows - TILE :])
    edge = jnp.where((row >= 6) & (row < 10), pltpu.roll(q_last, 12, 0), edge)
    out_ref[rows : rows + TILE, :] = edge.astype(jnp.bfloat16)
    half = jnp.where(row_index(8) < 2, pltpu.roll(q_last[8:], 2, 0), k[rows - 8 :])
    out_ref[rows + TILE :, :] = half.astype(jnp.bfloat16)


def chip_order(place_ref):
    first = first_link(place_ref)
    return (0, first, 6 - first, 6)


def pack_one(place_ref, kv_ref, q_ref, taps_ref, chip, p, out_ref):
    lanes = pl.ds(pl.multiple_of(((place_ref[0] & 1) ^ p) * LANES, LANES), LANES)
    owner = own_lanes(place_ref, chip_order(place_ref)[chip] ^ p)
    pack_block(
        kv_ref[chip, 0, :, lanes].astype(jnp.float32),
        kv_ref[chip, 1, :, lanes].astype(jnp.float32),
        q_ref[:, owner].astype(jnp.float32),
        lambda s, j: taps_ref[s, j : j + 1, owner],
        out_ref,
    )


def pack_first_kernel(
    place_ref, streams_ref, taps_hbm_ref, core_ref, first_ref, kv_ref, q_ref, taps_ref, sems
):
    rows = streams_ref.shape[1]
    order = chip_order(place_ref)
    shared = [
        pltpu.make_async_copy(taps_hbm_ref, taps_ref, sems.at[4]),
        pltpu.make_async_copy(
            streams_ref.at[0, pl.ds(rows - TILE, TILE), :], q_ref, sems.at[5]
        ),
    ]
    copies = {}
    for i in (1, 0, 3, 2):
        chip = (place_ref[0] ^ order[i]) >> 1
        lanes = pl.ds(pl.multiple_of(chip * (2 * LANES), 2 * LANES), 2 * LANES)
        copies[i] = pltpu.make_async_copy(
            streams_ref.at[pl.ds(1, 2), :, lanes], kv_ref.at[i], sems.at[i]
        )
        copies[i].start()
        if i == 1:
            for copy in shared:
                copy.start()
    for copy in shared:
        copy.wait()
    for i, p, out_ref in (
        (1, 0, first_ref.at[0]),
        (1, 1, first_ref.at[1]),
        (0, 1, core_ref.at[0]),
        (3, 1, core_ref.at[1]),
    ):
        if p == 0 or i != 1:
            copies[i].wait()
        pack_one(place_ref, kv_ref, q_ref, taps_ref, i, p, out_ref)
    copies[2].wait()


def pack_second_kernel(place_ref, kv_ref, q_ref, taps_ref, second_ref, far_ref):
    for i, p, out_ref in (
        (2, 0, second_ref.at[0]),
        (2, 1, second_ref.at[1]),
        (3, 0, far_ref),
    ):
        pack_one(place_ref, kv_ref, q_ref, taps_ref, i, p, out_ref)


def spectrum_kernel(quarter, place_ref, view_ref, kv_ref, q_ref, taps_ref, out_ref, own_ref):
    pack_one(place_ref, kv_ref, q_ref, taps_ref, 0, 0, own_ref)
    blocks = view_ref.shape[0] // (2 * LANES)
    per = quarter // LANES
    scale = 1.0 / (blocks * LANES)
    row = lax.broadcasted_iota(jnp.int32, (quarter + TILE, 2 * quarter), 0)
    col = lax.broadcasted_iota(jnp.int32, (quarter + TILE, 2 * quarter), 1)
    ahead = (col < quarter) & (row == col)
    back = (col >= quarter) & (row + col == 2 * quarter)
    turn = jnp.where(ahead | back, 1.0, 0.0).astype(jnp.bfloat16)

    def columns(part, start):
        return [
            view_ref[pl.ds(2 * (start + i) + part, LANES, stride=2 * blocks), :]
            for i in range(per)
        ]

    for part in range(2):
        sign = 1.0 if part == 0 else -1.0
        heads, tails = [], []
        for m in range(4):
            start = 2 * per * m
            values = columns(part, start) + [
                sign * v for v in columns(part, blocks - start - per)
            ]
            values = jnp.concatenate(values, axis=1)
            high = values.astype(jnp.bfloat16)
            low = (values - high.astype(jnp.float32)).astype(jnp.bfloat16)
            both = lax.dot_general(
                turn,
                jnp.concatenate([high, low], axis=0),
                (((1,), (1,)), ((), ())),
                preferred_element_type=jnp.float32,
            )
            folded = (both[: quarter + 8, :LANES] + both[: quarter + 8, LANES:]) * scale
            out_ref[2 * m + part, :, :] = folded
            heads.append(folded[0:1])
            tails.append(folded[quarter : quarter + 1])
        for m in range(4):
            out_ref[2 * m + part, 0:1, :] = 0.5 * (heads[m] + sign * heads[(4 - m) % 4])
            out_ref[2 * m + part, quarter : quarter + 1, :] = 0.5 * (
                tails[m] + sign * tails[3 - m]
            )


def forward_kernel(pair_ref, beside_ref, out_ref):
    out_ref[...] = pair_ref[1]


def merge_kernel(far_ref, core_ref, out_ref):
    out_ref[0] = far_ref[...]
    out_ref[1] = core_ref[1]


def received(place_ref, own, core, first, second, first_on, second_on, far):
    link = first_link(place_ref)
    blocks = [
        (0, own),
        (1, core.at[0]),
        (link, first.at[0]),
        (6 - link, second.at[0]),
        ((6 - link) ^ 1, first_on),
        (link ^ 1, second_on),
    ]
    if far is not None:
        blocks += [(6, far.at[0]), (7, far.at[1])]
    return blocks


def filter_kernel(
    place_ref,
    own_ref,
    core_ref,
    first_ref,
    second_ref,
    first_on_ref,
    second_on_ref,
    far_ref,
    taps_ref,
    h_ref,
    ahead_ref,
    back_ref,
    twist_ref,
    own_out,
    core_out,
    first_out,
    second_out,
    far_out,
    msg_ref,
    x_ref,
    z_ref,
    q_ref,
):
    shards = msg_ref.shape[0]
    rows = own_ref.shape[0] - 24
    quarter = back_ref.shape[0]
    blocks = received(
        place_ref,
        own_ref,
        core_ref,
        first_ref,
        second_ref,
        first_on_ref,
        second_on_ref,
        far_ref,
    )
    for k, block in blocks:
        msg_ref[place_ref[0] ^ k] = block[...]
    row = row_index(TILE)
    own = own_lanes(place_ref, 0)

    before = None
    for s in range(shards):
        top = msg_ref[s, :TILE, :].astype(jnp.float32)
        edge = msg_ref[s, rows : rows + TILE, :].astype(jnp.float32)
        half = msg_ref[s, rows + TILE :, :].astype(jnp.float32)
        if before is None:
            above_k = above_v = jnp.zeros_like(edge)
            halo = jnp.zeros_like(half)
        else:
            above_v, half_before = before
            above_k = jnp.concatenate([half_before, half_before], axis=0)
            halo = jnp.where(
                row_index(8) < 6,
                pltpu.roll(above_v, 12, 0)[:8],
                pltpu.roll(half_before, 6, 0),
            )
        k_conv = short_conv_rolled(
            jnp.where(row < 8, top, above_k), lambda j: taps_ref[1, j : j + 1, own]
        )
        v_conv = short_conv_rolled(
            jnp.where(row < 8, edge, above_v), lambda j: taps_ref[2, j : j + 1, own]
        )
        x_ref[s * rows : s * rows + TILE, :] = jnp.where(row < 6, rounded(k_conv * v_conv), top)
        x_ref[s * rows + TILE : (s + 1) * rows, :] = msg_ref[s, TILE:rows, :].astype(jnp.float32)
        msg_ref[s, rows : rows + 8, :] = halo.astype(jnp.bfloat16)
        before = (edge, half)

    x = jnp.concatenate(
        [x_ref[pl.ds(a, quarter, stride=4), :].astype(jnp.bfloat16) for a in range(4)], axis=1
    )
    z_ref[...] = jnp.dot(
        ahead_ref[...],
        jnp.concatenate([x, x], axis=0),
        preferred_element_type=jnp.float32,
    )

    def combine(real, imag, g, count):
        u = []
        for a in range(4):
            if a == 0:
                u.append((real[0], imag[0]))
                continue
            wr = jnp.broadcast_to(twist_ref[g : g + count, 2 * a : 2 * a + 1], (count, LANES))
            wi = jnp.broadcast_to(
                twist_ref[g : g + count, 2 * a + 1 : 2 * a + 2], (count, LANES)
            )
            u.append((real[a] * wr - imag[a] * wi, real[a] * wi + imag[a] * wr, wr, wi))

        def four(v, sign):
            er, ei = v[0][0] + v[2][0], v[0][1] + v[2][1]
            dr, di = v[0][0] - v[2][0], v[0][1] - v[2][1]
            pr, pi = v[1][0] + v[3][0], v[1][1] + v[3][1]
            qr, qi = v[1][0] - v[3][0], v[1][1] - v[3][1]
            if sign < 0:
                one, three = (dr + qi, di - qr), (dr - qi, di + qr)
            else:
                one, three = (dr - qi, di + qr), (dr + qi, di - qr)
            return [(er + pr, ei + pi), one, (er - pr, ei - pi), three]

        freq = four(u, -1)
        prod = []
        for m in range(4):
            hr = h_ref[2 * m, g : g + count, :]
            hi = h_ref[2 * m + 1, g : g + count, :]
            xr, xi = freq[m]
            prod.append((xr * hr - xi * hi, xr * hi + xi * hr))
        v = four(prod, 1)
        out = [v[0]]
        for a in range(1, 4):
            wr, wi = u[a][2], u[a][3]
            vr, vi = v[a]
            out.append((vr * wr + vi * wi, vi * wr - vr * wi))
        return out

    for g in range(0, quarter, TILE):
        real = [z_ref[g : g + TILE, a * LANES : (a + 1) * LANES] for a in range(4)]
        imag = [
            z_ref[quarter + g : quarter + g + TILE, a * LANES : (a + 1) * LANES] for a in range(4)
        ]
        out = combine(real, imag, g, TILE)
        for a in range(4):
            lanes = slice(a * LANES, (a + 1) * LANES)
            for part in range(2):
                start = part * quarter + g
                q_ref[start : start + TILE, lanes] = out[a][part].astype(jnp.bfloat16)
    real = [z_ref[2 * quarter : 2 * quarter + 8, a * LANES : (a + 1) * LANES] for a in range(4)]
    last = combine(real, [jnp.zeros_like(r) for r in real], quarter, 8)

    y = jnp.dot(back_ref[...], q_ref[...], preferred_element_type=jnp.float32)
    sign = 1.0 - 2.0 * (row_index(quarter) % 2).astype(jnp.float32)
    for a in range(4):
        x_ref[pl.ds(a, quarter, stride=4), :] = (
            y[:, a * LANES : (a + 1) * LANES] + sign * last[a][0][0:1, :]
        )
    link = first_link(place_ref)
    for k, out_ref in (
        (link, first_out.at[0]),
        (link ^ 1, first_out.at[1]),
        (6 - link, second_out.at[0]),
        ((6 - link) ^ 1, second_out.at[1]),
        (6, far_out),
        (7, core_out.at[1]),
        (0, own_out),
        (1, core_out.at[0]),
    ):
        target = place_ref[0] ^ k
        start = pl.multiple_of(target * rows, rows)
        out_ref[:rows, :] = x_ref[pl.ds(start, rows), :].astype(jnp.bfloat16)
        out_ref[rows:, :] = msg_ref[target, rows : rows + 8, :]


def silu(values):
    return values / (1.0 + jnp.exp(-values))


def gain_kernel(q_ref, taps_ref, residual_ref, out_ref):
    for c in range(out_ref.shape[1] // LANES):
        lanes = slice(c * LANES, (c + 1) * LANES)
        conv = short_conv_rolled(
            q_ref[0, :, lanes].astype(jnp.float32), lambda j: taps_ref[0, j : j + 1, lanes]
        )
        out_ref[:, lanes] = silu(residual_ref[:, lanes].astype(jnp.float32)) * conv


def mixed_block(msg, lanes, gain_ref, residual_ref, q_ref, taps_ref, out_ref):
    rows = residual_ref.shape[0]
    row = row_index(TILE)
    halo = msg[rows:, :].astype(jnp.float32)
    window = jnp.where(
        row < 8, q_ref[0, :TILE, lanes].astype(jnp.float32), jnp.concatenate([halo, halo], axis=0)
    )
    conv = short_conv_rolled(window, lambda j: taps_ref[0, j : j + 1, lanes])
    resid = residual_ref[:TILE, lanes].astype(jnp.float32)
    gain = jnp.where(row < 6, silu(resid) * conv, gain_ref[:TILE, lanes])
    out_ref[:TILE, :] = (resid + gain * msg[:TILE, :].astype(jnp.float32)).astype(jnp.bfloat16)
    out_ref[TILE:, :] = (
        residual_ref[TILE:, lanes].astype(jnp.float32)
        + gain_ref[TILE:, lanes] * msg[TILE:rows, :].astype(jnp.float32)
    ).astype(jnp.bfloat16)


def mix_early_kernel(place_ref, *refs):
    arrived, rest, out_ref = refs[:6], refs[6:10], refs[10]
    for i, (k, block) in enumerate(received(place_ref, *arrived, None)):
        mixed_block(block, own_lanes(place_ref, k), *rest, out_ref.at[i])


def mix_late_kernel(place_ref, early_ref, far_ref, *refs):
    rest, (out_ref, held, sems) = refs[:4], refs[4:]
    link = first_link(place_ref)
    order = (0, 1, link, 6 - link, (6 - link) ^ 1, link ^ 1, 6, 7)
    copies = []
    for i, k in enumerate(order):
        lanes = own_lanes(place_ref, k)
        source = early_ref.at[i] if i < 6 else held.at[i - 6]
        if i >= 6:
            mixed_block(far_ref.at[i - 6], lanes, *rest, source)
        copy = pltpu.make_async_copy(source, out_ref.at[:, lanes], sems.at[i])
        copy.start()
        copies.append(copy)
    for copy in copies:
        copy.wait()


def filter_tables(quarter):
    index = np.arange(quarter)
    angle = 2.0 * np.pi * (index[:, None] * index[None, :] % (2 * quarter)) / (2 * quarter)
    alternate = np.zeros((TILE, quarter))
    alternate[0] = 1.0 - 2.0 * (index % 2)
    table = np.concatenate([np.cos(angle), -np.sin(angle), alternate], axis=0)
    high = table.astype(jnp.bfloat16)
    low = (table - high.astype(np.float64)).astype(jnp.bfloat16)
    ahead = np.concatenate([high, low], axis=1)
    back = np.concatenate([high[:quarter], high[quarter : 2 * quarter]], axis=1)
    g = np.arange(quarter + 8)[:, None]
    a = np.arange(4)[None, :]
    turn = 2.0 * np.pi * (g * a) / (8 * quarter)
    twist = np.stack([np.cos(turn), -np.sin(turn)], axis=-1).reshape(quarter + 8, 8)
    return ahead, back, twist.astype(np.float32)


def estimate(flops, moved):
    return pl.CostEstimate(flops=flops, bytes_accessed=moved, transcendentals=0)


def exchanged(beside, own, core, first, second, far):
    def swap(block, partner):
        return lax.ppermute(block, "seq", [(i, partner(i)) for i in range(8)])

    def arranged(kernel, name, shape, *blocks, spaces=(pltpu.VMEM, pltpu.VMEM)):
        return pl.pallas_call(
            kernel,
            in_specs=[pl.BlockSpec(memory_space=space) for space in spaces],
            out_shape=jax.ShapeDtypeStruct(shape, own.dtype),
            compiler_params=pltpu.CompilerParams(vmem_limit_bytes=VMEM_LIMIT),
            cost_estimate=estimate(1 << 10, 1 << 16),
            name=name,
        )(*blocks)

    def sent_on(pair):
        block = arranged(
            forward_kernel, "forward", own.shape, pair, beside, spaces=(pltpu.VMEM, pl.ANY)
        )
        return swap(block, lambda i: i ^ 1)

    core = swap(core, lambda i: i ^ 1)
    first = swap(first, lambda i: i ^ (2 + 2 * (i & 1)))
    second = swap(second, lambda i: i ^ (4 - 2 * (i & 1)))
    far = swap(arranged(merge_kernel, "merge", core.shape, far, core), lambda i: i ^ 6)
    return own, core, first, second, sent_on(first), sent_on(second), far


def local_kernels(streams, short_taps, spectrum, residual):
    rows, channels = residual.shape
    shards = lax.axis_size("seq")
    length = rows * shards
    quarter = length // 4
    params = pltpu.CompilerParams(vmem_limit_bytes=VMEM_LIMIT)
    place = lax.axis_index("seq").astype(jnp.int32).reshape(1)
    scalar = pl.BlockSpec(memory_space=pltpu.SMEM)
    vector = pl.BlockSpec(memory_space=pltpu.VMEM)
    hbm = pl.BlockSpec(memory_space=pltpu.HBM)
    half = lambda *shape: jax.ShapeDtypeStruct(shape, jnp.bfloat16)
    full = lambda *shape: jax.ShapeDtypeStruct(shape, jnp.float32)
    sent = rows + 24
    core, first, kv, q_last, taps = pl.pallas_call(
        pack_first_kernel,
        in_specs=[scalar, hbm, hbm],
        out_shape=[
            half(2, sent, LANES),
            half(2, sent, LANES),
            half(4, 2, rows, 2 * LANES),
            half(TILE, channels),
            full(*short_taps.shape),
        ],
        scratch_shapes=[pltpu.SemaphoreType.DMA((6,))],
        compiler_params=params,
        cost_estimate=estimate(1 << 30, 1 << 20),
        name="pack_first",
    )(
        place,
        pltpu.with_memory_space_constraint(streams, pltpu.HBM),
        pltpu.with_memory_space_constraint(short_taps, pltpu.HBM),
    )
    second, far = pl.pallas_call(
        pack_second_kernel,
        in_specs=[scalar] + [vector] * 3,
        out_shape=[half(2, sent, LANES), half(sent, LANES)],
        compiler_params=params,
        cost_estimate=estimate(1 << 30, 1 << 20),
        name="pack_second",
    )(place, kv, q_last, taps)
    blocks = 2 * length // LANES
    view = jnp.transpose(spectrum.reshape(LANES, 2, blocks, LANES), (0, 2, 1, 3)).reshape(
        2 * blocks * LANES, LANES
    )
    folded, own = pl.pallas_call(
        functools.partial(spectrum_kernel, quarter),
        in_specs=[scalar] + [vector] * 4,
        out_shape=[full(8, quarter + 8, LANES), half(sent, LANES)],
        compiler_params=params,
        cost_estimate=estimate(1 << 32, 1 << 22),
        name="spectrum",
    )(place, view, kv, q_last, taps)
    arrived = exchanged(folded, own, core, first, second, far)
    ahead, back_table, twist = filter_tables(quarter)
    back = rows + 8
    filtered = pl.pallas_call(
        filter_kernel,
        in_specs=[scalar] + [vector] * 12,
        out_shape=[half(back, LANES)] + [half(2, back, LANES)] * 3 + [half(back, LANES)],
        scratch_shapes=[
            pltpu.VMEM((shards, sent, LANES), jnp.bfloat16),
            pltpu.VMEM((length, LANES), jnp.float32),
            pltpu.VMEM((2 * quarter + TILE, 4 * LANES), jnp.float32),
            pltpu.VMEM((2 * quarter, 4 * LANES), jnp.bfloat16),
        ],
        compiler_params=params,
        cost_estimate=estimate(1 << 30, 1 << 22),
        name="filter",
    )(place, *arrived, taps, folded, ahead, back_table, twist)
    whole = lambda *shape: pl.BlockSpec(shape, lambda i: (0,) * len(shape))
    gain = pl.pallas_call(
        gain_kernel,
        grid=(1,),
        in_specs=[
            whole(1, rows, channels),
            whole(*short_taps.shape),
            whole(rows, channels),
        ],
        out_specs=whole(rows, channels),
        out_shape=full(rows, channels),
        compiler_params=params,
        cost_estimate=estimate(1 << 32, 1 << 20),
        name="gain",
    )(streams, taps, residual)
    *near, far = exchanged(gain, *filtered)
    rest = (gain, residual, streams, taps)
    early = pl.pallas_call(
        mix_early_kernel,
        in_specs=[scalar] + [vector] * 10,
        out_shape=half(6, rows, LANES),
        compiler_params=params,
        cost_estimate=estimate(1 << 20, 1 << 20),
        name="mix_early",
    )(place, *near, *rest)
    return pl.pallas_call(
        mix_late_kernel,
        in_specs=[scalar] + [vector] * 6,
        out_specs=hbm,
        out_shape=half(rows, channels),
        scratch_shapes=[
            pltpu.VMEM((2, rows, LANES), jnp.bfloat16),
            pltpu.SemaphoreType.DMA((shards,)),
        ],
        compiler_params=params,
        cost_estimate=estimate(1 << 20, 1 << 20),
        name="mix_late",
    )(place, early, far, *rest)


def local(streams, short_taps, spectrum, residual):
    rows, channels = residual.shape
    shards = lax.axis_size("seq")
    length = rows * shards
    fits = (
        channels == shards * LANES
        and rows % TILE == 0
        and rows >= 2 * TILE
        and length % (4 * LANES) == 0
        and length <= 2048
        and short_taps.shape[1] == 7
        and shards == 8
    )
    if fits:
        return local_kernels(streams, short_taps, spectrum, residual)
    return local_general(streams, short_taps, spectrum, residual)


def solution(mesh):
    placed = (
        P(None, "seq", "chan"),
        P(None, None, "chan"),
        P(("chan", "seq"), None, None),
        P("seq", "chan"),
    )
    return jax.shard_map(
        local, mesh=mesh, in_specs=placed, out_specs=P("seq", "chan"), check_vma=False
    )
```

```python
import functools
import math

import jax
import jax.numpy as jnp
import numpy as np
from jax import lax
from jax.experimental import pallas as pl
from jax.experimental.pallas import tpu as pltpu
from jax.sharding import PartitionSpec as P

LANES = 128
TILE = 16
VMEM_LIMIT = 16 * 1024 * 1024


def passed_along(block, axis, distance):
    devices = range(lax.axis_size(axis))
    route = [(i - distance, i) for i in devices if i - distance in devices]
    return lax.ppermute(block, axis, route)


def section_sizes(length_all):
    power = length_all.bit_length() - 1
    first = (power + 2) // 3
    second = (power - first + 1) // 2
    third = power - first - second
    result = [2**first, 2**second]
    result.append(2**third)
    return result


def matmul_high(left, right):
    return jnp.dot(left, right, precision=lax.Precision.HIGHEST, preferred_element_type=jnp.float32)


def section_high(table, values):
    return jnp.einsum(
        "ka,cab->ckb",
        table,
        values,
        precision=lax.Precision.HIGHEST,
        preferred_element_type=jnp.float32,
    )


def dft_table(order, direction):
    index = jnp.arange(order, dtype=jnp.int32)
    product = index[:, None] * index[None, :] % order
    angle = direction * 2.0 * math.pi * product.astype(jnp.float32) / order
    return (jnp.cos(angle), jnp.sin(angle))


def transform(real_part, imag_part, factors, direction):
    columns, length_now = real_part.shape
    first = factors[0]
    table_cos, table_sin = dft_table(first, direction)
    if len(factors) == 1:
        real_out = matmul_high(real_part, table_cos) - matmul_high(imag_part, table_sin)
        imag_out = matmul_high(imag_part, table_cos) + matmul_high(real_part, table_sin)
        return (real_out, imag_out)
    rest = length_now // first
    real_wide = real_part.reshape(columns, first, rest)
    if imag_part is None:
        section_real = section_high(table_cos, real_wide)
        section_imag = section_high(table_sin, real_wide)
    else:
        imag_wide = imag_part.reshape(columns, first, rest)
        section_real = section_high(table_cos, real_wide) - section_high(table_sin, imag_wide)
        section_imag = section_high(table_cos, imag_wide) + section_high(table_sin, real_wide)
    outer = jnp.arange(first, dtype=jnp.int32)[:, None]
    inner = jnp.arange(rest, dtype=jnp.int32)[None, :]
    twist = (
        direction * 2.0 * math.pi * (outer * inner % length_now).astype(jnp.float32) / length_now
    )
    twist_cos = jnp.cos(twist)[None, :, :]
    twist_sin = jnp.sin(twist)[None, :, :]
    turned_real = (section_real * twist_cos - section_imag * twist_sin).reshape(
        columns * first, rest
    )
    turned_imag = (section_real * twist_sin + section_imag * twist_cos).reshape(
        columns * first, rest
    )
    real_out, imag_out = transform(turned_real, turned_imag, factors[1:], direction)
    real_out = jnp.transpose(real_out.reshape(columns, first, rest), (0, 2, 1)).reshape(
        columns, length_now
    )
    imag_out = jnp.transpose(imag_out.reshape(columns, first, rest), (0, 2, 1)).reshape(
        columns, length_now
    )
    return (real_out, imag_out)


def long_filter(gated_rows, spectrum):
    columns, length_all = gated_rows.shape
    padded = jnp.concatenate(
        [gated_rows.astype(jnp.float32), jnp.zeros((columns, length_all), jnp.float32)], axis=1
    )
    factors = section_sizes(2 * length_all)
    freq_real, freq_imag = transform(padded, None, factors, -1.0)
    spec_real = spectrum[:, 0, :]
    spec_imag = spectrum[:, 1, :]
    prod_real = freq_real * spec_real - freq_imag * spec_imag
    prod_imag = freq_real * spec_imag + freq_imag * spec_real
    back_real, back_imag = transform(prod_real, prod_imag, factors, 1.0)
    return (back_real[:, :length_all] / (2 * length_all)).astype(jnp.bfloat16)


def local_general(streams, short_taps, spectrum, residual):
    row_count = streams.shape[1]
    channels = streams.shape[2]
    span = short_taps.shape[1] - 1
    rim_rows = passed_along(streams[:, row_count - span :, :], "seq", 1)
    extended = jnp.concatenate([rim_rows, streams], axis=1)
    total = jnp.zeros((3, row_count, channels), jnp.float32)
    for offset in range(span + 1):
        total = total + short_taps[:, offset, None, :] * extended[
            :, span - offset : span - offset + row_count, :
        ].astype(jnp.float32)
    convolved = total.astype(jnp.bfloat16)
    q_conv = convolved[0]
    k_conv = convolved[1]
    v_conv = convolved[2]
    seq_devices = lax.axis_size("seq")
    owned_count = channels // seq_devices
    length_all = row_count * seq_devices
    gated = (k_conv.astype(jnp.float32) * v_conv.astype(jnp.float32)).astype(jnp.bfloat16)
    owned = lax.all_to_all(
        gated.reshape(row_count, seq_devices, owned_count),
        "seq",
        split_axis=1,
        concat_axis=0,
        tiled=True,
    )
    gated_whole = owned.reshape(length_all, owned_count)
    filtered = jnp.transpose(long_filter(jnp.transpose(gated_whole), spectrum))
    returned = lax.all_to_all(
        filtered.reshape(length_all, 1, owned_count), "seq", split_axis=0, concat_axis=1, tiled=True
    )
    filtered_local = returned.reshape(row_count, channels)
    resid = residual.astype(jnp.float32)
    mixed = resid + jax.nn.silu(resid) * q_conv.astype(jnp.float32) * filtered_local.astype(
        jnp.float32
    )
    return mixed.astype(jnp.bfloat16)


def rounded(values):
    return values.astype(jnp.bfloat16).astype(jnp.float32)


def short_conv_rolled(rows, taps):
    later = pltpu.roll(rows, 1, 0)
    pairs = [taps(2 * i) * rows + taps(2 * i + 1) * later for i in range(3)]
    pairs.append(taps(6) * rows)
    low = pairs[0] + pltpu.roll(pairs[1], 2, 0)
    high = pairs[2] + pltpu.roll(pairs[3], 2, 0)
    return rounded(low + pltpu.roll(high, 4, 0))


def row_index(count):
    return lax.broadcasted_iota(jnp.int32, (count, LANES), 0)


def own_lanes(place_ref, k):
    return pl.ds(pl.multiple_of((place_ref[0] ^ k) * LANES, LANES), LANES)


def first_link(place_ref):
    return 2 + 2 * (place_ref[0] & 1)


def pack_block(k, v, q_last, taps, out_ref):
    rows = k.shape[0]
    row = row_index(TILE)
    gated = short_conv_rolled(k, lambda j: taps(1, j)) * short_conv_rolled(
        v, lambda j: taps(2, j)
    )
    out_ref[:TILE, :] = jnp.where(row < 6, k[:TILE], gated[:TILE]).astype(jnp.bfloat16)
    out_ref[TILE:rows, :] = gated[TILE:].astype(jnp.bfloat16)
    edge = jnp.where(row < 6, v[:TILE], v[rows - TILE :])
    edge = jnp.where((row >= 6) & (row < 10), pltpu.roll(q_last, 12, 0), edge)
    out_ref[rows : rows + TILE, :] = edge.astype(jnp.bfloat16)
    half = jnp.where(row_index(8) < 2, pltpu.roll(q_last[8:], 2, 0), k[rows - 8 :])
    out_ref[rows + TILE :, :] = half.astype(jnp.bfloat16)


def chip_order(place_ref):
    first = first_link(place_ref)
    return (0, first, 6 - first, 6)


def pack_one(place_ref, kv_ref, q_ref, taps_ref, chip, p, out_ref):
    lanes = pl.ds(pl.multiple_of(((place_ref[0] & 1) ^ p) * LANES, LANES), LANES)
    owner = own_lanes(place_ref, chip_order(place_ref)[chip] ^ p)
    pack_block(
        kv_ref[chip, 0, :, lanes].astype(jnp.float32),
        kv_ref[chip, 1, :, lanes].astype(jnp.float32),
        q_ref[:, owner].astype(jnp.float32),
        lambda s, j: taps_ref[s, j : j + 1, owner],
        out_ref,
    )


def pack_first_kernel(
    place_ref, streams_ref, taps_hbm_ref, core_ref, first_ref, kv_ref, q_ref, taps_ref, sems
):
    rows = streams_ref.shape[1]
    order = chip_order(place_ref)
    shared = [
        pltpu.make_async_copy(taps_hbm_ref, taps_ref, sems.at[4]),
        pltpu.make_async_copy(
            streams_ref.at[0, pl.ds(rows - TILE, TILE), :], q_ref, sems.at[5]
        ),
    ]
    copies = {}
    for i in (1, 0, 3, 2):
        chip = (place_ref[0] ^ order[i]) >> 1
        lanes = pl.ds(pl.multiple_of(chip * (2 * LANES), 2 * LANES), 2 * LANES)
        copies[i] = pltpu.make_async_copy(
            streams_ref.at[pl.ds(1, 2), :, lanes], kv_ref.at[i], sems.at[i]
        )
        copies[i].start()
        if i == 1:
            for copy in shared:
                copy.start()
    for copy in shared:
        copy.wait()
    for i, p, out_ref in (
        (1, 0, first_ref.at[0]),
        (1, 1, first_ref.at[1]),
        (0, 1, core_ref.at[0]),
        (3, 1, core_ref.at[1]),
    ):
        if p == 0 or i != 1:
            copies[i].wait()
        pack_one(place_ref, kv_ref, q_ref, taps_ref, i, p, out_ref)
    copies[2].wait()


def pack_second_kernel(place_ref, kv_ref, q_ref, taps_ref, second_ref, far_ref):
    for i, p, out_ref in (
        (2, 0, second_ref.at[0]),
        (2, 1, second_ref.at[1]),
        (3, 0, far_ref),
    ):
        pack_one(place_ref, kv_ref, q_ref, taps_ref, i, p, out_ref)


def pack_own_kernel(place_ref, kv_ref, q_ref, taps_ref, beside_ref, own_ref):
    pack_one(place_ref, kv_ref, q_ref, taps_ref, 0, 0, own_ref)


def spectrum_kernel(quarter, part, view_ref, beside_ref, out_ref):
    blocks = view_ref.shape[0] // (2 * LANES)
    per = quarter // LANES
    scale = 1.0 / (blocks * LANES)
    row = lax.broadcasted_iota(jnp.int32, (quarter + TILE, 2 * quarter), 0)
    col = lax.broadcasted_iota(jnp.int32, (quarter + TILE, 2 * quarter), 1)
    ahead = (col < quarter) & (row == col)
    back = (col >= quarter) & (row + col == 2 * quarter)
    turn = jnp.where(ahead | back, 1.0, 0.0).astype(jnp.bfloat16)

    def columns(part, start):
        return [
            view_ref[pl.ds(2 * (start + i) + part, LANES, stride=2 * blocks), :]
            for i in range(per)
        ]

    sign = 1.0 if part == 0 else -1.0
    heads, tails = [], []
    for m in range(4):
        start = 2 * per * m
        values = columns(part, start) + [sign * v for v in columns(part, blocks - start - per)]
        values = jnp.concatenate(values, axis=1)
        high = values.astype(jnp.bfloat16)
        low = (values - high.astype(jnp.float32)).astype(jnp.bfloat16)
        both = lax.dot_general(
            turn,
            jnp.concatenate([high, low], axis=0),
            (((1,), (1,)), ((), ())),
            preferred_element_type=jnp.float32,
        )
        folded = (both[: quarter + 8, :LANES] + both[: quarter + 8, LANES:]) * scale
        out_ref[m, :, :] = folded
        heads.append(folded[0:1])
        tails.append(folded[quarter : quarter + 1])
    for m in range(4):
        out_ref[m, 0:1, :] = 0.5 * (heads[m] + sign * heads[(4 - m) % 4])
        out_ref[m, quarter : quarter + 1, :] = 0.5 * (tails[m] + sign * tails[3 - m])


def forward_kernel(pair_ref, beside_ref, out_ref):
    out_ref[...] = pair_ref[1]


def merge_kernel(far_ref, core_ref, out_ref):
    out_ref[0] = far_ref[...]
    out_ref[1] = core_ref[1]


def received(place_ref, own, core, first, second, first_on, second_on, far):
    link = first_link(place_ref)
    blocks = [
        (0, own),
        (1, core.at[0]),
        (link, first.at[0]),
        (6 - link, second.at[0]),
        ((6 - link) ^ 1, first_on),
        (link ^ 1, second_on),
    ]
    if far is not None:
        blocks += [(6, far.at[0]), (7, far.at[1])]
    return blocks


def filter_kernel(
    place_ref,
    own_ref,
    core_ref,
    first_ref,
    second_ref,
    first_on_ref,
    second_on_ref,
    far_ref,
    taps_ref,
    real_ref,
    imag_ref,
    ahead_ref,
    back_ref,
    twist_ref,
    own_out,
    core_out,
    first_out,
    second_out,
    far_out,
    msg_ref,
    x_ref,
    z_ref,
    q_ref,
):
    shards = msg_ref.shape[0]
    rows = own_ref.shape[0] - 24
    quarter = back_ref.shape[0]
    blocks = received(
        place_ref,
        own_ref,
        core_ref,
        first_ref,
        second_ref,
        first_on_ref,
        second_on_ref,
        far_ref,
    )
    for k, block in blocks:
        msg_ref[place_ref[0] ^ k] = block[...]
    row = row_index(TILE)
    own = own_lanes(place_ref, 0)

    before = None
    for s in range(shards):
        top = msg_ref[s, :TILE, :].astype(jnp.float32)
        edge = msg_ref[s, rows : rows + TILE, :].astype(jnp.float32)
        half = msg_ref[s, rows + TILE :, :].astype(jnp.float32)
        if before is None:
            above_k = above_v = jnp.zeros_like(edge)
            halo = jnp.zeros_like(half)
        else:
            above_v, half_before = before
            above_k = jnp.concatenate([half_before, half_before], axis=0)
            halo = jnp.where(
                row_index(8) < 6,
                pltpu.roll(above_v, 12, 0)[:8],
                pltpu.roll(half_before, 6, 0),
            )
        k_conv = short_conv_rolled(
            jnp.where(row < 8, top, above_k), lambda j: taps_ref[1, j : j + 1, own]
        )
        v_conv = short_conv_rolled(
            jnp.where(row < 8, edge, above_v), lambda j: taps_ref[2, j : j + 1, own]
        )
        x_ref[s * rows : s * rows + TILE, :] = jnp.where(row < 6, rounded(k_conv * v_conv), top)
        x_ref[s * rows + TILE : (s + 1) * rows, :] = msg_ref[s, TILE:rows, :].astype(jnp.float32)
        msg_ref[s, rows : rows + 8, :] = halo.astype(jnp.bfloat16)
        before = (edge, half)

    x = jnp.concatenate(
        [x_ref[pl.ds(a, quarter, stride=4), :].astype(jnp.bfloat16) for a in range(4)], axis=1
    )
    x = jnp.concatenate([x, x], axis=0)

    def combine(real, imag, g, count):
        u = []
        for a in range(4):
            if a == 0:
                u.append((real[0], imag[0]))
                continue
            wr = jnp.broadcast_to(twist_ref[g : g + count, 2 * a : 2 * a + 1], (count, LANES))
            wi = jnp.broadcast_to(
                twist_ref[g : g + count, 2 * a + 1 : 2 * a + 2], (count, LANES)
            )
            u.append((real[a] * wr - imag[a] * wi, real[a] * wi + imag[a] * wr, wr, wi))

        def four(v, sign):
            er, ei = v[0][0] + v[2][0], v[0][1] + v[2][1]
            dr, di = v[0][0] - v[2][0], v[0][1] - v[2][1]
            pr, pi = v[1][0] + v[3][0], v[1][1] + v[3][1]
            qr, qi = v[1][0] - v[3][0], v[1][1] - v[3][1]
            if sign < 0:
                one, three = (dr + qi, di - qr), (dr - qi, di + qr)
            else:
                one, three = (dr - qi, di + qr), (dr + qi, di - qr)
            return [(er + pr, ei + pi), one, (er - pr, ei - pi), three]

        freq = four(u, -1)
        prod = []
        for m in range(4):
            hr = real_ref[m, g : g + count, :]
            hi = imag_ref[m, g : g + count, :]
            xr, xi = freq[m]
            prod.append((xr * hr - xi * hi, xr * hi + xi * hr))
        v = four(prod, 1)
        out = [v[0]]
        for a in range(1, 4):
            wr, wi = u[a][2], u[a][3]
            vr, vi = v[a]
            out.append((vr * wr + vi * wi, vi * wr - vr * wi))
        return out

    part = quarter // 2
    y = None
    for half in range(2):
        base = half * quarter
        count = quarter + half * TILE
        z_ref[base : base + count, :] = jnp.dot(
            ahead_ref[base : base + count, :], x, preferred_element_type=jnp.float32
        )
        for g in range(0, part, TILE):
            real, imag = [
                [
                    z_ref[start : start + TILE, a * LANES : (a + 1) * LANES]
                    for a in range(4)
                ]
                for start in (base + g, base + part + g)
            ]
            out = combine(real, imag, half * part + g, TILE)
            for a in range(4):
                lanes = slice(a * LANES, (a + 1) * LANES)
                for i in range(2):
                    start = base + i * part + g
                    q_ref[start : start + TILE, lanes] = out[a][i].astype(jnp.bfloat16)
        term = jnp.dot(
            back_ref[:, base : base + quarter],
            q_ref[base : base + quarter, :],
            preferred_element_type=jnp.float32,
        )
        y = term if y is None else y + term
    real = [z_ref[2 * quarter : 2 * quarter + 8, a * LANES : (a + 1) * LANES] for a in range(4)]
    last = combine(real, [jnp.zeros_like(r) for r in real], quarter, 8)

    sign = 1.0 - 2.0 * (row_index(quarter) % 2).astype(jnp.float32)
    for a in range(4):
        x_ref[pl.ds(a, quarter, stride=4), :] = (
            y[:, a * LANES : (a + 1) * LANES] + sign * last[a][0][0:1, :]
        )
    link = first_link(place_ref)
    for k, out_ref in (
        (link, first_out.at[0]),
        (link ^ 1, first_out.at[1]),
        (6 - link, second_out.at[0]),
        ((6 - link) ^ 1, second_out.at[1]),
        (6, far_out),
        (7, core_out.at[1]),
        (0, own_out),
        (1, core_out.at[0]),
    ):
        target = place_ref[0] ^ k
        start = pl.multiple_of(target * rows, rows)
        out_ref[:rows, :] = x_ref[pl.ds(start, rows), :].astype(jnp.bfloat16)
        out_ref[rows:, :] = msg_ref[target, rows : rows + 8, :]


def silu(values):
    return values / (1.0 + jnp.exp(-values))


def gain_kernel(q_ref, taps_ref, residual_ref, out_ref):
    for c in range(out_ref.shape[1] // LANES):
        lanes = slice(c * LANES, (c + 1) * LANES)
        conv = short_conv_rolled(
            q_ref[0, :, lanes].astype(jnp.float32), lambda j: taps_ref[0, j : j + 1, lanes]
        )
        out_ref[:, lanes] = silu(residual_ref[:, lanes].astype(jnp.float32)) * conv


def mixed_block(msg, lanes, gain_ref, residual_ref, q_ref, taps_ref, out_ref):
    rows = residual_ref.shape[0]
    row = row_index(TILE)
    halo = msg[rows:, :].astype(jnp.float32)
    window = jnp.where(
        row < 8, q_ref[0, :TILE, lanes].astype(jnp.float32), jnp.concatenate([halo, halo], axis=0)
    )
    conv = short_conv_rolled(window, lambda j: taps_ref[0, j : j + 1, lanes])
    resid = residual_ref[:TILE, lanes].astype(jnp.float32)
    gain = jnp.where(row < 6, silu(resid) * conv, gain_ref[:TILE, lanes])
    out_ref[:TILE, :] = (resid + gain * msg[:TILE, :].astype(jnp.float32)).astype(jnp.bfloat16)
    out_ref[TILE:, :] = (
        residual_ref[TILE:, lanes].astype(jnp.float32)
        + gain_ref[TILE:, lanes] * msg[TILE:rows, :].astype(jnp.float32)
    ).astype(jnp.bfloat16)


def mix_early_kernel(place_ref, *refs):
    arrived, rest, out_ref = refs[:6], refs[6:10], refs[10]
    for i, (k, block) in enumerate(received(place_ref, *arrived, None)):
        mixed_block(block, own_lanes(place_ref, k), *rest, out_ref.at[i])


def mix_late_kernel(place_ref, early_ref, far_ref, *refs):
    rest, (out_ref, held, sems) = refs[:4], refs[4:]
    link = first_link(place_ref)
    order = (0, 1, link, 6 - link, (6 - link) ^ 1, link ^ 1, 6, 7)
    copies = []
    for i, k in enumerate(order):
        lanes = own_lanes(place_ref, k)
        source = early_ref.at[i] if i < 6 else held.at[i - 6]
        if i >= 6:
            mixed_block(far_ref.at[i - 6], lanes, *rest, source)
        copy = pltpu.make_async_copy(source, out_ref.at[:, lanes], sems.at[i])
        copy.start()
        copies.append(copy)
    for copy in copies:
        copy.wait()


def filter_tables(quarter):
    index = np.arange(quarter)
    angle = 2.0 * np.pi * (index[:, None] * index[None, :] % (2 * quarter)) / (2 * quarter)
    alternate = np.zeros((TILE, quarter))
    alternate[0] = 1.0 - 2.0 * (index % 2)
    part = quarter // 2
    cos, sin = np.cos(angle), -np.sin(angle)
    table = np.concatenate([cos[:part], sin[:part], cos[part:], sin[part:], alternate], axis=0)
    high = table.astype(jnp.bfloat16)
    low = (table - high.astype(np.float64)).astype(jnp.bfloat16)
    ahead = np.concatenate([high, low], axis=1)
    back = np.ascontiguousarray(high[: 2 * quarter].T)
    g = np.arange(quarter + 8)[:, None]
    a = np.arange(4)[None, :]
    turn = 2.0 * np.pi * (g * a) / (8 * quarter)
    twist = np.stack([np.cos(turn), -np.sin(turn)], axis=-1).reshape(quarter + 8, 8)
    return ahead, back, twist.astype(np.float32)


def estimate(flops, moved):
    return pl.CostEstimate(flops=flops, bytes_accessed=moved, transcendentals=0)


def swap(block, partner):
    return lax.ppermute(block, "seq", [(i, partner(i)) for i in range(8)])


def arranged(kernel, name, shape, *blocks, spaces=(pltpu.VMEM, pltpu.VMEM)):
    return pl.pallas_call(
        kernel,
        in_specs=[pl.BlockSpec(memory_space=space) for space in spaces],
        out_shape=jax.ShapeDtypeStruct(shape, jnp.bfloat16),
        compiler_params=pltpu.CompilerParams(vmem_limit_bytes=VMEM_LIMIT),
        cost_estimate=estimate(1 << 10, 1 << 16),
        name=name,
    )(*blocks)


def exchanged(core, first, second, far):
    core = swap(core, lambda i: i ^ 1)
    first = swap(first, lambda i: i ^ (2 + 2 * (i & 1)))
    second = swap(second, lambda i: i ^ (4 - 2 * (i & 1)))
    merged = arranged(merge_kernel, "merge", core.shape, far, core)
    return core, first, second, swap(merged, lambda i: i ^ 6), merged


def sibling_block(pair, beside):
    return arranged(
        forward_kernel, "forward", pair.shape[1:], pair, beside, spaces=(pltpu.VMEM, pl.ANY)
    )


def local_kernels(streams, short_taps, spectrum, residual):
    rows, channels = residual.shape
    shards = lax.axis_size("seq")
    length = rows * shards
    quarter = length // 4
    params = pltpu.CompilerParams(vmem_limit_bytes=VMEM_LIMIT)
    place = lax.axis_index("seq").astype(jnp.int32).reshape(1)
    scalar = pl.BlockSpec(memory_space=pltpu.SMEM)
    vector = pl.BlockSpec(memory_space=pltpu.VMEM)
    hbm = pl.BlockSpec(memory_space=pltpu.HBM)
    half = lambda *shape: jax.ShapeDtypeStruct(shape, jnp.bfloat16)
    full = lambda *shape: jax.ShapeDtypeStruct(shape, jnp.float32)
    sent = rows + 24
    core, first, kv, q_last, taps = pl.pallas_call(
        pack_first_kernel,
        in_specs=[scalar, hbm, hbm],
        out_shape=[
            half(2, sent, LANES),
            half(2, sent, LANES),
            half(4, 2, rows, 2 * LANES),
            half(TILE, channels),
            full(*short_taps.shape),
        ],
        scratch_shapes=[pltpu.SemaphoreType.DMA((6,))],
        compiler_params=params,
        cost_estimate=estimate(1 << 30, 1 << 20),
        name="pack_first",
    )(
        place,
        pltpu.with_memory_space_constraint(streams, pltpu.HBM),
        pltpu.with_memory_space_constraint(short_taps, pltpu.HBM),
    )
    second, far = pl.pallas_call(
        pack_second_kernel,
        in_specs=[scalar] + [vector] * 3,
        out_shape=[half(2, sent, LANES), half(sent, LANES)],
        compiler_params=params,
        cost_estimate=estimate(1 << 30, 1 << 20),
        name="pack_second",
    )(place, kv, q_last, taps)
    blocks = 2 * length // LANES
    view = jnp.transpose(spectrum.reshape(LANES, 2, blocks, LANES), (0, 2, 1, 3)).reshape(
        2 * blocks * LANES, LANES
    )
    core, first, second, far, merged = exchanged(core, first, second, far)

    def spectrum_part(part, beside):
        return pl.pallas_call(
            functools.partial(spectrum_kernel, quarter, part),
            in_specs=[vector, pl.BlockSpec(memory_space=pl.ANY)],
            out_shape=full(4, quarter + 8, LANES),
            compiler_params=params,
            cost_estimate=estimate(1 << (32 - 20 * part), 1 << 22),
            name="spectrum",
        )(view, beside)

    real = spectrum_part(0, merged)
    first_on = swap(sibling_block(first, real), lambda i: i ^ 1)
    second_on = sibling_block(second, real)
    imag = spectrum_part(1, first_on)
    own = pl.pallas_call(
        pack_own_kernel,
        in_specs=[scalar] + [vector] * 3 + [pl.BlockSpec(memory_space=pl.ANY)],
        out_shape=half(sent, LANES),
        compiler_params=params,
        cost_estimate=estimate(1 << 22, 1 << 20),
        name="pack_own",
    )(place, kv, q_last, taps, second_on)
    second_on = swap(second_on, lambda i: i ^ 1)
    ahead, back_table, twist = filter_tables(quarter)
    back = rows + 8
    own, *sent_back = pl.pallas_call(
        filter_kernel,
        in_specs=[scalar] + [vector] * 13,
        out_shape=[half(back, LANES)] + [half(2, back, LANES)] * 3 + [half(back, LANES)],
        scratch_shapes=[
            pltpu.VMEM((shards, sent, LANES), jnp.bfloat16),
            pltpu.VMEM((length, LANES), jnp.float32),
            pltpu.VMEM((2 * quarter + TILE, 4 * LANES), jnp.float32),
            pltpu.VMEM((2 * quarter, 4 * LANES), jnp.bfloat16),
        ],
        compiler_params=params,
        cost_estimate=estimate(1 << 30, 1 << 22),
        name="filter",
    )(
        place,
        own,
        core,
        first,
        second,
        first_on,
        second_on,
        far,
        taps,
        real,
        imag,
        ahead,
        back_table,
        twist,
    )
    whole = lambda *shape: pl.BlockSpec(shape, lambda i: (0,) * len(shape))
    gain = pl.pallas_call(
        gain_kernel,
        grid=(1,),
        in_specs=[
            whole(1, rows, channels),
            whole(*short_taps.shape),
            whole(rows, channels),
        ],
        out_specs=whole(rows, channels),
        out_shape=full(rows, channels),
        compiler_params=params,
        cost_estimate=estimate(1 << 32, 1 << 20),
        name="gain",
    )(streams, taps, residual)
    core, first, second, far, _ = exchanged(*sent_back)
    first_on, second_on = [
        swap(sibling_block(pair, gain), lambda i: i ^ 1) for pair in (first, second)
    ]
    rest = (gain, residual, streams, taps)
    early = pl.pallas_call(
        mix_early_kernel,
        in_specs=[scalar] + [vector] * 10,
        out_shape=half(6, rows, LANES),
        compiler_params=params,
        cost_estimate=estimate(1 << 20, 1 << 20),
        name="mix_early",
    )(place, own, core, first, second, first_on, second_on, *rest)
    return pl.pallas_call(
        mix_late_kernel,
        in_specs=[scalar] + [vector] * 6,
        out_specs=hbm,
        out_shape=half(rows, channels),
        scratch_shapes=[
            pltpu.VMEM((2, rows, LANES), jnp.bfloat16),
            pltpu.SemaphoreType.DMA((shards,)),
        ],
        compiler_params=params,
        cost_estimate=estimate(1 << 20, 1 << 20),
        name="mix_late",
    )(place, early, far, *rest)


def local(streams, short_taps, spectrum, residual):
    rows, channels = residual.shape
    shards = lax.axis_size("seq")
    length = rows * shards
    fits = (
        channels == shards * LANES
        and rows % TILE == 0
        and rows >= 2 * TILE
        and length % (4 * LANES) == 0
        and length <= 2048
        and short_taps.shape[1] == 7
        and shards == 8
    )
    if fits:
        return local_kernels(streams, short_taps, spectrum, residual)
    return local_general(streams, short_taps, spectrum, residual)


def solution(mesh):
    placed = (
        P(None, "seq", "chan"),
        P(None, None, "chan"),
        P(("chan", "seq"), None, None),
        P("seq", "chan"),
    )
    return jax.shard_map(
        local, mesh=mesh, in_specs=placed, out_specs=P("seq", "chan"), check_vma=False
    )
```

```python
import functools
import math

import jax
import jax.numpy as jnp
import numpy as np
from jax import lax
from jax.experimental import pallas as pl
from jax.experimental.pallas import tpu as pltpu
from jax.sharding import PartitionSpec as P

LANES = 128
TILE = 16
VMEM_LIMIT = 16 * 1024 * 1024


def passed_along(block, axis, distance):
    devices = range(lax.axis_size(axis))
    route = [(i - distance, i) for i in devices if i - distance in devices]
    return lax.ppermute(block, axis, route)


def section_sizes(length_all):
    power = length_all.bit_length() - 1
    first = (power + 2) // 3
    second = (power - first + 1) // 2
    third = power - first - second
    result = [2**first, 2**second]
    result.append(2**third)
    return result


def matmul_high(left, right):
    return jnp.dot(left, right, precision=lax.Precision.HIGHEST, preferred_element_type=jnp.float32)


def section_high(table, values):
    return jnp.einsum(
        "ka,cab->ckb",
        table,
        values,
        precision=lax.Precision.HIGHEST,
        preferred_element_type=jnp.float32,
    )


def dft_table(order, direction):
    index = jnp.arange(order, dtype=jnp.int32)
    product = index[:, None] * index[None, :] % order
    angle = direction * 2.0 * math.pi * product.astype(jnp.float32) / order
    return (jnp.cos(angle), jnp.sin(angle))


def transform(real_part, imag_part, factors, direction):
    columns, length_now = real_part.shape
    first = factors[0]
    table_cos, table_sin = dft_table(first, direction)
    if len(factors) == 1:
        real_out = matmul_high(real_part, table_cos) - matmul_high(imag_part, table_sin)
        imag_out = matmul_high(imag_part, table_cos) + matmul_high(real_part, table_sin)
        return (real_out, imag_out)
    rest = length_now // first
    real_wide = real_part.reshape(columns, first, rest)
    if imag_part is None:
        section_real = section_high(table_cos, real_wide)
        section_imag = section_high(table_sin, real_wide)
    else:
        imag_wide = imag_part.reshape(columns, first, rest)
        section_real = section_high(table_cos, real_wide) - section_high(table_sin, imag_wide)
        section_imag = section_high(table_cos, imag_wide) + section_high(table_sin, real_wide)
    outer = jnp.arange(first, dtype=jnp.int32)[:, None]
    inner = jnp.arange(rest, dtype=jnp.int32)[None, :]
    twist = (
        direction * 2.0 * math.pi * (outer * inner % length_now).astype(jnp.float32) / length_now
    )
    twist_cos = jnp.cos(twist)[None, :, :]
    twist_sin = jnp.sin(twist)[None, :, :]
    turned_real = (section_real * twist_cos - section_imag * twist_sin).reshape(
        columns * first, rest
    )
    turned_imag = (section_real * twist_sin + section_imag * twist_cos).reshape(
        columns * first, rest
    )
    real_out, imag_out = transform(turned_real, turned_imag, factors[1:], direction)
    real_out = jnp.transpose(real_out.reshape(columns, first, rest), (0, 2, 1)).reshape(
        columns, length_now
    )
    imag_out = jnp.transpose(imag_out.reshape(columns, first, rest), (0, 2, 1)).reshape(
        columns, length_now
    )
    return (real_out, imag_out)


def long_filter(gated_rows, spectrum):
    columns, length_all = gated_rows.shape
    padded = jnp.concatenate(
        [gated_rows.astype(jnp.float32), jnp.zeros((columns, length_all), jnp.float32)], axis=1
    )
    factors = section_sizes(2 * length_all)
    freq_real, freq_imag = transform(padded, None, factors, -1.0)
    spec_real = spectrum[:, 0, :]
    spec_imag = spectrum[:, 1, :]
    prod_real = freq_real * spec_real - freq_imag * spec_imag
    prod_imag = freq_real * spec_imag + freq_imag * spec_real
    back_real, back_imag = transform(prod_real, prod_imag, factors, 1.0)
    return (back_real[:, :length_all] / (2 * length_all)).astype(jnp.bfloat16)


def local_general(streams, short_taps, spectrum, residual):
    row_count = streams.shape[1]
    channels = streams.shape[2]
    span = short_taps.shape[1] - 1
    rim_rows = passed_along(streams[:, row_count - span :, :], "seq", 1)
    extended = jnp.concatenate([rim_rows, streams], axis=1)
    total = jnp.zeros((3, row_count, channels), jnp.float32)
    for offset in range(span + 1):
        total = total + short_taps[:, offset, None, :] * extended[
            :, span - offset : span - offset + row_count, :
        ].astype(jnp.float32)
    convolved = total.astype(jnp.bfloat16)
    q_conv = convolved[0]
    k_conv = convolved[1]
    v_conv = convolved[2]
    seq_devices = lax.axis_size("seq")
    owned_count = channels // seq_devices
    length_all = row_count * seq_devices
    gated = (k_conv.astype(jnp.float32) * v_conv.astype(jnp.float32)).astype(jnp.bfloat16)
    owned = lax.all_to_all(
        gated.reshape(row_count, seq_devices, owned_count),
        "seq",
        split_axis=1,
        concat_axis=0,
        tiled=True,
    )
    gated_whole = owned.reshape(length_all, owned_count)
    filtered = jnp.transpose(long_filter(jnp.transpose(gated_whole), spectrum))
    returned = lax.all_to_all(
        filtered.reshape(length_all, 1, owned_count), "seq", split_axis=0, concat_axis=1, tiled=True
    )
    filtered_local = returned.reshape(row_count, channels)
    resid = residual.astype(jnp.float32)
    mixed = resid + jax.nn.silu(resid) * q_conv.astype(jnp.float32) * filtered_local.astype(
        jnp.float32
    )
    return mixed.astype(jnp.bfloat16)


def rounded(values):
    return values.astype(jnp.bfloat16).astype(jnp.float32)


def short_conv_rolled(rows, taps):
    later = pltpu.roll(rows, 1, 0)
    pairs = [taps(2 * i) * rows + taps(2 * i + 1) * later for i in range(3)]
    pairs.append(taps(6) * rows)
    low = pairs[0] + pltpu.roll(pairs[1], 2, 0)
    high = pairs[2] + pltpu.roll(pairs[3], 2, 0)
    return rounded(low + pltpu.roll(high, 4, 0))


def row_index(count):
    return lax.broadcasted_iota(jnp.int32, (count, LANES), 0)


def own_lanes(place_ref, k):
    return pl.ds(pl.multiple_of((place_ref[0] ^ k) * LANES, LANES), LANES)


def first_link(place_ref):
    return 2 + 2 * (place_ref[0] & 1)


def pack_block(k, v, q_last, taps, out_ref):
    rows = k.shape[0]
    row = row_index(TILE)
    gated = short_conv_rolled(k, lambda j: taps(1, j)) * short_conv_rolled(
        v, lambda j: taps(2, j)
    )
    out_ref[:TILE, :] = jnp.where(row < 6, k[:TILE], gated[:TILE]).astype(jnp.bfloat16)
    out_ref[TILE:rows, :] = gated[TILE:].astype(jnp.bfloat16)
    edge = jnp.where(row < 6, v[:TILE], v[rows - TILE :])
    edge = jnp.where((row >= 6) & (row < 10), pltpu.roll(q_last, 12, 0), edge)
    out_ref[rows : rows + TILE, :] = edge.astype(jnp.bfloat16)
    half = jnp.where(row_index(8) < 2, pltpu.roll(q_last[8:], 2, 0), k[rows - 8 :])
    out_ref[rows + TILE :, :] = half.astype(jnp.bfloat16)


def chip_order(place_ref):
    first = first_link(place_ref)
    return (0, first, 6 - first, 6)


def pack_one(place_ref, kv_ref, q_ref, taps_ref, chip, p, out_ref):
    lanes = pl.ds(pl.multiple_of(((place_ref[0] & 1) ^ p) * LANES, LANES), LANES)
    owner = own_lanes(place_ref, chip_order(place_ref)[chip] ^ p)
    pack_block(
        kv_ref[chip, 0, :, lanes].astype(jnp.float32),
        kv_ref[chip, 1, :, lanes].astype(jnp.float32),
        q_ref[:, owner].astype(jnp.float32),
        lambda s, j: taps_ref[s, j : j + 1, owner],
        out_ref,
    )


def pack_first_kernel(
    place_ref, streams_ref, taps_hbm_ref, core_ref, first_ref, kv_ref, q_ref, taps_ref, sems
):
    rows = streams_ref.shape[1]
    order = chip_order(place_ref)
    shared = [
        pltpu.make_async_copy(taps_hbm_ref, taps_ref, sems.at[4]),
        pltpu.make_async_copy(
            streams_ref.at[0, pl.ds(rows - TILE, TILE), :], q_ref, sems.at[5]
        ),
    ]
    copies = {}
    for i in (1, 0, 3, 2):
        chip = (place_ref[0] ^ order[i]) >> 1
        lanes = pl.ds(pl.multiple_of(chip * (2 * LANES), 2 * LANES), 2 * LANES)
        copies[i] = pltpu.make_async_copy(
            streams_ref.at[pl.ds(1, 2), :, lanes], kv_ref.at[i], sems.at[i]
        )
        copies[i].start()
        if i == 1:
            for copy in shared:
                copy.start()
    for copy in shared:
        copy.wait()
    for i, p, out_ref in (
        (1, 0, first_ref.at[0]),
        (1, 1, first_ref.at[1]),
        (0, 1, core_ref.at[0]),
        (3, 1, core_ref.at[1]),
    ):
        if p == 0 or i != 1:
            copies[i].wait()
        pack_one(place_ref, kv_ref, q_ref, taps_ref, i, p, out_ref)
    copies[2].wait()


def pack_second_kernel(place_ref, kv_ref, q_ref, taps_ref, second_ref, far_ref):
    for i, p, out_ref in (
        (2, 0, second_ref.at[0]),
        (2, 1, second_ref.at[1]),
        (3, 0, far_ref),
    ):
        pack_one(place_ref, kv_ref, q_ref, taps_ref, i, p, out_ref)


def pack_own_kernel(place_ref, kv_ref, q_ref, taps_ref, beside_ref, own_ref):
    pack_one(place_ref, kv_ref, q_ref, taps_ref, 0, 0, own_ref)


def spectrum_kernel(quarter, part, view_ref, beside_ref, out_ref):
    blocks = view_ref.shape[0] // (2 * LANES)
    per = quarter // LANES
    scale = 1.0 / (blocks * LANES)
    row = lax.broadcasted_iota(jnp.int32, (quarter + TILE, 2 * quarter), 0)
    col = lax.broadcasted_iota(jnp.int32, (quarter + TILE, 2 * quarter), 1)
    ahead = (col < quarter) & (row == col)
    back = (col >= quarter) & (row + col == 2 * quarter)
    turn = jnp.where(ahead | back, 1.0, 0.0).astype(jnp.bfloat16)

    def columns(part, start):
        return [
            view_ref[pl.ds(2 * (start + i) + part, LANES, stride=2 * blocks), :]
            for i in range(per)
        ]

    sign = 1.0 if part == 0 else -1.0
    heads, tails = [], []
    for m in range(4):
        start = 2 * per * m
        values = columns(part, start) + [sign * v for v in columns(part, blocks - start - per)]
        values = jnp.concatenate(values, axis=1)
        high = values.astype(jnp.bfloat16)
        low = (values - high.astype(jnp.float32)).astype(jnp.bfloat16)
        both = lax.dot_general(
            turn,
            jnp.concatenate([high, low], axis=0),
            (((1,), (1,)), ((), ())),
            preferred_element_type=jnp.float32,
        )
        folded = (both[: quarter + 8, :LANES] + both[: quarter + 8, LANES:]) * scale
        out_ref[m, :, :] = folded
        heads.append(folded[0:1])
        tails.append(folded[quarter : quarter + 1])
    for m in range(4):
        out_ref[m, 0:1, :] = 0.5 * (heads[m] + sign * heads[(4 - m) % 4])
        out_ref[m, quarter : quarter + 1, :] = 0.5 * (tails[m] + sign * tails[3 - m])


def forward_kernel(pair_ref, beside_ref, out_ref):
    out_ref[...] = pair_ref[1]


def merge_kernel(far_ref, core_ref, out_ref):
    out_ref[0] = far_ref[...]
    out_ref[1] = core_ref[1]


def received(place_ref, own, core, first, second, first_on, second_on, far):
    link = first_link(place_ref)
    blocks = [
        (0, own),
        (1, core.at[0]),
        (link, first.at[0]),
        (6 - link, second.at[0]),
        ((6 - link) ^ 1, first_on),
        (link ^ 1, second_on),
    ]
    if far is not None:
        blocks += [(6, far.at[0]), (7, far.at[1])]
    return blocks


def filter_kernel(
    place_ref,
    own_ref,
    core_ref,
    first_ref,
    second_ref,
    first_on_ref,
    second_on_ref,
    far_ref,
    taps_ref,
    real_ref,
    imag_ref,
    ahead_ref,
    back_ref,
    twist_ref,
    own_out,
    core_out,
    first_out,
    second_out,
    far_out,
    msg_ref,
    x_ref,
    z_ref,
    q_ref,
):
    shards = msg_ref.shape[0]
    rows = own_ref.shape[0] - 24
    quarter = back_ref.shape[0]
    blocks = received(
        place_ref,
        own_ref,
        core_ref,
        first_ref,
        second_ref,
        first_on_ref,
        second_on_ref,
        far_ref,
    )
    for k, block in blocks:
        msg_ref[place_ref[0] ^ k] = block[...]
    row = row_index(TILE)
    own = own_lanes(place_ref, 0)

    before = None
    for s in range(shards):
        top = msg_ref[s, :TILE, :].astype(jnp.float32)
        edge = msg_ref[s, rows : rows + TILE, :].astype(jnp.float32)
        half = msg_ref[s, rows + TILE :, :].astype(jnp.float32)
        if before is None:
            above_k = above_v = jnp.zeros_like(edge)
            halo = jnp.zeros_like(half)
        else:
            above_v, half_before = before
            above_k = jnp.concatenate([half_before, half_before], axis=0)
            halo = jnp.where(
                row_index(8) < 6,
                pltpu.roll(above_v, 12, 0)[:8],
                pltpu.roll(half_before, 6, 0),
            )
        k_conv = short_conv_rolled(
            jnp.where(row < 8, top, above_k), lambda j: taps_ref[1, j : j + 1, own]
        )
        v_conv = short_conv_rolled(
            jnp.where(row < 8, edge, above_v), lambda j: taps_ref[2, j : j + 1, own]
        )
        x_ref[s * rows : s * rows + TILE, :] = jnp.where(row < 6, rounded(k_conv * v_conv), top)
        x_ref[s * rows + TILE : (s + 1) * rows, :] = msg_ref[s, TILE:rows, :].astype(jnp.float32)
        msg_ref[s, rows : rows + 8, :] = halo.astype(jnp.bfloat16)
        before = (edge, half)

    x = jnp.concatenate(
        [x_ref[pl.ds(a, quarter, stride=4), :].astype(jnp.bfloat16) for a in range(4)], axis=1
    )
    x = jnp.concatenate([x, x], axis=0)

    def combine(real, imag, g, count):
        u = []
        for a in range(4):
            if a == 0:
                u.append((real[0], imag[0]))
                continue
            wr = jnp.broadcast_to(twist_ref[g : g + count, 2 * a : 2 * a + 1], (count, LANES))
            wi = jnp.broadcast_to(
                twist_ref[g : g + count, 2 * a + 1 : 2 * a + 2], (count, LANES)
            )
            u.append((real[a] * wr - imag[a] * wi, real[a] * wi + imag[a] * wr, wr, wi))

        def four(v, sign):
            er, ei = v[0][0] + v[2][0], v[0][1] + v[2][1]
            dr, di = v[0][0] - v[2][0], v[0][1] - v[2][1]
            pr, pi = v[1][0] + v[3][0], v[1][1] + v[3][1]
            qr, qi = v[1][0] - v[3][0], v[1][1] - v[3][1]
            if sign < 0:
                one, three = (dr + qi, di - qr), (dr - qi, di + qr)
            else:
                one, three = (dr - qi, di + qr), (dr + qi, di - qr)
            return [(er + pr, ei + pi), one, (er - pr, ei - pi), three]

        freq = four(u, -1)
        prod = []
        for m in range(4):
            hr = real_ref[m, g : g + count, :]
            hi = imag_ref[m, g : g + count, :]
            xr, xi = freq[m]
            prod.append((xr * hr - xi * hi, xr * hi + xi * hr))
        v = four(prod, 1)
        out = [v[0]]
        for a in range(1, 4):
            wr, wi = u[a][2], u[a][3]
            vr, vi = v[a]
            out.append((vr * wr + vi * wi, vi * wr - vr * wi))
        return out

    part = quarter // 2
    y = None
    for half in range(2):
        base = half * quarter
        count = quarter + half * TILE
        z_ref[base : base + count, :] = jnp.dot(
            ahead_ref[base : base + count, :], x, preferred_element_type=jnp.float32
        )
        for g in range(0, part, TILE):
            real, imag = [
                [
                    z_ref[start : start + TILE, a * LANES : (a + 1) * LANES]
                    for a in range(4)
                ]
                for start in (base + g, base + part + g)
            ]
            out = combine(real, imag, half * part + g, TILE)
            for a in range(4):
                lanes = slice(a * LANES, (a + 1) * LANES)
                for i in range(2):
                    start = base + i * part + g
                    q_ref[start : start + TILE, lanes] = out[a][i].astype(jnp.bfloat16)
        term = jnp.dot(
            back_ref[:, base : base + quarter],
            q_ref[base : base + quarter, :],
            preferred_element_type=jnp.float32,
        )
        y = term if y is None else y + term
    real = [z_ref[2 * quarter : 2 * quarter + 8, a * LANES : (a + 1) * LANES] for a in range(4)]
    last = combine(real, [jnp.zeros_like(r) for r in real], quarter, 8)

    sign = 1.0 - 2.0 * (row_index(quarter) % 2).astype(jnp.float32)
    for a in range(4):
        x_ref[pl.ds(a, quarter, stride=4), :] = (
            y[:, a * LANES : (a + 1) * LANES] + sign * last[a][0][0:1, :]
        )
    link = first_link(place_ref)
    for k, out_ref in (
        (link, first_out.at[0]),
        (link ^ 1, first_out.at[1]),
        (6 - link, second_out.at[0]),
        ((6 - link) ^ 1, second_out.at[1]),
        (6, far_out),
        (7, core_out.at[1]),
        (0, own_out),
        (1, core_out.at[0]),
    ):
        target = place_ref[0] ^ k
        start = pl.multiple_of(target * rows, rows)
        out_ref[:rows, :] = x_ref[pl.ds(start, rows), :].astype(jnp.bfloat16)
        out_ref[rows:, :] = msg_ref[target, rows : rows + 8, :]


def silu(values):
    return values / (1.0 + jnp.exp(-values))


def gain_kernel(q_ref, taps_ref, residual_ref, out_ref):
    for c in range(out_ref.shape[1] // LANES):
        lanes = slice(c * LANES, (c + 1) * LANES)
        conv = short_conv_rolled(
            q_ref[0, :, lanes].astype(jnp.float32), lambda j: taps_ref[0, j : j + 1, lanes]
        )
        out_ref[:, lanes] = silu(residual_ref[:, lanes].astype(jnp.float32)) * conv


def mixed_block(msg, lanes, gain_ref, residual_ref, q_ref, taps_ref, out_ref):
    rows = residual_ref.shape[0]
    row = row_index(TILE)
    halo = msg[rows:, :].astype(jnp.float32)
    window = jnp.where(
        row < 8, q_ref[0, :TILE, lanes].astype(jnp.float32), jnp.concatenate([halo, halo], axis=0)
    )
    conv = short_conv_rolled(window, lambda j: taps_ref[0, j : j + 1, lanes])
    resid = residual_ref[:TILE, lanes].astype(jnp.float32)
    gain = jnp.where(row < 6, silu(resid) * conv, gain_ref[:TILE, lanes])
    out_ref[:TILE, :] = (resid + gain * msg[:TILE, :].astype(jnp.float32)).astype(jnp.bfloat16)
    out_ref[TILE:, :] = (
        residual_ref[TILE:, lanes].astype(jnp.float32)
        + gain_ref[TILE:, lanes] * msg[TILE:rows, :].astype(jnp.float32)
    ).astype(jnp.bfloat16)


def mix_early_kernel(place_ref, own, core, first, second, first_on, *refs):
    rest, out_ref = refs[:4], refs[4]
    blocks = received(place_ref, own, core, first, second, first_on, None, None)
    for i, (k, block) in enumerate(blocks[:5]):
        mixed_block(block, own_lanes(place_ref, k), *rest, out_ref.at[i])


def mix_late_kernel(place_ref, early_ref, second_on, far_ref, *refs):
    rest, (out_ref, held, sems) = refs[:4], refs[4:]
    link = first_link(place_ref)
    order = (0, 1, link, 6 - link, (6 - link) ^ 1, link ^ 1, 6, 7)
    late = (second_on, far_ref.at[0], far_ref.at[1])
    copies = []
    for i, k in enumerate(order):
        lanes = own_lanes(place_ref, k)
        source = early_ref.at[i] if i < 5 else held.at[i - 5]
        if i >= 5:
            mixed_block(late[i - 5], lanes, *rest, source)
        copy = pltpu.make_async_copy(source, out_ref.at[:, lanes], sems.at[i])
        copy.start()
        copies.append(copy)
    for copy in copies:
        copy.wait()


def filter_tables(quarter):
    index = np.arange(quarter)
    angle = 2.0 * np.pi * (index[:, None] * index[None, :] % (2 * quarter)) / (2 * quarter)
    alternate = np.zeros((TILE, quarter))
    alternate[0] = 1.0 - 2.0 * (index % 2)
    part = quarter // 2
    cos, sin = np.cos(angle), -np.sin(angle)
    table = np.concatenate([cos[:part], sin[:part], cos[part:], sin[part:], alternate], axis=0)
    high = table.astype(jnp.bfloat16)
    low = (table - high.astype(np.float64)).astype(jnp.bfloat16)
    ahead = np.concatenate([high, low], axis=1)
    back = np.ascontiguousarray(high[: 2 * quarter].T)
    g = np.arange(quarter + 8)[:, None]
    a = np.arange(4)[None, :]
    turn = 2.0 * np.pi * (g * a) / (8 * quarter)
    twist = np.stack([np.cos(turn), -np.sin(turn)], axis=-1).reshape(quarter + 8, 8)
    return ahead, back, twist.astype(np.float32)


def estimate(flops, moved):
    return pl.CostEstimate(flops=flops, bytes_accessed=moved, transcendentals=0)


def swap(block, partner):
    return lax.ppermute(block, "seq", [(i, partner(i)) for i in range(8)])


def arranged(kernel, name, shape, *blocks, spaces=(pltpu.VMEM, pltpu.VMEM)):
    return pl.pallas_call(
        kernel,
        in_specs=[pl.BlockSpec(memory_space=space) for space in spaces],
        out_shape=jax.ShapeDtypeStruct(shape, jnp.bfloat16),
        compiler_params=pltpu.CompilerParams(vmem_limit_bytes=VMEM_LIMIT),
        cost_estimate=estimate(1 << 10, 1 << 16),
        name=name,
    )(*blocks)


def exchanged(core, first, second, far):
    core = swap(core, lambda i: i ^ 1)
    first = swap(first, lambda i: i ^ (2 + 2 * (i & 1)))
    second = swap(second, lambda i: i ^ (4 - 2 * (i & 1)))
    merged = arranged(merge_kernel, "merge", core.shape, far, core)
    return core, first, second, swap(merged, lambda i: i ^ 6), merged


def sibling_block(pair, beside):
    return arranged(
        forward_kernel, "forward", pair.shape[1:], pair, beside, spaces=(pltpu.VMEM, pl.ANY)
    )


def local_kernels(streams, short_taps, spectrum, residual):
    rows, channels = residual.shape
    shards = lax.axis_size("seq")
    length = rows * shards
    quarter = length // 4
    params = pltpu.CompilerParams(vmem_limit_bytes=VMEM_LIMIT)
    place = lax.axis_index("seq").astype(jnp.int32).reshape(1)
    scalar = pl.BlockSpec(memory_space=pltpu.SMEM)
    vector = pl.BlockSpec(memory_space=pltpu.VMEM)
    hbm = pl.BlockSpec(memory_space=pltpu.HBM)
    half = lambda *shape: jax.ShapeDtypeStruct(shape, jnp.bfloat16)
    full = lambda *shape: jax.ShapeDtypeStruct(shape, jnp.float32)
    sent = rows + 24
    core, first, kv, q_last, taps = pl.pallas_call(
        pack_first_kernel,
        in_specs=[scalar, hbm, hbm],
        out_shape=[
            half(2, sent, LANES),
            half(2, sent, LANES),
            half(4, 2, rows, 2 * LANES),
            half(TILE, channels),
            full(*short_taps.shape),
        ],
        scratch_shapes=[pltpu.SemaphoreType.DMA((6,))],
        compiler_params=params,
        cost_estimate=estimate(1 << 30, 1 << 20),
        name="pack_first",
    )(
        place,
        pltpu.with_memory_space_constraint(streams, pltpu.HBM),
        pltpu.with_memory_space_constraint(short_taps, pltpu.HBM),
    )
    second, far = pl.pallas_call(
        pack_second_kernel,
        in_specs=[scalar] + [vector] * 3,
        out_shape=[half(2, sent, LANES), half(sent, LANES)],
        compiler_params=params,
        cost_estimate=estimate(1 << 30, 1 << 20),
        name="pack_second",
    )(place, kv, q_last, taps)
    blocks = 2 * length // LANES
    view = jnp.transpose(spectrum.reshape(LANES, 2, blocks, LANES), (0, 2, 1, 3)).reshape(
        2 * blocks * LANES, LANES
    )
    core, first, second, far, merged = exchanged(core, first, second, far)

    def spectrum_part(part, beside):
        return pl.pallas_call(
            functools.partial(spectrum_kernel, quarter, part),
            in_specs=[vector, pl.BlockSpec(memory_space=pl.ANY)],
            out_shape=full(4, quarter + 8, LANES),
            compiler_params=params,
            cost_estimate=estimate(1 << (32 - 20 * part), 1 << 22),
            name="spectrum",
        )(view, beside)

    real = spectrum_part(0, merged)
    second_on = swap(sibling_block(second, real), lambda i: i ^ 1)
    first_on = sibling_block(first, real)
    imag = spectrum_part(1, second_on)
    own = pl.pallas_call(
        pack_own_kernel,
        in_specs=[scalar] + [vector] * 3 + [pl.BlockSpec(memory_space=pl.ANY)],
        out_shape=half(sent, LANES),
        compiler_params=params,
        cost_estimate=estimate(1 << 22, 1 << 20),
        name="pack_own",
    )(place, kv, q_last, taps, first_on)
    first_on = swap(first_on, lambda i: i ^ 1)
    ahead, back_table, twist = filter_tables(quarter)
    back = rows + 8
    own, *sent_back = pl.pallas_call(
        filter_kernel,
        in_specs=[scalar] + [vector] * 13,
        out_shape=[half(back, LANES)] + [half(2, back, LANES)] * 3 + [half(back, LANES)],
        scratch_shapes=[
            pltpu.VMEM((shards, sent, LANES), jnp.bfloat16),
            pltpu.VMEM((length, LANES), jnp.float32),
            pltpu.VMEM((2 * quarter + TILE, 4 * LANES), jnp.float32),
            pltpu.VMEM((2 * quarter, 4 * LANES), jnp.bfloat16),
        ],
        compiler_params=params,
        cost_estimate=estimate(1 << 30, 1 << 22),
        name="filter",
    )(
        place,
        own,
        core,
        first,
        second,
        first_on,
        second_on,
        far,
        taps,
        real,
        imag,
        ahead,
        back_table,
        twist,
    )
    whole = lambda *shape: pl.BlockSpec(shape, lambda i: (0,) * len(shape))
    gain = pl.pallas_call(
        gain_kernel,
        grid=(1,),
        in_specs=[
            whole(1, rows, channels),
            whole(*short_taps.shape),
            whole(rows, channels),
        ],
        out_specs=whole(rows, channels),
        out_shape=full(rows, channels),
        compiler_params=params,
        cost_estimate=estimate(1 << 32, 1 << 20),
        name="gain",
    )(streams, taps, residual)
    core, first, second, far, _ = exchanged(*sent_back)
    first_on, second_on = [
        swap(sibling_block(pair, gain), lambda i: i ^ 1) for pair in (first, second)
    ]
    rest = (gain, residual, streams, taps)
    early = pl.pallas_call(
        mix_early_kernel,
        in_specs=[scalar] + [vector] * 9,
        out_shape=half(5, rows, LANES),
        compiler_params=params,
        cost_estimate=estimate(1 << 20, 1 << 20),
        name="mix_early",
    )(place, own, core, first, second, first_on, *rest)
    return pl.pallas_call(
        mix_late_kernel,
        in_specs=[scalar] + [vector] * 7,
        out_specs=hbm,
        out_shape=half(rows, channels),
        scratch_shapes=[
            pltpu.VMEM((3, rows, LANES), jnp.bfloat16),
            pltpu.SemaphoreType.DMA((shards,)),
        ],
        compiler_params=params,
        cost_estimate=estimate(1 << 20, 1 << 20),
        name="mix_late",
    )(place, early, second_on, far, *rest)


def local(streams, short_taps, spectrum, residual):
    rows, channels = residual.shape
    shards = lax.axis_size("seq")
    length = rows * shards
    fits = (
        channels == shards * LANES
        and rows % TILE == 0
        and rows >= 2 * TILE
        and length % (4 * LANES) == 0
        and length <= 2048
        and short_taps.shape[1] == 7
        and shards == 8
    )
    if fits:
        return local_kernels(streams, short_taps, spectrum, residual)
    return local_general(streams, short_taps, spectrum, residual)


def solution(mesh):
    placed = (
        P(None, "seq", "chan"),
        P(None, None, "chan"),
        P(("chan", "seq"), None, None),
        P("seq", "chan"),
    )
    return jax.shard_map(
        local, mesh=mesh, in_specs=placed, out_specs=P("seq", "chan"), check_vma=False
    )
```

```python
import functools
import math

import jax
import jax.numpy as jnp
import numpy as np
from jax import lax
from jax.experimental import pallas as pl
from jax.experimental.pallas import tpu as pltpu
from jax.sharding import PartitionSpec as P

LANES = 128
TILE = 16
VMEM_LIMIT = 16 * 1024 * 1024


def passed_along(block, axis, distance):
    devices = range(lax.axis_size(axis))
    route = [(i - distance, i) for i in devices if i - distance in devices]
    return lax.ppermute(block, axis, route)


def section_sizes(length_all):
    power = length_all.bit_length() - 1
    first = (power + 2) // 3
    second = (power - first + 1) // 2
    third = power - first - second
    result = [2**first, 2**second]
    result.append(2**third)
    return result


def matmul_high(left, right):
    return jnp.dot(left, right, precision=lax.Precision.HIGHEST, preferred_element_type=jnp.float32)


def section_high(table, values):
    return jnp.einsum(
        "ka,cab->ckb",
        table,
        values,
        precision=lax.Precision.HIGHEST,
        preferred_element_type=jnp.float32,
    )


def dft_table(order, direction):
    index = jnp.arange(order, dtype=jnp.int32)
    product = index[:, None] * index[None, :] % order
    angle = direction * 2.0 * math.pi * product.astype(jnp.float32) / order
    return (jnp.cos(angle), jnp.sin(angle))


def transform(real_part, imag_part, factors, direction):
    columns, length_now = real_part.shape
    first = factors[0]
    table_cos, table_sin = dft_table(first, direction)
    if len(factors) == 1:
        real_out = matmul_high(real_part, table_cos) - matmul_high(imag_part, table_sin)
        imag_out = matmul_high(imag_part, table_cos) + matmul_high(real_part, table_sin)
        return (real_out, imag_out)
    rest = length_now // first
    real_wide = real_part.reshape(columns, first, rest)
    if imag_part is None:
        section_real = section_high(table_cos, real_wide)
        section_imag = section_high(table_sin, real_wide)
    else:
        imag_wide = imag_part.reshape(columns, first, rest)
        section_real = section_high(table_cos, real_wide) - section_high(table_sin, imag_wide)
        section_imag = section_high(table_cos, imag_wide) + section_high(table_sin, real_wide)
    outer = jnp.arange(first, dtype=jnp.int32)[:, None]
    inner = jnp.arange(rest, dtype=jnp.int32)[None, :]
    twist = (
        direction * 2.0 * math.pi * (outer * inner % length_now).astype(jnp.float32) / length_now
    )
    twist_cos = jnp.cos(twist)[None, :, :]
    twist_sin = jnp.sin(twist)[None, :, :]
    turned_real = (section_real * twist_cos - section_imag * twist_sin).reshape(
        columns * first, rest
    )
    turned_imag = (section_real * twist_sin + section_imag * twist_cos).reshape(
        columns * first, rest
    )
    real_out, imag_out = transform(turned_real, turned_imag, factors[1:], direction)
    real_out = jnp.transpose(real_out.reshape(columns, first, rest), (0, 2, 1)).reshape(
        columns, length_now
    )
    imag_out = jnp.transpose(imag_out.reshape(columns, first, rest), (0, 2, 1)).reshape(
        columns, length_now
    )
    return (real_out, imag_out)


def long_filter(gated_rows, spectrum):
    columns, length_all = gated_rows.shape
    padded = jnp.concatenate(
        [gated_rows.astype(jnp.float32), jnp.zeros((columns, length_all), jnp.float32)], axis=1
    )
    factors = section_sizes(2 * length_all)
    freq_real, freq_imag = transform(padded, None, factors, -1.0)
    spec_real = spectrum[:, 0, :]
    spec_imag = spectrum[:, 1, :]
    prod_real = freq_real * spec_real - freq_imag * spec_imag
    prod_imag = freq_real * spec_imag + freq_imag * spec_real
    back_real, back_imag = transform(prod_real, prod_imag, factors, 1.0)
    return (back_real[:, :length_all] / (2 * length_all)).astype(jnp.bfloat16)


def local_general(streams, short_taps, spectrum, residual):
    row_count = streams.shape[1]
    channels = streams.shape[2]
    span = short_taps.shape[1] - 1
    rim_rows = passed_along(streams[:, row_count - span :, :], "seq", 1)
    extended = jnp.concatenate([rim_rows, streams], axis=1)
    total = jnp.zeros((3, row_count, channels), jnp.float32)
    for offset in range(span + 1):
        total = total + short_taps[:, offset, None, :] * extended[
            :, span - offset : span - offset + row_count, :
        ].astype(jnp.float32)
    convolved = total.astype(jnp.bfloat16)
    q_conv = convolved[0]
    k_conv = convolved[1]
    v_conv = convolved[2]
    seq_devices = lax.axis_size("seq")
    owned_count = channels // seq_devices
    length_all = row_count * seq_devices
    gated = (k_conv.astype(jnp.float32) * v_conv.astype(jnp.float32)).astype(jnp.bfloat16)
    owned = lax.all_to_all(
        gated.reshape(row_count, seq_devices, owned_count),
        "seq",
        split_axis=1,
        concat_axis=0,
        tiled=True,
    )
    gated_whole = owned.reshape(length_all, owned_count)
    filtered = jnp.transpose(long_filter(jnp.transpose(gated_whole), spectrum))
    returned = lax.all_to_all(
        filtered.reshape(length_all, 1, owned_count), "seq", split_axis=0, concat_axis=1, tiled=True
    )
    filtered_local = returned.reshape(row_count, channels)
    resid = residual.astype(jnp.float32)
    mixed = resid + jax.nn.silu(resid) * q_conv.astype(jnp.float32) * filtered_local.astype(
        jnp.float32
    )
    return mixed.astype(jnp.bfloat16)


def rounded(values):
    return values.astype(jnp.bfloat16).astype(jnp.float32)


def short_conv_rolled(rows, taps):
    later = pltpu.roll(rows, 1, 0)
    pairs = [taps(2 * i) * rows + taps(2 * i + 1) * later for i in range(3)]
    pairs.append(taps(6) * rows)
    low = pairs[0] + pltpu.roll(pairs[1], 2, 0)
    high = pairs[2] + pltpu.roll(pairs[3], 2, 0)
    return rounded(low + pltpu.roll(high, 4, 0))


def row_index(count):
    return lax.broadcasted_iota(jnp.int32, (count, LANES), 0)


def own_lanes(place_ref, k):
    return pl.ds(pl.multiple_of((place_ref[0] ^ k) * LANES, LANES), LANES)


def first_link(place_ref):
    return 2 + 2 * (place_ref[0] & 1)


def pack_block(k, v, q_last, taps, out_ref):
    rows = k.shape[0]
    row = row_index(TILE)
    gated = short_conv_rolled(k, lambda j: taps(1, j)) * short_conv_rolled(
        v, lambda j: taps(2, j)
    )
    out_ref[:TILE, :] = jnp.where(row < 6, k[:TILE], gated[:TILE]).astype(jnp.bfloat16)
    out_ref[TILE:rows, :] = gated[TILE:].astype(jnp.bfloat16)
    edge = jnp.where(row < 6, v[:TILE], v[rows - TILE :])
    edge = jnp.where((row >= 6) & (row < 10), pltpu.roll(q_last, 12, 0), edge)
    out_ref[rows : rows + TILE, :] = edge.astype(jnp.bfloat16)
    half = jnp.where(row_index(8) < 2, pltpu.roll(q_last[8:], 2, 0), k[rows - 8 :])
    out_ref[rows + TILE :, :] = half.astype(jnp.bfloat16)


def chip_order(place_ref):
    first = first_link(place_ref)
    return (0, first, 6 - first, 6)


def pack_one(place_ref, kv_ref, q_ref, taps_ref, chip, p, out_ref):
    lanes = pl.ds(pl.multiple_of(((place_ref[0] & 1) ^ p) * LANES, LANES), LANES)
    owner = own_lanes(place_ref, chip_order(place_ref)[chip] ^ p)
    pack_block(
        kv_ref[chip, 0, :, lanes].astype(jnp.float32),
        kv_ref[chip, 1, :, lanes].astype(jnp.float32),
        q_ref[:, owner].astype(jnp.float32),
        lambda s, j: taps_ref[s, j : j + 1, owner],
        out_ref,
    )


def pack_first_kernel(
    place_ref, streams_ref, taps_hbm_ref, core_ref, first_ref, kv_ref, q_ref, taps_ref, sems
):
    rows = streams_ref.shape[1]
    order = chip_order(place_ref)
    shared = [
        pltpu.make_async_copy(taps_hbm_ref, taps_ref, sems.at[4]),
        pltpu.make_async_copy(
            streams_ref.at[0, pl.ds(rows - TILE, TILE), :], q_ref, sems.at[5]
        ),
    ]
    copies = {}
    for i in (1, 0, 3, 2):
        chip = (place_ref[0] ^ order[i]) >> 1
        lanes = pl.ds(pl.multiple_of(chip * (2 * LANES), 2 * LANES), 2 * LANES)
        copies[i] = pltpu.make_async_copy(
            streams_ref.at[pl.ds(1, 2), :, lanes], kv_ref.at[i], sems.at[i]
        )
        copies[i].start()
        if i == 1:
            for copy in shared:
                copy.start()
    for copy in shared:
        copy.wait()
    for i, p, out_ref in (
        (1, 0, first_ref.at[0]),
        (1, 1, first_ref.at[1]),
        (0, 1, core_ref.at[0]),
        (3, 1, core_ref.at[1]),
    ):
        if p == 0 or i != 1:
            copies[i].wait()
        pack_one(place_ref, kv_ref, q_ref, taps_ref, i, p, out_ref)
    copies[2].wait()


def pack_second_kernel(place_ref, kv_ref, q_ref, taps_ref, second_ref, far_ref):
    for i, p, out_ref in (
        (2, 0, second_ref.at[0]),
        (2, 1, second_ref.at[1]),
        (3, 0, far_ref),
    ):
        pack_one(place_ref, kv_ref, q_ref, taps_ref, i, p, out_ref)


def pack_own_kernel(place_ref, kv_ref, q_ref, taps_ref, beside_ref, own_ref):
    pack_one(place_ref, kv_ref, q_ref, taps_ref, 0, 0, own_ref)


def spectrum_kernel(quarter, part, view_ref, beside_ref, out_ref):
    blocks = view_ref.shape[0] // (2 * LANES)
    per = quarter // LANES
    scale = 1.0 / (blocks * LANES)
    row = lax.broadcasted_iota(jnp.int32, (quarter + TILE, 2 * quarter), 0)
    col = lax.broadcasted_iota(jnp.int32, (quarter + TILE, 2 * quarter), 1)
    ahead = (col < quarter) & (row == col)
    back = (col >= quarter) & (row + col == 2 * quarter)
    turn = jnp.where(ahead | back, 1.0, 0.0).astype(jnp.bfloat16)

    def columns(part, start):
        return [
            view_ref[pl.ds(2 * (start + i) + part, LANES, stride=2 * blocks), :]
            for i in range(per)
        ]

    sign = 1.0 if part == 0 else -1.0
    heads, tails = [], []
    for m in range(4):
        start = 2 * per * m
        values = columns(part, start) + [sign * v for v in columns(part, blocks - start - per)]
        values = jnp.concatenate(values, axis=1)
        high = values.astype(jnp.bfloat16)
        low = (values - high.astype(jnp.float32)).astype(jnp.bfloat16)
        both = lax.dot_general(
            turn,
            jnp.concatenate([high, low], axis=0),
            (((1,), (1,)), ((), ())),
            preferred_element_type=jnp.float32,
        )
        folded = (both[: quarter + 8, :LANES] + both[: quarter + 8, LANES:]) * scale
        out_ref[m, :, :] = folded
        heads.append(folded[0:1])
        tails.append(folded[quarter : quarter + 1])
    for m in range(4):
        out_ref[m, 0:1, :] = 0.5 * (heads[m] + sign * heads[(4 - m) % 4])
        out_ref[m, quarter : quarter + 1, :] = 0.5 * (tails[m] + sign * tails[3 - m])


def forward_kernel(pair_ref, beside_ref, out_ref):
    out_ref[...] = pair_ref[1]


def merge_kernel(far_ref, core_ref, out_ref):
    out_ref[0] = far_ref[...]
    out_ref[1] = core_ref[1]


def received(place_ref, own, core, first, second, first_on, second_on, far):
    link = first_link(place_ref)
    blocks = [
        (0, own),
        (1, core.at[0]),
        (link, first.at[0]),
        (6 - link, second.at[0]),
        ((6 - link) ^ 1, first_on),
        (link ^ 1, second_on),
    ]
    if far is not None:
        blocks += [(6, far.at[0]), (7, far.at[1])]
    return blocks


def filter_kernel(
    place_ref,
    own_ref,
    core_ref,
    first_ref,
    second_ref,
    first_on_ref,
    second_on_ref,
    far_ref,
    taps_ref,
    real_ref,
    imag_ref,
    ahead_ref,
    back_ref,
    twist_ref,
    own_out,
    core_out,
    first_out,
    second_out,
    far_out,
    msg_ref,
    x_ref,
    z_ref,
    q_ref,
):
    shards = msg_ref.shape[0]
    rows = own_ref.shape[0] - 24
    quarter = back_ref.shape[0]
    blocks = received(
        place_ref,
        own_ref,
        core_ref,
        first_ref,
        second_ref,
        first_on_ref,
        second_on_ref,
        far_ref,
    )
    for k, block in blocks:
        msg_ref[place_ref[0] ^ k] = block[...]
    row = row_index(TILE)
    own = own_lanes(place_ref, 0)

    before = None
    for s in range(shards):
        top = msg_ref[s, :TILE, :].astype(jnp.float32)
        edge = msg_ref[s, rows : rows + TILE, :].astype(jnp.float32)
        half = msg_ref[s, rows + TILE :, :].astype(jnp.float32)
        if before is None:
            above_k = above_v = jnp.zeros_like(edge)
            halo = jnp.zeros_like(half)
        else:
            above_v, half_before = before
            above_k = jnp.concatenate([half_before, half_before], axis=0)
            halo = jnp.where(
                row_index(8) < 6,
                pltpu.roll(above_v, 12, 0)[:8],
                pltpu.roll(half_before, 6, 0),
            )
        k_conv = short_conv_rolled(
            jnp.where(row < 8, top, above_k), lambda j: taps_ref[1, j : j + 1, own]
        )
        v_conv = short_conv_rolled(
            jnp.where(row < 8, edge, above_v), lambda j: taps_ref[2, j : j + 1, own]
        )
        x_ref[s * rows : s * rows + TILE, :] = jnp.where(row < 6, rounded(k_conv * v_conv), top)
        x_ref[s * rows + TILE : (s + 1) * rows, :] = msg_ref[s, TILE:rows, :].astype(jnp.float32)
        msg_ref[s, rows : rows + 8, :] = halo.astype(jnp.bfloat16)
        before = (edge, half)

    x = jnp.concatenate(
        [x_ref[pl.ds(a, quarter, stride=4), :].astype(jnp.bfloat16) for a in range(4)], axis=1
    )
    x = jnp.concatenate([x, x], axis=0)

    def combine(real, imag, g, count):
        u = []
        for a in range(4):
            if a == 0:
                u.append((real[0], imag[0]))
                continue
            wr = jnp.broadcast_to(twist_ref[g : g + count, 2 * a : 2 * a + 1], (count, LANES))
            wi = jnp.broadcast_to(
                twist_ref[g : g + count, 2 * a + 1 : 2 * a + 2], (count, LANES)
            )
            u.append((real[a] * wr - imag[a] * wi, real[a] * wi + imag[a] * wr, wr, wi))

        def four(v, sign):
            er, ei = v[0][0] + v[2][0], v[0][1] + v[2][1]
            dr, di = v[0][0] - v[2][0], v[0][1] - v[2][1]
            pr, pi = v[1][0] + v[3][0], v[1][1] + v[3][1]
            qr, qi = v[1][0] - v[3][0], v[1][1] - v[3][1]
            if sign < 0:
                one, three = (dr + qi, di - qr), (dr - qi, di + qr)
            else:
                one, three = (dr - qi, di + qr), (dr + qi, di - qr)
            return [(er + pr, ei + pi), one, (er - pr, ei - pi), three]

        freq = four(u, -1)
        prod = []
        for m in range(4):
            hr = real_ref[m, g : g + count, :]
            hi = imag_ref[m, g : g + count, :]
            xr, xi = freq[m]
            prod.append((xr * hr - xi * hi, xr * hi + xi * hr))
        v = four(prod, 1)
        out = [v[0]]
        for a in range(1, 4):
            wr, wi = u[a][2], u[a][3]
            vr, vi = v[a]
            out.append((vr * wr + vi * wi, vi * wr - vr * wi))
        return out

    part = quarter // 2
    y = None
    for half in range(2):
        base = half * quarter
        count = quarter + half * TILE
        z_ref[base : base + count, :] = jnp.dot(
            ahead_ref[base : base + count, :], x, preferred_element_type=jnp.float32
        )
        for g in range(0, part, TILE):
            real, imag = [
                [
                    z_ref[start : start + TILE, a * LANES : (a + 1) * LANES]
                    for a in range(4)
                ]
                for start in (base + g, base + part + g)
            ]
            out = combine(real, imag, half * part + g, TILE)
            for a in range(4):
                lanes = slice(a * LANES, (a + 1) * LANES)
                for i in range(2):
                    start = base + i * part + g
                    q_ref[start : start + TILE, lanes] = out[a][i].astype(jnp.bfloat16)
        term = jnp.dot(
            back_ref[:, base : base + quarter],
            q_ref[base : base + quarter, :],
            preferred_element_type=jnp.float32,
        )
        y = term if y is None else y + term
    real = [z_ref[2 * quarter : 2 * quarter + 8, a * LANES : (a + 1) * LANES] for a in range(4)]
    last = combine(real, [jnp.zeros_like(r) for r in real], quarter, 8)

    sign = 1.0 - 2.0 * (row_index(quarter) % 2).astype(jnp.float32)
    for a in range(4):
        x_ref[pl.ds(a, quarter, stride=4), :] = (
            y[:, a * LANES : (a + 1) * LANES] + sign * last[a][0][0:1, :]
        )
    link = first_link(place_ref)
    for k, out_ref in (
        (link, first_out.at[0]),
        (link ^ 1, first_out.at[1]),
        (6 - link, second_out.at[0]),
        ((6 - link) ^ 1, second_out.at[1]),
        (6, far_out),
        (7, core_out.at[1]),
        (0, own_out),
        (1, core_out.at[0]),
    ):
        target = place_ref[0] ^ k
        start = pl.multiple_of(target * rows, rows)
        out_ref[:rows, :] = x_ref[pl.ds(start, rows), :].astype(jnp.bfloat16)
        out_ref[rows:, :] = msg_ref[target, rows : rows + 8, :]


def silu(values):
    return values / (1.0 + jnp.exp(-values))


def gain_kernel(q_ref, taps_ref, residual_ref, out_ref):
    for c in range(out_ref.shape[1] // LANES):
        lanes = slice(c * LANES, (c + 1) * LANES)
        conv = short_conv_rolled(
            q_ref[0, :, lanes].astype(jnp.float32), lambda j: taps_ref[0, j : j + 1, lanes]
        )
        out_ref[:, lanes] = silu(residual_ref[:, lanes].astype(jnp.float32)) * conv


def mixed_block(msg, lanes, gain_ref, residual_ref, q_ref, taps_ref, out_ref):
    rows = residual_ref.shape[0]
    row = row_index(TILE)
    halo = msg[rows:, :].astype(jnp.float32)
    window = jnp.where(
        row < 8, q_ref[0, :TILE, lanes].astype(jnp.float32), jnp.concatenate([halo, halo], axis=0)
    )
    conv = short_conv_rolled(window, lambda j: taps_ref[0, j : j + 1, lanes])
    resid = residual_ref[:TILE, lanes].astype(jnp.float32)
    gain = jnp.where(row < 6, silu(resid) * conv, gain_ref[:TILE, lanes])
    out_ref[:TILE, :] = (resid + gain * msg[:TILE, :].astype(jnp.float32)).astype(jnp.bfloat16)
    out_ref[TILE:, :] = (
        residual_ref[TILE:, lanes].astype(jnp.float32)
        + gain_ref[TILE:, lanes] * msg[TILE:rows, :].astype(jnp.float32)
    ).astype(jnp.bfloat16)


def mix_early_kernel(place_ref, own, core, first, second, first_on, *refs):
    rest, out_ref = refs[:4], refs[4]
    blocks = received(place_ref, own, core, first, second, first_on, None, None)
    for i, (k, block) in enumerate(blocks[:5]):
        mixed_block(block, own_lanes(place_ref, k), *rest, out_ref.at[i])


def mix_late_kernel(place_ref, early_ref, second_on, far_ref, *refs):
    rest, (out_ref, held, sems) = refs[:4], refs[4:]
    link = first_link(place_ref)
    order = (0, 1, link, 6 - link, (6 - link) ^ 1, link ^ 1, 6, 7)
    late = (second_on, far_ref.at[0], far_ref.at[1])
    copies = []
    for i, k in enumerate(order):
        lanes = own_lanes(place_ref, k)
        source = early_ref.at[i] if i < 5 else held.at[i - 5]
        if i >= 5:
            mixed_block(late[i - 5], lanes, *rest, source)
        copy = pltpu.make_async_copy(source, out_ref.at[:, lanes], sems.at[i])
        copy.start()
        copies.append(copy)
    for copy in copies:
        copy.wait()


def filter_tables(quarter):
    index = np.arange(quarter)
    angle = 2.0 * np.pi * (index[:, None] * index[None, :] % (2 * quarter)) / (2 * quarter)
    alternate = np.zeros((TILE, quarter))
    alternate[0] = 1.0 - 2.0 * (index % 2)
    part = quarter // 2
    cos, sin = np.cos(angle), -np.sin(angle)
    table = np.concatenate([cos[:part], sin[:part], cos[part:], sin[part:], alternate], axis=0)
    high = table.astype(jnp.bfloat16)
    low = (table - high.astype(np.float64)).astype(jnp.bfloat16)
    ahead = np.concatenate([high, low], axis=1)
    back = np.ascontiguousarray(high[: 2 * quarter].T)
    g = np.arange(quarter + 8)[:, None]
    a = np.arange(4)[None, :]
    turn = 2.0 * np.pi * (g * a) / (8 * quarter)
    twist = np.stack([np.cos(turn), -np.sin(turn)], axis=-1).reshape(quarter + 8, 8)
    return ahead, back, twist.astype(np.float32)


def estimate(flops, moved):
    return pl.CostEstimate(flops=flops, bytes_accessed=moved, transcendentals=0)


def swap(block, partner):
    return lax.ppermute(block, "seq", [(i, partner(i)) for i in range(8)])


def arranged(kernel, name, shape, *blocks, spaces=(pltpu.VMEM, pltpu.VMEM)):
    return pl.pallas_call(
        kernel,
        in_specs=[pl.BlockSpec(memory_space=space) for space in spaces],
        out_shape=jax.ShapeDtypeStruct(shape, jnp.bfloat16),
        compiler_params=pltpu.CompilerParams(vmem_limit_bytes=VMEM_LIMIT),
        cost_estimate=estimate(1 << 10, 1 << 16),
        name=name,
    )(*blocks)


def exchanged(core, first, second, far):
    core = swap(core, lambda i: i ^ 1)
    first = swap(first, lambda i: i ^ (2 + 2 * (i & 1)))
    second = swap(second, lambda i: i ^ (4 - 2 * (i & 1)))
    merged = arranged(merge_kernel, "merge", core.shape, far, core)
    return core, first, second, swap(merged, lambda i: i ^ 6), merged


def sibling_block(pair, beside):
    return arranged(
        forward_kernel, "forward", pair.shape[1:], pair, beside, spaces=(pltpu.VMEM, pl.ANY)
    )


def local_kernels(streams, short_taps, spectrum, residual):
    rows, channels = residual.shape
    shards = lax.axis_size("seq")
    length = rows * shards
    quarter = length // 4
    params = pltpu.CompilerParams(vmem_limit_bytes=VMEM_LIMIT)
    place = lax.axis_index("seq").astype(jnp.int32).reshape(1)
    scalar = pl.BlockSpec(memory_space=pltpu.SMEM)
    vector = pl.BlockSpec(memory_space=pltpu.VMEM)
    hbm = pl.BlockSpec(memory_space=pltpu.HBM)
    half = lambda *shape: jax.ShapeDtypeStruct(shape, jnp.bfloat16)
    full = lambda *shape: jax.ShapeDtypeStruct(shape, jnp.float32)
    sent = rows + 24
    core, first, kv, q_last, taps = pl.pallas_call(
        pack_first_kernel,
        in_specs=[scalar, hbm, hbm],
        out_shape=[
            half(2, sent, LANES),
            half(2, sent, LANES),
            half(4, 2, rows, 2 * LANES),
            half(TILE, channels),
            full(*short_taps.shape),
        ],
        scratch_shapes=[pltpu.SemaphoreType.DMA((6,))],
        compiler_params=params,
        cost_estimate=estimate(1 << 30, 1 << 20),
        name="pack_first",
    )(
        place,
        pltpu.with_memory_space_constraint(streams, pltpu.HBM),
        pltpu.with_memory_space_constraint(short_taps, pltpu.HBM),
    )
    second, far = pl.pallas_call(
        pack_second_kernel,
        in_specs=[scalar] + [vector] * 3,
        out_shape=[half(2, sent, LANES), half(sent, LANES)],
        compiler_params=params,
        cost_estimate=estimate(1 << 30, 1 << 20),
        name="pack_second",
    )(place, kv, q_last, taps)
    blocks = 2 * length // LANES
    view = jnp.transpose(spectrum.reshape(LANES, 2, blocks, LANES), (0, 2, 1, 3)).reshape(
        2 * blocks * LANES, LANES
    )
    core, first, second, far, merged = exchanged(core, first, second, far)

    def spectrum_part(part, beside):
        return pl.pallas_call(
            functools.partial(spectrum_kernel, quarter, part),
            in_specs=[vector, pl.BlockSpec(memory_space=pl.ANY)],
            out_shape=full(4, quarter + 8, LANES),
            compiler_params=params,
            cost_estimate=estimate(1 << (32 - 20 * part), 1 << 22),
            name="spectrum",
        )(view, beside)

    real = spectrum_part(0, merged)
    first_block = sibling_block(first, real)
    first_on = swap(first_block, lambda i: i ^ 1)
    second_on = swap(sibling_block(second, real), lambda i: i ^ 1)
    imag = spectrum_part(1, first_on)
    own = pl.pallas_call(
        pack_own_kernel,
        in_specs=[scalar] + [vector] * 3 + [pl.BlockSpec(memory_space=pl.ANY)],
        out_shape=half(sent, LANES),
        compiler_params=params,
        cost_estimate=estimate(1 << 22, 1 << 20),
        name="pack_own",
    )(place, kv, q_last, taps, first_block)
    ahead, back_table, twist = filter_tables(quarter)
    back = rows + 8
    own, *sent_back = pl.pallas_call(
        filter_kernel,
        in_specs=[scalar] + [vector] * 13,
        out_shape=[half(back, LANES)] + [half(2, back, LANES)] * 3 + [half(back, LANES)],
        scratch_shapes=[
            pltpu.VMEM((shards, sent, LANES), jnp.bfloat16),
            pltpu.VMEM((length, LANES), jnp.float32),
            pltpu.VMEM((2 * quarter + TILE, 4 * LANES), jnp.float32),
            pltpu.VMEM((2 * quarter, 4 * LANES), jnp.bfloat16),
        ],
        compiler_params=params,
        cost_estimate=estimate(1 << 30, 1 << 22),
        name="filter",
    )(
        place,
        own,
        core,
        first,
        second,
        first_on,
        second_on,
        far,
        taps,
        real,
        imag,
        ahead,
        back_table,
        twist,
    )
    whole = lambda *shape: pl.BlockSpec(shape, lambda i: (0,) * len(shape))
    gain = pl.pallas_call(
        gain_kernel,
        grid=(1,),
        in_specs=[
            whole(1, rows, channels),
            whole(*short_taps.shape),
            whole(rows, channels),
        ],
        out_specs=whole(rows, channels),
        out_shape=full(rows, channels),
        compiler_params=params,
        cost_estimate=estimate(1 << 32, 1 << 20),
        name="gain",
    )(streams, taps, residual)
    core, first, second, far, _ = exchanged(*sent_back)
    first_on, second_on = [
        swap(sibling_block(pair, gain), lambda i: i ^ 1) for pair in (first, second)
    ]
    rest = (gain, residual, streams, taps)
    early = pl.pallas_call(
        mix_early_kernel,
        in_specs=[scalar] + [vector] * 9,
        out_shape=half(5, rows, LANES),
        compiler_params=params,
        cost_estimate=estimate(1 << 20, 1 << 20),
        name="mix_early",
    )(place, own, core, first, second, first_on, *rest)
    return pl.pallas_call(
        mix_late_kernel,
        in_specs=[scalar] + [vector] * 7,
        out_specs=hbm,
        out_shape=half(rows, channels),
        scratch_shapes=[
            pltpu.VMEM((3, rows, LANES), jnp.bfloat16),
            pltpu.SemaphoreType.DMA((shards,)),
        ],
        compiler_params=params,
        cost_estimate=estimate(1 << 20, 1 << 20),
        name="mix_late",
    )(place, early, second_on, far, *rest)


def local(streams, short_taps, spectrum, residual):
    rows, channels = residual.shape
    shards = lax.axis_size("seq")
    length = rows * shards
    fits = (
        channels == shards * LANES
        and rows % TILE == 0
        and rows >= 2 * TILE
        and length % (4 * LANES) == 0
        and length <= 2048
        and short_taps.shape[1] == 7
        and shards == 8
    )
    if fits:
        return local_kernels(streams, short_taps, spectrum, residual)
    return local_general(streams, short_taps, spectrum, residual)


def solution(mesh):
    placed = (
        P(None, "seq", "chan"),
        P(None, None, "chan"),
        P(("chan", "seq"), None, None),
        P("seq", "chan"),
    )
    return jax.shard_map(
        local, mesh=mesh, in_specs=placed, out_specs=P("seq", "chan"), check_vma=False
    )
```

```python
import functools
import math

import jax
import jax.numpy as jnp
import numpy as np
from jax import lax
from jax.experimental import pallas as pl
from jax.experimental.pallas import tpu as pltpu
from jax.sharding import PartitionSpec as P

LANES = 128
TILE = 16
VMEM_LIMIT = 16 * 1024 * 1024


def passed_along(block, axis, distance):
    devices = range(lax.axis_size(axis))
    route = [(i - distance, i) for i in devices if i - distance in devices]
    return lax.ppermute(block, axis, route)


def section_sizes(length_all):
    power = length_all.bit_length() - 1
    first = (power + 2) // 3
    second = (power - first + 1) // 2
    third = power - first - second
    result = [2**first, 2**second]
    result.append(2**third)
    return result


def matmul_high(left, right):
    return jnp.dot(left, right, precision=lax.Precision.HIGHEST, preferred_element_type=jnp.float32)


def section_high(table, values):
    return jnp.einsum(
        "ka,cab->ckb",
        table,
        values,
        precision=lax.Precision.HIGHEST,
        preferred_element_type=jnp.float32,
    )


def dft_table(order, direction):
    index = jnp.arange(order, dtype=jnp.int32)
    product = index[:, None] * index[None, :] % order
    angle = direction * 2.0 * math.pi * product.astype(jnp.float32) / order
    return (jnp.cos(angle), jnp.sin(angle))


def transform(real_part, imag_part, factors, direction):
    columns, length_now = real_part.shape
    first = factors[0]
    table_cos, table_sin = dft_table(first, direction)
    if len(factors) == 1:
        real_out = matmul_high(real_part, table_cos) - matmul_high(imag_part, table_sin)
        imag_out = matmul_high(imag_part, table_cos) + matmul_high(real_part, table_sin)
        return (real_out, imag_out)
    rest = length_now // first
    real_wide = real_part.reshape(columns, first, rest)
    if imag_part is None:
        section_real = section_high(table_cos, real_wide)
        section_imag = section_high(table_sin, real_wide)
    else:
        imag_wide = imag_part.reshape(columns, first, rest)
        section_real = section_high(table_cos, real_wide) - section_high(table_sin, imag_wide)
        section_imag = section_high(table_cos, imag_wide) + section_high(table_sin, real_wide)
    outer = jnp.arange(first, dtype=jnp.int32)[:, None]
    inner = jnp.arange(rest, dtype=jnp.int32)[None, :]
    twist = (
        direction * 2.0 * math.pi * (outer * inner % length_now).astype(jnp.float32) / length_now
    )
    twist_cos = jnp.cos(twist)[None, :, :]
    twist_sin = jnp.sin(twist)[None, :, :]
    turned_real = (section_real * twist_cos - section_imag * twist_sin).reshape(
        columns * first, rest
    )
    turned_imag = (section_real * twist_sin + section_imag * twist_cos).reshape(
        columns * first, rest
    )
    real_out, imag_out = transform(turned_real, turned_imag, factors[1:], direction)
    real_out = jnp.transpose(real_out.reshape(columns, first, rest), (0, 2, 1)).reshape(
        columns, length_now
    )
    imag_out = jnp.transpose(imag_out.reshape(columns, first, rest), (0, 2, 1)).reshape(
        columns, length_now
    )
    return (real_out, imag_out)


def long_filter(gated_rows, spectrum):
    columns, length_all = gated_rows.shape
    padded = jnp.concatenate(
        [gated_rows.astype(jnp.float32), jnp.zeros((columns, length_all), jnp.float32)], axis=1
    )
    factors = section_sizes(2 * length_all)
    freq_real, freq_imag = transform(padded, None, factors, -1.0)
    spec_real = spectrum[:, 0, :]
    spec_imag = spectrum[:, 1, :]
    prod_real = freq_real * spec_real - freq_imag * spec_imag
    prod_imag = freq_real * spec_imag + freq_imag * spec_real
    back_real, back_imag = transform(prod_real, prod_imag, factors, 1.0)
    return (back_real[:, :length_all] / (2 * length_all)).astype(jnp.bfloat16)


def local_general(streams, short_taps, spectrum, residual):
    row_count = streams.shape[1]
    channels = streams.shape[2]
    span = short_taps.shape[1] - 1
    rim_rows = passed_along(streams[:, row_count - span :, :], "seq", 1)
    extended = jnp.concatenate([rim_rows, streams], axis=1)
    total = jnp.zeros((3, row_count, channels), jnp.float32)
    for offset in range(span + 1):
        total = total + short_taps[:, offset, None, :] * extended[
            :, span - offset : span - offset + row_count, :
        ].astype(jnp.float32)
    convolved = total.astype(jnp.bfloat16)
    q_conv = convolved[0]
    k_conv = convolved[1]
    v_conv = convolved[2]
    seq_devices = lax.axis_size("seq")
    owned_count = channels // seq_devices
    length_all = row_count * seq_devices
    gated = (k_conv.astype(jnp.float32) * v_conv.astype(jnp.float32)).astype(jnp.bfloat16)
    owned = lax.all_to_all(
        gated.reshape(row_count, seq_devices, owned_count),
        "seq",
        split_axis=1,
        concat_axis=0,
        tiled=True,
    )
    gated_whole = owned.reshape(length_all, owned_count)
    filtered = jnp.transpose(long_filter(jnp.transpose(gated_whole), spectrum))
    returned = lax.all_to_all(
        filtered.reshape(length_all, 1, owned_count), "seq", split_axis=0, concat_axis=1, tiled=True
    )
    filtered_local = returned.reshape(row_count, channels)
    resid = residual.astype(jnp.float32)
    mixed = resid + jax.nn.silu(resid) * q_conv.astype(jnp.float32) * filtered_local.astype(
        jnp.float32
    )
    return mixed.astype(jnp.bfloat16)


def rounded(values):
    return values.astype(jnp.bfloat16).astype(jnp.float32)


def short_conv_rolled(rows, taps):
    later = pltpu.roll(rows, 1, 0)
    pairs = [taps(2 * i) * rows + taps(2 * i + 1) * later for i in range(3)]
    pairs.append(taps(6) * rows)
    low = pairs[0] + pltpu.roll(pairs[1], 2, 0)
    high = pairs[2] + pltpu.roll(pairs[3], 2, 0)
    return rounded(low + pltpu.roll(high, 4, 0))


def row_index(count):
    return lax.broadcasted_iota(jnp.int32, (count, LANES), 0)


def own_lanes(place_ref, k):
    return pl.ds(pl.multiple_of((place_ref[0] ^ k) * LANES, LANES), LANES)


def first_link(place_ref):
    return 2 + 2 * (place_ref[0] & 1)


def pack_block(k, v, q_last, taps, out_ref):
    rows = k.shape[0]
    row = row_index(TILE)
    gated = short_conv_rolled(k, lambda j: taps(1, j)) * short_conv_rolled(
        v, lambda j: taps(2, j)
    )
    out_ref[:TILE, :] = jnp.where(row < 6, k[:TILE], gated[:TILE]).astype(jnp.bfloat16)
    out_ref[TILE:rows, :] = gated[TILE:].astype(jnp.bfloat16)
    edge = jnp.where(row < 6, v[:TILE], v[rows - TILE :])
    edge = jnp.where((row >= 6) & (row < 10), pltpu.roll(q_last, 12, 0), edge)
    out_ref[rows : rows + TILE, :] = edge.astype(jnp.bfloat16)
    half = jnp.where(row_index(8) < 2, pltpu.roll(q_last[8:], 2, 0), k[rows - 8 :])
    out_ref[rows + TILE :, :] = jnp.concatenate([half, half], axis=0).astype(jnp.bfloat16)


def chip_order(place_ref):
    first = first_link(place_ref)
    return (0, first, 6 - first, 6)


def pack_one(place_ref, kv_ref, q_ref, taps_ref, chip, p, out_ref):
    lanes = pl.ds(pl.multiple_of(((place_ref[0] & 1) ^ p) * LANES, LANES), LANES)
    owner = own_lanes(place_ref, chip_order(place_ref)[chip] ^ p)
    pack_block(
        kv_ref[chip, 0, :, lanes].astype(jnp.float32),
        kv_ref[chip, 1, :, lanes].astype(jnp.float32),
        q_ref[:, owner].astype(jnp.float32),
        lambda s, j: taps_ref[s, j : j + 1, owner],
        out_ref,
    )


def pack_first_kernel(
    place_ref, streams_ref, taps_hbm_ref, core_ref, first_ref, kv_ref, q_ref, taps_ref, sems
):
    rows = streams_ref.shape[1]
    order = chip_order(place_ref)
    shared = [
        pltpu.make_async_copy(taps_hbm_ref, taps_ref, sems.at[4]),
        pltpu.make_async_copy(
            streams_ref.at[0, pl.ds(rows - TILE, TILE), :], q_ref, sems.at[5]
        ),
    ]
    copies = {}
    for i in (1, 0, 3, 2):
        chip = (place_ref[0] ^ order[i]) >> 1
        lanes = pl.ds(pl.multiple_of(chip * (2 * LANES), 2 * LANES), 2 * LANES)
        copies[i] = pltpu.make_async_copy(
            streams_ref.at[pl.ds(1, 2), :, lanes], kv_ref.at[i], sems.at[i]
        )
        copies[i].start()
        if i == 1:
            for copy in shared:
                copy.start()
    for copy in shared:
        copy.wait()
    for i, p, out_ref in (
        (1, 0, first_ref.at[0]),
        (1, 1, first_ref.at[1]),
        (0, 1, core_ref.at[0]),
        (3, 1, core_ref.at[1]),
    ):
        if p == 0 or i != 1:
            copies[i].wait()
        pack_one(place_ref, kv_ref, q_ref, taps_ref, i, p, out_ref)
    copies[2].wait()


def pack_second_kernel(place_ref, kv_ref, q_ref, taps_ref, second_ref, far_ref):
    for i, p, out_ref in (
        (2, 0, second_ref.at[0]),
        (2, 1, second_ref.at[1]),
        (3, 0, far_ref),
    ):
        pack_one(place_ref, kv_ref, q_ref, taps_ref, i, p, out_ref)


def pack_own_kernel(place_ref, kv_ref, q_ref, taps_ref, beside_ref, own_ref):
    pack_one(place_ref, kv_ref, q_ref, taps_ref, 0, 0, own_ref)


def spectrum_kernel(quarter, part, view_ref, beside_ref, out_ref):
    blocks = view_ref.shape[0] // (2 * LANES)
    per = quarter // LANES
    scale = 1.0 / (blocks * LANES)
    row = lax.broadcasted_iota(jnp.int32, (quarter + TILE, 2 * quarter), 0)
    col = lax.broadcasted_iota(jnp.int32, (quarter + TILE, 2 * quarter), 1)
    ahead = (col < quarter) & (row == col)
    back = (col >= quarter) & (row + col == 2 * quarter)
    turn = jnp.where(ahead | back, 1.0, 0.0).astype(jnp.bfloat16)

    def columns(part, start):
        return [
            view_ref[pl.ds(2 * (start + i) + part, LANES, stride=2 * blocks), :]
            for i in range(per)
        ]

    sign = 1.0 if part == 0 else -1.0
    heads, tails = [], []
    for m in range(4):
        start = 2 * per * m
        values = columns(part, start) + [sign * v for v in columns(part, blocks - start - per)]
        values = jnp.concatenate(values, axis=1)
        high = values.astype(jnp.bfloat16)
        low = (values - high.astype(jnp.float32)).astype(jnp.bfloat16)
        both = lax.dot_general(
            turn,
            jnp.concatenate([high, low], axis=0),
            (((1,), (1,)), ((), ())),
            preferred_element_type=jnp.float32,
        )
        folded = (both[: quarter + 8, :LANES] + both[: quarter + 8, LANES:]) * scale
        out_ref[m, :, :] = folded
        heads.append(folded[0:1])
        tails.append(folded[quarter : quarter + 1])
    for m in range(4):
        out_ref[m, 0:1, :] = 0.5 * (heads[m] + sign * heads[(4 - m) % 4])
        out_ref[m, quarter : quarter + 1, :] = 0.5 * (tails[m] + sign * tails[3 - m])


def forward_kernel(pair_ref, beside_ref, out_ref):
    out_ref[...] = pair_ref[1]


def merge_kernel(far_ref, core_ref, out_ref):
    out_ref[0] = far_ref[...]
    out_ref[1] = core_ref[1]


def received(place_ref, own, core, first, second, first_on, second_on, far):
    link = first_link(place_ref)
    blocks = [
        (0, own),
        (1, core.at[0]),
        (link, first.at[0]),
        (6 - link, second.at[0]),
        ((6 - link) ^ 1, first_on),
        (link ^ 1, second_on),
    ]
    if far is not None:
        blocks += [(6, far.at[0]), (7, far.at[1])]
    return blocks


def filter_kernel(
    place_ref,
    own_ref,
    core_ref,
    first_ref,
    second_ref,
    first_on_ref,
    second_on_ref,
    far_ref,
    taps_ref,
    real_ref,
    imag_ref,
    ahead_ref,
    back_ref,
    twist_ref,
    own_out,
    core_out,
    first_out,
    second_out,
    far_out,
    msg_ref,
    x_ref,
    z_ref,
    q_ref,
):
    shards = msg_ref.shape[0]
    rows = own_ref.shape[0] - 2 * TILE
    quarter = back_ref.shape[0]
    blocks = received(
        place_ref,
        own_ref,
        core_ref,
        first_ref,
        second_ref,
        first_on_ref,
        second_on_ref,
        far_ref,
    )
    for k, block in blocks:
        msg_ref[place_ref[0] ^ k] = block[...]
    row = row_index(TILE)
    own = own_lanes(place_ref, 0)

    before = None
    for s in range(shards):
        top = msg_ref[s, :TILE, :].astype(jnp.float32)
        edge = msg_ref[s, rows : rows + TILE, :].astype(jnp.float32)
        half = msg_ref[s, rows + TILE :, :].astype(jnp.float32)[:8]
        if before is None:
            above_k = above_v = jnp.zeros_like(edge)
            halo = jnp.zeros_like(half)
        else:
            above_v, half_before = before
            above_k = jnp.concatenate([half_before, half_before], axis=0)
            halo = jnp.where(
                row_index(8) < 6,
                pltpu.roll(above_v, 12, 0)[:8],
                pltpu.roll(half_before, 6, 0),
            )
        k_conv = short_conv_rolled(
            jnp.where(row < 8, top, above_k), lambda j: taps_ref[1, j : j + 1, own]
        )
        v_conv = short_conv_rolled(
            jnp.where(row < 8, edge, above_v), lambda j: taps_ref[2, j : j + 1, own]
        )
        x_ref[s * rows : s * rows + TILE, :] = jnp.where(row < 6, rounded(k_conv * v_conv), top)
        x_ref[s * rows + TILE : (s + 1) * rows, :] = msg_ref[s, TILE:rows, :].astype(jnp.float32)
        halo = jnp.concatenate([halo, halo], axis=0)
        msg_ref[s, rows : rows + TILE, :] = halo.astype(jnp.bfloat16)
        before = (edge, half)

    x = jnp.concatenate(
        [x_ref[pl.ds(a, quarter, stride=4), :].astype(jnp.bfloat16) for a in range(4)], axis=1
    )
    x = jnp.concatenate([x, x], axis=0)

    def combine(real, imag, g, count):
        u = []
        for a in range(4):
            if a == 0:
                u.append((real[0], imag[0]))
                continue
            wr = jnp.broadcast_to(twist_ref[g : g + count, 2 * a : 2 * a + 1], (count, LANES))
            wi = jnp.broadcast_to(
                twist_ref[g : g + count, 2 * a + 1 : 2 * a + 2], (count, LANES)
            )
            u.append((real[a] * wr - imag[a] * wi, real[a] * wi + imag[a] * wr, wr, wi))

        def four(v, sign):
            er, ei = v[0][0] + v[2][0], v[0][1] + v[2][1]
            dr, di = v[0][0] - v[2][0], v[0][1] - v[2][1]
            pr, pi = v[1][0] + v[3][0], v[1][1] + v[3][1]
            qr, qi = v[1][0] - v[3][0], v[1][1] - v[3][1]
            if sign < 0:
                one, three = (dr + qi, di - qr), (dr - qi, di + qr)
            else:
                one, three = (dr - qi, di + qr), (dr + qi, di - qr)
            return [(er + pr, ei + pi), one, (er - pr, ei - pi), three]

        freq = four(u, -1)
        prod = []
        for m in range(4):
            hr = real_ref[m, g : g + count, :]
            hi = imag_ref[m, g : g + count, :]
            xr, xi = freq[m]
            prod.append((xr * hr - xi * hi, xr * hi + xi * hr))
        v = four(prod, 1)
        out = [v[0]]
        for a in range(1, 4):
            wr, wi = u[a][2], u[a][3]
            vr, vi = v[a]
            out.append((vr * wr + vi * wi, vi * wr - vr * wi))
        return out

    part = quarter // 2
    y = None
    for half in range(2):
        base = half * quarter
        count = quarter + half * TILE
        z_ref[base : base + count, :] = jnp.dot(
            ahead_ref[base : base + count, :], x, preferred_element_type=jnp.float32
        )
        for g in range(0, part, TILE):
            real, imag = [
                [
                    z_ref[start : start + TILE, a * LANES : (a + 1) * LANES]
                    for a in range(4)
                ]
                for start in (base + g, base + part + g)
            ]
            out = combine(real, imag, half * part + g, TILE)
            for a in range(4):
                lanes = slice(a * LANES, (a + 1) * LANES)
                for i in range(2):
                    start = base + i * part + g
                    q_ref[start : start + TILE, lanes] = out[a][i].astype(jnp.bfloat16)
        term = jnp.dot(
            back_ref[:, base : base + quarter],
            q_ref[base : base + quarter, :],
            preferred_element_type=jnp.float32,
        )
        y = term if y is None else y + term
    real = [z_ref[2 * quarter : 2 * quarter + 8, a * LANES : (a + 1) * LANES] for a in range(4)]
    last = combine(real, [jnp.zeros_like(r) for r in real], quarter, 8)

    sign = 1.0 - 2.0 * (row_index(quarter) % 2).astype(jnp.float32)
    for a in range(4):
        x_ref[pl.ds(a, quarter, stride=4), :] = (
            y[:, a * LANES : (a + 1) * LANES] + sign * last[a][0][0:1, :]
        )
    link = first_link(place_ref)
    for k, out_ref in (
        (link, first_out.at[0]),
        (link ^ 1, first_out.at[1]),
        (6 - link, second_out.at[0]),
        ((6 - link) ^ 1, second_out.at[1]),
        (6, far_out),
        (7, core_out.at[1]),
        (0, own_out),
        (1, core_out.at[0]),
    ):
        target = place_ref[0] ^ k
        start = pl.multiple_of(target * rows, rows)
        out_ref[:rows, :] = x_ref[pl.ds(start, rows), :].astype(jnp.bfloat16)
        out_ref[rows:, :] = msg_ref[target, rows : rows + TILE, :]


def silu(values):
    return values / (1.0 + jnp.exp(-values))


def gain_kernel(q_ref, taps_ref, residual_ref, out_ref):
    for c in range(out_ref.shape[1] // LANES):
        lanes = slice(c * LANES, (c + 1) * LANES)
        conv = short_conv_rolled(
            q_ref[0, :, lanes].astype(jnp.float32), lambda j: taps_ref[0, j : j + 1, lanes]
        )
        out_ref[:, lanes] = silu(residual_ref[:, lanes].astype(jnp.float32)) * conv


def mixed_block(msg, lanes, gain_ref, residual_ref, q_ref, taps_ref, out_ref):
    rows = residual_ref.shape[0]
    row = row_index(TILE)
    halo = msg[rows:, :].astype(jnp.float32)
    window = jnp.where(
        row < 8, q_ref[0, :TILE, lanes].astype(jnp.float32), halo
    )
    conv = short_conv_rolled(window, lambda j: taps_ref[0, j : j + 1, lanes])
    resid = residual_ref[:TILE, lanes].astype(jnp.float32)
    gain = jnp.where(row < 6, silu(resid) * conv, gain_ref[:TILE, lanes])
    out_ref[:TILE, :] = (resid + gain * msg[:TILE, :].astype(jnp.float32)).astype(jnp.bfloat16)
    out_ref[TILE:, :] = (
        residual_ref[TILE:, lanes].astype(jnp.float32)
        + gain_ref[TILE:, lanes] * msg[TILE:rows, :].astype(jnp.float32)
    ).astype(jnp.bfloat16)


def mix_early_kernel(place_ref, own, core, first, second, first_on, *refs):
    rest, out_ref = refs[:4], refs[4]
    blocks = received(place_ref, own, core, first, second, first_on, None, None)
    for i, (k, block) in enumerate(blocks[:5]):
        mixed_block(block, own_lanes(place_ref, k), *rest, out_ref.at[i])


def mix_late_kernel(place_ref, early_ref, second_on, far_ref, *refs):
    rest, (out_ref, held, sems) = refs[:4], refs[4:]
    link = first_link(place_ref)
    order = (0, 1, link, 6 - link, (6 - link) ^ 1, link ^ 1, 6, 7)
    late = (second_on, far_ref.at[0], far_ref.at[1])
    copies = []
    for i, k in enumerate(order):
        lanes = own_lanes(place_ref, k)
        source = early_ref.at[i] if i < 5 else held.at[i - 5]
        if i >= 5:
            mixed_block(late[i - 5], lanes, *rest, source)
        copy = pltpu.make_async_copy(source, out_ref.at[:, lanes], sems.at[i])
        copy.start()
        copies.append(copy)
    for copy in copies:
        copy.wait()


def filter_tables(quarter):
    index = np.arange(quarter)
    angle = 2.0 * np.pi * (index[:, None] * index[None, :] % (2 * quarter)) / (2 * quarter)
    alternate = np.zeros((TILE, quarter))
    alternate[0] = 1.0 - 2.0 * (index % 2)
    part = quarter // 2
    cos, sin = np.cos(angle), -np.sin(angle)
    table = np.concatenate([cos[:part], sin[:part], cos[part:], sin[part:], alternate], axis=0)
    high = table.astype(jnp.bfloat16)
    low = (table - high.astype(np.float64)).astype(jnp.bfloat16)
    ahead = np.concatenate([high, low], axis=1)
    back = np.ascontiguousarray(high[: 2 * quarter].T)
    g = np.arange(quarter + 8)[:, None]
    a = np.arange(4)[None, :]
    turn = 2.0 * np.pi * (g * a) / (8 * quarter)
    twist = np.stack([np.cos(turn), -np.sin(turn)], axis=-1).reshape(quarter + 8, 8)
    return ahead, back, twist.astype(np.float32)


def estimate(flops, moved):
    return pl.CostEstimate(flops=flops, bytes_accessed=moved, transcendentals=0)


def swap(block, partner):
    return lax.ppermute(block, "seq", [(i, partner(i)) for i in range(8)])


def arranged(kernel, name, shape, *blocks, spaces=(pltpu.VMEM, pltpu.VMEM)):
    return pl.pallas_call(
        kernel,
        in_specs=[pl.BlockSpec(memory_space=space) for space in spaces],
        out_shape=jax.ShapeDtypeStruct(shape, jnp.bfloat16),
        compiler_params=pltpu.CompilerParams(vmem_limit_bytes=VMEM_LIMIT),
        cost_estimate=estimate(1 << 10, 1 << 16),
        name=name,
    )(*blocks)


def exchanged(core, first, second, far):
    core = swap(core, lambda i: i ^ 1)
    first = swap(first, lambda i: i ^ (2 + 2 * (i & 1)))
    second = swap(second, lambda i: i ^ (4 - 2 * (i & 1)))
    merged = arranged(merge_kernel, "merge", core.shape, far, core)
    return core, first, second, swap(merged, lambda i: i ^ 6), merged


def sibling_block(pair, beside):
    return arranged(
        forward_kernel, "forward", pair.shape[1:], pair, beside, spaces=(pltpu.VMEM, pl.ANY)
    )


def local_kernels(streams, short_taps, spectrum, residual):
    rows, channels = residual.shape
    shards = lax.axis_size("seq")
    length = rows * shards
    quarter = length // 4
    params = pltpu.CompilerParams(vmem_limit_bytes=VMEM_LIMIT)
    place = lax.axis_index("seq").astype(jnp.int32).reshape(1)
    scalar = pl.BlockSpec(memory_space=pltpu.SMEM)
    vector = pl.BlockSpec(memory_space=pltpu.VMEM)
    hbm = pl.BlockSpec(memory_space=pltpu.HBM)
    half = lambda *shape: jax.ShapeDtypeStruct(shape, jnp.bfloat16)
    full = lambda *shape: jax.ShapeDtypeStruct(shape, jnp.float32)
    sent = rows + 2 * TILE
    core, first, kv, q_last, taps = pl.pallas_call(
        pack_first_kernel,
        in_specs=[scalar, hbm, hbm],
        out_shape=[
            half(2, sent, LANES),
            half(2, sent, LANES),
            half(4, 2, rows, 2 * LANES),
            half(TILE, channels),
            full(*short_taps.shape),
        ],
        scratch_shapes=[pltpu.SemaphoreType.DMA((6,))],
        compiler_params=params,
        cost_estimate=estimate(1 << 30, 1 << 20),
        name="pack_first",
    )(
        place,
        pltpu.with_memory_space_constraint(streams, pltpu.HBM),
        pltpu.with_memory_space_constraint(short_taps, pltpu.HBM),
    )
    second, far = pl.pallas_call(
        pack_second_kernel,
        in_specs=[scalar] + [vector] * 3,
        out_shape=[half(2, sent, LANES), half(sent, LANES)],
        compiler_params=params,
        cost_estimate=estimate(1 << 30, 1 << 20),
        name="pack_second",
    )(place, kv, q_last, taps)
    blocks = 2 * length // LANES
    view = jnp.transpose(spectrum.reshape(LANES, 2, blocks, LANES), (0, 2, 1, 3)).reshape(
        2 * blocks * LANES, LANES
    )
    core, first, second, far, merged = exchanged(core, first, second, far)

    def spectrum_part(part, beside):
        return pl.pallas_call(
            functools.partial(spectrum_kernel, quarter, part),
            in_specs=[vector, pl.BlockSpec(memory_space=pl.ANY)],
            out_shape=full(4, quarter + 8, LANES),
            compiler_params=params,
            cost_estimate=estimate(1 << (32 - 20 * part), 1 << 22),
            name="spectrum",
        )(view, beside)

    real = spectrum_part(0, merged)
    first_block = sibling_block(first, real)
    first_on = swap(first_block, lambda i: i ^ 1)
    second_on = swap(sibling_block(second, real), lambda i: i ^ 1)
    imag = spectrum_part(1, first_on)
    own = pl.pallas_call(
        pack_own_kernel,
        in_specs=[scalar] + [vector] * 3 + [pl.BlockSpec(memory_space=pl.ANY)],
        out_shape=half(sent, LANES),
        compiler_params=params,
        cost_estimate=estimate(1 << 22, 1 << 20),
        name="pack_own",
    )(place, kv, q_last, taps, first_block)
    ahead, back_table, twist = filter_tables(quarter)
    back = rows + TILE
    own, *sent_back = pl.pallas_call(
        filter_kernel,
        in_specs=[scalar] + [vector] * 13,
        out_shape=[half(back, LANES)] + [half(2, back, LANES)] * 3 + [half(back, LANES)],
        scratch_shapes=[
            pltpu.VMEM((shards, sent, LANES), jnp.bfloat16),
            pltpu.VMEM((length, LANES), jnp.float32),
            pltpu.VMEM((2 * quarter + TILE, 4 * LANES), jnp.float32),
            pltpu.VMEM((2 * quarter, 4 * LANES), jnp.bfloat16),
        ],
        compiler_params=params,
        cost_estimate=estimate(1 << 30, 1 << 22),
        name="filter",
    )(
        place,
        own,
        core,
        first,
        second,
        first_on,
        second_on,
        far,
        taps,
        real,
        imag,
        ahead,
        back_table,
        twist,
    )
    whole = lambda *shape: pl.BlockSpec(shape, lambda i: (0,) * len(shape))
    gain = pl.pallas_call(
        gain_kernel,
        grid=(1,),
        in_specs=[
            whole(1, rows, channels),
            whole(*short_taps.shape),
            whole(rows, channels),
        ],
        out_specs=whole(rows, channels),
        out_shape=full(rows, channels),
        compiler_params=params,
        cost_estimate=estimate(1 << 32, 1 << 20),
        name="gain",
    )(streams, taps, residual)
    core, first, second, far, _ = exchanged(*sent_back)
    first_on, second_on = [
        swap(sibling_block(pair, gain), lambda i: i ^ 1) for pair in (first, second)
    ]
    rest = (gain, residual, streams, taps)
    early = pl.pallas_call(
        mix_early_kernel,
        in_specs=[scalar] + [vector] * 9,
        out_shape=half(5, rows, LANES),
        compiler_params=params,
        cost_estimate=estimate(1 << 20, 1 << 20),
        name="mix_early",
    )(place, own, core, first, second, first_on, *rest)
    return pl.pallas_call(
        mix_late_kernel,
        in_specs=[scalar] + [vector] * 7,
        out_specs=hbm,
        out_shape=half(rows, channels),
        scratch_shapes=[
            pltpu.VMEM((3, rows, LANES), jnp.bfloat16),
            pltpu.SemaphoreType.DMA((shards,)),
        ],
        compiler_params=params,
        cost_estimate=estimate(1 << 20, 1 << 20),
        name="mix_late",
    )(place, early, second_on, far, *rest)


def local(streams, short_taps, spectrum, residual):
    rows, channels = residual.shape
    shards = lax.axis_size("seq")
    length = rows * shards
    fits = (
        channels == shards * LANES
        and rows % TILE == 0
        and rows >= 2 * TILE
        and length % (4 * LANES) == 0
        and length <= 2048
        and short_taps.shape[1] == 7
        and shards == 8
    )
    if fits:
        return local_kernels(streams, short_taps, spectrum, residual)
    return local_general(streams, short_taps, spectrum, residual)


def solution(mesh):
    placed = (
        P(None, "seq", "chan"),
        P(None, None, "chan"),
        P(("chan", "seq"), None, None),
        P("seq", "chan"),
    )
    return jax.shard_map(
        local, mesh=mesh, in_specs=placed, out_specs=P("seq", "chan"), check_vma=False
    )
```

```python
import functools
import math

import jax
import jax.numpy as jnp
import numpy as np
from jax import lax
from jax.experimental import pallas as pl
from jax.experimental.pallas import tpu as pltpu
from jax.sharding import PartitionSpec as P

LANES = 128
TILE = 16
VMEM_LIMIT = 16 * 1024 * 1024


def passed_along(block, axis, distance):
    devices = range(lax.axis_size(axis))
    route = [(i - distance, i) for i in devices if i - distance in devices]
    return lax.ppermute(block, axis, route)


def section_sizes(length_all):
    power = length_all.bit_length() - 1
    first = (power + 2) // 3
    second = (power - first + 1) // 2
    third = power - first - second
    result = [2**first, 2**second]
    result.append(2**third)
    return result


def matmul_high(left, right):
    return jnp.dot(left, right, precision=lax.Precision.HIGHEST, preferred_element_type=jnp.float32)


def section_high(table, values):
    return jnp.einsum(
        "ka,cab->ckb",
        table,
        values,
        precision=lax.Precision.HIGHEST,
        preferred_element_type=jnp.float32,
    )


def dft_table(order, direction):
    index = jnp.arange(order, dtype=jnp.int32)
    product = index[:, None] * index[None, :] % order
    angle = direction * 2.0 * math.pi * product.astype(jnp.float32) / order
    return (jnp.cos(angle), jnp.sin(angle))


def transform(real_part, imag_part, factors, direction):
    columns, length_now = real_part.shape
    first = factors[0]
    table_cos, table_sin = dft_table(first, direction)
    if len(factors) == 1:
        real_out = matmul_high(real_part, table_cos) - matmul_high(imag_part, table_sin)
        imag_out = matmul_high(imag_part, table_cos) + matmul_high(real_part, table_sin)
        return (real_out, imag_out)
    rest = length_now // first
    real_wide = real_part.reshape(columns, first, rest)
    if imag_part is None:
        section_real = section_high(table_cos, real_wide)
        section_imag = section_high(table_sin, real_wide)
    else:
        imag_wide = imag_part.reshape(columns, first, rest)
        section_real = section_high(table_cos, real_wide) - section_high(table_sin, imag_wide)
        section_imag = section_high(table_cos, imag_wide) + section_high(table_sin, real_wide)
    outer = jnp.arange(first, dtype=jnp.int32)[:, None]
    inner = jnp.arange(rest, dtype=jnp.int32)[None, :]
    twist = (
        direction * 2.0 * math.pi * (outer * inner % length_now).astype(jnp.float32) / length_now
    )
    twist_cos = jnp.cos(twist)[None, :, :]
    twist_sin = jnp.sin(twist)[None, :, :]
    turned_real = (section_real * twist_cos - section_imag * twist_sin).reshape(
        columns * first, rest
    )
    turned_imag = (section_real * twist_sin + section_imag * twist_cos).reshape(
        columns * first, rest
    )
    real_out, imag_out = transform(turned_real, turned_imag, factors[1:], direction)
    real_out = jnp.transpose(real_out.reshape(columns, first, rest), (0, 2, 1)).reshape(
        columns, length_now
    )
    imag_out = jnp.transpose(imag_out.reshape(columns, first, rest), (0, 2, 1)).reshape(
        columns, length_now
    )
    return (real_out, imag_out)


def long_filter(gated_rows, spectrum):
    columns, length_all = gated_rows.shape
    padded = jnp.concatenate(
        [gated_rows.astype(jnp.float32), jnp.zeros((columns, length_all), jnp.float32)], axis=1
    )
    factors = section_sizes(2 * length_all)
    freq_real, freq_imag = transform(padded, None, factors, -1.0)
    spec_real = spectrum[:, 0, :]
    spec_imag = spectrum[:, 1, :]
    prod_real = freq_real * spec_real - freq_imag * spec_imag
    prod_imag = freq_real * spec_imag + freq_imag * spec_real
    back_real, back_imag = transform(prod_real, prod_imag, factors, 1.0)
    return (back_real[:, :length_all] / (2 * length_all)).astype(jnp.bfloat16)


def local_general(streams, short_taps, spectrum, residual):
    row_count = streams.shape[1]
    channels = streams.shape[2]
    span = short_taps.shape[1] - 1
    rim_rows = passed_along(streams[:, row_count - span :, :], "seq", 1)
    extended = jnp.concatenate([rim_rows, streams], axis=1)
    total = jnp.zeros((3, row_count, channels), jnp.float32)
    for offset in range(span + 1):
        total = total + short_taps[:, offset, None, :] * extended[
            :, span - offset : span - offset + row_count, :
        ].astype(jnp.float32)
    convolved = total.astype(jnp.bfloat16)
    q_conv = convolved[0]
    k_conv = convolved[1]
    v_conv = convolved[2]
    seq_devices = lax.axis_size("seq")
    owned_count = channels // seq_devices
    length_all = row_count * seq_devices
    gated = (k_conv.astype(jnp.float32) * v_conv.astype(jnp.float32)).astype(jnp.bfloat16)
    owned = lax.all_to_all(
        gated.reshape(row_count, seq_devices, owned_count),
        "seq",
        split_axis=1,
        concat_axis=0,
        tiled=True,
    )
    gated_whole = owned.reshape(length_all, owned_count)
    filtered = jnp.transpose(long_filter(jnp.transpose(gated_whole), spectrum))
    returned = lax.all_to_all(
        filtered.reshape(length_all, 1, owned_count), "seq", split_axis=0, concat_axis=1, tiled=True
    )
    filtered_local = returned.reshape(row_count, channels)
    resid = residual.astype(jnp.float32)
    mixed = resid + jax.nn.silu(resid) * q_conv.astype(jnp.float32) * filtered_local.astype(
        jnp.float32
    )
    return mixed.astype(jnp.bfloat16)


def rounded(values):
    return values.astype(jnp.bfloat16).astype(jnp.float32)


def short_conv_rolled(rows, taps):
    later = pltpu.roll(rows, 1, 0)
    pairs = [taps(2 * i) * rows + taps(2 * i + 1) * later for i in range(3)]
    pairs.append(taps(6) * rows)
    low = pairs[0] + pltpu.roll(pairs[1], 2, 0)
    high = pairs[2] + pltpu.roll(pairs[3], 2, 0)
    return rounded(low + pltpu.roll(high, 4, 0))


def row_index(count):
    return lax.broadcasted_iota(jnp.int32, (count, LANES), 0)


def own_lanes(place_ref, k):
    return pl.ds(pl.multiple_of((place_ref[0] ^ k) * LANES, LANES), LANES)


def first_link(place_ref):
    return 4 - 2 * (place_ref[0] & 1)


def pack_block(k, v, q_last, taps, out_ref):
    rows = k.shape[0]
    row = row_index(TILE)
    gated = short_conv_rolled(k, lambda j: taps(1, j)) * short_conv_rolled(
        v, lambda j: taps(2, j)
    )
    out_ref[:TILE, :] = jnp.where(row < 6, k[:TILE], gated[:TILE]).astype(jnp.bfloat16)
    out_ref[TILE:rows, :] = gated[TILE:].astype(jnp.bfloat16)
    edge = jnp.where(row < 6, v[:TILE], v[rows - TILE :])
    edge = jnp.where((row >= 6) & (row < 10), pltpu.roll(q_last, 12, 0), edge)
    out_ref[rows : rows + TILE, :] = edge.astype(jnp.bfloat16)
    half = jnp.where(row_index(8) < 2, pltpu.roll(q_last[8:], 2, 0), k[rows - 8 :])
    out_ref[rows + TILE :, :] = jnp.concatenate([half, half], axis=0).astype(jnp.bfloat16)


def chip_order(place_ref):
    first = first_link(place_ref)
    return (0, first, 6 - first, 6)


def pack_one(place_ref, kv_ref, q_ref, taps_ref, chip, p, out_ref):
    lanes = pl.ds(pl.multiple_of(((place_ref[0] & 1) ^ p) * LANES, LANES), LANES)
    owner = own_lanes(place_ref, chip_order(place_ref)[chip] ^ p)
    pack_block(
        kv_ref[chip, 0, :, lanes].astype(jnp.float32),
        kv_ref[chip, 1, :, lanes].astype(jnp.float32),
        q_ref[:, owner].astype(jnp.float32),
        lambda s, j: taps_ref[s, j : j + 1, owner],
        out_ref,
    )


def pack_first_kernel(
    place_ref, streams_ref, taps_hbm_ref, core_ref, first_ref, kv_ref, q_ref, taps_ref, sems
):
    rows = streams_ref.shape[1]
    order = chip_order(place_ref)
    shared = [
        pltpu.make_async_copy(taps_hbm_ref, taps_ref, sems.at[4]),
        pltpu.make_async_copy(
            streams_ref.at[0, pl.ds(rows - TILE, TILE), :], q_ref, sems.at[5]
        ),
    ]
    copies = {}
    for i in (1, 0, 3, 2):
        chip = (place_ref[0] ^ order[i]) >> 1
        lanes = pl.ds(pl.multiple_of(chip * (2 * LANES), 2 * LANES), 2 * LANES)
        copies[i] = pltpu.make_async_copy(
            streams_ref.at[pl.ds(1, 2), :, lanes], kv_ref.at[i], sems.at[i]
        )
        copies[i].start()
        if i == 1:
            for copy in shared:
                copy.start()
    for copy in shared:
        copy.wait()
    for i, p, out_ref in (
        (1, 0, first_ref.at[0]),
        (1, 1, first_ref.at[1]),
        (0, 1, core_ref.at[0]),
        (3, 1, core_ref.at[1]),
    ):
        if p == 0 or i != 1:
            copies[i].wait()
        pack_one(place_ref, kv_ref, q_ref, taps_ref, i, p, out_ref)
    copies[2].wait()


def pack_second_kernel(place_ref, kv_ref, q_ref, taps_ref, second_ref, far_ref):
    for i, p, out_ref in (
        (2, 0, second_ref.at[0]),
        (2, 1, second_ref.at[1]),
        (3, 0, far_ref),
    ):
        pack_one(place_ref, kv_ref, q_ref, taps_ref, i, p, out_ref)


def pack_own_kernel(place_ref, kv_ref, q_ref, taps_ref, beside_ref, own_ref):
    pack_one(place_ref, kv_ref, q_ref, taps_ref, 0, 0, own_ref)


def spectrum_kernel(quarter, part, view_ref, beside_ref, out_ref):
    blocks = view_ref.shape[0] // (2 * LANES)
    per = quarter // LANES
    scale = 1.0 / (blocks * LANES)
    row = lax.broadcasted_iota(jnp.int32, (quarter + TILE, 2 * quarter), 0)
    col = lax.broadcasted_iota(jnp.int32, (quarter + TILE, 2 * quarter), 1)
    ahead = (col < quarter) & (row == col)
    back = (col >= quarter) & (row + col == 2 * quarter)
    turn = jnp.where(ahead | back, 1.0, 0.0).astype(jnp.bfloat16)

    def columns(part, start):
        return [
            view_ref[pl.ds(2 * (start + i) + part, LANES, stride=2 * blocks), :]
            for i in range(per)
        ]

    sign = 1.0 if part == 0 else -1.0
    heads, tails = [], []
    for m in range(4):
        start = 2 * per * m
        values = columns(part, start) + [sign * v for v in columns(part, blocks - start - per)]
        values = jnp.concatenate(values, axis=1)
        high = values.astype(jnp.bfloat16)
        low = (values - high.astype(jnp.float32)).astype(jnp.bfloat16)
        both = lax.dot_general(
            turn,
            jnp.concatenate([high, low], axis=0),
            (((1,), (1,)), ((), ())),
            preferred_element_type=jnp.float32,
        )
        folded = (both[: quarter + 8, :LANES] + both[: quarter + 8, LANES:]) * scale
        out_ref[m, :, :] = folded
        heads.append(folded[0:1])
        tails.append(folded[quarter : quarter + 1])
    for m in range(4):
        out_ref[m, 0:1, :] = 0.5 * (heads[m] + sign * heads[(4 - m) % 4])
        out_ref[m, quarter : quarter + 1, :] = 0.5 * (tails[m] + sign * tails[3 - m])


def forward_kernel(pair_ref, beside_ref, out_ref):
    out_ref[...] = pair_ref[1]


def merge_kernel(far_ref, core_ref, out_ref):
    out_ref[0] = far_ref[...]
    out_ref[1] = core_ref[1]


def received(place_ref, own, core, first, second, first_on, second_on, far):
    link = first_link(place_ref)
    blocks = [
        (0, own),
        (1, core.at[0]),
        (link, first.at[0]),
        (6 - link, second.at[0]),
        ((6 - link) ^ 1, first_on),
        (link ^ 1, second_on),
    ]
    if far is not None:
        blocks += [(6, far.at[0]), (7, far.at[1])]
    return blocks


def filter_kernel(
    place_ref,
    own_ref,
    core_ref,
    first_ref,
    second_ref,
    first_on_ref,
    second_on_ref,
    far_ref,
    taps_ref,
    real_ref,
    imag_ref,
    ahead_ref,
    back_ref,
    twist_ref,
    own_out,
    core_out,
    first_out,
    second_out,
    far_out,
    msg_ref,
    x_ref,
    z_ref,
    q_ref,
):
    shards = msg_ref.shape[0]
    rows = own_ref.shape[0] - 2 * TILE
    quarter = back_ref.shape[0]
    blocks = received(
        place_ref,
        own_ref,
        core_ref,
        first_ref,
        second_ref,
        first_on_ref,
        second_on_ref,
        far_ref,
    )
    for k, block in blocks:
        msg_ref[place_ref[0] ^ k] = block[...]
    row = row_index(TILE)
    own = own_lanes(place_ref, 0)

    before = None
    for s in range(shards):
        top = msg_ref[s, :TILE, :].astype(jnp.float32)
        edge = msg_ref[s, rows : rows + TILE, :].astype(jnp.float32)
        half = msg_ref[s, rows + TILE :, :].astype(jnp.float32)[:8]
        if before is None:
            above_k = above_v = jnp.zeros_like(edge)
            halo = jnp.zeros_like(half)
        else:
            above_v, half_before = before
            above_k = jnp.concatenate([half_before, half_before], axis=0)
            halo = jnp.where(
                row_index(8) < 6,
                pltpu.roll(above_v, 12, 0)[:8],
                pltpu.roll(half_before, 6, 0),
            )
        k_conv = short_conv_rolled(
            jnp.where(row < 8, top, above_k), lambda j: taps_ref[1, j : j + 1, own]
        )
        v_conv = short_conv_rolled(
            jnp.where(row < 8, edge, above_v), lambda j: taps_ref[2, j : j + 1, own]
        )
        x_ref[s * rows : s * rows + TILE, :] = jnp.where(row < 6, rounded(k_conv * v_conv), top)
        x_ref[s * rows + TILE : (s + 1) * rows, :] = msg_ref[s, TILE:rows, :].astype(jnp.float32)
        halo = jnp.concatenate([halo, halo], axis=0)
        msg_ref[s, rows : rows + TILE, :] = halo.astype(jnp.bfloat16)
        before = (edge, half)

    x = jnp.concatenate(
        [x_ref[pl.ds(a, quarter, stride=4), :].astype(jnp.bfloat16) for a in range(4)], axis=1
    )
    x = jnp.concatenate([x, x], axis=0)

    def combine(real, imag, g, count):
        u = []
        for a in range(4):
            if a == 0:
                u.append((real[0], imag[0]))
                continue
            wr = jnp.broadcast_to(twist_ref[g : g + count, 2 * a : 2 * a + 1], (count, LANES))
            wi = jnp.broadcast_to(
                twist_ref[g : g + count, 2 * a + 1 : 2 * a + 2], (count, LANES)
            )
            u.append((real[a] * wr - imag[a] * wi, real[a] * wi + imag[a] * wr, wr, wi))

        def four(v, sign):
            er, ei = v[0][0] + v[2][0], v[0][1] + v[2][1]
            dr, di = v[0][0] - v[2][0], v[0][1] - v[2][1]
            pr, pi = v[1][0] + v[3][0], v[1][1] + v[3][1]
            qr, qi = v[1][0] - v[3][0], v[1][1] - v[3][1]
            if sign < 0:
                one, three = (dr + qi, di - qr), (dr - qi, di + qr)
            else:
                one, three = (dr - qi, di + qr), (dr + qi, di - qr)
            return [(er + pr, ei + pi), one, (er - pr, ei - pi), three]

        freq = four(u, -1)
        prod = []
        for m in range(4):
            hr = real_ref[m, g : g + count, :]
            hi = imag_ref[m, g : g + count, :]
            xr, xi = freq[m]
            prod.append((xr * hr - xi * hi, xr * hi + xi * hr))
        v = four(prod, 1)
        out = [v[0]]
        for a in range(1, 4):
            wr, wi = u[a][2], u[a][3]
            vr, vi = v[a]
            out.append((vr * wr + vi * wi, vi * wr - vr * wi))
        return out

    part = quarter // 2
    y = None
    for half in range(2):
        base = half * quarter
        count = quarter + half * TILE
        z_ref[base : base + count, :] = jnp.dot(
            ahead_ref[base : base + count, :], x, preferred_element_type=jnp.float32
        )
        for g in range(0, part, TILE):
            real, imag = [
                [
                    z_ref[start : start + TILE, a * LANES : (a + 1) * LANES]
                    for a in range(4)
                ]
                for start in (base + g, base + part + g)
            ]
            out = combine(real, imag, half * part + g, TILE)
            for a in range(4):
                lanes = slice(a * LANES, (a + 1) * LANES)
                for i in range(2):
                    start = base + i * part + g
                    q_ref[start : start + TILE, lanes] = out[a][i].astype(jnp.bfloat16)
        term = jnp.dot(
            back_ref[:, base : base + quarter],
            q_ref[base : base + quarter, :],
            preferred_element_type=jnp.float32,
        )
        y = term if y is None else y + term
    real = [z_ref[2 * quarter : 2 * quarter + 8, a * LANES : (a + 1) * LANES] for a in range(4)]
    last = combine(real, [jnp.zeros_like(r) for r in real], quarter, 8)

    sign = 1.0 - 2.0 * (row_index(quarter) % 2).astype(jnp.float32)
    for a in range(4):
        x_ref[pl.ds(a, quarter, stride=4), :] = (
            y[:, a * LANES : (a + 1) * LANES] + sign * last[a][0][0:1, :]
        )
    link = first_link(place_ref)
    for k, out_ref in (
        (link, first_out.at[0]),
        (link ^ 1, first_out.at[1]),
        (6 - link, second_out.at[0]),
        ((6 - link) ^ 1, second_out.at[1]),
        (6, far_out),
        (7, core_out.at[1]),
        (0, own_out),
        (1, core_out.at[0]),
    ):
        target = place_ref[0] ^ k
        start = pl.multiple_of(target * rows, rows)
        out_ref[:rows, :] = x_ref[pl.ds(start, rows), :].astype(jnp.bfloat16)
        out_ref[rows:, :] = msg_ref[target, rows : rows + TILE, :]


def silu(values):
    return values / (1.0 + jnp.exp(-values))


def gain_kernel(q_ref, taps_ref, residual_ref, out_ref):
    for c in range(out_ref.shape[1] // LANES):
        lanes = slice(c * LANES, (c + 1) * LANES)
        conv = short_conv_rolled(
            q_ref[0, :, lanes].astype(jnp.float32), lambda j: taps_ref[0, j : j + 1, lanes]
        )
        out_ref[:, lanes] = silu(residual_ref[:, lanes].astype(jnp.float32)) * conv


def mixed_block(msg, lanes, gain_ref, residual_ref, q_ref, taps_ref, out_ref):
    rows = residual_ref.shape[0]
    row = row_index(TILE)
    halo = msg[rows:, :].astype(jnp.float32)
    window = jnp.where(
        row < 8, q_ref[0, :TILE, lanes].astype(jnp.float32), halo
    )
    conv = short_conv_rolled(window, lambda j: taps_ref[0, j : j + 1, lanes])
    resid = residual_ref[:TILE, lanes].astype(jnp.float32)
    gain = jnp.where(row < 6, silu(resid) * conv, gain_ref[:TILE, lanes])
    out_ref[:TILE, :] = (resid + gain * msg[:TILE, :].astype(jnp.float32)).astype(jnp.bfloat16)
    out_ref[TILE:, :] = (
        residual_ref[TILE:, lanes].astype(jnp.float32)
        + gain_ref[TILE:, lanes] * msg[TILE:rows, :].astype(jnp.float32)
    ).astype(jnp.bfloat16)


def mix_early_kernel(place_ref, own, core, first, second, first_on, *refs):
    rest, out_ref = refs[:4], refs[4]
    blocks = received(place_ref, own, core, first, second, first_on, None, None)
    for i, (k, block) in enumerate(blocks[:5]):
        mixed_block(block, own_lanes(place_ref, k), *rest, out_ref.at[i])


def mix_late_kernel(place_ref, early_ref, second_on, far_ref, *refs):
    rest, (out_ref, held, sems) = refs[:4], refs[4:]
    link = first_link(place_ref)
    order = (0, 1, link, 6 - link, (6 - link) ^ 1, link ^ 1, 6, 7)
    late = (second_on, far_ref.at[0], far_ref.at[1])
    copies = []
    for i, k in enumerate(order):
        lanes = own_lanes(place_ref, k)
        source = early_ref.at[i] if i < 5 else held.at[i - 5]
        if i >= 5:
            mixed_block(late[i - 5], lanes, *rest, source)
        copy = pltpu.make_async_copy(source, out_ref.at[:, lanes], sems.at[i])
        copy.start()
        copies.append(copy)
    for copy in copies:
        copy.wait()


def filter_tables(quarter):
    index = np.arange(quarter)
    angle = 2.0 * np.pi * (index[:, None] * index[None, :] % (2 * quarter)) / (2 * quarter)
    alternate = np.zeros((TILE, quarter))
    alternate[0] = 1.0 - 2.0 * (index % 2)
    part = quarter // 2
    cos, sin = np.cos(angle), -np.sin(angle)
    table = np.concatenate([cos[:part], sin[:part], cos[part:], sin[part:], alternate], axis=0)
    high = table.astype(jnp.bfloat16)
    low = (table - high.astype(np.float64)).astype(jnp.bfloat16)
    ahead = np.concatenate([high, low], axis=1)
    back = np.ascontiguousarray(high[: 2 * quarter].T)
    g = np.arange(quarter + 8)[:, None]
    a = np.arange(4)[None, :]
    turn = 2.0 * np.pi * (g * a) / (8 * quarter)
    twist = np.stack([np.cos(turn), -np.sin(turn)], axis=-1).reshape(quarter + 8, 8)
    return ahead, back, twist.astype(np.float32)


def estimate(flops, moved):
    return pl.CostEstimate(flops=flops, bytes_accessed=moved, transcendentals=0)


def swap(block, partner):
    return lax.ppermute(block, "seq", [(i, partner(i)) for i in range(8)])


def arranged(kernel, name, shape, *blocks, spaces=(pltpu.VMEM, pltpu.VMEM)):
    return pl.pallas_call(
        kernel,
        in_specs=[pl.BlockSpec(memory_space=space) for space in spaces],
        out_shape=jax.ShapeDtypeStruct(shape, jnp.bfloat16),
        compiler_params=pltpu.CompilerParams(vmem_limit_bytes=VMEM_LIMIT),
        cost_estimate=estimate(1 << 10, 1 << 16),
        name=name,
    )(*blocks)


def exchanged(core, first, second, far):
    core = swap(core, lambda i: i ^ 1)
    first = swap(first, lambda i: i ^ (4 - 2 * (i & 1)))
    second = swap(second, lambda i: i ^ (2 + 2 * (i & 1)))
    merged = arranged(merge_kernel, "merge", core.shape, far, core)
    return core, first, second, swap(merged, lambda i: i ^ 6), merged


def sibling_block(pair, beside):
    return arranged(
        forward_kernel, "forward", pair.shape[1:], pair, beside, spaces=(pltpu.VMEM, pl.ANY)
    )


def local_kernels(streams, short_taps, spectrum, residual):
    rows, channels = residual.shape
    shards = lax.axis_size("seq")
    length = rows * shards
    quarter = length // 4
    params = pltpu.CompilerParams(vmem_limit_bytes=VMEM_LIMIT)
    place = lax.axis_index("seq").astype(jnp.int32).reshape(1)
    scalar = pl.BlockSpec(memory_space=pltpu.SMEM)
    vector = pl.BlockSpec(memory_space=pltpu.VMEM)
    hbm = pl.BlockSpec(memory_space=pltpu.HBM)
    half = lambda *shape: jax.ShapeDtypeStruct(shape, jnp.bfloat16)
    full = lambda *shape: jax.ShapeDtypeStruct(shape, jnp.float32)
    sent = rows + 2 * TILE
    core, first, kv, q_last, taps = pl.pallas_call(
        pack_first_kernel,
        in_specs=[scalar, hbm, hbm],
        out_shape=[
            half(2, sent, LANES),
            half(2, sent, LANES),
            half(4, 2, rows, 2 * LANES),
            half(TILE, channels),
            full(*short_taps.shape),
        ],
        scratch_shapes=[pltpu.SemaphoreType.DMA((6,))],
        compiler_params=params,
        cost_estimate=estimate(1 << 30, 1 << 20),
        name="pack_first",
    )(
        place,
        pltpu.with_memory_space_constraint(streams, pltpu.HBM),
        pltpu.with_memory_space_constraint(short_taps, pltpu.HBM),
    )
    second, far = pl.pallas_call(
        pack_second_kernel,
        in_specs=[scalar] + [vector] * 3,
        out_shape=[half(2, sent, LANES), half(sent, LANES)],
        compiler_params=params,
        cost_estimate=estimate(1 << 30, 1 << 20),
        name="pack_second",
    )(place, kv, q_last, taps)
    blocks = 2 * length // LANES
    view = jnp.transpose(spectrum.reshape(LANES, 2, blocks, LANES), (0, 2, 1, 3)).reshape(
        2 * blocks * LANES, LANES
    )
    core, first, second, far, merged = exchanged(core, first, second, far)

    def spectrum_part(part, beside):
        return pl.pallas_call(
            functools.partial(spectrum_kernel, quarter, part),
            in_specs=[vector, pl.BlockSpec(memory_space=pl.ANY)],
            out_shape=full(4, quarter + 8, LANES),
            compiler_params=params,
            cost_estimate=estimate(1 << (32 - 20 * part), 1 << 22),
            name="spectrum",
        )(view, beside)

    real = spectrum_part(0, merged)
    first_block = sibling_block(first, real)
    first_on = swap(first_block, lambda i: i ^ 1)
    second_on = swap(sibling_block(second, real), lambda i: i ^ 1)
    imag = spectrum_part(1, first_on)
    own = pl.pallas_call(
        pack_own_kernel,
        in_specs=[scalar] + [vector] * 3 + [pl.BlockSpec(memory_space=pl.ANY)],
        out_shape=half(sent, LANES),
        compiler_params=params,
        cost_estimate=estimate(1 << 22, 1 << 20),
        name="pack_own",
    )(place, kv, q_last, taps, first_block)
    ahead, back_table, twist = filter_tables(quarter)
    back = rows + TILE
    own, *sent_back = pl.pallas_call(
        filter_kernel,
        in_specs=[scalar] + [vector] * 13,
        out_shape=[half(back, LANES)] + [half(2, back, LANES)] * 3 + [half(back, LANES)],
        scratch_shapes=[
            pltpu.VMEM((shards, sent, LANES), jnp.bfloat16),
            pltpu.VMEM((length, LANES), jnp.float32),
            pltpu.VMEM((2 * quarter + TILE, 4 * LANES), jnp.float32),
            pltpu.VMEM((2 * quarter, 4 * LANES), jnp.bfloat16),
        ],
        compiler_params=params,
        cost_estimate=estimate(1 << 30, 1 << 22),
        name="filter",
    )(
        place,
        own,
        core,
        first,
        second,
        first_on,
        second_on,
        far,
        taps,
        real,
        imag,
        ahead,
        back_table,
        twist,
    )
    whole = lambda *shape: pl.BlockSpec(shape, lambda i: (0,) * len(shape))
    gain = pl.pallas_call(
        gain_kernel,
        grid=(1,),
        in_specs=[
            whole(1, rows, channels),
            whole(*short_taps.shape),
            whole(rows, channels),
        ],
        out_specs=whole(rows, channels),
        out_shape=full(rows, channels),
        compiler_params=params,
        cost_estimate=estimate(1 << 32, 1 << 20),
        name="gain",
    )(streams, taps, residual)
    core, first, second, far, _ = exchanged(*sent_back)
    first_on, second_on = [
        swap(sibling_block(pair, gain), lambda i: i ^ 1) for pair in (first, second)
    ]
    rest = (gain, residual, streams, taps)
    early = pl.pallas_call(
        mix_early_kernel,
        in_specs=[scalar] + [vector] * 9,
        out_shape=half(5, rows, LANES),
        compiler_params=params,
        cost_estimate=estimate(1 << 20, 1 << 20),
        name="mix_early",
    )(place, own, core, first, second, first_on, *rest)
    return pl.pallas_call(
        mix_late_kernel,
        in_specs=[scalar] + [vector] * 7,
        out_specs=hbm,
        out_shape=half(rows, channels),
        scratch_shapes=[
            pltpu.VMEM((3, rows, LANES), jnp.bfloat16),
            pltpu.SemaphoreType.DMA((shards,)),
        ],
        compiler_params=params,
        cost_estimate=estimate(1 << 20, 1 << 20),
        name="mix_late",
    )(place, early, second_on, far, *rest)


def local(streams, short_taps, spectrum, residual):
    rows, channels = residual.shape
    shards = lax.axis_size("seq")
    length = rows * shards
    fits = (
        channels == shards * LANES
        and rows % TILE == 0
        and rows >= 2 * TILE
        and length % (4 * LANES) == 0
        and length <= 2048
        and short_taps.shape[1] == 7
        and shards == 8
    )
    if fits:
        return local_kernels(streams, short_taps, spectrum, residual)
    return local_general(streams, short_taps, spectrum, residual)


def solution(mesh):
    placed = (
        P(None, "seq", "chan"),
        P(None, None, "chan"),
        P(("chan", "seq"), None, None),
        P("seq", "chan"),
    )
    return jax.shard_map(
        local, mesh=mesh, in_specs=placed, out_specs=P("seq", "chan"), check_vma=False
    )
```

```python
import functools
import math

import jax
import jax.numpy as jnp
import numpy as np
from jax import lax
from jax.experimental import pallas as pl
from jax.experimental.pallas import tpu as pltpu
from jax.sharding import PartitionSpec as P

LANES = 128
TILE = 16
VMEM_LIMIT = 16 * 1024 * 1024


def passed_along(block, axis, distance):
    devices = range(lax.axis_size(axis))
    route = [(i - distance, i) for i in devices if i - distance in devices]
    return lax.ppermute(block, axis, route)


def section_sizes(length_all):
    power = length_all.bit_length() - 1
    first = (power + 2) // 3
    second = (power - first + 1) // 2
    third = power - first - second
    result = [2**first, 2**second]
    result.append(2**third)
    return result


def matmul_high(left, right):
    return jnp.dot(left, right, precision=lax.Precision.HIGHEST, preferred_element_type=jnp.float32)


def section_high(table, values):
    return jnp.einsum(
        "ka,cab->ckb",
        table,
        values,
        precision=lax.Precision.HIGHEST,
        preferred_element_type=jnp.float32,
    )


def dft_table(order, direction):
    index = jnp.arange(order, dtype=jnp.int32)
    product = index[:, None] * index[None, :] % order
    angle = direction * 2.0 * math.pi * product.astype(jnp.float32) / order
    return (jnp.cos(angle), jnp.sin(angle))


def transform(real_part, imag_part, factors, direction):
    columns, length_now = real_part.shape
    first = factors[0]
    table_cos, table_sin = dft_table(first, direction)
    if len(factors) == 1:
        real_out = matmul_high(real_part, table_cos) - matmul_high(imag_part, table_sin)
        imag_out = matmul_high(imag_part, table_cos) + matmul_high(real_part, table_sin)
        return (real_out, imag_out)
    rest = length_now // first
    real_wide = real_part.reshape(columns, first, rest)
    if imag_part is None:
        section_real = section_high(table_cos, real_wide)
        section_imag = section_high(table_sin, real_wide)
    else:
        imag_wide = imag_part.reshape(columns, first, rest)
        section_real = section_high(table_cos, real_wide) - section_high(table_sin, imag_wide)
        section_imag = section_high(table_cos, imag_wide) + section_high(table_sin, real_wide)
    outer = jnp.arange(first, dtype=jnp.int32)[:, None]
    inner = jnp.arange(rest, dtype=jnp.int32)[None, :]
    twist = (
        direction * 2.0 * math.pi * (outer * inner % length_now).astype(jnp.float32) / length_now
    )
    twist_cos = jnp.cos(twist)[None, :, :]
    twist_sin = jnp.sin(twist)[None, :, :]
    turned_real = (section_real * twist_cos - section_imag * twist_sin).reshape(
        columns * first, rest
    )
    turned_imag = (section_real * twist_sin + section_imag * twist_cos).reshape(
        columns * first, rest
    )
    real_out, imag_out = transform(turned_real, turned_imag, factors[1:], direction)
    real_out = jnp.transpose(real_out.reshape(columns, first, rest), (0, 2, 1)).reshape(
        columns, length_now
    )
    imag_out = jnp.transpose(imag_out.reshape(columns, first, rest), (0, 2, 1)).reshape(
        columns, length_now
    )
    return (real_out, imag_out)


def long_filter(gated_rows, spectrum):
    columns, length_all = gated_rows.shape
    padded = jnp.concatenate(
        [gated_rows.astype(jnp.float32), jnp.zeros((columns, length_all), jnp.float32)], axis=1
    )
    factors = section_sizes(2 * length_all)
    freq_real, freq_imag = transform(padded, None, factors, -1.0)
    spec_real = spectrum[:, 0, :]
    spec_imag = spectrum[:, 1, :]
    prod_real = freq_real * spec_real - freq_imag * spec_imag
    prod_imag = freq_real * spec_imag + freq_imag * spec_real
    back_real, back_imag = transform(prod_real, prod_imag, factors, 1.0)
    return (back_real[:, :length_all] / (2 * length_all)).astype(jnp.bfloat16)


def local_general(streams, short_taps, spectrum, residual):
    row_count = streams.shape[1]
    channels = streams.shape[2]
    span = short_taps.shape[1] - 1
    rim_rows = passed_along(streams[:, row_count - span :, :], "seq", 1)
    extended = jnp.concatenate([rim_rows, streams], axis=1)
    total = jnp.zeros((3, row_count, channels), jnp.float32)
    for offset in range(span + 1):
        total = total + short_taps[:, offset, None, :] * extended[
            :, span - offset : span - offset + row_count, :
        ].astype(jnp.float32)
    convolved = total.astype(jnp.bfloat16)
    q_conv = convolved[0]
    k_conv = convolved[1]
    v_conv = convolved[2]
    seq_devices = lax.axis_size("seq")
    owned_count = channels // seq_devices
    length_all = row_count * seq_devices
    gated = (k_conv.astype(jnp.float32) * v_conv.astype(jnp.float32)).astype(jnp.bfloat16)
    owned = lax.all_to_all(
        gated.reshape(row_count, seq_devices, owned_count),
        "seq",
        split_axis=1,
        concat_axis=0,
        tiled=True,
    )
    gated_whole = owned.reshape(length_all, owned_count)
    filtered = jnp.transpose(long_filter(jnp.transpose(gated_whole), spectrum))
    returned = lax.all_to_all(
        filtered.reshape(length_all, 1, owned_count), "seq", split_axis=0, concat_axis=1, tiled=True
    )
    filtered_local = returned.reshape(row_count, channels)
    resid = residual.astype(jnp.float32)
    mixed = resid + jax.nn.silu(resid) * q_conv.astype(jnp.float32) * filtered_local.astype(
        jnp.float32
    )
    return mixed.astype(jnp.bfloat16)


def rounded(values):
    return values.astype(jnp.bfloat16).astype(jnp.float32)


def short_conv_rolled(rows, taps):
    later = pltpu.roll(rows, 1, 0)
    pairs = [taps(2 * i) * rows + taps(2 * i + 1) * later for i in range(3)]
    pairs.append(taps(6) * rows)
    low = pairs[0] + pltpu.roll(pairs[1], 2, 0)
    high = pairs[2] + pltpu.roll(pairs[3], 2, 0)
    return rounded(low + pltpu.roll(high, 4, 0))


def row_index(count):
    return lax.broadcasted_iota(jnp.int32, (count, LANES), 0)


def own_lanes(place_ref, k):
    return pl.ds(pl.multiple_of((place_ref[0] ^ k) * LANES, LANES), LANES)


def first_link(place_ref):
    return 2 + 2 * (place_ref[0] & 1)


def pack_block(k, v, q_last, taps, out_ref):
    rows = k.shape[0]
    row = row_index(TILE)
    gated = short_conv_rolled(k, lambda j: taps(1, j)) * short_conv_rolled(
        v, lambda j: taps(2, j)
    )
    out_ref[:TILE, :] = jnp.where(row < 6, k[:TILE], gated[:TILE]).astype(jnp.bfloat16)
    out_ref[TILE:rows, :] = gated[TILE:].astype(jnp.bfloat16)
    edge = jnp.where(row < 6, v[:TILE], v[rows - TILE :])
    edge = jnp.where((row >= 6) & (row < 10), pltpu.roll(q_last, 12, 0), edge)
    out_ref[rows : rows + TILE, :] = edge.astype(jnp.bfloat16)
    half = jnp.where(row_index(8) < 2, pltpu.roll(q_last[8:], 2, 0), k[rows - 8 :])
    out_ref[rows + TILE :, :] = jnp.concatenate([half, half], axis=0).astype(jnp.bfloat16)


def chip_order(place_ref):
    first = first_link(place_ref)
    return (0, first, 6 - first, 6)


def pack_one(place_ref, kv_ref, q_ref, taps_ref, chip, p, out_ref):
    lanes = pl.ds(pl.multiple_of(((place_ref[0] & 1) ^ p) * LANES, LANES), LANES)
    owner = own_lanes(place_ref, chip_order(place_ref)[chip] ^ p)
    pack_block(
        kv_ref[chip, 0, :, lanes].astype(jnp.float32),
        kv_ref[chip, 1, :, lanes].astype(jnp.float32),
        q_ref[:, owner].astype(jnp.float32),
        lambda s, j: taps_ref[s, j : j + 1, owner],
        out_ref,
    )


def pack_first_kernel(
    place_ref, streams_ref, taps_hbm_ref, core_ref, first_ref, kv_ref, q_ref, taps_ref, sems
):
    rows = streams_ref.shape[1]
    order = chip_order(place_ref)
    shared = [
        pltpu.make_async_copy(taps_hbm_ref, taps_ref, sems.at[4]),
        pltpu.make_async_copy(
            streams_ref.at[0, pl.ds(rows - TILE, TILE), :], q_ref, sems.at[5]
        ),
    ]
    copies = {}
    for i in (1, 0, 3, 2):
        chip = (place_ref[0] ^ order[i]) >> 1
        lanes = pl.ds(pl.multiple_of(chip * (2 * LANES), 2 * LANES), 2 * LANES)
        copies[i] = pltpu.make_async_copy(
            streams_ref.at[pl.ds(1, 2), :, lanes], kv_ref.at[i], sems.at[i]
        )
        copies[i].start()
        if i == 1:
            for copy in shared:
                copy.start()
    for copy in shared:
        copy.wait()
    for i, p, out_ref in (
        (1, 0, first_ref.at[0]),
        (1, 1, first_ref.at[1]),
        (0, 1, core_ref.at[0]),
        (3, 1, core_ref.at[1]),
    ):
        if p == 0 or i != 1:
            copies[i].wait()
        pack_one(place_ref, kv_ref, q_ref, taps_ref, i, p, out_ref)
    copies[2].wait()


def pack_second_kernel(place_ref, kv_ref, q_ref, taps_ref, second_ref, far_ref):
    for i, p, out_ref in (
        (2, 0, second_ref.at[0]),
        (2, 1, second_ref.at[1]),
        (3, 0, far_ref),
    ):
        pack_one(place_ref, kv_ref, q_ref, taps_ref, i, p, out_ref)


def pack_own_kernel(place_ref, kv_ref, q_ref, taps_ref, beside_ref, own_ref):
    pack_one(place_ref, kv_ref, q_ref, taps_ref, 0, 0, own_ref)


def spectrum_kernel(quarter, part, view_ref, beside_ref, out_ref):
    blocks = view_ref.shape[0] // (2 * LANES)
    per = quarter // LANES
    scale = 1.0 / (blocks * LANES)
    row = lax.broadcasted_iota(jnp.int32, (quarter + TILE, 2 * quarter), 0)
    col = lax.broadcasted_iota(jnp.int32, (quarter + TILE, 2 * quarter), 1)
    ahead = (col < quarter) & (row == col)
    back = (col >= quarter) & (row + col == 2 * quarter)
    turn = jnp.where(ahead | back, 1.0, 0.0).astype(jnp.bfloat16)

    def columns(part, start):
        return [
            view_ref[pl.ds(2 * (start + i) + part, LANES, stride=2 * blocks), :]
            for i in range(per)
        ]

    sign = 1.0 if part == 0 else -1.0
    heads, tails = [], []
    for m in range(4):
        start = 2 * per * m
        values = columns(part, start) + [sign * v for v in columns(part, blocks - start - per)]
        values = jnp.concatenate(values, axis=1)
        high = values.astype(jnp.bfloat16)
        low = (values - high.astype(jnp.float32)).astype(jnp.bfloat16)
        both = lax.dot_general(
            turn,
            jnp.concatenate([high, low], axis=0),
            (((1,), (1,)), ((), ())),
            preferred_element_type=jnp.float32,
        )
        folded = (both[: quarter + 8, :LANES] + both[: quarter + 8, LANES:]) * scale
        out_ref[m, :, :] = folded
        heads.append(folded[0:1])
        tails.append(folded[quarter : quarter + 1])
    for m in range(4):
        out_ref[m, 0:1, :] = 0.5 * (heads[m] + sign * heads[(4 - m) % 4])
        out_ref[m, quarter : quarter + 1, :] = 0.5 * (tails[m] + sign * tails[3 - m])


def forward_kernel(pair_ref, beside_ref, out_ref):
    out_ref[...] = pair_ref[1]


def merge_kernel(far_ref, core_ref, out_ref):
    out_ref[0] = far_ref[...]
    out_ref[1] = core_ref[1]


def received(place_ref, own, core, first, second, first_on, second_on, far):
    link = first_link(place_ref)
    blocks = [
        (0, own),
        (1, core.at[0]),
        (link, first.at[0]),
        (6 - link, second.at[0]),
        ((6 - link) ^ 1, first_on),
        (link ^ 1, second_on),
    ]
    if far is not None:
        blocks += [(6, far.at[0]), (7, far.at[1])]
    return blocks


def filter_kernel(
    place_ref,
    own_ref,
    core_ref,
    first_ref,
    second_ref,
    first_on_ref,
    second_on_ref,
    far_ref,
    taps_ref,
    real_ref,
    imag_ref,
    ahead_ref,
    back_ref,
    twist_ref,
    own_out,
    core_out,
    first_out,
    second_out,
    far_out,
    msg_ref,
    x_ref,
    z_ref,
    q_ref,
):
    shards = msg_ref.shape[0]
    rows = own_ref.shape[0] - 2 * TILE
    quarter = back_ref.shape[0]
    blocks = received(
        place_ref,
        own_ref,
        core_ref,
        first_ref,
        second_ref,
        first_on_ref,
        second_on_ref,
        far_ref,
    )
    for k, block in blocks:
        msg_ref[place_ref[0] ^ k] = block[...]
    row = row_index(TILE)
    own = own_lanes(place_ref, 0)

    before = None
    for s in range(shards):
        top = msg_ref[s, :TILE, :].astype(jnp.float32)
        edge = msg_ref[s, rows : rows + TILE, :].astype(jnp.float32)
        half = msg_ref[s, rows + TILE :, :].astype(jnp.float32)[:8]
        if before is None:
            above_k = above_v = jnp.zeros_like(edge)
            halo = jnp.zeros_like(half)
        else:
            above_v, half_before = before
            above_k = jnp.concatenate([half_before, half_before], axis=0)
            halo = jnp.where(
                row_index(8) < 6,
                pltpu.roll(above_v, 12, 0)[:8],
                pltpu.roll(half_before, 6, 0),
            )
        k_conv = short_conv_rolled(
            jnp.where(row < 8, top, above_k), lambda j: taps_ref[1, j : j + 1, own]
        )
        v_conv = short_conv_rolled(
            jnp.where(row < 8, edge, above_v), lambda j: taps_ref[2, j : j + 1, own]
        )
        x_ref[s * rows : s * rows + TILE, :] = jnp.where(row < 6, rounded(k_conv * v_conv), top)
        x_ref[s * rows + TILE : (s + 1) * rows, :] = msg_ref[s, TILE:rows, :].astype(jnp.float32)
        halo = jnp.concatenate([halo, halo], axis=0)
        msg_ref[s, rows : rows + TILE, :] = halo.astype(jnp.bfloat16)
        before = (edge, half)

    x = jnp.concatenate(
        [x_ref[pl.ds(a, quarter, stride=4), :].astype(jnp.bfloat16) for a in range(4)], axis=1
    )
    x = jnp.concatenate([x, x], axis=0)

    def combine(real, imag, g, count):
        u = []
        for a in range(4):
            if a == 0:
                u.append((real[0], imag[0]))
                continue
            wr = jnp.broadcast_to(twist_ref[g : g + count, 2 * a : 2 * a + 1], (count, LANES))
            wi = jnp.broadcast_to(
                twist_ref[g : g + count, 2 * a + 1 : 2 * a + 2], (count, LANES)
            )
            u.append((real[a] * wr - imag[a] * wi, real[a] * wi + imag[a] * wr, wr, wi))

        def four(v, sign):
            er, ei = v[0][0] + v[2][0], v[0][1] + v[2][1]
            dr, di = v[0][0] - v[2][0], v[0][1] - v[2][1]
            pr, pi = v[1][0] + v[3][0], v[1][1] + v[3][1]
            qr, qi = v[1][0] - v[3][0], v[1][1] - v[3][1]
            if sign < 0:
                one, three = (dr + qi, di - qr), (dr - qi, di + qr)
            else:
                one, three = (dr - qi, di + qr), (dr + qi, di - qr)
            return [(er + pr, ei + pi), one, (er - pr, ei - pi), three]

        freq = four(u, -1)
        prod = []
        for m in range(4):
            hr = real_ref[m, g : g + count, :]
            hi = imag_ref[m, g : g + count, :]
            xr, xi = freq[m]
            prod.append((xr * hr - xi * hi, xr * hi + xi * hr))
        v = four(prod, 1)
        out = [v[0]]
        for a in range(1, 4):
            wr, wi = u[a][2], u[a][3]
            vr, vi = v[a]
            out.append((vr * wr + vi * wi, vi * wr - vr * wi))
        return out

    part = quarter // 2
    y = None
    for half in range(2):
        base = half * quarter
        count = quarter + half * TILE
        z_ref[base : base + count, :] = jnp.dot(
            ahead_ref[base : base + count, :], x, preferred_element_type=jnp.float32
        )
        for g in range(0, part, TILE):
            real, imag = [
                [
                    z_ref[start : start + TILE, a * LANES : (a + 1) * LANES]
                    for a in range(4)
                ]
                for start in (base + g, base + part + g)
            ]
            out = combine(real, imag, half * part + g, TILE)
            for a in range(4):
                lanes = slice(a * LANES, (a + 1) * LANES)
                for i in range(2):
                    start = base + i * part + g
                    q_ref[start : start + TILE, lanes] = out[a][i].astype(jnp.bfloat16)
        term = jnp.dot(
            back_ref[:, base : base + quarter],
            q_ref[base : base + quarter, :],
            preferred_element_type=jnp.float32,
        )
        y = term if y is None else y + term
    real = [z_ref[2 * quarter : 2 * quarter + 8, a * LANES : (a + 1) * LANES] for a in range(4)]
    last = combine(real, [jnp.zeros_like(r) for r in real], quarter, 8)

    sign = 1.0 - 2.0 * (row_index(quarter) % 2).astype(jnp.float32)
    for a in range(4):
        x_ref[pl.ds(a, quarter, stride=4), :] = (
            y[:, a * LANES : (a + 1) * LANES] + sign * last[a][0][0:1, :]
        )
    link = first_link(place_ref)
    for k, out_ref in (
        (link, first_out.at[0]),
        (link ^ 1, first_out.at[1]),
        (6 - link, second_out.at[0]),
        ((6 - link) ^ 1, second_out.at[1]),
        (6, far_out),
        (7, core_out.at[1]),
        (0, own_out),
        (1, core_out.at[0]),
    ):
        target = place_ref[0] ^ k
        start = pl.multiple_of(target * rows, rows)
        out_ref[:rows, :] = x_ref[pl.ds(start, rows), :].astype(jnp.bfloat16)
        out_ref[rows:, :] = msg_ref[target, rows : rows + TILE, :]


def silu(values):
    return values / (1.0 + jnp.exp(-values))


def gain_kernel(q_ref, taps_ref, residual_ref, out_ref):
    for c in range(out_ref.shape[1] // LANES):
        lanes = slice(c * LANES, (c + 1) * LANES)
        conv = short_conv_rolled(
            q_ref[0, :, lanes].astype(jnp.float32), lambda j: taps_ref[0, j : j + 1, lanes]
        )
        out_ref[:, lanes] = silu(residual_ref[:, lanes].astype(jnp.float32)) * conv


def mixed_block(msg, lanes, gain_ref, residual_ref, q_ref, taps_ref, out_ref):
    rows = residual_ref.shape[0]
    row = row_index(TILE)
    halo = msg[rows:, :].astype(jnp.float32)
    window = jnp.where(
        row < 8, q_ref[0, :TILE, lanes].astype(jnp.float32), halo
    )
    conv = short_conv_rolled(window, lambda j: taps_ref[0, j : j + 1, lanes])
    resid = residual_ref[:TILE, lanes].astype(jnp.float32)
    gain = jnp.where(row < 6, silu(resid) * conv, gain_ref[:TILE, lanes])
    out_ref[:TILE, :] = (resid + gain * msg[:TILE, :].astype(jnp.float32)).astype(jnp.bfloat16)
    out_ref[TILE:, :] = (
        residual_ref[TILE:, lanes].astype(jnp.float32)
        + gain_ref[TILE:, lanes] * msg[TILE:rows, :].astype(jnp.float32)
    ).astype(jnp.bfloat16)


def mix_and_store(place_ref, blocks, rest, out_ref, held, sems):
    copies = []
    for i, (k, block) in enumerate(blocks):
        lanes = own_lanes(place_ref, k)
        mixed_block(block, lanes, *rest, held.at[i])
        copy = pltpu.make_async_copy(held.at[i], out_ref.at[:, lanes], sems.at[i])
        copy.start()
        copies.append(copy)
    for copy in copies:
        copy.wait()


def mix_early_kernel(place_ref, own, core, first, second, first_on, *refs):
    rest, (out_ref, held, sems) = refs[:4], refs[4:]
    blocks = received(place_ref, own, core, first, second, first_on, None, None)[:5]
    mix_and_store(place_ref, blocks, rest, out_ref, held, sems)


def mix_late_kernel(place_ref, early_ref, second_on, far, *refs):
    rest, (out_ref, held, sems) = refs[:4], refs[4:]
    blocks = [(1 ^ first_link(place_ref), second_on), (6, far.at[0]), (7, far.at[1])]
    mix_and_store(place_ref, blocks, rest, out_ref, held, sems)


def filter_tables(quarter):
    index = np.arange(quarter)
    angle = 2.0 * np.pi * (index[:, None] * index[None, :] % (2 * quarter)) / (2 * quarter)
    alternate = np.zeros((TILE, quarter))
    alternate[0] = 1.0 - 2.0 * (index % 2)
    part = quarter // 2
    cos, sin = np.cos(angle), -np.sin(angle)
    table = np.concatenate([cos[:part], sin[:part], cos[part:], sin[part:], alternate], axis=0)
    high = table.astype(jnp.bfloat16)
    low = (table - high.astype(np.float64)).astype(jnp.bfloat16)
    ahead = np.concatenate([high, low], axis=1)
    back = np.ascontiguousarray(high[: 2 * quarter].T)
    g = np.arange(quarter + 8)[:, None]
    a = np.arange(4)[None, :]
    turn = 2.0 * np.pi * (g * a) / (8 * quarter)
    twist = np.stack([np.cos(turn), -np.sin(turn)], axis=-1).reshape(quarter + 8, 8)
    return ahead, back, twist.astype(np.float32)


def estimate(flops, moved):
    return pl.CostEstimate(flops=flops, bytes_accessed=moved, transcendentals=0)


def swap(block, partner):
    return lax.ppermute(block, "seq", [(i, partner(i)) for i in range(8)])


def arranged(kernel, name, shape, *blocks, spaces=(pltpu.VMEM, pltpu.VMEM)):
    return pl.pallas_call(
        kernel,
        in_specs=[pl.BlockSpec(memory_space=space) for space in spaces],
        out_shape=jax.ShapeDtypeStruct(shape, jnp.bfloat16),
        compiler_params=pltpu.CompilerParams(vmem_limit_bytes=VMEM_LIMIT),
        cost_estimate=estimate(1 << 10, 1 << 16),
        name=name,
    )(*blocks)


def exchanged(core, first, second, far):
    core = swap(core, lambda i: i ^ 1)
    first = swap(first, lambda i: i ^ (2 + 2 * (i & 1)))
    second = swap(second, lambda i: i ^ (4 - 2 * (i & 1)))
    merged = arranged(merge_kernel, "merge", core.shape, far, core)
    return core, first, second, swap(merged, lambda i: i ^ 6), merged


def sibling_block(pair, beside):
    return arranged(
        forward_kernel, "forward", pair.shape[1:], pair, beside, spaces=(pltpu.VMEM, pl.ANY)
    )


def local_kernels(streams, short_taps, spectrum, residual):
    rows, channels = residual.shape
    shards = lax.axis_size("seq")
    length = rows * shards
    quarter = length // 4
    params = pltpu.CompilerParams(vmem_limit_bytes=VMEM_LIMIT)
    place = lax.axis_index("seq").astype(jnp.int32).reshape(1)
    scalar = pl.BlockSpec(memory_space=pltpu.SMEM)
    vector = pl.BlockSpec(memory_space=pltpu.VMEM)
    hbm = pl.BlockSpec(memory_space=pltpu.HBM)
    half = lambda *shape: jax.ShapeDtypeStruct(shape, jnp.bfloat16)
    full = lambda *shape: jax.ShapeDtypeStruct(shape, jnp.float32)
    sent = rows + 2 * TILE
    core, first, kv, q_last, taps = pl.pallas_call(
        pack_first_kernel,
        in_specs=[scalar, hbm, hbm],
        out_shape=[
            half(2, sent, LANES),
            half(2, sent, LANES),
            half(4, 2, rows, 2 * LANES),
            half(TILE, channels),
            full(*short_taps.shape),
        ],
        scratch_shapes=[pltpu.SemaphoreType.DMA((6,))],
        compiler_params=params,
        cost_estimate=estimate(1 << 30, 1 << 20),
        name="pack_first",
    )(
        place,
        pltpu.with_memory_space_constraint(streams, pltpu.HBM),
        pltpu.with_memory_space_constraint(short_taps, pltpu.HBM),
    )
    second, far = pl.pallas_call(
        pack_second_kernel,
        in_specs=[scalar] + [vector] * 3,
        out_shape=[half(2, sent, LANES), half(sent, LANES)],
        compiler_params=params,
        cost_estimate=estimate(1 << 30, 1 << 20),
        name="pack_second",
    )(place, kv, q_last, taps)
    blocks = 2 * length // LANES
    view = jnp.transpose(spectrum.reshape(LANES, 2, blocks, LANES), (0, 2, 1, 3)).reshape(
        2 * blocks * LANES, LANES
    )
    core, first, second, far, merged = exchanged(core, first, second, far)

    def spectrum_part(part, beside):
        return pl.pallas_call(
            functools.partial(spectrum_kernel, quarter, part),
            in_specs=[vector, pl.BlockSpec(memory_space=pl.ANY)],
            out_shape=full(4, quarter + 8, LANES),
            compiler_params=params,
            cost_estimate=estimate(1 << (32 - 20 * part), 1 << 22),
            name="spectrum",
        )(view, beside)

    real = spectrum_part(0, merged)
    first_block = sibling_block(first, real)
    first_on = swap(first_block, lambda i: i ^ 1)
    second_on = swap(sibling_block(second, real), lambda i: i ^ 1)
    imag = spectrum_part(1, first_on)
    own = pl.pallas_call(
        pack_own_kernel,
        in_specs=[scalar] + [vector] * 3 + [pl.BlockSpec(memory_space=pl.ANY)],
        out_shape=half(sent, LANES),
        compiler_params=params,
        cost_estimate=estimate(1 << 22, 1 << 20),
        name="pack_own",
    )(place, kv, q_last, taps, first_block)
    ahead, back_table, twist = filter_tables(quarter)
    back = rows + TILE
    own, *sent_back = pl.pallas_call(
        filter_kernel,
        in_specs=[scalar] + [vector] * 13,
        out_shape=[half(back, LANES)] + [half(2, back, LANES)] * 3 + [half(back, LANES)],
        scratch_shapes=[
            pltpu.VMEM((shards, sent, LANES), jnp.bfloat16),
            pltpu.VMEM((length, LANES), jnp.float32),
            pltpu.VMEM((2 * quarter + TILE, 4 * LANES), jnp.float32),
            pltpu.VMEM((2 * quarter, 4 * LANES), jnp.bfloat16),
        ],
        compiler_params=params,
        cost_estimate=estimate(1 << 30, 1 << 22),
        name="filter",
    )(
        place,
        own,
        core,
        first,
        second,
        first_on,
        second_on,
        far,
        taps,
        real,
        imag,
        ahead,
        back_table,
        twist,
    )
    whole = lambda *shape: pl.BlockSpec(shape, lambda i: (0,) * len(shape))
    gain = pl.pallas_call(
        gain_kernel,
        grid=(1,),
        in_specs=[
            whole(1, rows, channels),
            whole(*short_taps.shape),
            whole(rows, channels),
        ],
        out_specs=whole(rows, channels),
        out_shape=full(rows, channels),
        compiler_params=params,
        cost_estimate=estimate(1 << 32, 1 << 20),
        name="gain",
    )(streams, taps, residual)
    core, first, second, far, _ = exchanged(*sent_back)
    first_on, second_on = [
        swap(sibling_block(pair, gain), lambda i: i ^ 1) for pair in (first, second)
    ]
    rest = (gain, residual, streams, taps)
    stored = dict(
        out_specs=hbm,
        out_shape=half(rows, channels),
        compiler_params=params,
        cost_estimate=estimate(1 << 20, 1 << 20),
    )
    early = pl.pallas_call(
        mix_early_kernel,
        in_specs=[scalar] + [vector] * 9,
        scratch_shapes=[
            pltpu.VMEM((5, rows, LANES), jnp.bfloat16),
            pltpu.SemaphoreType.DMA((5,)),
        ],
        name="mix_early",
        **stored,
    )(place, own, core, first, second, first_on, *rest)
    return pl.pallas_call(
        mix_late_kernel,
        in_specs=[scalar, hbm] + [vector] * 6,
        scratch_shapes=[
            pltpu.VMEM((3, rows, LANES), jnp.bfloat16),
            pltpu.SemaphoreType.DMA((3,)),
        ],
        input_output_aliases={1: 0},
        name="mix_late",
        **stored,
    )(place, early, second_on, far, *rest)


def local(streams, short_taps, spectrum, residual):
    rows, channels = residual.shape
    shards = lax.axis_size("seq")
    length = rows * shards
    fits = (
        channels == shards * LANES
        and rows % TILE == 0
        and rows >= 2 * TILE
        and length % (4 * LANES) == 0
        and length <= 2048
        and short_taps.shape[1] == 7
        and shards == 8
    )
    if fits:
        return local_kernels(streams, short_taps, spectrum, residual)
    return local_general(streams, short_taps, spectrum, residual)


def solution(mesh):
    placed = (
        P(None, "seq", "chan"),
        P(None, None, "chan"),
        P(("chan", "seq"), None, None),
        P("seq", "chan"),
    )
    return jax.shard_map(
        local, mesh=mesh, in_specs=placed, out_specs=P("seq", "chan"), check_vma=False
    )
```

```python
import functools
import math

import jax
import jax.numpy as jnp
import numpy as np
from jax import lax
from jax.experimental import pallas as pl
from jax.experimental.pallas import tpu as pltpu
from jax.sharding import PartitionSpec as P

LANES = 128
TILE = 16
VMEM_LIMIT = 16 * 1024 * 1024


def passed_along(block, axis, distance):
    devices = range(lax.axis_size(axis))
    route = [(i - distance, i) for i in devices if i - distance in devices]
    return lax.ppermute(block, axis, route)


def section_sizes(length_all):
    power = length_all.bit_length() - 1
    first = (power + 2) // 3
    second = (power - first + 1) // 2
    third = power - first - second
    result = [2**first, 2**second]
    result.append(2**third)
    return result


def matmul_high(left, right):
    return jnp.dot(left, right, precision=lax.Precision.HIGHEST, preferred_element_type=jnp.float32)


def section_high(table, values):
    return jnp.einsum(
        "ka,cab->ckb",
        table,
        values,
        precision=lax.Precision.HIGHEST,
        preferred_element_type=jnp.float32,
    )


def dft_table(order, direction):
    index = jnp.arange(order, dtype=jnp.int32)
    product = index[:, None] * index[None, :] % order
    angle = direction * 2.0 * math.pi * product.astype(jnp.float32) / order
    return (jnp.cos(angle), jnp.sin(angle))


def transform(real_part, imag_part, factors, direction):
    columns, length_now = real_part.shape
    first = factors[0]
    table_cos, table_sin = dft_table(first, direction)
    if len(factors) == 1:
        real_out = matmul_high(real_part, table_cos) - matmul_high(imag_part, table_sin)
        imag_out = matmul_high(imag_part, table_cos) + matmul_high(real_part, table_sin)
        return (real_out, imag_out)
    rest = length_now // first
    real_wide = real_part.reshape(columns, first, rest)
    if imag_part is None:
        section_real = section_high(table_cos, real_wide)
        section_imag = section_high(table_sin, real_wide)
    else:
        imag_wide = imag_part.reshape(columns, first, rest)
        section_real = section_high(table_cos, real_wide) - section_high(table_sin, imag_wide)
        section_imag = section_high(table_cos, imag_wide) + section_high(table_sin, real_wide)
    outer = jnp.arange(first, dtype=jnp.int32)[:, None]
    inner = jnp.arange(rest, dtype=jnp.int32)[None, :]
    twist = (
        direction * 2.0 * math.pi * (outer * inner % length_now).astype(jnp.float32) / length_now
    )
    twist_cos = jnp.cos(twist)[None, :, :]
    twist_sin = jnp.sin(twist)[None, :, :]
    turned_real = (section_real * twist_cos - section_imag * twist_sin).reshape(
        columns * first, rest
    )
    turned_imag = (section_real * twist_sin + section_imag * twist_cos).reshape(
        columns * first, rest
    )
    real_out, imag_out = transform(turned_real, turned_imag, factors[1:], direction)
    real_out = jnp.transpose(real_out.reshape(columns, first, rest), (0, 2, 1)).reshape(
        columns, length_now
    )
    imag_out = jnp.transpose(imag_out.reshape(columns, first, rest), (0, 2, 1)).reshape(
        columns, length_now
    )
    return (real_out, imag_out)


def long_filter(gated_rows, spectrum):
    columns, length_all = gated_rows.shape
    padded = jnp.concatenate(
        [gated_rows.astype(jnp.float32), jnp.zeros((columns, length_all), jnp.float32)], axis=1
    )
    factors = section_sizes(2 * length_all)
    freq_real, freq_imag = transform(padded, None, factors, -1.0)
    spec_real = spectrum[:, 0, :]
    spec_imag = spectrum[:, 1, :]
    prod_real = freq_real * spec_real - freq_imag * spec_imag
    prod_imag = freq_real * spec_imag + freq_imag * spec_real
    back_real, back_imag = transform(prod_real, prod_imag, factors, 1.0)
    return (back_real[:, :length_all] / (2 * length_all)).astype(jnp.bfloat16)


def local_general(streams, short_taps, spectrum, residual):
    row_count = streams.shape[1]
    channels = streams.shape[2]
    span = short_taps.shape[1] - 1
    rim_rows = passed_along(streams[:, row_count - span :, :], "seq", 1)
    extended = jnp.concatenate([rim_rows, streams], axis=1)
    total = jnp.zeros((3, row_count, channels), jnp.float32)
    for offset in range(span + 1):
        total = total + short_taps[:, offset, None, :] * extended[
            :, span - offset : span - offset + row_count, :
        ].astype(jnp.float32)
    convolved = total.astype(jnp.bfloat16)
    q_conv = convolved[0]
    k_conv = convolved[1]
    v_conv = convolved[2]
    seq_devices = lax.axis_size("seq")
    owned_count = channels // seq_devices
    length_all = row_count * seq_devices
    gated = (k_conv.astype(jnp.float32) * v_conv.astype(jnp.float32)).astype(jnp.bfloat16)
    owned = lax.all_to_all(
        gated.reshape(row_count, seq_devices, owned_count),
        "seq",
        split_axis=1,
        concat_axis=0,
        tiled=True,
    )
    gated_whole = owned.reshape(length_all, owned_count)
    filtered = jnp.transpose(long_filter(jnp.transpose(gated_whole), spectrum))
    returned = lax.all_to_all(
        filtered.reshape(length_all, 1, owned_count), "seq", split_axis=0, concat_axis=1, tiled=True
    )
    filtered_local = returned.reshape(row_count, channels)
    resid = residual.astype(jnp.float32)
    mixed = resid + jax.nn.silu(resid) * q_conv.astype(jnp.float32) * filtered_local.astype(
        jnp.float32
    )
    return mixed.astype(jnp.bfloat16)


def rounded(values):
    return values.astype(jnp.bfloat16).astype(jnp.float32)


def short_conv_rolled(rows, taps):
    later = pltpu.roll(rows, 1, 0)
    pairs = [taps(2 * i) * rows + taps(2 * i + 1) * later for i in range(3)]
    pairs.append(taps(6) * rows)
    low = pairs[0] + pltpu.roll(pairs[1], 2, 0)
    high = pairs[2] + pltpu.roll(pairs[3], 2, 0)
    return rounded(low + pltpu.roll(high, 4, 0))


def row_index(count):
    return lax.broadcasted_iota(jnp.int32, (count, LANES), 0)


def own_lanes(place_ref, k):
    return pl.ds(pl.multiple_of((place_ref[0] ^ k) * LANES, LANES), LANES)


def first_link(place_ref):
    return 2 + 2 * (place_ref[0] & 1)


def pack_block(k, v, q_last, taps, out_ref):
    rows = k.shape[0]
    row = row_index(TILE)
    gated = short_conv_rolled(k, lambda j: taps(1, j)) * short_conv_rolled(
        v, lambda j: taps(2, j)
    )
    out_ref[:TILE, :] = jnp.where(row < 6, k[:TILE], gated[:TILE]).astype(jnp.bfloat16)
    out_ref[TILE:rows, :] = gated[TILE:].astype(jnp.bfloat16)
    edge = jnp.where(row < 6, v[:TILE], v[rows - TILE :])
    edge = jnp.where((row >= 6) & (row < 10), pltpu.roll(q_last, 12, 0), edge)
    out_ref[rows : rows + TILE, :] = edge.astype(jnp.bfloat16)
    half = jnp.where(row_index(8) < 2, pltpu.roll(q_last[8:], 2, 0), k[rows - 8 :])
    out_ref[rows + TILE :, :] = half.astype(jnp.bfloat16)


def chip_order(place_ref):
    first = first_link(place_ref)
    return (0, first, 6 - first, 6)


def pack_one(place_ref, kv_ref, q_ref, taps_ref, chip, p, out_ref):
    lanes = pl.ds(pl.multiple_of(((place_ref[0] & 1) ^ p) * LANES, LANES), LANES)
    owner = own_lanes(place_ref, chip_order(place_ref)[chip] ^ p)
    pack_block(
        kv_ref[chip, 0, :, lanes].astype(jnp.float32),
        kv_ref[chip, 1, :, lanes].astype(jnp.float32),
        q_ref[:, owner].astype(jnp.float32),
        lambda s, j: taps_ref[s, j : j + 1, owner],
        out_ref,
    )


def pack_first_kernel(
    place_ref, streams_ref, taps_hbm_ref, core_ref, first_ref, kv_ref, q_ref, taps_ref, sems
):
    rows = streams_ref.shape[1]
    order = chip_order(place_ref)
    shared = [
        pltpu.make_async_copy(taps_hbm_ref, taps_ref, sems.at[4]),
        pltpu.make_async_copy(
            streams_ref.at[0, pl.ds(rows - TILE, TILE), :], q_ref, sems.at[5]
        ),
    ]
    copies = {}
    for i in (1, 0, 3, 2):
        chip = (place_ref[0] ^ order[i]) >> 1
        lanes = pl.ds(pl.multiple_of(chip * (2 * LANES), 2 * LANES), 2 * LANES)
        copies[i] = pltpu.make_async_copy(
            streams_ref.at[pl.ds(1, 2), :, lanes], kv_ref.at[i], sems.at[i]
        )
        copies[i].start()
        if i == 1:
            for copy in shared:
                copy.start()
    for copy in shared:
        copy.wait()
    for i, p, out_ref in (
        (1, 0, first_ref.at[0]),
        (1, 1, first_ref.at[1]),
        (0, 1, core_ref.at[0]),
        (3, 1, core_ref.at[1]),
    ):
        if p == 0 or i != 1:
            copies[i].wait()
        pack_one(place_ref, kv_ref, q_ref, taps_ref, i, p, out_ref)
    copies[2].wait()


def pack_second_kernel(place_ref, kv_ref, q_ref, taps_ref, second_ref, far_ref):
    for i, p, out_ref in (
        (2, 0, second_ref.at[0]),
        (2, 1, second_ref.at[1]),
        (3, 0, far_ref),
    ):
        pack_one(place_ref, kv_ref, q_ref, taps_ref, i, p, out_ref)


def pack_own_kernel(place_ref, kv_ref, q_ref, taps_ref, beside_ref, own_ref):
    pack_one(place_ref, kv_ref, q_ref, taps_ref, 0, 0, own_ref)


def spectrum_kernel(quarter, part, view_ref, beside_ref, out_ref):
    blocks = view_ref.shape[0] // (2 * LANES)
    per = quarter // LANES
    scale = 1.0 / (blocks * LANES)
    row = lax.broadcasted_iota(jnp.int32, (quarter + TILE, 2 * quarter), 0)
    col = lax.broadcasted_iota(jnp.int32, (quarter + TILE, 2 * quarter), 1)
    ahead = (col < quarter) & (row == col)
    back = (col >= quarter) & (row + col == 2 * quarter)
    turn = jnp.where(ahead | back, 1.0, 0.0).astype(jnp.bfloat16)

    def columns(part, start):
        return [
            view_ref[pl.ds(2 * (start + i) + part, LANES, stride=2 * blocks), :]
            for i in range(per)
        ]

    sign = 1.0 if part == 0 else -1.0
    heads, tails = [], []
    for m in range(4):
        start = 2 * per * m
        values = columns(part, start) + [sign * v for v in columns(part, blocks - start - per)]
        values = jnp.concatenate(values, axis=1)
        high = values.astype(jnp.bfloat16)
        low = (values - high.astype(jnp.float32)).astype(jnp.bfloat16)
        both = lax.dot_general(
            turn,
            jnp.concatenate([high, low], axis=0),
            (((1,), (1,)), ((), ())),
            preferred_element_type=jnp.float32,
        )
        folded = (both[: quarter + 8, :LANES] + both[: quarter + 8, LANES:]) * scale
        out_ref[m, :, :] = folded
        heads.append(folded[0:1])
        tails.append(folded[quarter : quarter + 1])
    for m in range(4):
        out_ref[m, 0:1, :] = 0.5 * (heads[m] + sign * heads[(4 - m) % 4])
        out_ref[m, quarter : quarter + 1, :] = 0.5 * (tails[m] + sign * tails[3 - m])


def forward_kernel(pair_ref, beside_ref, out_ref):
    out_ref[...] = pair_ref[1]


def merge_kernel(far_ref, core_ref, out_ref):
    out_ref[0] = far_ref[...]
    out_ref[1] = core_ref[1]


def received(place_ref, own, core, first, second, first_on, second_on, far):
    link = first_link(place_ref)
    blocks = [
        (0, own),
        (1, core.at[0]),
        (link, first.at[0]),
        (6 - link, second.at[0]),
        ((6 - link) ^ 1, first_on),
        (link ^ 1, second_on),
    ]
    if far is not None:
        blocks += [(6, far.at[0]), (7, far.at[1])]
    return blocks


def filter_kernel(
    place_ref,
    own_ref,
    core_ref,
    first_ref,
    second_ref,
    first_on_ref,
    second_on_ref,
    far_ref,
    taps_ref,
    real_ref,
    imag_ref,
    ahead_ref,
    back_ref,
    twist_ref,
    own_out,
    core_out,
    first_out,
    second_out,
    far_out,
    msg_ref,
    x_ref,
    z_ref,
    q_ref,
):
    shards = msg_ref.shape[0]
    rows = own_ref.shape[0] - 24
    quarter = back_ref.shape[0]
    blocks = received(
        place_ref,
        own_ref,
        core_ref,
        first_ref,
        second_ref,
        first_on_ref,
        second_on_ref,
        far_ref,
    )
    for k, block in blocks:
        msg_ref[place_ref[0] ^ k] = block[...]
    row = row_index(TILE)
    own = own_lanes(place_ref, 0)

    before = None
    for s in range(shards):
        top = msg_ref[s, :TILE, :].astype(jnp.float32)
        edge = msg_ref[s, rows : rows + TILE, :].astype(jnp.float32)
        half = msg_ref[s, rows + TILE :, :].astype(jnp.float32)
        if before is None:
            above_k = above_v = jnp.zeros_like(edge)
            halo = jnp.zeros_like(half)
        else:
            above_v, half_before = before
            above_k = jnp.concatenate([half_before, half_before], axis=0)
            halo = jnp.where(
                row_index(8) < 6,
                pltpu.roll(above_v, 12, 0)[:8],
                pltpu.roll(half_before, 6, 0),
            )
        k_conv = short_conv_rolled(
            jnp.where(row < 8, top, above_k), lambda j: taps_ref[1, j : j + 1, own]
        )
        v_conv = short_conv_rolled(
            jnp.where(row < 8, edge, above_v), lambda j: taps_ref[2, j : j + 1, own]
        )
        x_ref[s * rows : s * rows + TILE, :] = jnp.where(row < 6, rounded(k_conv * v_conv), top)
        x_ref[s * rows + TILE : (s + 1) * rows, :] = msg_ref[s, TILE:rows, :].astype(jnp.float32)
        msg_ref[s, rows : rows + 8, :] = halo.astype(jnp.bfloat16)
        before = (edge, half)

    x = jnp.concatenate(
        [x_ref[pl.ds(a, quarter, stride=4), :].astype(jnp.bfloat16) for a in range(4)], axis=1
    )
    x = jnp.concatenate([x, x], axis=0)

    def combine(real, imag, g, count):
        u = []
        for a in range(4):
            if a == 0:
                u.append((real[0], imag[0]))
                continue
            wr = jnp.broadcast_to(twist_ref[g : g + count, 2 * a : 2 * a + 1], (count, LANES))
            wi = jnp.broadcast_to(
                twist_ref[g : g + count, 2 * a + 1 : 2 * a + 2], (count, LANES)
            )
            u.append((real[a] * wr - imag[a] * wi, real[a] * wi + imag[a] * wr, wr, wi))

        def four(v, sign):
            er, ei = v[0][0] + v[2][0], v[0][1] + v[2][1]
            dr, di = v[0][0] - v[2][0], v[0][1] - v[2][1]
            pr, pi = v[1][0] + v[3][0], v[1][1] + v[3][1]
            qr, qi = v[1][0] - v[3][0], v[1][1] - v[3][1]
            if sign < 0:
                one, three = (dr + qi, di - qr), (dr - qi, di + qr)
            else:
                one, three = (dr - qi, di + qr), (dr + qi, di - qr)
            return [(er + pr, ei + pi), one, (er - pr, ei - pi), three]

        freq = four(u, -1)
        prod = []
        for m in range(4):
            hr = real_ref[m, g : g + count, :]
            hi = imag_ref[m, g : g + count, :]
            xr, xi = freq[m]
            prod.append((xr * hr - xi * hi, xr * hi + xi * hr))
        v = four(prod, 1)
        out = [v[0]]
        for a in range(1, 4):
            wr, wi = u[a][2], u[a][3]
            vr, vi = v[a]
            out.append((vr * wr + vi * wi, vi * wr - vr * wi))
        return out

    part = quarter // 2
    y = None
    for half in range(2):
        base = half * quarter
        count = quarter + half * TILE
        z_ref[base : base + count, :] = jnp.dot(
            ahead_ref[base : base + count, :], x, preferred_element_type=jnp.float32
        )
        for g in range(0, part, TILE):
            real, imag = [
                [
                    z_ref[start : start + TILE, a * LANES : (a + 1) * LANES]
                    for a in range(4)
                ]
                for start in (base + g, base + part + g)
            ]
            out = combine(real, imag, half * part + g, TILE)
            for a in range(4):
                lanes = slice(a * LANES, (a + 1) * LANES)
                for i in range(2):
                    start = base + i * part + g
                    q_ref[start : start + TILE, lanes] = out[a][i].astype(jnp.bfloat16)
        term = jnp.dot(
            back_ref[:, base : base + quarter],
            q_ref[base : base + quarter, :],
            preferred_element_type=jnp.float32,
        )
        y = term if y is None else y + term
    real = [z_ref[2 * quarter : 2 * quarter + 8, a * LANES : (a + 1) * LANES] for a in range(4)]
    last = combine(real, [jnp.zeros_like(r) for r in real], quarter, 8)

    sign = 1.0 - 2.0 * (row_index(quarter) % 2).astype(jnp.float32)
    for a in range(4):
        x_ref[pl.ds(a, quarter, stride=4), :] = (
            y[:, a * LANES : (a + 1) * LANES] + sign * last[a][0][0:1, :]
        )
    link = first_link(place_ref)
    for k, out_ref in (
        (link, first_out.at[0]),
        (link ^ 1, first_out.at[1]),
        (6 - link, second_out.at[0]),
        ((6 - link) ^ 1, second_out.at[1]),
        (6, far_out),
        (7, core_out.at[1]),
        (0, own_out),
        (1, core_out.at[0]),
    ):
        target = place_ref[0] ^ k
        start = pl.multiple_of(target * rows, rows)
        out_ref[:rows, :] = x_ref[pl.ds(start, rows), :].astype(jnp.bfloat16)
        out_ref[rows:, :] = msg_ref[target, rows : rows + 8, :]


def silu(values):
    return values / (1.0 + jnp.exp(-values))


def gain_kernel(q_ref, taps_ref, residual_ref, out_ref):
    for c in range(out_ref.shape[1] // LANES):
        lanes = slice(c * LANES, (c + 1) * LANES)
        conv = short_conv_rolled(
            q_ref[0, :, lanes].astype(jnp.float32), lambda j: taps_ref[0, j : j + 1, lanes]
        )
        out_ref[:, lanes] = silu(residual_ref[:, lanes].astype(jnp.float32)) * conv


def mixed_block(msg, lanes, gain_ref, residual_ref, q_ref, taps_ref, out_ref):
    rows = residual_ref.shape[0]
    row = row_index(TILE)
    halo = msg[rows:, :].astype(jnp.float32)
    window = jnp.where(
        row < 8, q_ref[0, :TILE, lanes].astype(jnp.float32), jnp.concatenate([halo, halo], axis=0)
    )
    conv = short_conv_rolled(window, lambda j: taps_ref[0, j : j + 1, lanes])
    resid = residual_ref[:TILE, lanes].astype(jnp.float32)
    gain = jnp.where(row < 6, silu(resid) * conv, gain_ref[:TILE, lanes])
    out_ref[:TILE, :] = (resid + gain * msg[:TILE, :].astype(jnp.float32)).astype(jnp.bfloat16)
    out_ref[TILE:, :] = (
        residual_ref[TILE:, lanes].astype(jnp.float32)
        + gain_ref[TILE:, lanes] * msg[TILE:rows, :].astype(jnp.float32)
    ).astype(jnp.bfloat16)


def mix_and_store(place_ref, blocks, rest, out_ref, held, sems):
    copies = []
    for i, (k, block) in enumerate(blocks):
        lanes = own_lanes(place_ref, k)
        mixed_block(block, lanes, *rest, held.at[i])
        copy = pltpu.make_async_copy(held.at[i], out_ref.at[:, lanes], sems.at[i])
        copy.start()
        copies.append(copy)
    for copy in copies:
        copy.wait()


def mix_early_kernel(place_ref, own, core, first, second, first_on, *refs):
    rest, (out_ref, held, sems) = refs[:4], refs[4:]
    blocks = received(place_ref, own, core, first, second, first_on, None, None)[:5]
    mix_and_store(place_ref, blocks, rest, out_ref, held, sems)


def mix_late_kernel(place_ref, early_ref, second_on, far, *refs):
    rest, (out_ref, held, sems) = refs[:4], refs[4:]
    blocks = [(1 ^ first_link(place_ref), second_on), (6, far.at[0]), (7, far.at[1])]
    mix_and_store(place_ref, blocks, rest, out_ref, held, sems)


def filter_tables(quarter):
    index = np.arange(quarter)
    angle = 2.0 * np.pi * (index[:, None] * index[None, :] % (2 * quarter)) / (2 * quarter)
    alternate = np.zeros((TILE, quarter))
    alternate[0] = 1.0 - 2.0 * (index % 2)
    part = quarter // 2
    cos, sin = np.cos(angle), -np.sin(angle)
    table = np.concatenate([cos[:part], sin[:part], cos[part:], sin[part:], alternate], axis=0)
    high = table.astype(jnp.bfloat16)
    low = (table - high.astype(np.float64)).astype(jnp.bfloat16)
    ahead = np.concatenate([high, low], axis=1)
    back = np.ascontiguousarray(high[: 2 * quarter].T)
    g = np.arange(quarter + 8)[:, None]
    a = np.arange(4)[None, :]
    turn = 2.0 * np.pi * (g * a) / (8 * quarter)
    twist = np.stack([np.cos(turn), -np.sin(turn)], axis=-1).reshape(quarter + 8, 8)
    return ahead, back, twist.astype(np.float32)


def estimate(flops, moved):
    return pl.CostEstimate(flops=flops, bytes_accessed=moved, transcendentals=0)


def swap(block, partner):
    return lax.ppermute(block, "seq", [(i, partner(i)) for i in range(8)])


def arranged(kernel, name, shape, *blocks, spaces=(pltpu.VMEM, pltpu.VMEM)):
    return pl.pallas_call(
        kernel,
        in_specs=[pl.BlockSpec(memory_space=space) for space in spaces],
        out_shape=jax.ShapeDtypeStruct(shape, jnp.bfloat16),
        compiler_params=pltpu.CompilerParams(vmem_limit_bytes=VMEM_LIMIT),
        cost_estimate=estimate(1 << 10, 1 << 16),
        name=name,
    )(*blocks)


def exchanged(core, first, second, far):
    core = swap(core, lambda i: i ^ 1)
    first = swap(first, lambda i: i ^ (2 + 2 * (i & 1)))
    second = swap(second, lambda i: i ^ (4 - 2 * (i & 1)))
    merged = arranged(merge_kernel, "merge", core.shape, far, core)
    return core, first, second, swap(merged, lambda i: i ^ 6), merged


def sibling_block(pair, beside):
    return arranged(
        forward_kernel, "forward", pair.shape[1:], pair, beside, spaces=(pltpu.VMEM, pl.ANY)
    )


def local_kernels(streams, short_taps, spectrum, residual):
    rows, channels = residual.shape
    shards = lax.axis_size("seq")
    length = rows * shards
    quarter = length // 4
    params = pltpu.CompilerParams(vmem_limit_bytes=VMEM_LIMIT)
    place = lax.axis_index("seq").astype(jnp.int32).reshape(1)
    scalar = pl.BlockSpec(memory_space=pltpu.SMEM)
    vector = pl.BlockSpec(memory_space=pltpu.VMEM)
    hbm = pl.BlockSpec(memory_space=pltpu.HBM)
    half = lambda *shape: jax.ShapeDtypeStruct(shape, jnp.bfloat16)
    full = lambda *shape: jax.ShapeDtypeStruct(shape, jnp.float32)
    sent = rows + 24
    core, first, kv, q_last, taps = pl.pallas_call(
        pack_first_kernel,
        in_specs=[scalar, hbm, hbm],
        out_shape=[
            half(2, sent, LANES),
            half(2, sent, LANES),
            half(4, 2, rows, 2 * LANES),
            half(TILE, channels),
            full(*short_taps.shape),
        ],
        scratch_shapes=[pltpu.SemaphoreType.DMA((6,))],
        compiler_params=params,
        cost_estimate=estimate(1 << 30, 1 << 20),
        name="pack_first",
    )(
        place,
        pltpu.with_memory_space_constraint(streams, pltpu.HBM),
        pltpu.with_memory_space_constraint(short_taps, pltpu.HBM),
    )
    second, far = pl.pallas_call(
        pack_second_kernel,
        in_specs=[scalar] + [vector] * 3,
        out_shape=[half(2, sent, LANES), half(sent, LANES)],
        compiler_params=params,
        cost_estimate=estimate(1 << 30, 1 << 20),
        name="pack_second",
    )(place, kv, q_last, taps)
    blocks = 2 * length // LANES
    view = jnp.transpose(spectrum.reshape(LANES, 2, blocks, LANES), (0, 2, 1, 3)).reshape(
        2 * blocks * LANES, LANES
    )
    core, first, second, far, merged = exchanged(core, first, second, far)

    def spectrum_part(part, beside):
        return pl.pallas_call(
            functools.partial(spectrum_kernel, quarter, part),
            in_specs=[vector, pl.BlockSpec(memory_space=pl.ANY)],
            out_shape=full(4, quarter + 8, LANES),
            compiler_params=params,
            cost_estimate=estimate(1 << (32 - 20 * part), 1 << 22),
            name="spectrum",
        )(view, beside)

    real = spectrum_part(0, merged)
    first_block = sibling_block(first, real)
    first_on = swap(first_block, lambda i: i ^ 1)
    second_on = swap(sibling_block(second, real), lambda i: i ^ 1)
    imag = spectrum_part(1, first_on)
    own = pl.pallas_call(
        pack_own_kernel,
        in_specs=[scalar] + [vector] * 3 + [pl.BlockSpec(memory_space=pl.ANY)],
        out_shape=half(sent, LANES),
        compiler_params=params,
        cost_estimate=estimate(1 << 22, 1 << 20),
        name="pack_own",
    )(place, kv, q_last, taps, first_block)
    ahead, back_table, twist = filter_tables(quarter)
    back = rows + 8
    own, *sent_back = pl.pallas_call(
        filter_kernel,
        in_specs=[scalar] + [vector] * 13,
        out_shape=[half(back, LANES)] + [half(2, back, LANES)] * 3 + [half(back, LANES)],
        scratch_shapes=[
            pltpu.VMEM((shards, sent, LANES), jnp.bfloat16),
            pltpu.VMEM((length, LANES), jnp.float32),
            pltpu.VMEM((2 * quarter + TILE, 4 * LANES), jnp.float32),
            pltpu.VMEM((2 * quarter, 4 * LANES), jnp.bfloat16),
        ],
        compiler_params=params,
        cost_estimate=estimate(1 << 30, 1 << 22),
        name="filter",
    )(
        place,
        own,
        core,
        first,
        second,
        first_on,
        second_on,
        far,
        taps,
        real,
        imag,
        ahead,
        back_table,
        twist,
    )
    whole = lambda *shape: pl.BlockSpec(shape, lambda i: (0,) * len(shape))
    gain = pl.pallas_call(
        gain_kernel,
        grid=(1,),
        in_specs=[
            whole(1, rows, channels),
            whole(*short_taps.shape),
            whole(rows, channels),
        ],
        out_specs=whole(rows, channels),
        out_shape=full(rows, channels),
        compiler_params=params,
        cost_estimate=estimate(1 << 32, 1 << 20),
        name="gain",
    )(streams, taps, residual)
    core, first, second, far, _ = exchanged(*sent_back)
    first_on, second_on = [
        swap(sibling_block(pair, gain), lambda i: i ^ 1) for pair in (first, second)
    ]
    rest = (gain, residual, streams, taps)
    stored = dict(
        out_specs=hbm,
        out_shape=half(rows, channels),
        compiler_params=params,
        cost_estimate=estimate(1 << 20, 1 << 20),
    )
    early = pl.pallas_call(
        mix_early_kernel,
        in_specs=[scalar] + [vector] * 9,
        scratch_shapes=[
            pltpu.VMEM((5, rows, LANES), jnp.bfloat16),
            pltpu.SemaphoreType.DMA((5,)),
        ],
        name="mix_early",
        **stored,
    )(place, own, core, first, second, first_on, *rest)
    return pl.pallas_call(
        mix_late_kernel,
        in_specs=[scalar, hbm] + [vector] * 6,
        scratch_shapes=[
            pltpu.VMEM((3, rows, LANES), jnp.bfloat16),
            pltpu.SemaphoreType.DMA((3,)),
        ],
        input_output_aliases={1: 0},
        name="mix_late",
        **stored,
    )(place, early, second_on, far, *rest)


def local(streams, short_taps, spectrum, residual):
    rows, channels = residual.shape
    shards = lax.axis_size("seq")
    length = rows * shards
    fits = (
        channels == shards * LANES
        and rows % TILE == 0
        and rows >= 2 * TILE
        and length % (4 * LANES) == 0
        and length <= 2048
        and short_taps.shape[1] == 7
        and shards == 8
    )
    if fits:
        return local_kernels(streams, short_taps, spectrum, residual)
    return local_general(streams, short_taps, spectrum, residual)


def solution(mesh):
    placed = (
        P(None, "seq", "chan"),
        P(None, None, "chan"),
        P(("chan", "seq"), None, None),
        P("seq", "chan"),
    )
    return jax.shard_map(
        local, mesh=mesh, in_specs=placed, out_specs=P("seq", "chan"), check_vma=False
    )
```

```python
import functools
import math

import jax
import jax.numpy as jnp
import numpy as np
from jax import lax
from jax.experimental import pallas as pl
from jax.experimental.pallas import tpu as pltpu
from jax.sharding import PartitionSpec as P

LANES = 128
TILE = 16
VMEM_LIMIT = 16 * 1024 * 1024


def passed_along(block, axis, distance):
    devices = range(lax.axis_size(axis))
    route = [(i - distance, i) for i in devices if i - distance in devices]
    return lax.ppermute(block, axis, route)


def section_sizes(length_all):
    power = length_all.bit_length() - 1
    first = (power + 2) // 3
    second = (power - first + 1) // 2
    third = power - first - second
    result = [2**first, 2**second]
    result.append(2**third)
    return result


def matmul_high(left, right):
    return jnp.dot(left, right, precision=lax.Precision.HIGHEST, preferred_element_type=jnp.float32)


def section_high(table, values):
    return jnp.einsum(
        "ka,cab->ckb",
        table,
        values,
        precision=lax.Precision.HIGHEST,
        preferred_element_type=jnp.float32,
    )


def dft_table(order, direction):
    index = jnp.arange(order, dtype=jnp.int32)
    product = index[:, None] * index[None, :] % order
    angle = direction * 2.0 * math.pi * product.astype(jnp.float32) / order
    return (jnp.cos(angle), jnp.sin(angle))


def transform(real_part, imag_part, factors, direction):
    columns, length_now = real_part.shape
    first = factors[0]
    table_cos, table_sin = dft_table(first, direction)
    if len(factors) == 1:
        real_out = matmul_high(real_part, table_cos) - matmul_high(imag_part, table_sin)
        imag_out = matmul_high(imag_part, table_cos) + matmul_high(real_part, table_sin)
        return (real_out, imag_out)
    rest = length_now // first
    real_wide = real_part.reshape(columns, first, rest)
    if imag_part is None:
        section_real = section_high(table_cos, real_wide)
        section_imag = section_high(table_sin, real_wide)
    else:
        imag_wide = imag_part.reshape(columns, first, rest)
        section_real = section_high(table_cos, real_wide) - section_high(table_sin, imag_wide)
        section_imag = section_high(table_cos, imag_wide) + section_high(table_sin, real_wide)
    outer = jnp.arange(first, dtype=jnp.int32)[:, None]
    inner = jnp.arange(rest, dtype=jnp.int32)[None, :]
    twist = (
        direction * 2.0 * math.pi * (outer * inner % length_now).astype(jnp.float32) / length_now
    )
    twist_cos = jnp.cos(twist)[None, :, :]
    twist_sin = jnp.sin(twist)[None, :, :]
    turned_real = (section_real * twist_cos - section_imag * twist_sin).reshape(
        columns * first, rest
    )
    turned_imag = (section_real * twist_sin + section_imag * twist_cos).reshape(
        columns * first, rest
    )
    real_out, imag_out = transform(turned_real, turned_imag, factors[1:], direction)
    real_out = jnp.transpose(real_out.reshape(columns, first, rest), (0, 2, 1)).reshape(
        columns, length_now
    )
    imag_out = jnp.transpose(imag_out.reshape(columns, first, rest), (0, 2, 1)).reshape(
        columns, length_now
    )
    return (real_out, imag_out)


def long_filter(gated_rows, spectrum):
    columns, length_all = gated_rows.shape
    padded = jnp.concatenate(
        [gated_rows.astype(jnp.float32), jnp.zeros((columns, length_all), jnp.float32)], axis=1
    )
    factors = section_sizes(2 * length_all)
    freq_real, freq_imag = transform(padded, None, factors, -1.0)
    spec_real = spectrum[:, 0, :]
    spec_imag = spectrum[:, 1, :]
    prod_real = freq_real * spec_real - freq_imag * spec_imag
    prod_imag = freq_real * spec_imag + freq_imag * spec_real
    back_real, back_imag = transform(prod_real, prod_imag, factors, 1.0)
    return (back_real[:, :length_all] / (2 * length_all)).astype(jnp.bfloat16)


def local_general(streams, short_taps, spectrum, residual):
    row_count = streams.shape[1]
    channels = streams.shape[2]
    span = short_taps.shape[1] - 1
    rim_rows = passed_along(streams[:, row_count - span :, :], "seq", 1)
    extended = jnp.concatenate([rim_rows, streams], axis=1)
    total = jnp.zeros((3, row_count, channels), jnp.float32)
    for offset in range(span + 1):
        total = total + short_taps[:, offset, None, :] * extended[
            :, span - offset : span - offset + row_count, :
        ].astype(jnp.float32)
    convolved = total.astype(jnp.bfloat16)
    q_conv = convolved[0]
    k_conv = convolved[1]
    v_conv = convolved[2]
    seq_devices = lax.axis_size("seq")
    owned_count = channels // seq_devices
    length_all = row_count * seq_devices
    gated = (k_conv.astype(jnp.float32) * v_conv.astype(jnp.float32)).astype(jnp.bfloat16)
    owned = lax.all_to_all(
        gated.reshape(row_count, seq_devices, owned_count),
        "seq",
        split_axis=1,
        concat_axis=0,
        tiled=True,
    )
    gated_whole = owned.reshape(length_all, owned_count)
    filtered = jnp.transpose(long_filter(jnp.transpose(gated_whole), spectrum))
    returned = lax.all_to_all(
        filtered.reshape(length_all, 1, owned_count), "seq", split_axis=0, concat_axis=1, tiled=True
    )
    filtered_local = returned.reshape(row_count, channels)
    resid = residual.astype(jnp.float32)
    mixed = resid + jax.nn.silu(resid) * q_conv.astype(jnp.float32) * filtered_local.astype(
        jnp.float32
    )
    return mixed.astype(jnp.bfloat16)


def rounded(values):
    return values.astype(jnp.bfloat16).astype(jnp.float32)


def short_conv_rolled(rows, taps):
    later = pltpu.roll(rows, 1, 0)
    pairs = [taps(2 * i) * rows + taps(2 * i + 1) * later for i in range(3)]
    pairs.append(taps(6) * rows)
    low = pairs[0] + pltpu.roll(pairs[1], 2, 0)
    high = pairs[2] + pltpu.roll(pairs[3], 2, 0)
    return rounded(low + pltpu.roll(high, 4, 0))


def row_index(count):
    return lax.broadcasted_iota(jnp.int32, (count, LANES), 0)


def own_lanes(place_ref, k):
    return pl.ds(pl.multiple_of((place_ref[0] ^ k) * LANES, LANES), LANES)


def first_link(place_ref):
    return 2 + 2 * (place_ref[0] & 1)


def pack_block(k, v, q_last, taps, out_ref):
    rows = k.shape[0]
    row = row_index(TILE)
    gated = short_conv_rolled(k, lambda j: taps(1, j)) * short_conv_rolled(
        v, lambda j: taps(2, j)
    )
    out_ref[:TILE, :] = jnp.where(row < 6, k[:TILE], gated[:TILE]).astype(jnp.bfloat16)
    out_ref[TILE:rows, :] = gated[TILE:].astype(jnp.bfloat16)
    edge = jnp.where(row < 6, v[:TILE], v[rows - TILE :])
    edge = jnp.where((row >= 6) & (row < 10), pltpu.roll(q_last, 12, 0), edge)
    out_ref[rows : rows + TILE, :] = edge.astype(jnp.bfloat16)
    half = jnp.where(row_index(8) < 2, pltpu.roll(q_last[8:], 2, 0), k[rows - 8 :])
    out_ref[rows + TILE :, :] = jnp.concatenate([half, half], axis=0).astype(jnp.bfloat16)


def chip_order(place_ref):
    first = first_link(place_ref)
    return (0, first, 6 - first, 6)


def pack_one(place_ref, kv_ref, q_ref, taps_ref, chip, p, out_ref):
    lanes = pl.ds(pl.multiple_of(((place_ref[0] & 1) ^ p) * LANES, LANES), LANES)
    owner = own_lanes(place_ref, chip_order(place_ref)[chip] ^ p)
    pack_block(
        kv_ref[chip, 0, :, lanes].astype(jnp.float32),
        kv_ref[chip, 1, :, lanes].astype(jnp.float32),
        q_ref[:, owner].astype(jnp.float32),
        lambda s, j: taps_ref[s, j : j + 1, owner],
        out_ref,
    )


def pack_first_kernel(
    place_ref, streams_ref, taps_hbm_ref, core_ref, first_ref, kv_ref, q_ref, taps_ref, sems
):
    rows = streams_ref.shape[1]
    order = chip_order(place_ref)
    shared = [
        pltpu.make_async_copy(taps_hbm_ref, taps_ref, sems.at[4]),
        pltpu.make_async_copy(
            streams_ref.at[0, pl.ds(rows - TILE, TILE), :], q_ref, sems.at[5]
        ),
    ]
    copies = {}
    for i in (1, 0, 3, 2):
        chip = (place_ref[0] ^ order[i]) >> 1
        lanes = pl.ds(pl.multiple_of(chip * (2 * LANES), 2 * LANES), 2 * LANES)
        copies[i] = pltpu.make_async_copy(
            streams_ref.at[pl.ds(1, 2), :, lanes], kv_ref.at[i], sems.at[i]
        )
        copies[i].start()
        if i == 1:
            for copy in shared:
                copy.start()
    for copy in shared:
        copy.wait()
    for i, p, out_ref in (
        (1, 0, first_ref.at[0]),
        (1, 1, first_ref.at[1]),
        (0, 1, core_ref.at[0]),
        (3, 1, core_ref.at[1]),
    ):
        if p == 0 or i != 1:
            copies[i].wait()
        pack_one(place_ref, kv_ref, q_ref, taps_ref, i, p, out_ref)
    copies[2].wait()


def pack_second_kernel(place_ref, kv_ref, q_ref, taps_ref, second_ref, far_ref):
    for i, p, out_ref in (
        (2, 0, second_ref.at[0]),
        (2, 1, second_ref.at[1]),
        (3, 0, far_ref),
    ):
        pack_one(place_ref, kv_ref, q_ref, taps_ref, i, p, out_ref)


def pack_own_kernel(place_ref, kv_ref, q_ref, taps_ref, beside_ref, own_ref):
    pack_one(place_ref, kv_ref, q_ref, taps_ref, 0, 0, own_ref)


def spectrum_kernel(quarter, part, view_ref, beside_ref, out_ref):
    blocks = view_ref.shape[0] // (2 * LANES)
    per = quarter // LANES
    scale = 1.0 / (blocks * LANES)
    row = lax.broadcasted_iota(jnp.int32, (quarter + TILE, 2 * quarter), 0)
    col = lax.broadcasted_iota(jnp.int32, (quarter + TILE, 2 * quarter), 1)
    ahead = (col < quarter) & (row == col)
    back = (col >= quarter) & (row + col == 2 * quarter)
    turn = jnp.where(ahead | back, 1.0, 0.0).astype(jnp.bfloat16)

    def columns(part, start):
        return [
            view_ref[pl.ds(2 * (start + i) + part, LANES, stride=2 * blocks), :]
            for i in range(per)
        ]

    sign = 1.0 if part == 0 else -1.0
    heads, tails = [], []
    for m in range(4):
        start = 2 * per * m
        values = columns(part, start) + [sign * v for v in columns(part, blocks - start - per)]
        values = jnp.concatenate(values, axis=1)
        high = values.astype(jnp.bfloat16)
        low = (values - high.astype(jnp.float32)).astype(jnp.bfloat16)
        both = lax.dot_general(
            turn,
            jnp.concatenate([high, low], axis=0),
            (((1,), (1,)), ((), ())),
            preferred_element_type=jnp.float32,
        )
        folded = (both[: quarter + 8, :LANES] + both[: quarter + 8, LANES:]) * scale
        out_ref[m, :, :] = folded
        heads.append(folded[0:1])
        tails.append(folded[quarter : quarter + 1])
    for m in range(4):
        out_ref[m, 0:1, :] = 0.5 * (heads[m] + sign * heads[(4 - m) % 4])
        out_ref[m, quarter : quarter + 1, :] = 0.5 * (tails[m] + sign * tails[3 - m])


def forward_kernel(pair_ref, beside_ref, out_ref):
    out_ref[...] = pair_ref[1]


def merge_kernel(far_ref, core_ref, out_ref):
    out_ref[0] = far_ref[...]
    out_ref[1] = core_ref[1]


def received(place_ref, own, core, first, second, first_on, second_on, far):
    link = first_link(place_ref)
    blocks = [
        (0, own),
        (1, core.at[0]),
        (link, first.at[0]),
        (6 - link, second.at[0]),
        ((6 - link) ^ 1, first_on),
        (link ^ 1, second_on),
    ]
    if far is not None:
        blocks += [(6, far.at[0]), (7, far.at[1])]
    return blocks


def filter_kernel(
    place_ref,
    own_ref,
    core_ref,
    first_ref,
    second_ref,
    first_on_ref,
    second_on_ref,
    far_ref,
    taps_ref,
    real_ref,
    imag_ref,
    ahead_ref,
    back_ref,
    twist_ref,
    own_out,
    core_out,
    first_out,
    second_out,
    far_out,
    edge_ref,
    halo_ref,
    x_ref,
    z_ref,
    q_ref,
):
    shards = edge_ref.shape[0]
    rows = own_ref.shape[0] - 2 * TILE
    quarter = back_ref.shape[0]
    blocks = received(
        place_ref,
        own_ref,
        core_ref,
        first_ref,
        second_ref,
        first_on_ref,
        second_on_ref,
        far_ref,
    )
    for k, block in blocks:
        source = place_ref[0] ^ k
        start = pl.multiple_of(source * rows, rows)
        x_ref[pl.ds(start, rows), :] = block[:rows, :].astype(jnp.float32)
        edge_ref[source] = block[rows:, :].astype(jnp.float32)
    row = row_index(TILE)
    own = own_lanes(place_ref, 0)

    before = None
    for s in range(shards):
        top = x_ref[s * rows : s * rows + TILE, :]
        edge = edge_ref[s, :TILE, :]
        half = edge_ref[s, TILE : TILE + 8, :]
        if before is None:
            above_k = above_v = jnp.zeros_like(edge)
            halo = jnp.zeros_like(half)
        else:
            above_v, half_before = before
            above_k = jnp.concatenate([half_before, half_before], axis=0)
            halo = jnp.where(
                row_index(8) < 6,
                pltpu.roll(above_v, 12, 0)[:8],
                pltpu.roll(half_before, 6, 0),
            )
        k_conv = short_conv_rolled(
            jnp.where(row < 8, top, above_k), lambda j: taps_ref[1, j : j + 1, own]
        )
        v_conv = short_conv_rolled(
            jnp.where(row < 8, edge, above_v), lambda j: taps_ref[2, j : j + 1, own]
        )
        x_ref[s * rows : s * rows + TILE, :] = jnp.where(row < 6, rounded(k_conv * v_conv), top)
        halo = jnp.concatenate([halo, halo], axis=0)
        halo_ref[s] = halo.astype(jnp.bfloat16)
        before = (edge, half)

    x = jnp.concatenate(
        [x_ref[pl.ds(a, quarter, stride=4), :].astype(jnp.bfloat16) for a in range(4)], axis=1
    )
    x = jnp.concatenate([x, x], axis=0)

    def combine(real, imag, g, count):
        u = []
        for a in range(4):
            if a == 0:
                u.append((real[0], imag[0]))
                continue
            wr = jnp.broadcast_to(twist_ref[g : g + count, 2 * a : 2 * a + 1], (count, LANES))
            wi = jnp.broadcast_to(
                twist_ref[g : g + count, 2 * a + 1 : 2 * a + 2], (count, LANES)
            )
            u.append((real[a] * wr - imag[a] * wi, real[a] * wi + imag[a] * wr, wr, wi))

        def four(v, sign):
            er, ei = v[0][0] + v[2][0], v[0][1] + v[2][1]
            dr, di = v[0][0] - v[2][0], v[0][1] - v[2][1]
            pr, pi = v[1][0] + v[3][0], v[1][1] + v[3][1]
            qr, qi = v[1][0] - v[3][0], v[1][1] - v[3][1]
            if sign < 0:
                one, three = (dr + qi, di - qr), (dr - qi, di + qr)
            else:
                one, three = (dr - qi, di + qr), (dr + qi, di - qr)
            return [(er + pr, ei + pi), one, (er - pr, ei - pi), three]

        freq = four(u, -1)
        prod = []
        for m in range(4):
            hr = real_ref[m, g : g + count, :]
            hi = imag_ref[m, g : g + count, :]
            xr, xi = freq[m]
            prod.append((xr * hr - xi * hi, xr * hi + xi * hr))
        v = four(prod, 1)
        out = [v[0]]
        for a in range(1, 4):
            wr, wi = u[a][2], u[a][3]
            vr, vi = v[a]
            out.append((vr * wr + vi * wi, vi * wr - vr * wi))
        return out

    part = quarter // 2
    y = None
    for half in range(2):
        base = half * quarter
        count = quarter + half * TILE
        z_ref[base : base + count, :] = jnp.dot(
            ahead_ref[base : base + count, :], x, preferred_element_type=jnp.float32
        )
        for g in range(0, part, TILE):
            real, imag = [
                [
                    z_ref[start : start + TILE, a * LANES : (a + 1) * LANES]
                    for a in range(4)
                ]
                for start in (base + g, base + part + g)
            ]
            out = combine(real, imag, half * part + g, TILE)
            for a in range(4):
                lanes = slice(a * LANES, (a + 1) * LANES)
                for i in range(2):
                    start = base + i * part + g
                    q_ref[start : start + TILE, lanes] = out[a][i].astype(jnp.bfloat16)
        term = jnp.dot(
            back_ref[:, base : base + quarter],
            q_ref[base : base + quarter, :],
            preferred_element_type=jnp.float32,
        )
        y = term if y is None else y + term
    real = [z_ref[2 * quarter : 2 * quarter + 8, a * LANES : (a + 1) * LANES] for a in range(4)]
    last = combine(real, [jnp.zeros_like(r) for r in real], quarter, 8)

    sign = 1.0 - 2.0 * (row_index(quarter) % 2).astype(jnp.float32)
    for a in range(4):
        x_ref[pl.ds(a, quarter, stride=4), :] = (
            y[:, a * LANES : (a + 1) * LANES] + sign * last[a][0][0:1, :]
        )
    link = first_link(place_ref)
    for k, out_ref in (
        (link, first_out.at[0]),
        (link ^ 1, first_out.at[1]),
        (6 - link, second_out.at[0]),
        ((6 - link) ^ 1, second_out.at[1]),
        (6, far_out),
        (7, core_out.at[1]),
        (0, own_out),
        (1, core_out.at[0]),
    ):
        target = place_ref[0] ^ k
        start = pl.multiple_of(target * rows, rows)
        out_ref[:rows, :] = x_ref[pl.ds(start, rows), :].astype(jnp.bfloat16)
        out_ref[rows:, :] = halo_ref[target]


def silu(values):
    return values / (1.0 + jnp.exp(-values))


def gain_kernel(q_ref, taps_ref, residual_ref, out_ref):
    for c in range(out_ref.shape[1] // LANES):
        lanes = slice(c * LANES, (c + 1) * LANES)
        conv = short_conv_rolled(
            q_ref[0, :, lanes].astype(jnp.float32), lambda j: taps_ref[0, j : j + 1, lanes]
        )
        out_ref[:, lanes] = silu(residual_ref[:, lanes].astype(jnp.float32)) * conv


def mixed_block(msg, lanes, gain_ref, residual_ref, q_ref, taps_ref, out_ref):
    rows = residual_ref.shape[0]
    row = row_index(TILE)
    halo = msg[rows:, :].astype(jnp.float32)
    window = jnp.where(
        row < 8, q_ref[0, :TILE, lanes].astype(jnp.float32), halo
    )
    conv = short_conv_rolled(window, lambda j: taps_ref[0, j : j + 1, lanes])
    resid = residual_ref[:TILE, lanes].astype(jnp.float32)
    gain = jnp.where(row < 6, silu(resid) * conv, gain_ref[:TILE, lanes])
    out_ref[:TILE, :] = (resid + gain * msg[:TILE, :].astype(jnp.float32)).astype(jnp.bfloat16)
    out_ref[TILE:, :] = (
        residual_ref[TILE:, lanes].astype(jnp.float32)
        + gain_ref[TILE:, lanes] * msg[TILE:rows, :].astype(jnp.float32)
    ).astype(jnp.bfloat16)


def mix_and_store(place_ref, blocks, rest, out_ref, held, sems):
    copies = []
    for i, (k, block) in enumerate(blocks):
        lanes = own_lanes(place_ref, k)
        mixed_block(block, lanes, *rest, held.at[i])
        copy = pltpu.make_async_copy(held.at[i], out_ref.at[:, lanes], sems.at[i])
        copy.start()
        copies.append(copy)
    for copy in copies:
        copy.wait()


def mix_early_kernel(place_ref, own, core, first, second, first_on, *refs):
    rest, (out_ref, held, sems) = refs[:4], refs[4:]
    blocks = received(place_ref, own, core, first, second, first_on, None, None)[:5]
    mix_and_store(place_ref, blocks, rest, out_ref, held, sems)


def mix_late_kernel(place_ref, early_ref, second_on, far, *refs):
    rest, (out_ref, held, sems) = refs[:4], refs[4:]
    blocks = [(1 ^ first_link(place_ref), second_on), (6, far.at[0]), (7, far.at[1])]
    mix_and_store(place_ref, blocks, rest, out_ref, held, sems)


def filter_tables(quarter):
    index = np.arange(quarter)
    angle = 2.0 * np.pi * (index[:, None] * index[None, :] % (2 * quarter)) / (2 * quarter)
    alternate = np.zeros((TILE, quarter))
    alternate[0] = 1.0 - 2.0 * (index % 2)
    part = quarter // 2
    cos, sin = np.cos(angle), -np.sin(angle)
    table = np.concatenate([cos[:part], sin[:part], cos[part:], sin[part:], alternate], axis=0)
    high = table.astype(jnp.bfloat16)
    low = (table - high.astype(np.float64)).astype(jnp.bfloat16)
    ahead = np.concatenate([high, low], axis=1)
    back = np.ascontiguousarray(high[: 2 * quarter].T)
    g = np.arange(quarter + 8)[:, None]
    a = np.arange(4)[None, :]
    turn = 2.0 * np.pi * (g * a) / (8 * quarter)
    twist = np.stack([np.cos(turn), -np.sin(turn)], axis=-1).reshape(quarter + 8, 8)
    return ahead, back, twist.astype(np.float32)


def estimate(flops, moved):
    return pl.CostEstimate(flops=flops, bytes_accessed=moved, transcendentals=0)


def swap(block, partner):
    return lax.ppermute(block, "seq", [(i, partner(i)) for i in range(8)])


def arranged(kernel, name, shape, *blocks, spaces=(pltpu.VMEM, pltpu.VMEM)):
    return pl.pallas_call(
        kernel,
        in_specs=[pl.BlockSpec(memory_space=space) for space in spaces],
        out_shape=jax.ShapeDtypeStruct(shape, jnp.bfloat16),
        compiler_params=pltpu.CompilerParams(vmem_limit_bytes=VMEM_LIMIT),
        cost_estimate=estimate(1 << 10, 1 << 16),
        name=name,
    )(*blocks)


def exchanged(core, first, second, far):
    core = swap(core, lambda i: i ^ 1)
    first = swap(first, lambda i: i ^ (2 + 2 * (i & 1)))
    second = swap(second, lambda i: i ^ (4 - 2 * (i & 1)))
    merged = arranged(merge_kernel, "merge", core.shape, far, core)
    return core, first, second, swap(merged, lambda i: i ^ 6), merged


def sibling_block(pair, beside):
    return arranged(
        forward_kernel, "forward", pair.shape[1:], pair, beside, spaces=(pltpu.VMEM, pl.ANY)
    )


def local_kernels(streams, short_taps, spectrum, residual):
    rows, channels = residual.shape
    shards = lax.axis_size("seq")
    length = rows * shards
    quarter = length // 4
    params = pltpu.CompilerParams(vmem_limit_bytes=VMEM_LIMIT)
    place = lax.axis_index("seq").astype(jnp.int32).reshape(1)
    scalar = pl.BlockSpec(memory_space=pltpu.SMEM)
    vector = pl.BlockSpec(memory_space=pltpu.VMEM)
    hbm = pl.BlockSpec(memory_space=pltpu.HBM)
    half = lambda *shape: jax.ShapeDtypeStruct(shape, jnp.bfloat16)
    full = lambda *shape: jax.ShapeDtypeStruct(shape, jnp.float32)
    sent = rows + 2 * TILE
    core, first, kv, q_last, taps = pl.pallas_call(
        pack_first_kernel,
        in_specs=[scalar, hbm, hbm],
        out_shape=[
            half(2, sent, LANES),
            half(2, sent, LANES),
            half(4, 2, rows, 2 * LANES),
            half(TILE, channels),
            full(*short_taps.shape),
        ],
        scratch_shapes=[pltpu.SemaphoreType.DMA((6,))],
        compiler_params=params,
        cost_estimate=estimate(1 << 30, 1 << 20),
        name="pack_first",
    )(
        place,
        pltpu.with_memory_space_constraint(streams, pltpu.HBM),
        pltpu.with_memory_space_constraint(short_taps, pltpu.HBM),
    )
    second, far = pl.pallas_call(
        pack_second_kernel,
        in_specs=[scalar] + [vector] * 3,
        out_shape=[half(2, sent, LANES), half(sent, LANES)],
        compiler_params=params,
        cost_estimate=estimate(1 << 30, 1 << 20),
        name="pack_second",
    )(place, kv, q_last, taps)
    blocks = 2 * length // LANES
    view = jnp.transpose(spectrum.reshape(LANES, 2, blocks, LANES), (0, 2, 1, 3)).reshape(
        2 * blocks * LANES, LANES
    )
    core, first, second, far, merged = exchanged(core, first, second, far)

    def spectrum_part(part, beside):
        return pl.pallas_call(
            functools.partial(spectrum_kernel, quarter, part),
            in_specs=[vector, pl.BlockSpec(memory_space=pl.ANY)],
            out_shape=full(4, quarter + 8, LANES),
            compiler_params=params,
            cost_estimate=estimate(1 << (32 - 20 * part), 1 << 22),
            name="spectrum",
        )(view, beside)

    real = spectrum_part(0, merged)
    first_block = sibling_block(first, real)
    first_on = swap(first_block, lambda i: i ^ 1)
    second_on = swap(sibling_block(second, real), lambda i: i ^ 1)
    imag = spectrum_part(1, first_on)
    own = pl.pallas_call(
        pack_own_kernel,
        in_specs=[scalar] + [vector] * 3 + [pl.BlockSpec(memory_space=pl.ANY)],
        out_shape=half(sent, LANES),
        compiler_params=params,
        cost_estimate=estimate(1 << 22, 1 << 20),
        name="pack_own",
    )(place, kv, q_last, taps, first_block)
    ahead, back_table, twist = filter_tables(quarter)
    back = rows + TILE
    own, *sent_back = pl.pallas_call(
        filter_kernel,
        in_specs=[scalar] + [vector] * 13,
        out_shape=[half(back, LANES)] + [half(2, back, LANES)] * 3 + [half(back, LANES)],
        scratch_shapes=[
            pltpu.VMEM((shards, sent - rows, LANES), jnp.float32),
            pltpu.VMEM((shards, back - rows, LANES), jnp.bfloat16),
            pltpu.VMEM((length, LANES), jnp.float32),
            pltpu.VMEM((2 * quarter + TILE, 4 * LANES), jnp.float32),
            pltpu.VMEM((2 * quarter, 4 * LANES), jnp.bfloat16),
        ],
        compiler_params=params,
        cost_estimate=estimate(1 << 30, 1 << 22),
        name="filter",
    )(
        place,
        own,
        core,
        first,
        second,
        first_on,
        second_on,
        far,
        taps,
        real,
        imag,
        ahead,
        back_table,
        twist,
    )
    whole = lambda *shape: pl.BlockSpec(shape, lambda i: (0,) * len(shape))
    gain = pl.pallas_call(
        gain_kernel,
        grid=(1,),
        in_specs=[
            whole(1, rows, channels),
            whole(*short_taps.shape),
            whole(rows, channels),
        ],
        out_specs=whole(rows, channels),
        out_shape=full(rows, channels),
        compiler_params=params,
        cost_estimate=estimate(1 << 32, 1 << 20),
        name="gain",
    )(streams, taps, residual)
    core, first, second, far, _ = exchanged(*sent_back)
    first_on, second_on = [
        swap(sibling_block(pair, gain), lambda i: i ^ 1) for pair in (first, second)
    ]
    rest = (gain, residual, streams, taps)
    stored = dict(
        out_specs=hbm,
        out_shape=half(rows, channels),
        compiler_params=params,
        cost_estimate=estimate(1 << 20, 1 << 20),
    )
    early = pl.pallas_call(
        mix_early_kernel,
        in_specs=[scalar] + [vector] * 9,
        scratch_shapes=[
            pltpu.VMEM((5, rows, LANES), jnp.bfloat16),
            pltpu.SemaphoreType.DMA((5,)),
        ],
        name="mix_early",
        **stored,
    )(place, own, core, first, second, first_on, *rest)
    return pl.pallas_call(
        mix_late_kernel,
        in_specs=[scalar, hbm] + [vector] * 6,
        scratch_shapes=[
            pltpu.VMEM((3, rows, LANES), jnp.bfloat16),
            pltpu.SemaphoreType.DMA((3,)),
        ],
        input_output_aliases={1: 0},
        name="mix_late",
        **stored,
    )(place, early, second_on, far, *rest)


def local(streams, short_taps, spectrum, residual):
    rows, channels = residual.shape
    shards = lax.axis_size("seq")
    length = rows * shards
    fits = (
        channels == shards * LANES
        and rows % TILE == 0
        and rows >= 2 * TILE
        and length % (4 * LANES) == 0
        and length <= 2048
        and short_taps.shape[1] == 7
        and shards == 8
    )
    if fits:
        return local_kernels(streams, short_taps, spectrum, residual)
    return local_general(streams, short_taps, spectrum, residual)


def solution(mesh):
    placed = (
        P(None, "seq", "chan"),
        P(None, None, "chan"),
        P(("chan", "seq"), None, None),
        P("seq", "chan"),
    )
    return jax.shard_map(
        local, mesh=mesh, in_specs=placed, out_specs=P("seq", "chan"), check_vma=False
    )
```

```python
import functools
import math

import jax
import jax.numpy as jnp
import numpy as np
from jax import lax
from jax.experimental import pallas as pl
from jax.experimental.pallas import tpu as pltpu
from jax.sharding import PartitionSpec as P

LANES = 128
TILE = 16
VMEM_LIMIT = 16 * 1024 * 1024


def passed_along(block, axis, distance):
    devices = range(lax.axis_size(axis))
    route = [(i - distance, i) for i in devices if i - distance in devices]
    return lax.ppermute(block, axis, route)


def section_sizes(length_all):
    power = length_all.bit_length() - 1
    first = (power + 2) // 3
    second = (power - first + 1) // 2
    third = power - first - second
    result = [2**first, 2**second]
    result.append(2**third)
    return result


def matmul_high(left, right):
    return jnp.dot(left, right, precision=lax.Precision.HIGHEST, preferred_element_type=jnp.float32)


def section_high(table, values):
    return jnp.einsum(
        "ka,cab->ckb",
        table,
        values,
        precision=lax.Precision.HIGHEST,
        preferred_element_type=jnp.float32,
    )


def dft_table(order, direction):
    index = jnp.arange(order, dtype=jnp.int32)
    product = index[:, None] * index[None, :] % order
    angle = direction * 2.0 * math.pi * product.astype(jnp.float32) / order
    return (jnp.cos(angle), jnp.sin(angle))


def transform(real_part, imag_part, factors, direction):
    columns, length_now = real_part.shape
    first = factors[0]
    table_cos, table_sin = dft_table(first, direction)
    if len(factors) == 1:
        real_out = matmul_high(real_part, table_cos) - matmul_high(imag_part, table_sin)
        imag_out = matmul_high(imag_part, table_cos) + matmul_high(real_part, table_sin)
        return (real_out, imag_out)
    rest = length_now // first
    real_wide = real_part.reshape(columns, first, rest)
    if imag_part is None:
        section_real = section_high(table_cos, real_wide)
        section_imag = section_high(table_sin, real_wide)
    else:
        imag_wide = imag_part.reshape(columns, first, rest)
        section_real = section_high(table_cos, real_wide) - section_high(table_sin, imag_wide)
        section_imag = section_high(table_cos, imag_wide) + section_high(table_sin, real_wide)
    outer = jnp.arange(first, dtype=jnp.int32)[:, None]
    inner = jnp.arange(rest, dtype=jnp.int32)[None, :]
    twist = (
        direction * 2.0 * math.pi * (outer * inner % length_now).astype(jnp.float32) / length_now
    )
    twist_cos = jnp.cos(twist)[None, :, :]
    twist_sin = jnp.sin(twist)[None, :, :]
    turned_real = (section_real * twist_cos - section_imag * twist_sin).reshape(
        columns * first, rest
    )
    turned_imag = (section_real * twist_sin + section_imag * twist_cos).reshape(
        columns * first, rest
    )
    real_out, imag_out = transform(turned_real, turned_imag, factors[1:], direction)
    real_out = jnp.transpose(real_out.reshape(columns, first, rest), (0, 2, 1)).reshape(
        columns, length_now
    )
    imag_out = jnp.transpose(imag_out.reshape(columns, first, rest), (0, 2, 1)).reshape(
        columns, length_now
    )
    return (real_out, imag_out)


def long_filter(gated_rows, spectrum):
    columns, length_all = gated_rows.shape
    padded = jnp.concatenate(
        [gated_rows.astype(jnp.float32), jnp.zeros((columns, length_all), jnp.float32)], axis=1
    )
    factors = section_sizes(2 * length_all)
    freq_real, freq_imag = transform(padded, None, factors, -1.0)
    spec_real = spectrum[:, 0, :]
    spec_imag = spectrum[:, 1, :]
    prod_real = freq_real * spec_real - freq_imag * spec_imag
    prod_imag = freq_real * spec_imag + freq_imag * spec_real
    back_real, back_imag = transform(prod_real, prod_imag, factors, 1.0)
    return (back_real[:, :length_all] / (2 * length_all)).astype(jnp.bfloat16)


def local_general(streams, short_taps, spectrum, residual):
    row_count = streams.shape[1]
    channels = streams.shape[2]
    span = short_taps.shape[1] - 1
    rim_rows = passed_along(streams[:, row_count - span :, :], "seq", 1)
    extended = jnp.concatenate([rim_rows, streams], axis=1)
    total = jnp.zeros((3, row_count, channels), jnp.float32)
    for offset in range(span + 1):
        total = total + short_taps[:, offset, None, :] * extended[
            :, span - offset : span - offset + row_count, :
        ].astype(jnp.float32)
    convolved = total.astype(jnp.bfloat16)
    q_conv = convolved[0]
    k_conv = convolved[1]
    v_conv = convolved[2]
    seq_devices = lax.axis_size("seq")
    owned_count = channels // seq_devices
    length_all = row_count * seq_devices
    gated = (k_conv.astype(jnp.float32) * v_conv.astype(jnp.float32)).astype(jnp.bfloat16)
    owned = lax.all_to_all(
        gated.reshape(row_count, seq_devices, owned_count),
        "seq",
        split_axis=1,
        concat_axis=0,
        tiled=True,
    )
    gated_whole = owned.reshape(length_all, owned_count)
    filtered = jnp.transpose(long_filter(jnp.transpose(gated_whole), spectrum))
    returned = lax.all_to_all(
        filtered.reshape(length_all, 1, owned_count), "seq", split_axis=0, concat_axis=1, tiled=True
    )
    filtered_local = returned.reshape(row_count, channels)
    resid = residual.astype(jnp.float32)
    mixed = resid + jax.nn.silu(resid) * q_conv.astype(jnp.float32) * filtered_local.astype(
        jnp.float32
    )
    return mixed.astype(jnp.bfloat16)


def rounded(values):
    return values.astype(jnp.bfloat16).astype(jnp.float32)


def short_conv_rolled(rows, taps):
    later = pltpu.roll(rows, 1, 0)
    pairs = [taps(2 * i) * rows + taps(2 * i + 1) * later for i in range(3)]
    pairs.append(taps(6) * rows)
    low = pairs[0] + pltpu.roll(pairs[1], 2, 0)
    high = pairs[2] + pltpu.roll(pairs[3], 2, 0)
    return rounded(low + pltpu.roll(high, 4, 0))


def row_index(count):
    return lax.broadcasted_iota(jnp.int32, (count, LANES), 0)


def own_lanes(place_ref, k):
    return pl.ds(pl.multiple_of((place_ref[0] ^ k) * LANES, LANES), LANES)


def first_link(place_ref):
    return 2 + 2 * (place_ref[0] & 1)


def pack_block(k, v, q_last, taps, out_ref):
    rows = k.shape[0]
    row = row_index(TILE)
    gated = short_conv_rolled(k, lambda j: taps(1, j)) * short_conv_rolled(
        v, lambda j: taps(2, j)
    )
    out_ref[:TILE, :] = jnp.where(row < 6, k[:TILE], gated[:TILE]).astype(jnp.bfloat16)
    out_ref[TILE:rows, :] = gated[TILE:].astype(jnp.bfloat16)
    edge = jnp.where(row < 6, v[:TILE], v[rows - TILE :])
    edge = jnp.where((row >= 6) & (row < 10), pltpu.roll(q_last, 12, 0), edge)
    out_ref[rows : rows + TILE, :] = edge.astype(jnp.bfloat16)
    half = jnp.where(row_index(8) < 2, pltpu.roll(q_last[8:], 2, 0), k[rows - 8 :])
    out_ref[rows + TILE :, :] = jnp.concatenate([half, half], axis=0).astype(jnp.bfloat16)


def chip_order(place_ref):
    first = first_link(place_ref)
    return (0, first, 6 - first, 6)


def pack_one(place_ref, kv_ref, q_ref, taps_ref, chip, p, out_ref):
    lanes = pl.ds(pl.multiple_of(((place_ref[0] & 1) ^ p) * LANES, LANES), LANES)
    owner = own_lanes(place_ref, chip_order(place_ref)[chip] ^ p)
    pack_block(
        kv_ref[chip, 0, :, lanes].astype(jnp.float32),
        kv_ref[chip, 1, :, lanes].astype(jnp.float32),
        q_ref[:, owner].astype(jnp.float32),
        lambda s, j: taps_ref[s, j : j + 1, owner],
        out_ref,
    )


def pack_first_kernel(
    place_ref, streams_ref, taps_hbm_ref, core_ref, first_ref, kv_ref, q_ref, taps_ref, sems
):
    rows = streams_ref.shape[1]
    order = chip_order(place_ref)
    shared = [
        pltpu.make_async_copy(taps_hbm_ref, taps_ref, sems.at[4]),
        pltpu.make_async_copy(
            streams_ref.at[0, pl.ds(rows - TILE, TILE), :], q_ref, sems.at[5]
        ),
    ]
    copies = {}
    for i in (1, 0, 3, 2):
        chip = (place_ref[0] ^ order[i]) >> 1
        lanes = pl.ds(pl.multiple_of(chip * (2 * LANES), 2 * LANES), 2 * LANES)
        copies[i] = pltpu.make_async_copy(
            streams_ref.at[pl.ds(1, 2), :, lanes], kv_ref.at[i], sems.at[i]
        )
        copies[i].start()
        if i == 1:
            for copy in shared:
                copy.start()
    for copy in shared:
        copy.wait()
    for i, p, out_ref in (
        (1, 0, first_ref.at[0]),
        (1, 1, first_ref.at[1]),
        (0, 1, core_ref.at[0]),
        (3, 1, core_ref.at[1]),
    ):
        if p == 0 or i != 1:
            copies[i].wait()
        pack_one(place_ref, kv_ref, q_ref, taps_ref, i, p, out_ref)
    copies[2].wait()


def pack_second_kernel(place_ref, kv_ref, q_ref, taps_ref, second_ref, far_ref):
    for i, p, out_ref in (
        (2, 0, second_ref.at[0]),
        (2, 1, second_ref.at[1]),
        (3, 0, far_ref),
    ):
        pack_one(place_ref, kv_ref, q_ref, taps_ref, i, p, out_ref)


def pack_own_kernel(place_ref, kv_ref, q_ref, taps_ref, beside_ref, own_ref):
    pack_one(place_ref, kv_ref, q_ref, taps_ref, 0, 0, own_ref)


def spectrum_kernel(quarter, part, view_ref, beside_ref, out_ref):
    blocks = view_ref.shape[0] // (2 * LANES)
    per = quarter // LANES
    scale = 1.0 / (blocks * LANES)
    row = lax.broadcasted_iota(jnp.int32, (quarter + TILE, 2 * quarter), 0)
    col = lax.broadcasted_iota(jnp.int32, (quarter + TILE, 2 * quarter), 1)
    ahead = (col < quarter) & (row == col)
    back = (col >= quarter) & (row + col == 2 * quarter)
    turn = jnp.where(ahead | back, 1.0, 0.0).astype(jnp.bfloat16)

    def columns(part, start):
        return [
            view_ref[pl.ds(2 * (start + i) + part, LANES, stride=2 * blocks), :]
            for i in range(per)
        ]

    sign = 1.0 if part == 0 else -1.0
    heads, tails = [], []
    for m in range(4):
        start = 2 * per * m
        values = columns(part, start) + [sign * v for v in columns(part, blocks - start - per)]
        values = jnp.concatenate(values, axis=1)
        high = values.astype(jnp.bfloat16)
        low = (values - high.astype(jnp.float32)).astype(jnp.bfloat16)
        both = lax.dot_general(
            turn,
            jnp.concatenate([high, low], axis=0),
            (((1,), (1,)), ((), ())),
            preferred_element_type=jnp.float32,
        )
        folded = (both[: quarter + 8, :LANES] + both[: quarter + 8, LANES:]) * scale
        out_ref[m, :, :] = folded
        heads.append(folded[0:1])
        tails.append(folded[quarter : quarter + 1])
    for m in range(4):
        out_ref[m, 0:1, :] = 0.5 * (heads[m] + sign * heads[(4 - m) % 4])
        out_ref[m, quarter : quarter + 1, :] = 0.5 * (tails[m] + sign * tails[3 - m])


def forward_kernel(pair_ref, beside_ref, out_ref):
    out_ref[...] = pair_ref[1]


def merge_kernel(far_ref, core_ref, out_ref):
    out_ref[0] = far_ref[...]
    out_ref[1] = core_ref[1]


def received(place_ref, own, core, first, second, first_on, second_on, far):
    link = first_link(place_ref)
    blocks = [
        (0, own),
        (1, core.at[0]),
        (link, first.at[0]),
        (6 - link, second.at[0]),
        ((6 - link) ^ 1, first_on),
        (link ^ 1, second_on),
    ]
    if far is not None:
        blocks += [(6, far.at[0]), (7, far.at[1])]
    return blocks


def filter_kernel(
    place_ref,
    own_ref,
    core_ref,
    first_ref,
    second_ref,
    first_on_ref,
    second_on_ref,
    far_ref,
    taps_ref,
    real_ref,
    imag_ref,
    ahead_ref,
    back_ref,
    twist_ref,
    own_out,
    core_out,
    first_out,
    second_out,
    far_out,
    edge_ref,
    halo_ref,
    x_ref,
    z_ref,
    q_ref,
):
    shards = edge_ref.shape[0]
    rows = own_ref.shape[0] - 2 * TILE
    quarter = back_ref.shape[0]
    blocks = received(
        place_ref,
        own_ref,
        core_ref,
        first_ref,
        second_ref,
        first_on_ref,
        second_on_ref,
        far_ref,
    )
    for k, block in blocks:
        source = place_ref[0] ^ k
        start = pl.multiple_of(source * rows, rows)
        x_ref[pl.ds(start, rows), :] = block[:rows, :].astype(jnp.float32)
        edge_ref[source] = block[rows:, :].astype(jnp.float32)
    row = row_index(TILE)
    own = own_lanes(place_ref, 0)

    before = None
    for s in range(shards):
        top = x_ref[s * rows : s * rows + TILE, :]
        edge = edge_ref[s, :TILE, :]
        half = edge_ref[s, TILE : TILE + 8, :]
        if before is None:
            above_k = above_v = jnp.zeros_like(edge)
            halo = jnp.zeros_like(half)
        else:
            above_v, half_before = before
            above_k = jnp.concatenate([half_before, half_before], axis=0)
            halo = jnp.where(
                row_index(8) < 6,
                pltpu.roll(above_v, 12, 0)[:8],
                pltpu.roll(half_before, 6, 0),
            )
        k_conv = short_conv_rolled(
            jnp.where(row < 8, top, above_k), lambda j: taps_ref[1, j : j + 1, own]
        )
        v_conv = short_conv_rolled(
            jnp.where(row < 8, edge, above_v), lambda j: taps_ref[2, j : j + 1, own]
        )
        x_ref[s * rows : s * rows + TILE, :] = jnp.where(row < 6, rounded(k_conv * v_conv), top)
        halo = jnp.concatenate([halo, halo], axis=0)
        halo_ref[s] = halo.astype(jnp.bfloat16)
        before = (edge, half)

    x = jnp.concatenate(
        [x_ref[pl.ds(a, quarter, stride=4), :].astype(jnp.bfloat16) for a in range(4)], axis=1
    )
    x = jnp.concatenate([x, x], axis=0)

    def combine(real, imag, g, count):
        u = []
        for a in range(4):
            if a == 0:
                u.append((real[0], imag[0]))
                continue
            wr = twist_ref[2 * a - 2, g : g + count, :]
            wi = twist_ref[2 * a - 1, g : g + count, :]
            u.append((real[a] * wr - imag[a] * wi, real[a] * wi + imag[a] * wr, wr, wi))

        def four(v, sign):
            er, ei = v[0][0] + v[2][0], v[0][1] + v[2][1]
            dr, di = v[0][0] - v[2][0], v[0][1] - v[2][1]
            pr, pi = v[1][0] + v[3][0], v[1][1] + v[3][1]
            qr, qi = v[1][0] - v[3][0], v[1][1] - v[3][1]
            if sign < 0:
                one, three = (dr + qi, di - qr), (dr - qi, di + qr)
            else:
                one, three = (dr - qi, di + qr), (dr + qi, di - qr)
            return [(er + pr, ei + pi), one, (er - pr, ei - pi), three]

        freq = four(u, -1)
        prod = []
        for m in range(4):
            hr = real_ref[m, g : g + count, :]
            hi = imag_ref[m, g : g + count, :]
            xr, xi = freq[m]
            prod.append((xr * hr - xi * hi, xr * hi + xi * hr))
        v = four(prod, 1)
        out = [v[0]]
        for a in range(1, 4):
            wr, wi = u[a][2], u[a][3]
            vr, vi = v[a]
            out.append((vr * wr + vi * wi, vi * wr - vr * wi))
        return out

    part = quarter // 2
    y = None
    for half in range(2):
        base = half * quarter
        count = quarter + half * TILE
        z_ref[base : base + count, :] = jnp.dot(
            ahead_ref[base : base + count, :], x, preferred_element_type=jnp.float32
        )
        for g in range(0, part, TILE):
            real, imag = [
                [
                    z_ref[start : start + TILE, a * LANES : (a + 1) * LANES]
                    for a in range(4)
                ]
                for start in (base + g, base + part + g)
            ]
            out = combine(real, imag, half * part + g, TILE)
            for a in range(4):
                lanes = slice(a * LANES, (a + 1) * LANES)
                for i in range(2):
                    start = base + i * part + g
                    q_ref[start : start + TILE, lanes] = out[a][i].astype(jnp.bfloat16)
        term = jnp.dot(
            back_ref[:, base : base + quarter],
            q_ref[base : base + quarter, :],
            preferred_element_type=jnp.float32,
        )
        y = term if y is None else y + term
    real = [z_ref[2 * quarter : 2 * quarter + 8, a * LANES : (a + 1) * LANES] for a in range(4)]
    last = combine(real, [jnp.zeros_like(r) for r in real], quarter, 8)

    sign = 1.0 - 2.0 * (row_index(quarter) % 2).astype(jnp.float32)
    for a in range(4):
        x_ref[pl.ds(a, quarter, stride=4), :] = (
            y[:, a * LANES : (a + 1) * LANES] + sign * last[a][0][0:1, :]
        )
    link = first_link(place_ref)
    for k, out_ref in (
        (link, first_out.at[0]),
        (link ^ 1, first_out.at[1]),
        (6 - link, second_out.at[0]),
        ((6 - link) ^ 1, second_out.at[1]),
        (6, far_out),
        (7, core_out.at[1]),
        (0, own_out),
        (1, core_out.at[0]),
    ):
        target = place_ref[0] ^ k
        start = pl.multiple_of(target * rows, rows)
        out_ref[:rows, :] = x_ref[pl.ds(start, rows), :].astype(jnp.bfloat16)
        out_ref[rows:, :] = halo_ref[target]


def silu(values):
    return values / (1.0 + jnp.exp(-values))


def gain_kernel(q_ref, taps_ref, residual_ref, out_ref):
    for c in range(out_ref.shape[1] // LANES):
        lanes = slice(c * LANES, (c + 1) * LANES)
        conv = short_conv_rolled(
            q_ref[0, :, lanes].astype(jnp.float32), lambda j: taps_ref[0, j : j + 1, lanes]
        )
        out_ref[:, lanes] = silu(residual_ref[:, lanes].astype(jnp.float32)) * conv


def mixed_block(msg, lanes, gain_ref, residual_ref, q_ref, taps_ref, out_ref):
    rows = residual_ref.shape[0]
    row = row_index(TILE)
    halo = msg[rows:, :].astype(jnp.float32)
    window = jnp.where(
        row < 8, q_ref[0, :TILE, lanes].astype(jnp.float32), halo
    )
    conv = short_conv_rolled(window, lambda j: taps_ref[0, j : j + 1, lanes])
    resid = residual_ref[:TILE, lanes].astype(jnp.float32)
    gain = jnp.where(row < 6, silu(resid) * conv, gain_ref[:TILE, lanes])
    out_ref[:TILE, :] = (resid + gain * msg[:TILE, :].astype(jnp.float32)).astype(jnp.bfloat16)
    out_ref[TILE:, :] = (
        residual_ref[TILE:, lanes].astype(jnp.float32)
        + gain_ref[TILE:, lanes] * msg[TILE:rows, :].astype(jnp.float32)
    ).astype(jnp.bfloat16)


def mix_and_store(place_ref, blocks, rest, out_ref, held, sems):
    copies = []
    for i, (k, block) in enumerate(blocks):
        lanes = own_lanes(place_ref, k)
        mixed_block(block, lanes, *rest, held.at[i])
        copy = pltpu.make_async_copy(held.at[i], out_ref.at[:, lanes], sems.at[i])
        copy.start()
        copies.append(copy)
    for copy in copies:
        copy.wait()


def mix_early_kernel(place_ref, own, core, first, second, first_on, *refs):
    rest, (out_ref, held, sems) = refs[:4], refs[4:]
    blocks = received(place_ref, own, core, first, second, first_on, None, None)[:5]
    mix_and_store(place_ref, blocks, rest, out_ref, held, sems)


def mix_late_kernel(place_ref, early_ref, second_on, far, *refs):
    rest, (out_ref, held, sems) = refs[:4], refs[4:]
    blocks = [(1 ^ first_link(place_ref), second_on), (6, far.at[0]), (7, far.at[1])]
    mix_and_store(place_ref, blocks, rest, out_ref, held, sems)


def filter_tables(quarter):
    index = np.arange(quarter)
    angle = 2.0 * np.pi * (index[:, None] * index[None, :] % (2 * quarter)) / (2 * quarter)
    alternate = np.zeros((TILE, quarter))
    alternate[0] = 1.0 - 2.0 * (index % 2)
    part = quarter // 2
    cos, sin = np.cos(angle), -np.sin(angle)
    table = np.concatenate([cos[:part], sin[:part], cos[part:], sin[part:], alternate], axis=0)
    high = table.astype(jnp.bfloat16)
    low = (table - high.astype(np.float64)).astype(jnp.bfloat16)
    ahead = np.concatenate([high, low], axis=1)
    back = np.ascontiguousarray(high[: 2 * quarter].T)
    g = np.arange(quarter + 8)[:, None]
    a = np.arange(4)[None, :]
    turn = 2.0 * np.pi * (g * a) / (8 * quarter)
    twist = np.stack([np.cos(turn), -np.sin(turn)], axis=-1).reshape(quarter + 8, 8)
    twist = np.repeat(twist.T[2:, :, None], LANES, axis=2)
    return ahead, back, twist.astype(np.float32)


def estimate(flops, moved):
    return pl.CostEstimate(flops=flops, bytes_accessed=moved, transcendentals=0)


def swap(block, partner):
    return lax.ppermute(block, "seq", [(i, partner(i)) for i in range(8)])


def arranged(kernel, name, shape, *blocks, spaces=(pltpu.VMEM, pltpu.VMEM)):
    return pl.pallas_call(
        kernel,
        in_specs=[pl.BlockSpec(memory_space=space) for space in spaces],
        out_shape=jax.ShapeDtypeStruct(shape, jnp.bfloat16),
        compiler_params=pltpu.CompilerParams(vmem_limit_bytes=VMEM_LIMIT),
        cost_estimate=estimate(1 << 10, 1 << 16),
        name=name,
    )(*blocks)


def exchanged(core, first, second, far):
    core = swap(core, lambda i: i ^ 1)
    first = swap(first, lambda i: i ^ (2 + 2 * (i & 1)))
    second = swap(second, lambda i: i ^ (4 - 2 * (i & 1)))
    merged = arranged(merge_kernel, "merge", core.shape, far, core)
    return core, first, second, swap(merged, lambda i: i ^ 6), merged


def sibling_block(pair, beside):
    return arranged(
        forward_kernel, "forward", pair.shape[1:], pair, beside, spaces=(pltpu.VMEM, pl.ANY)
    )


def local_kernels(streams, short_taps, spectrum, residual):
    rows, channels = residual.shape
    shards = lax.axis_size("seq")
    length = rows * shards
    quarter = length // 4
    params = pltpu.CompilerParams(vmem_limit_bytes=VMEM_LIMIT)
    place = lax.axis_index("seq").astype(jnp.int32).reshape(1)
    scalar = pl.BlockSpec(memory_space=pltpu.SMEM)
    vector = pl.BlockSpec(memory_space=pltpu.VMEM)
    hbm = pl.BlockSpec(memory_space=pltpu.HBM)
    half = lambda *shape: jax.ShapeDtypeStruct(shape, jnp.bfloat16)
    full = lambda *shape: jax.ShapeDtypeStruct(shape, jnp.float32)
    sent = rows + 2 * TILE
    core, first, kv, q_last, taps = pl.pallas_call(
        pack_first_kernel,
        in_specs=[scalar, hbm, hbm],
        out_shape=[
            half(2, sent, LANES),
            half(2, sent, LANES),
            half(4, 2, rows, 2 * LANES),
            half(TILE, channels),
            full(*short_taps.shape),
        ],
        scratch_shapes=[pltpu.SemaphoreType.DMA((6,))],
        compiler_params=params,
        cost_estimate=estimate(1 << 30, 1 << 20),
        name="pack_first",
    )(
        place,
        pltpu.with_memory_space_constraint(streams, pltpu.HBM),
        pltpu.with_memory_space_constraint(short_taps, pltpu.HBM),
    )
    second, far = pl.pallas_call(
        pack_second_kernel,
        in_specs=[scalar] + [vector] * 3,
        out_shape=[half(2, sent, LANES), half(sent, LANES)],
        compiler_params=params,
        cost_estimate=estimate(1 << 30, 1 << 20),
        name="pack_second",
    )(place, kv, q_last, taps)
    blocks = 2 * length // LANES
    view = jnp.transpose(spectrum.reshape(LANES, 2, blocks, LANES), (0, 2, 1, 3)).reshape(
        2 * blocks * LANES, LANES
    )
    core, first, second, far, merged = exchanged(core, first, second, far)

    def spectrum_part(part, beside):
        return pl.pallas_call(
            functools.partial(spectrum_kernel, quarter, part),
            in_specs=[vector, pl.BlockSpec(memory_space=pl.ANY)],
            out_shape=full(4, quarter + 8, LANES),
            compiler_params=params,
            cost_estimate=estimate(1 << (32 - 20 * part), 1 << 22),
            name="spectrum",
        )(view, beside)

    real = spectrum_part(0, merged)
    first_block = sibling_block(first, real)
    first_on = swap(first_block, lambda i: i ^ 1)
    second_on = swap(sibling_block(second, real), lambda i: i ^ 1)
    imag = spectrum_part(1, first_on)
    own = pl.pallas_call(
        pack_own_kernel,
        in_specs=[scalar] + [vector] * 3 + [pl.BlockSpec(memory_space=pl.ANY)],
        out_shape=half(sent, LANES),
        compiler_params=params,
        cost_estimate=estimate(1 << 22, 1 << 20),
        name="pack_own",
    )(place, kv, q_last, taps, first_block)
    ahead, back_table, twist = filter_tables(quarter)
    back = rows + TILE
    own, *sent_back = pl.pallas_call(
        filter_kernel,
        in_specs=[scalar] + [vector] * 13,
        out_shape=[half(back, LANES)] + [half(2, back, LANES)] * 3 + [half(back, LANES)],
        scratch_shapes=[
            pltpu.VMEM((shards, sent - rows, LANES), jnp.float32),
            pltpu.VMEM((shards, back - rows, LANES), jnp.bfloat16),
            pltpu.VMEM((length, LANES), jnp.float32),
            pltpu.VMEM((2 * quarter + TILE, 4 * LANES), jnp.float32),
            pltpu.VMEM((2 * quarter, 4 * LANES), jnp.bfloat16),
        ],
        compiler_params=params,
        cost_estimate=estimate(1 << 30, 1 << 22),
        name="filter",
    )(
        place,
        own,
        core,
        first,
        second,
        first_on,
        second_on,
        far,
        taps,
        real,
        imag,
        ahead,
        back_table,
        twist,
    )
    whole = lambda *shape: pl.BlockSpec(shape, lambda i: (0,) * len(shape))
    gain = pl.pallas_call(
        gain_kernel,
        grid=(1,),
        in_specs=[
            whole(1, rows, channels),
            whole(*short_taps.shape),
            whole(rows, channels),
        ],
        out_specs=whole(rows, channels),
        out_shape=full(rows, channels),
        compiler_params=params,
        cost_estimate=estimate(1 << 32, 1 << 20),
        name="gain",
    )(streams, taps, residual)
    core, first, second, far, _ = exchanged(*sent_back)
    first_on, second_on = [
        swap(sibling_block(pair, gain), lambda i: i ^ 1) for pair in (first, second)
    ]
    rest = (gain, residual, streams, taps)
    stored = dict(
        out_specs=hbm,
        out_shape=half(rows, channels),
        compiler_params=params,
        cost_estimate=estimate(1 << 20, 1 << 20),
    )
    early = pl.pallas_call(
        mix_early_kernel,
        in_specs=[scalar] + [vector] * 9,
        scratch_shapes=[
            pltpu.VMEM((5, rows, LANES), jnp.bfloat16),
            pltpu.SemaphoreType.DMA((5,)),
        ],
        name="mix_early",
        **stored,
    )(place, own, core, first, second, first_on, *rest)
    return pl.pallas_call(
        mix_late_kernel,
        in_specs=[scalar, hbm] + [vector] * 6,
        scratch_shapes=[
            pltpu.VMEM((3, rows, LANES), jnp.bfloat16),
            pltpu.SemaphoreType.DMA((3,)),
        ],
        input_output_aliases={1: 0},
        name="mix_late",
        **stored,
    )(place, early, second_on, far, *rest)


def local(streams, short_taps, spectrum, residual):
    rows, channels = residual.shape
    shards = lax.axis_size("seq")
    length = rows * shards
    fits = (
        channels == shards * LANES
        and rows % TILE == 0
        and rows >= 2 * TILE
        and length % (4 * LANES) == 0
        and length <= 2048
        and short_taps.shape[1] == 7
        and shards == 8
    )
    if fits:
        return local_kernels(streams, short_taps, spectrum, residual)
    return local_general(streams, short_taps, spectrum, residual)


def solution(mesh):
    placed = (
        P(None, "seq", "chan"),
        P(None, None, "chan"),
        P(("chan", "seq"), None, None),
        P("seq", "chan"),
    )
    return jax.shard_map(
        local, mesh=mesh, in_specs=placed, out_specs=P("seq", "chan"), check_vma=False
    )
```
